32 devices in a mesh: groups: 2 (over x), mem: 8 (over z, y), tp: 2 (over core).
Axes of the slice: x: 2, y: 2, z: 4, core: 2. Of those that a mesh axis runs over, the one named last changes fastest.
Arguments:
- hidden: bfloat16 [128, 8192], P('groups', 'mem'), parts along dimension 0, may hold values from -6 to 6
- adapter: int32 [128], P('groups'), parts along dimension 0, may hold values from 0 to 31
- page_cache_slot: int32 [256], P('groups'), parts along dimension 0, may hold values from 0 to 127, as said below
- selection: int32 [128, 128], P('groups'), parts along dimension 0, may hold values from 0 to 1, as said below
- query_projection_weight: bfloat16 [8192, 8192], P('mem', 'tp'), may hold values from -0.0625 to 0.0625
- key_projection_weight: bfloat16 [8192, 1024], P('mem', 'tp'), may hold values from -0.0625 to 0.0625
- value_projection_weight: bfloat16 [8192, 1024], P('mem', 'tp'), may hold values from -0.0625 to 0.0625
- adapter_down_weight: bfloat16 [8192, 2048], P('mem'), may hold values from -0.0625 to 0.0625
- adapter_up_weight: bfloat16 [64, 32, 8192], P('mem', None, 'tp'), may hold values from -0.75 to 0.75
- output_projection_weight: bfloat16 [8192, 8192], P('tp', 'mem'), may hold values from -0.0625 to 0.0625
- prefix_key_cache: bfloat16 [256, 128, 1024], P(('groups', 'mem'), None, 'tp'), parts along dimension 0, may hold values from -60 to 60
- prefix_value_cache: bfloat16 [256, 128, 1024], P(('groups', 'mem'), None, 'tp'), parts along dimension 0, may hold values from -6 to 6
Outputs:
- attn_out: bfloat16 [128, 8192], P('groups', 'mem'), parts along dimension 0
The draws below stay inside these ranges and needn't reach their ends.
There are 2 independent parts, one for each index of `groups`. The reference program is written for one: setup_inputs(seed, part) draws one part's arguments, and reference() takes and returns one part's arrays. A program takes and returns all parts, laid end to end along the dimension named above; an argument that names none is the same for every part. Nothing has to cross between parts.
Inputs may be any that keep to these rules, and one draw needn't show every extreme that they name: A permutation: page p is held in cache slot page_cache_slot[p], and slot s lies with index s // 16 of mem. `selection`: every page is selected by 1 to 32 forks; on some index of mem every page held there is selected by exactly 32 forks. A fork may select no page.
All inputs are finite; a program needn't handle non-finite values.
Results may differ from the reference program's by a relative error of at most 0.006.
The reference program's roundings to bfloat16 on the way count: a program that leaves them out, or rounds other values in their place, can miss the bound.
Values may be sent and summed in bfloat16 or wider, within the bound.
No kernel may reach another device: no remote copies, remote signals or barrier semaphores. Data moves between devices by JAX's collectives and lax.ppermute only.
A program may use at most 128 MiB of HBM per device.

```python
import math
import jax
import jax.numpy as jnp
import numpy as np
from jax import lax

MODEL_WIDTH = 8192
QUERY_HEADS = 64
KV_HEADS = 8
HEAD_WIDTH = 128
ADAPTER_RANK = 64
ADAPTER_COUNT = 32
PAGE = 128
HOT = 32
PAGE_DEV = 16
FORKS = 64
PAGES = 128


def layout_tables(key):
    base = jax.random.fold_in(key, 4242)
    key_perm, key_count, key_hot, key_rank = jax.random.split(base, 4)
    page_cache_slot = jax.random.permutation(key_perm, PAGES).astype(jnp.int32)
    counts_slot = jax.random.randint(key_count, (PAGES,), 1, HOT + 1)
    devices_count = PAGES // PAGE_DEV
    hot_device = jax.random.randint(key_hot, (), 0, devices_count)
    slot_ids = jnp.arange(PAGES)
    counts_slot = jnp.where(slot_ids // PAGE_DEV == hot_device, HOT, counts_slot)
    counts_page = counts_slot[page_cache_slot]
    fork_orders = jax.vmap(lambda subkey: jax.random.permutation(subkey, FORKS))(jax.random.split(key_rank, PAGES))
    ranking = jnp.argsort(fork_orders, axis=1)
    chosen = (ranking < counts_page[:, None]).astype(jnp.int32)
    return (page_cache_slot, chosen.T)


def draw_page_cache_slot(key, part):
    return layout_tables(key)[0]


def draw_selection(key, part):
    return layout_tables(key)[1]


def draw_prefix_key_cache(key, part):
    key_value = jax.random.fold_in(jax.random.fold_in(key, 77), 1)
    raw = jax.random.normal(key_value, (PAGES, PAGE, KV_HEADS * HEAD_WIDTH))
    return jnp.clip(raw, -6.0, 6.0).astype(jnp.bfloat16)


def with_ends(array, own_key, smallest, high):
    dims = array.shape
    spot = [jax.random.randint(jax.random.fold_in(own_key, axis), (), 0, dims[axis]) for axis in range(len(dims))]
    array = array.at[tuple(spot)].set(smallest)
    longest = dims.index(max(dims))
    spot[longest] = (spot[longest] + 1) % dims[longest]
    return array.at[tuple(spot)].set(high)


def block_scale(rng, shape, pieces, least, high):
    level = 1.0
    for dim, blocks in pieces:
        steps = jax.random.uniform(jax.random.fold_in(jax.random.fold_in(rng, 6), dim), (blocks,), jnp.float32, least / len(pieces), high / len(pieces))
        level = level * jnp.repeat(jnp.exp(steps), shape[dim] // blocks).reshape((-1,) + (1,) * (len(shape) - 1 - dim))
    return level


def rank_table(amount, skew):
    loads = [(1 << 20) // math.isqrt(standing ** skew) + 1 for standing in range(1, amount + 1)]
    scale = 1 + sum(loads) // (1 << 30)
    return np.cumsum(np.array([max(1, weight // scale) for weight in loads]))


def skewed_ids(stream_key, dims, number_of, skew):
    table = rank_table(number_of, skew)
    ticket = jax.random.randint(jax.random.fold_in(stream_key, 1), dims, 0, int(table[number_of - 1]))
    rank = jnp.searchsorted(jnp.asarray(table, jnp.int32), ticket, side="right")
    return jax.random.permutation(jax.random.fold_in(stream_key, 2), number_of)[rank].astype(jnp.int32)


def normal_values(key, extent, width, bound, pieces=(), kind=jnp.bfloat16):
    entries = width * jax.random.normal(key, extent, jnp.float32)
    if pieces:
        entries = entries * block_scale(key, extent, pieces, -0.22, 0.18)
    return jnp.clip(entries, -bound, bound).astype(kind)


def setup_inputs(seed: int = 0, part: int = 0) -> dict:
    key_of = jax.random.split(jax.random.key(seed), 13)
    part_keys = jax.random.split(jax.random.fold_in(key_of[12], part), 13)
    return {
        "hidden": normal_values(part_keys[0], (FORKS, MODEL_WIDTH), 1.0, 6.0, ((1, 8),)),
        "adapter": with_ends(skewed_ids(part_keys[1], (FORKS,), ADAPTER_COUNT, 2), jax.random.fold_in(part_keys[1], 3), 0, ADAPTER_COUNT - 1).astype(jnp.int32),
        "page_cache_slot": draw_page_cache_slot(jax.random.fold_in(jax.random.fold_in(key_of[12], part), 71), part),
        "selection": draw_selection(jax.random.fold_in(jax.random.fold_in(key_of[12], part), 71), part),
        "query_projection_weight": normal_values(key_of[4], (MODEL_WIDTH, QUERY_HEADS * HEAD_WIDTH), MODEL_WIDTH ** -0.5, 0.0625, ((0, 8), (1, 2))),
        "key_projection_weight": normal_values(key_of[5], (MODEL_WIDTH, KV_HEADS * HEAD_WIDTH), MODEL_WIDTH ** -0.5, 0.0625, ((0, 8), (1, 2))),
        "value_projection_weight": normal_values(key_of[6], (MODEL_WIDTH, KV_HEADS * HEAD_WIDTH), MODEL_WIDTH ** -0.5, 0.0625, ((0, 8), (1, 2))),
        "adapter_down_weight": normal_values(key_of[7], (MODEL_WIDTH, ADAPTER_COUNT * ADAPTER_RANK), MODEL_WIDTH ** -0.5, 0.0625, ((0, 8),)),
        "adapter_up_weight": normal_values(key_of[8], (ADAPTER_RANK, ADAPTER_COUNT, QUERY_HEADS * HEAD_WIDTH), ADAPTER_RANK ** -0.5, 0.75, ((0, 8), (2, 2))),
        "output_projection_weight": normal_values(key_of[9], (QUERY_HEADS * HEAD_WIDTH, MODEL_WIDTH), (QUERY_HEADS * HEAD_WIDTH) ** -0.5, 0.0625, ((0, 2), (1, 8))),
        "prefix_key_cache": draw_prefix_key_cache(jax.random.fold_in(jax.random.fold_in(key_of[12], part), 71), part),
        "prefix_value_cache": normal_values(part_keys[11], (PAGES, PAGE, KV_HEADS * HEAD_WIDTH), 1.0, 6.0, ((0, 8), (2, 2))),
    }


adapter_scale = 1.0
neg_floor = -1e30


def reference(hidden, adapter, page_cache_slot, selection, query_projection_weight, key_projection_weight, value_projection_weight, adapter_down_weight, adapter_up_weight, output_projection_weight, prefix_key_cache, prefix_value_cache):
    every_fork_list = hidden.shape[0]
    group_size = QUERY_HEADS // KV_HEADS
    score_scale = HEAD_WIDTH ** -0.5
    onehot = (adapter[:, None] == jnp.arange(ADAPTER_COUNT, dtype=jnp.int32)[None, :]).astype(jnp.float32)
    down_activations = jnp.dot(hidden, adapter_down_weight, preferred_element_type=jnp.float32).reshape(every_fork_list, ADAPTER_COUNT, ADAPTER_RANK)
    rank_acts = jnp.sum(down_activations * onehot[:, None, :].transpose(0, 2, 1), axis=1).astype(jnp.bfloat16)
    spread_factor = (rank_acts.astype(jnp.float32)[:, :, None] * onehot[:, None, :]).astype(jnp.bfloat16)
    spread_factor = spread_factor.reshape(every_fork_list, ADAPTER_RANK * ADAPTER_COUNT)
    adapter_query_delta = jnp.dot(spread_factor, adapter_up_weight.reshape(ADAPTER_RANK * ADAPTER_COUNT, QUERY_HEADS * HEAD_WIDTH), preferred_element_type=jnp.float32)
    query_vectors = (jnp.dot(hidden, query_projection_weight, preferred_element_type=jnp.float32) + adapter_scale * adapter_query_delta).astype(jnp.bfloat16)
    key_new = jnp.dot(hidden, key_projection_weight, preferred_element_type=jnp.float32).astype(jnp.bfloat16)
    value_new = jnp.dot(hidden, value_projection_weight, preferred_element_type=jnp.float32).astype(jnp.bfloat16)
    page_total = page_cache_slot.shape[0]
    page_of_slot = jnp.zeros((page_total,), jnp.int32).at[page_cache_slot].set(jnp.arange(page_total, dtype=jnp.int32))
    query_pad = jnp.concatenate([query_vectors, jnp.zeros((1, QUERY_HEADS * HEAD_WIDTH), jnp.bfloat16)], axis=0)
    query_pad = query_pad.reshape(every_fork_list + 1, KV_HEADS, group_size, HEAD_WIDTH)

    def visit(state_now, scan_items):
        maxima, totals, summed = state_now
        page_keys, page_values, page_id = scan_items
        column = jnp.take(selection, page_id, axis=1)
        chosen = jnp.nonzero(column > 0, size=HOT, fill_value=every_fork_list)[0].astype(jnp.int32)
        picked = query_pad[chosen].astype(jnp.float32)
        keys_f = page_keys.reshape(PAGE, KV_HEADS, HEAD_WIDTH).astype(jnp.float32)
        values_f = page_values.reshape(PAGE, KV_HEADS, HEAD_WIDTH).astype(jnp.float32)
        scores = jnp.einsum('hkgd,tkd->hkgt', picked, keys_f) * score_scale
        page_peak = jnp.max(scores, axis=-1)
        weights = jnp.exp(scores - page_peak[..., None]).astype(jnp.bfloat16).astype(jnp.float32)
        masses = jnp.sum(weights, axis=-1)
        partial_value = jnp.einsum('hkgt,tkd->hkgd', weights, values_f)
        old_max = maxima[chosen]
        new_max = jnp.maximum(old_max, page_peak)
        keep_old = jnp.exp(old_max - new_max)
        fresh_w = jnp.exp(page_peak - new_max)
        totals = totals.at[chosen].set(totals[chosen] * keep_old + masses * fresh_w)
        summed = summed.at[chosen].set(summed[chosen] * keep_old[..., None] + partial_value * fresh_w[..., None])
        maxima = maxima.at[chosen].set(new_max)
        return (maxima, totals, summed), None

    start_state = (jnp.full((every_fork_list + 1, KV_HEADS, group_size), neg_floor, jnp.float32),
                   jnp.zeros((every_fork_list + 1, KV_HEADS, group_size), jnp.float32),
                   jnp.zeros((every_fork_list + 1, KV_HEADS, group_size, HEAD_WIDTH), jnp.float32))
    final_state, unused = lax.scan(visit, start_state, (prefix_key_cache, prefix_value_cache, page_of_slot))
    maxima = final_state[0][:every_fork_list]
    totals = final_state[1][:every_fork_list]
    summed = final_state[2][:every_fork_list]
    query_f = query_vectors.reshape(every_fork_list, KV_HEADS, group_size, HEAD_WIDTH).astype(jnp.float32)
    key_f = key_new.reshape(every_fork_list, KV_HEADS, 1, HEAD_WIDTH).astype(jnp.float32)
    value_f = value_new.reshape(every_fork_list, KV_HEADS, 1, HEAD_WIDTH).astype(jnp.float32)
    own_score = jnp.sum(query_f * key_f, axis=-1) * score_scale
    final_max = jnp.maximum(maxima, own_score)
    old_weight = jnp.exp(maxima - final_max)
    own_weight = jnp.exp(own_score - final_max)
    normalized = (summed * old_weight[..., None] + own_weight[..., None] * value_f) / (totals * old_weight + own_weight)[..., None]
    attended = normalized.astype(jnp.bfloat16).reshape(every_fork_list, QUERY_HEADS * HEAD_WIDTH)
    return jnp.dot(attended, output_projection_weight, preferred_element_type=jnp.float32).astype(jnp.bfloat16)
```

```python
import functools

import jax
import jax.numpy as jnp
from jax import lax
from jax.experimental import pallas as pl
from jax.experimental.pallas import tpu as pltpu
from jax.sharding import PartitionSpec as P

HEAD_WIDTH = 128
ADAPTER_RANK = 64
ADAPTER_COUNT = 32
LOG2E = 1.4426950408889634
SCORE_SCALE = HEAD_WIDTH ** (-0.5)
neg_floor = -1e30
VMEM_LIMIT = 56 * 1024 * 1024
F32 = jnp.float32
BF16 = jnp.bfloat16


def params(*semantics):
    return pltpu.CompilerParams(
        dimension_semantics=semantics or None, vmem_limit_bytes=VMEM_LIMIT
    )


def whole(shape):
    return pl.BlockSpec(shape, lambda *_: (0,) * len(shape))


def down_kernel(adapter_ref, hidden_ref, down_ref, out_ref, acc_ref):
    step = pl.program_id(0)
    width = down_ref.shape[1]
    forks = hidden_ref.shape[0]
    block = jnp.dot(hidden_ref[...], down_ref[...], preferred_element_type=F32)
    lane_adapter = lax.broadcasted_iota(jnp.int32, (forks, HEAD_WIDTH), 1) // ADAPTER_RANK
    wanted = adapter_ref[...] - step * (width // ADAPTER_RANK) - lane_adapter
    total = jnp.zeros((forks, HEAD_WIDTH), F32)
    for piece in range(width // HEAD_WIDTH):
        part = block[:, piece * HEAD_WIDTH : (piece + 1) * HEAD_WIDTH]
        total += jnp.where(wanted == piece * (HEAD_WIDTH // ADAPTER_RANK), part, 0.0)

    @pl.when(step == 0)
    def _():
        acc_ref[...] = total

    @pl.when(step > 0)
    def _():
        acc_ref[...] += total

    @pl.when(step == pl.num_programs(0) - 1)
    def _():
        flipped = acc_ref[...].T
        out_ref[...] = flipped[:ADAPTER_RANK] + flipped[ADAPTER_RANK:]


def down_project(adapter, hidden, weight, width=512):
    forks, depth = hidden.shape
    columns = weight.shape[1]
    return pl.pallas_call(
        down_kernel,
        grid=(columns // width,),
        out_shape=jax.ShapeDtypeStruct((ADAPTER_RANK, forks), F32),
        in_specs=[
            whole((forks, 1)),
            whole((forks, depth)),
            pl.BlockSpec((depth, width), lambda i: (0, i)),
        ],
        out_specs=whole((ADAPTER_RANK, forks)),
        scratch_shapes=[pltpu.VMEM((forks, HEAD_WIDTH), F32)],
        compiler_params=params("arbitrary"),
        cost_estimate=pl.CostEstimate(
            flops=2 * forks * depth * columns, bytes_accessed=2 * depth * columns, transcendentals=0
        ),
        name="down_project",
    )(adapter.reshape(forks, 1), hidden, weight)


def project_kernel(q_steps, hidden_ref, q_ref, k_ref, v_ref, out_ref):
    step = pl.program_id(0)

    def put(weight_ref):
        out_ref[...] = jnp.dot(hidden_ref[...], weight_ref[...], preferred_element_type=F32)

    pl.when(step < q_steps)(lambda: put(q_ref))
    pl.when(step == q_steps)(lambda: put(k_ref))
    pl.when(step == q_steps + 1)(lambda: put(v_ref))


def project(hidden, q_weight, k_weight, v_weight):
    forks, depth = hidden.shape
    width = k_weight.shape[1]
    q_steps = q_weight.shape[1] // width
    columns = (q_steps + 2) * width
    return pl.pallas_call(
        functools.partial(project_kernel, q_steps),
        grid=(q_steps + 2,),
        out_shape=jax.ShapeDtypeStruct((forks, columns), F32),
        in_specs=[
            whole((forks, depth)),
            pl.BlockSpec((depth, width), lambda i: (0, jnp.minimum(i, q_steps - 1))),
            whole((depth, width)),
            whole((depth, width)),
        ],
        out_specs=pl.BlockSpec((forks, width), lambda i: (0, i)),
        compiler_params=params("arbitrary"),
        cost_estimate=pl.CostEstimate(
            flops=2 * forks * depth * columns, bytes_accessed=2 * depth * columns, transcendentals=0
        ),
        name="project",
    )(hidden, q_weight, k_weight, v_weight)


def delta_kernel(adapter_ref, rank_ref, up_ref, part_ref, out_ref, spread_ref):
    ranks = rank_ref.shape[1]
    forks = rank_ref.shape[2]

    @pl.when(pl.program_id(0) == 0)
    def _():
        acts = jnp.sum(rank_ref[...], axis=0).astype(BF16).astype(F32)
        adapters = lax.broadcasted_iota(jnp.int32, (ADAPTER_COUNT, forks), 0)
        onehot = (adapters == adapter_ref[...]).astype(F32)
        for r in range(ranks):
            spread_ref[r * ADAPTER_COUNT : (r + 1) * ADAPTER_COUNT, :] = (
                acts[r : r + 1, :] * onehot
            ).astype(BF16)

    delta = lax.dot_general(
        spread_ref[...], up_ref[...], (((0,), (0,)), ((), ())), preferred_element_type=F32
    )
    out_ref[...] = part_ref[...] + delta


def add_delta(adapter, rank_in, up, part, width=1024):
    mem_count, ranks, forks = rank_in.shape
    depth, columns = up.shape
    return pl.pallas_call(
        delta_kernel,
        grid=(columns // width,),
        out_shape=jax.ShapeDtypeStruct(part.shape, F32),
        in_specs=[
            whole((1, forks)),
            whole((mem_count, ranks, forks)),
            pl.BlockSpec((depth, width), lambda i: (0, i)),
            pl.BlockSpec((forks, width), lambda i: (0, i)),
        ],
        out_specs=pl.BlockSpec((forks, width), lambda i: (0, i)),
        scratch_shapes=[pltpu.VMEM((depth, forks), BF16)],
        input_output_aliases={3: 0},
        compiler_params=params("arbitrary"),
        cost_estimate=pl.CostEstimate(
            flops=2 * forks * depth * columns,
            bytes_accessed=2 * depth * columns + 8 * forks * columns,
            transcendentals=0,
        ),
        name="add_delta",
    )(adapter.reshape(1, forks), rank_in, up, part)


def attend_kernel(q_ref, k_ref, v_ref, mask_ref, out_ref, score_ref, lse_ref):
    kv_head = pl.program_id(0)
    forks = q_ref.shape[0]
    group = q_ref.shape[1] // HEAD_WIDTH
    pages, page_len = k_ref.shape[0], k_ref.shape[1]
    queries = jnp.concatenate(
        [q_ref[:, g * HEAD_WIDTH : (g + 1) * HEAD_WIDTH] for g in range(group)], axis=0
    )
    scale = SCORE_SCALE * LOG2E
    peaks = []
    top = None
    for p in range(pages):
        scores = lax.dot_general(
            k_ref[p], queries, (((1,), (1,)), ((), ())), preferred_element_type=F32
        )
        score_ref[p] = scores
        peak = jnp.max(scores, axis=0, keepdims=True)
        peaks.append(peak)
        chosen = jnp.where(mask_ref[p : p + 1, :] > 0, peak, neg_floor)
        top = chosen if top is None else jnp.maximum(top, chosen)
    acc = None
    mass = None
    for p in range(pages):
        weights = jnp.exp2((score_ref[p] - peaks[p]) * scale).astype(BF16)
        chosen = mask_ref[p : p + 1, :] > 0
        factor = jnp.where(
            chosen, jnp.exp2((jnp.where(chosen, peaks[p], neg_floor) - top) * scale), 0.0
        )
        page_mass = jnp.sum(weights.astype(F32), axis=0, keepdims=True) * factor
        page_acc = (
            lax.dot_general(
                v_ref[p], weights, (((0,), (0,)), ((), ())), preferred_element_type=F32
            )
            * factor
        )
        acc = page_acc if acc is None else acc + page_acc
        mass = page_mass if mass is None else mass + page_mass
    some = mass > 0
    safe = jnp.where(some, mass, 1.0)
    rows = (acc * jnp.where(some, 1.0 / safe, 0.0)).T
    lse = jnp.where(some, top * scale + jnp.log2(safe), neg_floor)
    for g in range(group):
        column = pl.multiple_of((kv_head * group + g) * HEAD_WIDTH, HEAD_WIDTH)
        out_ref[:, pl.ds(column, HEAD_WIDTH)] = rows[g * forks : (g + 1) * forks].astype(BF16)
    lse_ref[kv_head] = jnp.concatenate(
        [lse[:, g * forks : (g + 1) * forks] for g in range(group)], axis=0
    )

    @pl.when(kv_head == pl.num_programs(0) - 1)
    def _():
        heads = lse_ref.shape[0] * group
        all_lse = lse_ref[...].reshape(heads, forks)
        high = all_lse.astype(BF16).astype(F32)
        rest = all_lse - high
        middle = rest.astype(BF16).astype(F32)
        low = rest - middle
        spare = jnp.zeros((HEAD_WIDTH - 3 * heads, forks), F32)
        terms = jnp.concatenate([high, middle, low, spare], axis=0).T
        out_ref[:, pl.ds(heads * HEAD_WIDTH, HEAD_WIDTH)] = terms.astype(BF16)


def attend(queries, keys, values, mask):
    forks, width = queries.shape
    pages, page_len, kv_width = keys.shape
    kv_local = kv_width // HEAD_WIDTH
    group_width = width // kv_local
    rows = mask.shape[1]
    flops = 4 * pages * page_len * kv_local * rows * HEAD_WIDTH
    return pl.pallas_call(
        attend_kernel,
        grid=(kv_local,),
        out_shape=jax.ShapeDtypeStruct((forks, width + HEAD_WIDTH), BF16),
        in_specs=[
            pl.BlockSpec((forks, group_width), lambda i: (0, i)),
            pl.BlockSpec((pages, page_len, HEAD_WIDTH), lambda i: (0, 0, i)),
            pl.BlockSpec((pages, page_len, HEAD_WIDTH), lambda i: (0, 0, i)),
            whole((pages, rows)),
        ],
        out_specs=whole((forks, width + HEAD_WIDTH)),
        scratch_shapes=[
            pltpu.VMEM((pages, page_len, rows), F32),
            pltpu.VMEM((kv_local, group_width // HEAD_WIDTH, forks), F32),
        ],
        compiler_params=params("arbitrary"),
        cost_estimate=pl.CostEstimate(
            flops=flops,
            bytes_accessed=4 * pages * page_len * kv_width + 4 * forks * width,
            transcendentals=pages * page_len * kv_local * rows,
        ),
        name="attend",
    )(queries, keys, values, mask)


def merge_kernel(heads, kv_heads, part_ref, own_ref, out_ref):
    sources = part_ref.shape[0]
    group = heads // kv_heads
    width = heads * HEAD_WIDTH
    lses = []
    for s in range(sources):
        terms = part_ref[s, :, width : width + HEAD_WIDTH].astype(F32)
        lses.append(
            terms[:, :heads] + terms[:, heads : 2 * heads] + terms[:, 2 * heads : 3 * heads]
        )
    scores = []
    for h in range(heads):
        query = own_ref[:, h * HEAD_WIDTH : (h + 1) * HEAD_WIDTH].astype(F32)
        at = width + (h // group) * HEAD_WIDTH
        key = own_ref[:, at : at + HEAD_WIDTH].astype(F32)
        scores.append(jnp.sum(query * key, axis=1, keepdims=True))
    own = jnp.concatenate(scores, axis=1) * (SCORE_SCALE * LOG2E)
    top = functools.reduce(jnp.maximum, lses, own)
    own_weight = jnp.exp2(own - top)
    weights = [jnp.exp2(lse - top) for lse in lses]
    inverse = 1.0 / functools.reduce(jnp.add, weights, own_weight)
    own_weight = own_weight * inverse
    weights = [weight * inverse for weight in weights]
    for h in range(heads):
        at = width + (kv_heads + h // group) * HEAD_WIDTH
        value = own_ref[:, at : at + HEAD_WIDTH].astype(F32)
        total = own_weight[:, h : h + 1] * value
        for s in range(sources):
            part = part_ref[s, :, h * HEAD_WIDTH : (h + 1) * HEAD_WIDTH].astype(F32)
            total += weights[s][:, h : h + 1] * part
        out_ref[:, h * HEAD_WIDTH : (h + 1) * HEAD_WIDTH] = total.astype(BF16)


def merge(parts, own, heads, kv_heads):
    sources, fork_own, width = parts.shape
    return pl.pallas_call(
        functools.partial(merge_kernel, heads, kv_heads),
        out_shape=jax.ShapeDtypeStruct((fork_own, heads * HEAD_WIDTH), BF16),
        compiler_params=params(),
        cost_estimate=pl.CostEstimate(
            flops=4 * parts.size, bytes_accessed=2 * parts.size, transcendentals=0
        ),
        name="merge",
    )(parts, own)


def output_kernel(context_ref, weight_ref, out_ref):
    part = jnp.dot(context_ref[...], weight_ref[...], preferred_element_type=F32)

    @pl.when(pl.program_id(0) == 0)
    def _():
        out_ref[...] = part

    @pl.when(pl.program_id(0) > 0)
    def _():
        out_ref[...] += part


def output_project(context, weight, depth=1024):
    forks, rows = context.shape
    columns = weight.shape[1]
    return pl.pallas_call(
        output_kernel,
        grid=(rows // depth,),
        out_shape=jax.ShapeDtypeStruct((forks, columns), F32),
        in_specs=[
            pl.BlockSpec((forks, depth), lambda i: (0, i)),
            pl.BlockSpec((depth, columns), lambda i: (i, 0)),
        ],
        out_specs=whole((forks, columns)),
        compiler_params=params("arbitrary"),
        cost_estimate=pl.CostEstimate(
            flops=2 * forks * rows * columns, bytes_accessed=2 * rows * columns, transcendentals=0
        ),
        name="output_project",
    )(context, weight)


def shards(
    hidden,
    adapter,
    page_cache_slot,
    selection,
    query_projection_weight,
    key_projection_weight,
    value_projection_weight,
    adapter_down_weight,
    adapter_up_weight,
    output_projection_weight,
    prefix_key_cache,
    prefix_value_cache,
):
    mem_count = lax.axis_size("mem")
    mem_index = lax.axis_index("mem")
    forks = hidden.shape[0]
    fork_own = forks // mem_count
    q_width = query_projection_weight.shape[1]
    kv_width = key_projection_weight.shape[1]
    heads, kv_heads = q_width // HEAD_WIDTH, kv_width // HEAD_WIDTH
    pages = prefix_key_cache.shape[0]

    rank_part = down_project(adapter, hidden, adapter_down_weight)
    rank_in = lax.all_to_all(
        rank_part.reshape(mem_count, ADAPTER_RANK // mem_count, forks), "mem", 0, 0
    )
    part = project(hidden, query_projection_weight, key_projection_weight, value_projection_weight)

    slot_ids = mem_index * pages + jnp.arange(pages, dtype=jnp.int32)
    slot_match = (page_cache_slot[None, :] == slot_ids[:, None]).astype(BF16)
    chosen = lax.dot_general(
        slot_match, (selection > 0).astype(BF16), (((1,), (1,)), ((), ())), preferred_element_type=F32
    )
    mask = jnp.tile(chosen, (1, heads // kv_heads))

    up = adapter_up_weight.reshape(-1, q_width)
    part = add_delta(adapter, rank_in, up, part)
    part_in = lax.all_to_all(
        part.reshape(mem_count, fork_own, q_width + 2 * kv_width), "mem", 0, 0
    )
    own = jnp.sum(part_in, axis=0).astype(BF16)
    queries = lax.all_to_all(
        jnp.broadcast_to(own[None, :, :q_width], (mem_count, fork_own, q_width)), "mem", 0, 0
    ).reshape(forks, q_width)
    pieces = attend(queries, prefix_key_cache, prefix_value_cache, mask)
    pieces_in = lax.all_to_all(
        pieces.reshape(mem_count, fork_own, q_width + HEAD_WIDTH), "mem", 0, 0
    )
    context_own = merge(pieces_in, own, heads, kv_heads)
    context = [context_own]
    for shift in range(1, mem_count):
        pairs = [((i + shift) % mem_count, i) for i in range(mem_count)]
        context.append(lax.ppermute(context_own, "mem", pairs))
    context = jnp.roll(jnp.concatenate(context, axis=0), mem_index * fork_own, axis=0)
    projected = output_project(context, output_projection_weight)
    tp_count = lax.axis_size("tp")
    total = projected
    for shift in range(1, tp_count):
        pairs = [(i, (i + shift) % tp_count) for i in range(tp_count)]
        total = total + lax.ppermute(projected, "tp", pairs)
    return total.astype(BF16)


def solution(mesh):
    return jax.shard_map(
        shards,
        mesh=mesh,
        in_specs=(
            P("groups", "mem"),
            P("groups"),
            P("groups"),
            P("groups", None),
            P("mem", "tp"),
            P("mem", "tp"),
            P("mem", "tp"),
            P("mem", None),
            P("mem", None, "tp"),
            P("tp", "mem"),
            P(("groups", "mem"), None, "tp"),
            P(("groups", "mem"), None, "tp"),
        ),
        out_specs=P("groups", "mem"),
        check_vma=False,
    )
```

```python
import functools

import jax
import jax.numpy as jnp
from jax import lax
from jax.experimental import pallas as pl
from jax.experimental.pallas import tpu as pltpu
from jax.sharding import PartitionSpec as P

HEAD_WIDTH = 128
ADAPTER_RANK = 64
ADAPTER_COUNT = 32
LOG2E = 1.4426950408889634
SCORE_SCALE = HEAD_WIDTH ** (-0.5)
neg_floor = -1e30
MIB = 1024 * 1024
F32 = jnp.float32
BF16 = jnp.bfloat16


def params(limit, *semantics):
    return pltpu.CompilerParams(
        dimension_semantics=semantics or None, vmem_limit_bytes=int(limit)
    )


def whole(shape):
    return pl.BlockSpec(shape, lambda *_: (0,) * len(shape))


def down_kernel(adapter_ref, hidden_ref, down_ref, out_ref, held, sems):
    pieces, _, width = held.shape
    forks = hidden_ref.shape[0]
    copies = [
        pltpu.make_async_copy(down_ref.at[:, i * width : (i + 1) * width], held.at[i], sems.at[i])
        for i in range(pieces)
    ]
    for copy in copies:
        copy.start()
    fork_adapter = jnp.broadcast_to(adapter_ref[...].astype(F32), (HEAD_WIDTH, forks)).T
    lane_adapter = lax.broadcasted_iota(jnp.int32, (forks, HEAD_WIDTH), 1) // ADAPTER_RANK
    wanted = fork_adapter.astype(jnp.int32) - lane_adapter
    total = jnp.zeros((forks, HEAD_WIDTH), F32)
    for i in range(pieces):
        copies[i].wait()
        block = jnp.dot(hidden_ref[...], held[i], preferred_element_type=F32)
        for j in range(width // HEAD_WIDTH):
            first = (i * width + j * HEAD_WIDTH) // ADAPTER_RANK
            part = block[:, j * HEAD_WIDTH : (j + 1) * HEAD_WIDTH]
            total += jnp.where(wanted == first, part, 0.0)
    flipped = total.T
    out_ref[:, :forks] = flipped[:ADAPTER_RANK] + flipped[ADAPTER_RANK:]
    if out_ref.shape[1] > forks:
        out_ref[:, forks:] = jnp.zeros((ADAPTER_RANK, out_ref.shape[1] - forks), F32)


def down_project(adapter, hidden, weight, width=256):
    forks, depth = hidden.shape
    columns = weight.shape[1]
    lanes = -(-forks // HEAD_WIDTH) * HEAD_WIDTH
    pieces = columns // width
    return pl.pallas_call(
        down_kernel,
        out_shape=jax.ShapeDtypeStruct((ADAPTER_RANK, lanes), F32),
        in_specs=[
            pl.BlockSpec(memory_space=pltpu.VMEM),
            pl.BlockSpec(memory_space=pltpu.VMEM),
            pl.BlockSpec(memory_space=pl.ANY),
        ],
        out_specs=pl.BlockSpec(memory_space=pltpu.VMEM),
        scratch_shapes=[
            pltpu.VMEM((pieces, depth, width), BF16),
            pltpu.SemaphoreType.DMA((pieces,)),
        ],
        compiler_params=params(2 * depth * columns + 3 * MIB),
        cost_estimate=pl.CostEstimate(
            flops=2 * forks * depth * columns, bytes_accessed=2 * depth * columns, transcendentals=0
        ),
        name="down_project",
    )(adapter.reshape(1, forks), hidden, weight)


def split_parity(rows, parity, fork_own):
    blocks = [rows[i : i + fork_own] for i in range(0, rows.shape[0], fork_own)]
    even = jnp.concatenate(blocks[0::2], axis=0)
    odd = jnp.concatenate(blocks[1::2], axis=0)
    return jnp.where(parity == 0, even, odd), jnp.where(parity == 0, odd, even)


def query_kernel(
    fork_own, parity_ref, adapter_ref, rank_ref, hidden_ref, q_ref, up_ref, keep_ref, send_ref, spread_ref
):
    ranks = rank_ref.shape[1]
    forks = hidden_ref.shape[0]

    @pl.when(pl.program_id(0) == 0)
    def _():
        acts = jnp.sum(rank_ref[...], axis=0)[:, :forks].astype(BF16).astype(F32)
        adapters = lax.broadcasted_iota(jnp.int32, (ADAPTER_COUNT, forks), 0)
        onehot = (adapters == adapter_ref[...]).astype(F32)
        for r in range(ranks):
            spread_ref[r * ADAPTER_COUNT : (r + 1) * ADAPTER_COUNT, :] = (
                acts[r : r + 1, :] * onehot
            ).astype(BF16)

    part = jnp.dot(hidden_ref[...], q_ref[...], preferred_element_type=F32)
    delta = lax.dot_general(
        spread_ref[...], up_ref[...], (((0,), (0,)), ((), ())), preferred_element_type=F32
    )
    keep_ref[...], send_ref[...] = split_parity(part + delta, parity_ref[0], fork_own)


def project_queries(parity, adapter, rank_in, hidden, weight, up, fork_own, start, columns, width=512):
    mem_count, ranks, lanes = rank_in.shape
    forks, depth = hidden.shape
    first = start // width
    out = jax.ShapeDtypeStruct((forks // 2, columns), F32)
    return pl.pallas_call(
        functools.partial(query_kernel, fork_own),
        grid=(columns // width,),
        out_shape=(out, out),
        in_specs=[
            pl.BlockSpec(memory_space=pltpu.SMEM),
            whole((1, forks)),
            whole((mem_count, ranks, lanes)),
            whole((forks, depth)),
            pl.BlockSpec((depth, width), lambda i: (0, first + i)),
            pl.BlockSpec((up.shape[0], width), lambda i: (0, first + i)),
        ],
        out_specs=(pl.BlockSpec((forks // 2, width), lambda i: (0, i)),) * 2,
        scratch_shapes=[pltpu.VMEM((up.shape[0], forks), BF16)],
        compiler_params=params(8 * MIB, "arbitrary"),
        cost_estimate=pl.CostEstimate(
            flops=2 * forks * (depth + up.shape[0]) * columns,
            bytes_accessed=2 * (depth + up.shape[0]) * columns,
            transcendentals=0,
        ),
        name="project_queries",
    )(parity, adapter.reshape(1, forks), rank_in, hidden, weight, up)


def kv_kernel(fork_own, parity_ref, hidden_ref, k_ref, v_ref, keep_ref, send_ref):
    def put(weight_ref):
        part = jnp.dot(hidden_ref[...], weight_ref[...], preferred_element_type=F32)
        keep_ref[...], send_ref[...] = split_parity(part, parity_ref[0], fork_own)

    pl.when(pl.program_id(0) == 0)(lambda: put(k_ref))
    pl.when(pl.program_id(0) == 1)(lambda: put(v_ref))


def project_kv(parity, hidden, k_weight, v_weight, fork_own):
    forks, depth = hidden.shape
    width = k_weight.shape[1]
    out = jax.ShapeDtypeStruct((forks // 2, 2 * width), F32)
    return pl.pallas_call(
        functools.partial(kv_kernel, fork_own),
        grid=(2,),
        out_shape=(out, out),
        in_specs=[
            pl.BlockSpec(memory_space=pltpu.SMEM),
            whole((forks, depth)),
            whole((depth, width)),
            whole((depth, width)),
        ],
        out_specs=(pl.BlockSpec((forks // 2, width), lambda i: (0, i)),) * 2,
        compiler_params=params(8 * MIB, "arbitrary"),
        cost_estimate=pl.CostEstimate(
            flops=4 * forks * depth * width, bytes_accessed=4 * depth * width, transcendentals=0
        ),
        name="project_kv",
    )(parity, hidden, k_weight, v_weight)


def put_terms(lse):
    heads, forks = lse.shape
    high = lse.astype(BF16).astype(F32)
    rest = lse - high
    middle = rest.astype(BF16).astype(F32)
    low = rest - middle
    spare = jnp.zeros((HEAD_WIDTH - 3 * heads, forks), F32)
    return jnp.concatenate([high, middle, low, spare], axis=0).T.astype(BF16)


def get_terms(terms, heads):
    terms = terms.astype(F32)
    return terms[:, :heads] + terms[:, heads : 2 * heads] + terms[:, 2 * heads : 3 * heads]


def attend_kernel(qa_ref, qb_ref, k_ref, v_ref, mask_ref, out_ref, score_ref, lse_ref):
    kv_head = pl.program_id(0)
    steps = pl.num_programs(0)
    forks = qa_ref.shape[0]
    group = qa_ref.shape[1] // HEAD_WIDTH
    pages = k_ref.shape[0]
    block = jnp.where(kv_head < steps // 2, qa_ref[...], qb_ref[...])
    queries = jnp.concatenate(
        [block[:, g * HEAD_WIDTH : (g + 1) * HEAD_WIDTH] for g in range(group)], axis=0
    )
    scale = SCORE_SCALE * LOG2E
    peaks = []
    top = None
    for p in range(pages):
        scores = lax.dot_general(
            k_ref[p], queries, (((1,), (1,)), ((), ())), preferred_element_type=F32
        )
        score_ref[p] = scores
        peak = jnp.max(scores, axis=0, keepdims=True)
        peaks.append(peak)
        chosen = jnp.where(mask_ref[p : p + 1, :] > 0, peak, neg_floor)
        top = chosen if top is None else jnp.maximum(top, chosen)
    acc = None
    mass = None
    for p in range(pages):
        weights = jnp.exp2((score_ref[p] - peaks[p]) * scale).astype(BF16)
        chosen = mask_ref[p : p + 1, :] > 0
        factor = jnp.where(
            chosen, jnp.exp2((jnp.where(chosen, peaks[p], neg_floor) - top) * scale), 0.0
        )
        page_mass = jnp.sum(weights.astype(F32), axis=0, keepdims=True) * factor
        page_acc = (
            lax.dot_general(
                v_ref[p], weights, (((0,), (0,)), ((), ())), preferred_element_type=F32
            )
            * factor
        )
        acc = page_acc if acc is None else acc + page_acc
        mass = page_mass if mass is None else mass + page_mass
    some = mass > 0
    safe = jnp.where(some, mass, 1.0)
    rows = (acc * jnp.where(some, 1.0 / safe, 0.0)).T
    lse = jnp.where(some, top * scale + jnp.log2(safe), neg_floor)
    for g in range(group):
        column = pl.multiple_of((kv_head * group + g) * HEAD_WIDTH, HEAD_WIDTH)
        out_ref[:, pl.ds(column, HEAD_WIDTH)] = rows[g * forks : (g + 1) * forks].astype(BF16)
    lse_ref[kv_head] = jnp.concatenate(
        [lse[:, g * forks : (g + 1) * forks] for g in range(group)], axis=0
    )

    @pl.when(kv_head == steps - 1)
    def _():
        heads = lse_ref.shape[0] * group
        out_ref[:, pl.ds(heads * HEAD_WIDTH, HEAD_WIDTH)] = put_terms(
            lse_ref[...].reshape(heads, forks)
        )


def attend(first, second, keys, values, mask):
    forks, half_width = first.shape
    width = 2 * half_width
    pages, page_len, kv_width = keys.shape
    kv_local = kv_width // HEAD_WIDTH
    half = kv_local // 2
    group_width = width // kv_local
    rows = mask.shape[1]
    flops = 4 * pages * page_len * kv_local * rows * HEAD_WIDTH
    return pl.pallas_call(
        attend_kernel,
        grid=(kv_local,),
        out_shape=jax.ShapeDtypeStruct((forks, width + HEAD_WIDTH), BF16),
        in_specs=[
            pl.BlockSpec((forks, group_width), lambda i: (0, jnp.minimum(i, half - 1))),
            pl.BlockSpec((forks, group_width), lambda i: (0, jnp.maximum(i - half, 0))),
            pl.BlockSpec((pages, page_len, HEAD_WIDTH), lambda i: (0, 0, i)),
            pl.BlockSpec((pages, page_len, HEAD_WIDTH), lambda i: (0, 0, i)),
            whole((pages, rows)),
        ],
        out_specs=whole((forks, width + HEAD_WIDTH)),
        scratch_shapes=[
            pltpu.VMEM((pages, page_len, rows), F32),
            pltpu.VMEM((kv_local, group_width // HEAD_WIDTH, forks), F32),
        ],
        compiler_params=params(6 * pages * page_len * rows + 8 * MIB, "arbitrary"),
        cost_estimate=pl.CostEstimate(
            flops=flops,
            bytes_accessed=4 * pages * page_len * kv_width + 4 * forks * width,
            transcendentals=pages * page_len * kv_local * rows,
        ),
        name="attend",
    )(first, second, keys, values, mask)


def combine_kernel(heads, part_ref, out_ref):
    sources = part_ref.shape[0]
    width = heads * HEAD_WIDTH
    lses = [get_terms(part_ref[s, :, width : width + HEAD_WIDTH], heads) for s in range(sources)]
    top = functools.reduce(jnp.maximum, lses)
    weights = [jnp.exp2(lse - top) for lse in lses]
    mass = functools.reduce(jnp.add, weights)
    weights = [weight / mass for weight in weights]
    for h in range(heads):
        lanes = slice(h * HEAD_WIDTH, (h + 1) * HEAD_WIDTH)
        total = None
        for s in range(sources):
            term = weights[s][:, h : h + 1] * part_ref[s, :, lanes].astype(F32)
            total = term if total is None else total + term
        out_ref[:, lanes] = total.astype(BF16)
    lse = jnp.maximum(top + jnp.log2(mass), neg_floor)
    spare = jnp.zeros((lse.shape[0], HEAD_WIDTH - heads), F32)
    out_ref[:, width : width + HEAD_WIDTH] = put_terms(
        jnp.concatenate([lse, spare], axis=1).T[:heads]
    )


def combine(parts, heads):
    sources, fork_own, width = parts.shape
    return pl.pallas_call(
        functools.partial(combine_kernel, heads),
        out_shape=jax.ShapeDtypeStruct((fork_own, width), BF16),
        compiler_params=params(4 * parts.size + 4 * MIB),
        cost_estimate=pl.CostEstimate(
            flops=4 * parts.size, bytes_accessed=2 * parts.size, transcendentals=0
        ),
        name="combine",
    )(parts)


def merge_kernel(heads, kv_heads, part_ref, more_ref, qa_ref, qb_ref, out_ref):
    group = heads // kv_heads
    width = heads * HEAD_WIDTH
    half = qa_ref.shape[1]
    parts = [part_ref.at[s] for s in range(part_ref.shape[0])] + [more_ref]
    lses = [get_terms(ref[:, width : width + HEAD_WIDTH], heads) for ref in parts]

    def new_head(i):
        return qb_ref[:, half + i * HEAD_WIDTH : half + (i + 1) * HEAD_WIDTH].astype(F32)

    scores = []
    for h in range(heads):
        ref = qa_ref if h < heads // 2 else qb_ref
        at = (h % (heads // 2)) * HEAD_WIDTH
        query = ref[:, at : at + HEAD_WIDTH].astype(F32)
        scores.append(jnp.sum(query * new_head(h // group), axis=1, keepdims=True))
    own = jnp.concatenate(scores, axis=1) * (SCORE_SCALE * LOG2E)
    top = functools.reduce(jnp.maximum, lses, own)
    own_weight = jnp.exp2(own - top)
    weights = [jnp.exp2(lse - top) for lse in lses]
    inverse = 1.0 / functools.reduce(jnp.add, weights, own_weight)
    own_weight = own_weight * inverse
    weights = [weight * inverse for weight in weights]
    for h in range(heads):
        lanes = slice(h * HEAD_WIDTH, (h + 1) * HEAD_WIDTH)
        total = own_weight[:, h : h + 1] * new_head(kv_heads + h // group)
        for weight, ref in zip(weights, parts):
            total += weight[:, h : h + 1] * ref[:, lanes].astype(F32)
        out_ref[:, lanes] = total.astype(BF16)


def merge(parts, more, first, second, heads, kv_heads):
    sources, fork_own, width = parts.shape
    return pl.pallas_call(
        functools.partial(merge_kernel, heads, kv_heads),
        out_shape=jax.ShapeDtypeStruct((fork_own, heads * HEAD_WIDTH), BF16),
        compiler_params=params(4 * parts.size + 4 * MIB),
        cost_estimate=pl.CostEstimate(
            flops=4 * parts.size, bytes_accessed=2 * parts.size, transcendentals=0
        ),
        name="merge",
    )(parts, more, first, second)


def output_kernel(context_ref, weight_ref, out_ref):
    part = jnp.dot(context_ref[...], weight_ref[...], preferred_element_type=F32)

    @pl.when(pl.program_id(0) == 0)
    def _():
        out_ref[...] = part

    @pl.when(pl.program_id(0) > 0)
    def _():
        out_ref[...] += part


def output_project(context, weight, depth=1024):
    forks, rows = context.shape
    columns = weight.shape[1]
    return pl.pallas_call(
        output_kernel,
        grid=(rows // depth,),
        out_shape=jax.ShapeDtypeStruct((forks, columns), F32),
        in_specs=[
            pl.BlockSpec((forks, depth), lambda i: (0, i)),
            pl.BlockSpec((depth, columns), lambda i: (i, 0)),
        ],
        out_specs=whole((forks, columns)),
        compiler_params=params(8 * MIB, "arbitrary"),
        cost_estimate=pl.CostEstimate(
            flops=2 * forks * rows * columns, bytes_accessed=2 * rows * columns, transcendentals=0
        ),
        name="output_project",
    )(context, weight)


def shards(
    hidden,
    adapter,
    page_cache_slot,
    selection,
    query_projection_weight,
    key_projection_weight,
    value_projection_weight,
    adapter_down_weight,
    adapter_up_weight,
    output_projection_weight,
    prefix_key_cache,
    prefix_value_cache,
):
    mem_count = lax.axis_size("mem")
    mem_index = lax.axis_index("mem")
    forks = hidden.shape[0]
    fork_own = forks // mem_count
    q_width = query_projection_weight.shape[1]
    kv_width = key_projection_weight.shape[1]
    heads, kv_heads = q_width // HEAD_WIDTH, kv_width // HEAD_WIDTH
    pages = prefix_key_cache.shape[0]
    line = mem_count // 2
    parity = mem_index % 2
    parity_arg = parity.reshape(1)
    lines = [[2 * i + p for i in range(line)] for p in range(2)]
    swap = [(i, i ^ 1) for i in range(mem_count)]

    def pair(x):
        return lax.ppermute(x, "mem", swap)

    def along(x):
        blocks = x.reshape(line, x.shape[0] // line, x.shape[1])
        return lax.all_to_all(blocks, "mem", 0, 0, axis_index_groups=lines)

    def gather(x):
        spread = jnp.broadcast_to(x[None], (line,) + x.shape)
        got = lax.all_to_all(spread, "mem", 0, 0, axis_index_groups=lines)
        return got.reshape(line * x.shape[0], x.shape[1])

    rank_part = down_project(adapter, hidden, adapter_down_weight)
    rank_in = lax.all_to_all(
        rank_part.reshape(mem_count, ADAPTER_RANK // mem_count, -1), "mem", 0, 0
    )

    up = adapter_up_weight.reshape(-1, q_width)
    half = q_width // 2
    project = functools.partial(
        project_queries, parity_arg, adapter, rank_in, hidden, query_projection_weight, up, fork_own
    )
    keep_a, send_a = project(0, half)
    got_a = pair(send_a)
    keep_b, send_b = project(half, half)
    keep_kv, send_kv = project_kv(
        parity_arg, hidden, key_projection_weight, value_projection_weight, fork_own
    )
    got_b, got_kv = pair(send_b), pair(send_kv)
    own_a = jnp.sum(along(keep_a + got_a), axis=0).astype(BF16)
    sum_b = jnp.concatenate([keep_b + got_b, keep_kv + got_kv], axis=1)
    own_b = jnp.sum(along(sum_b), axis=0).astype(BF16)

    slot_ids = mem_index * pages + jnp.arange(pages, dtype=jnp.int32)
    slot_match = (page_cache_slot[None, :] == slot_ids[:, None]).astype(BF16)
    chosen = lax.dot_general(
        slot_match, (selection > 0).astype(BF16), (((1,), (1,)), ((), ())), preferred_element_type=F32
    ).reshape(pages, line, 2, fork_own)
    even, odd = (chosen[:, :, p].reshape(pages, line * fork_own) for p in range(2))
    mask_near = jnp.tile(jnp.where(parity == 0, even, odd), (1, heads // kv_heads))
    mask_far = jnp.tile(jnp.where(parity == 0, odd, even), (1, heads // kv_heads))

    near_a, near_b = gather(own_a), gather(own_b[:, :half])
    far_a, far_b = pair(near_a), pair(near_b)
    near = attend(near_a, near_b, prefix_key_cache, prefix_value_cache, mask_near)
    near_in = along(near)
    far = attend(far_a, far_b, prefix_key_cache, prefix_value_cache, mask_far)
    far_in = pair(combine(along(far), heads))
    context_own = merge(near_in, far_in, own_a, own_b, heads, kv_heads)

    near_context = gather(context_own)
    far_context = pair(near_context)
    near_out = output_project(near_context, output_projection_weight)
    far_out = output_project(far_context, output_projection_weight)
    tp_count = lax.axis_size("tp")
    outs = []
    for part in (near_out, far_out):
        total = part
        for shift in range(1, tp_count):
            pairs = [(i, (i + shift) % tp_count) for i in range(tp_count)]
            total = total + lax.ppermute(part, "tp", pairs)
        outs.append(total.astype(BF16).reshape(line, 1, fork_own, -1))
    near_out, far_out = outs
    return jnp.concatenate(
        [jnp.where(parity == 0, near_out, far_out), jnp.where(parity == 0, far_out, near_out)], axis=1
    ).reshape(forks, -1)


def solution(mesh):
    return jax.shard_map(
        shards,
        mesh=mesh,
        in_specs=(
            P("groups", "mem"),
            P("groups"),
            P("groups"),
            P("groups", None),
            P("mem", "tp"),
            P("mem", "tp"),
            P("mem", "tp"),
            P("mem", None),
            P("mem", None, "tp"),
            P("tp", "mem"),
            P(("groups", "mem"), None, "tp"),
            P(("groups", "mem"), None, "tp"),
        ),
        out_specs=P("groups", "mem"),
        check_vma=False,
    )
```

```python
import functools

import jax
import jax.numpy as jnp
from jax import lax
from jax.experimental import pallas as pl
from jax.experimental.pallas import tpu as pltpu
from jax.sharding import PartitionSpec as P

HEAD_WIDTH = 128
ADAPTER_RANK = 64
ADAPTER_COUNT = 32
LOG2E = 1.4426950408889634
SCORE_SCALE = HEAD_WIDTH ** (-0.5)
neg_floor = -1e30
MIB = 1024 * 1024
F32 = jnp.float32
BF16 = jnp.bfloat16


def params(limit, *semantics):
    return pltpu.CompilerParams(
        dimension_semantics=semantics or None, vmem_limit_bytes=int(limit)
    )


def whole(shape):
    return pl.BlockSpec(shape, lambda *_: (0,) * len(shape))


def in_hbm(x):
    return pltpu.with_memory_space_constraint(x, pltpu.HBM)


def stage_kernel(pieces, *refs):
    count = len(refs) // 2
    sems = refs[-1]
    copies = []
    for source, target in zip(refs[:count], refs[count : 2 * count]):
        step = source.shape[0] // pieces
        for i in range(pieces):
            rows = slice(i * step, (i + 1) * step)
            copies.append(
                pltpu.make_async_copy(source.at[rows], target.at[rows], sems.at[len(copies)])
            )
    for copy in copies:
        copy.start()
    for copy in copies:
        copy.wait()


def stage(*arrays, pieces=4):
    size = sum(2 * x.size for x in arrays)
    return pl.pallas_call(
        functools.partial(stage_kernel, pieces),
        out_shape=tuple(pltpu.VMEM(x.shape, x.dtype) for x in arrays),
        in_specs=[pl.BlockSpec(memory_space=pl.ANY)] * len(arrays),
        out_specs=(pl.BlockSpec(memory_space=pl.ANY),) * len(arrays),
        scratch_shapes=[pltpu.SemaphoreType.DMA((pieces * len(arrays),))],
        compiler_params=params(MIB),
        cost_estimate=pl.CostEstimate(flops=0, bytes_accessed=size, transcendentals=0),
        name="stage",
    )(*[in_hbm(x) for x in arrays])


def take_blocks(index, blocks_ref, near_ref, far_ref):
    line = near_ref.shape[0]
    place, parity = index // 2, index % 2
    for i in range(line):
        at = 2 * lax.rem(place + i, line)
        near_ref[i] = blocks_ref[at + parity]
        far_ref[i] = blocks_ref[at + 1 - parity]


def down_kernel(
    index_ref, adapter_ref, hidden_hbm, down_ref, near_ref, far_ref, hidden_ref, held, blocks_ref, sems
):
    pieces, _, width = held.shape
    forks = hidden_ref.shape[0]
    copies = [pltpu.make_async_copy(hidden_hbm, hidden_ref, sems.at[pieces])] + [
        pltpu.make_async_copy(down_ref.at[:, i * width : (i + 1) * width], held.at[i], sems.at[i])
        for i in range(pieces)
    ]
    for copy in copies:
        copy.start()
    fork_adapter = jnp.broadcast_to(adapter_ref[...].astype(F32), (HEAD_WIDTH, forks)).T
    lane_adapter = lax.broadcasted_iota(jnp.int32, (forks, HEAD_WIDTH), 1) // ADAPTER_RANK
    wanted = fork_adapter.astype(jnp.int32) - lane_adapter
    total = jnp.zeros((forks, HEAD_WIDTH), F32)
    copies[0].wait()
    for i in range(pieces):
        copies[1 + i].wait()
        block = jnp.dot(hidden_ref[...], held[i], preferred_element_type=F32)
        for j in range(width // HEAD_WIDTH):
            first = (i * width + j * HEAD_WIDTH) // ADAPTER_RANK
            part = block[:, j * HEAD_WIDTH : (j + 1) * HEAD_WIDTH]
            total += jnp.where(wanted == first, part, 0.0)
    flipped = total.T
    flipped = flipped[:ADAPTER_RANK] + flipped[ADAPTER_RANK:]
    lanes = blocks_ref.shape[2]
    if lanes > forks:
        flipped = jnp.concatenate([flipped, jnp.zeros((ADAPTER_RANK, lanes - forks), F32)], axis=1)
    ranks = blocks_ref.shape[1]
    for i in range(blocks_ref.shape[0]):
        blocks_ref[i] = flipped[i * ranks : (i + 1) * ranks]
    take_blocks(index_ref[0], blocks_ref, near_ref, far_ref)


def down_project(index, adapter, hidden, weight, mem_count, width=256):
    forks, depth = hidden.shape
    columns = weight.shape[1]
    lanes = -(-forks // HEAD_WIDTH) * HEAD_WIDTH
    ranks = ADAPTER_RANK // mem_count
    pieces = columns // width
    out = jax.ShapeDtypeStruct((mem_count // 2, ranks, lanes), F32)
    return pl.pallas_call(
        down_kernel,
        out_shape=(out, out),
        in_specs=[
            pl.BlockSpec(memory_space=pltpu.SMEM),
            pl.BlockSpec(memory_space=pltpu.VMEM),
            pl.BlockSpec(memory_space=pl.ANY),
            pl.BlockSpec(memory_space=pl.ANY),
        ],
        out_specs=(pl.BlockSpec(memory_space=pltpu.VMEM),) * 2,
        scratch_shapes=[
            pltpu.VMEM((forks, depth), BF16),
            pltpu.VMEM((pieces, depth, width), BF16),
            pltpu.VMEM((mem_count, ranks, lanes), F32),
            pltpu.SemaphoreType.DMA((pieces + 1,)),
        ],
        compiler_params=params(2 * depth * columns + 3 * MIB),
        cost_estimate=pl.CostEstimate(
            flops=2 * forks * depth * columns, bytes_accessed=2 * depth * columns, transcendentals=0
        ),
        name="down_project",
    )(index, adapter.reshape(1, forks), in_hbm(hidden), in_hbm(weight))


def put_blocks(index, value, blocks_ref, near_ref, far_ref):
    fork_own = blocks_ref.shape[1]
    for i in range(blocks_ref.shape[0]):
        blocks_ref[i] = value[i * fork_own : (i + 1) * fork_own]
    take_blocks(index, blocks_ref, near_ref, far_ref)


def query_kernel(
    line, index_ref, adapter_ref, *refs
):
    rank_refs = refs[:line]
    hidden_ref, q_ref, up_ref, near_ref, far_ref, spread_ref, blocks_ref = refs[line:]
    ranks = rank_refs[0].shape[0]
    forks = hidden_ref.shape[0]

    @pl.when(pl.program_id(0) == 0)
    def _():
        acts = functools.reduce(jnp.add, [ref[...] for ref in rank_refs])
        acts = acts[:, :forks].astype(BF16).astype(F32)
        adapters = lax.broadcasted_iota(jnp.int32, (ADAPTER_COUNT, forks), 0)
        onehot = (adapters == adapter_ref[...]).astype(F32)
        for r in range(ranks):
            spread_ref[r * ADAPTER_COUNT : (r + 1) * ADAPTER_COUNT, :] = (
                acts[r : r + 1, :] * onehot
            ).astype(BF16)

    part = jnp.dot(hidden_ref[...], q_ref[...], preferred_element_type=F32)
    delta = lax.dot_general(
        spread_ref[...], up_ref[...], (((0,), (0,)), ((), ())), preferred_element_type=F32
    )
    put_blocks(index_ref[0], part + delta, blocks_ref, near_ref, far_ref)


def project_queries(index, adapter, rank_parts, hidden, weight, up, mem_count, start, columns, width=512):
    ranks, lanes = rank_parts[0].shape
    forks, depth = hidden.shape
    first = start // width
    line, fork_own = mem_count // 2, forks // mem_count
    out = jax.ShapeDtypeStruct((line, fork_own, columns), F32)
    return pl.pallas_call(
        functools.partial(query_kernel, line),
        grid=(columns // width,),
        out_shape=(out, out),
        in_specs=[
            pl.BlockSpec(memory_space=pltpu.SMEM),
            whole((1, forks)),
            *[whole((ranks, lanes))] * line,
            whole((forks, depth)),
            pl.BlockSpec((depth, width), lambda i: (0, first + i)),
            pl.BlockSpec((up.shape[0], width), lambda i: (0, first + i)),
        ],
        out_specs=(pl.BlockSpec((line, fork_own, width), lambda i: (0, 0, i)),) * 2,
        scratch_shapes=[
            pltpu.VMEM((up.shape[0], forks), BF16),
            pltpu.VMEM((mem_count, fork_own, width), F32),
        ],
        compiler_params=params(8 * MIB, "arbitrary"),
        cost_estimate=pl.CostEstimate(
            flops=2 * forks * (depth + up.shape[0]) * columns,
            bytes_accessed=2 * (depth + up.shape[0]) * columns,
            transcendentals=0,
        ),
        name="project_queries",
    )(index, adapter.reshape(1, forks), *rank_parts, hidden, weight, up)


def kv_kernel(index_ref, hidden_ref, k_ref, v_ref, near_ref, far_ref, blocks_ref):
    def put(weight_ref):
        part = jnp.dot(hidden_ref[...], weight_ref[...], preferred_element_type=F32)
        put_blocks(index_ref[0], part, blocks_ref, near_ref, far_ref)

    pl.when(pl.program_id(0) == 0)(lambda: put(k_ref))
    pl.when(pl.program_id(0) == 1)(lambda: put(v_ref))


def project_kv(index, hidden, k_weight, v_weight, mem_count):
    forks, depth = hidden.shape
    width = k_weight.shape[1]
    line, fork_own = mem_count // 2, forks // mem_count
    out = jax.ShapeDtypeStruct((line, fork_own, 2 * width), F32)
    return pl.pallas_call(
        kv_kernel,
        grid=(2,),
        out_shape=(out, out),
        in_specs=[
            pl.BlockSpec(memory_space=pltpu.SMEM),
            whole((forks, depth)),
            whole((depth, width)),
            whole((depth, width)),
        ],
        out_specs=(pl.BlockSpec((line, fork_own, width), lambda i: (0, 0, i)),) * 2,
        scratch_shapes=[pltpu.VMEM((mem_count, fork_own, width), F32)],
        compiler_params=params(8 * MIB, "arbitrary"),
        cost_estimate=pl.CostEstimate(
            flops=4 * forks * depth * width, bytes_accessed=4 * depth * width, transcendentals=0
        ),
        name="project_kv",
    )(index, hidden, k_weight, v_weight)


def put_terms(lse):
    heads, forks = lse.shape
    high = lse.astype(BF16).astype(F32)
    rest = lse - high
    middle = rest.astype(BF16).astype(F32)
    low = rest - middle
    spare = jnp.zeros((HEAD_WIDTH - 3 * heads, forks), F32)
    return jnp.concatenate([high, middle, low, spare], axis=0).T.astype(BF16)


def get_terms(terms, heads):
    terms = terms.astype(F32)
    return terms[:, :heads] + terms[:, heads : 2 * heads] + terms[:, 2 * heads : 3 * heads]


def attend_kernel(qa_ref, qb_ref, k_ref, v_ref, mask_ref, out_ref, score_ref, lse_ref):
    kv_head = pl.program_id(0)
    steps = pl.num_programs(0)
    forks = qa_ref.shape[0]
    group = qa_ref.shape[1] // HEAD_WIDTH
    pages = k_ref.shape[0]
    block = jnp.where(kv_head < steps // 2, qa_ref[...], qb_ref[...])
    queries = jnp.concatenate(
        [block[:, g * HEAD_WIDTH : (g + 1) * HEAD_WIDTH] for g in range(group)], axis=0
    )
    scale = SCORE_SCALE * LOG2E
    peaks = []
    top = None
    for p in range(pages):
        scores = lax.dot_general(
            k_ref[p], queries, (((1,), (1,)), ((), ())), preferred_element_type=F32
        )
        score_ref[p] = scores
        peak = jnp.max(scores, axis=0, keepdims=True)
        peaks.append(peak)
        chosen = jnp.where(mask_ref[p : p + 1, :] > 0, peak, neg_floor)
        top = chosen if top is None else jnp.maximum(top, chosen)
    acc = None
    mass = None
    for p in range(pages):
        weights = jnp.exp2((score_ref[p] - peaks[p]) * scale).astype(BF16)
        chosen = mask_ref[p : p + 1, :] > 0
        factor = jnp.where(
            chosen, jnp.exp2((jnp.where(chosen, peaks[p], neg_floor) - top) * scale), 0.0
        )
        page_mass = jnp.sum(weights.astype(F32), axis=0, keepdims=True) * factor
        page_acc = (
            lax.dot_general(
                v_ref[p], weights, (((0,), (0,)), ((), ())), preferred_element_type=F32
            )
            * factor
        )
        acc = page_acc if acc is None else acc + page_acc
        mass = page_mass if mass is None else mass + page_mass
    some = mass > 0
    safe = jnp.where(some, mass, 1.0)
    rows = (acc * jnp.where(some, 1.0 / safe, 0.0)).T
    lse = jnp.where(some, top * scale + jnp.log2(safe), neg_floor)
    for g in range(group):
        column = pl.multiple_of((kv_head * group + g) * HEAD_WIDTH, HEAD_WIDTH)
        out_ref[:, pl.ds(column, HEAD_WIDTH)] = rows[g * forks : (g + 1) * forks].astype(BF16)
    lse_ref[kv_head] = jnp.concatenate(
        [lse[:, g * forks : (g + 1) * forks] for g in range(group)], axis=0
    )

    @pl.when(kv_head == steps - 1)
    def _():
        heads = lse_ref.shape[0] * group
        out_ref[:, pl.ds(heads * HEAD_WIDTH, HEAD_WIDTH)] = put_terms(
            lse_ref[...].reshape(heads, forks)
        )


def attend(first, second, keys, values, mask):
    forks, half_width = first.shape
    width = 2 * half_width
    pages, page_len, kv_width = keys.shape
    kv_local = kv_width // HEAD_WIDTH
    half = kv_local // 2
    group_width = width // kv_local
    rows = mask.shape[1]
    flops = 4 * pages * page_len * kv_local * rows * HEAD_WIDTH
    return pl.pallas_call(
        attend_kernel,
        grid=(kv_local,),
        out_shape=jax.ShapeDtypeStruct((forks, width + HEAD_WIDTH), BF16),
        in_specs=[
            pl.BlockSpec((forks, group_width), lambda i: (0, jnp.minimum(i, half - 1))),
            pl.BlockSpec((forks, group_width), lambda i: (0, jnp.maximum(i - half, 0))),
            pl.BlockSpec((pages, page_len, HEAD_WIDTH), lambda i: (0, 0, i)),
            pl.BlockSpec((pages, page_len, HEAD_WIDTH), lambda i: (0, 0, i)),
            whole((pages, rows)),
        ],
        out_specs=whole((forks, width + HEAD_WIDTH)),
        scratch_shapes=[
            pltpu.VMEM((pages, page_len, rows), F32),
            pltpu.VMEM((kv_local, group_width // HEAD_WIDTH, forks), F32),
        ],
        compiler_params=params(6 * pages * page_len * rows + 8 * MIB, "arbitrary"),
        cost_estimate=pl.CostEstimate(
            flops=flops,
            bytes_accessed=4 * pages * page_len * kv_width + 4 * forks * width,
            transcendentals=pages * page_len * kv_local * rows,
        ),
        name="attend",
    )(first, second, keys, values, mask)


def merge_kernel(heads, kv_heads, sources, *refs):
    parts, (qa_ref, qb_ref, new_ref, out_ref) = refs[:sources], refs[sources:]
    group = heads // kv_heads
    width = heads * HEAD_WIDTH
    lses = [get_terms(ref[:, width : width + HEAD_WIDTH], heads) for ref in parts]

    def new_head(i):
        return new_ref[:, i * HEAD_WIDTH : (i + 1) * HEAD_WIDTH].astype(F32)

    scores = []
    for h in range(heads):
        ref = qa_ref if h < heads // 2 else qb_ref
        at = (h % (heads // 2)) * HEAD_WIDTH
        query = ref[:, at : at + HEAD_WIDTH].astype(F32)
        scores.append(jnp.sum(query * new_head(h // group), axis=1, keepdims=True))
    own = jnp.concatenate(scores, axis=1) * (SCORE_SCALE * LOG2E)
    top = functools.reduce(jnp.maximum, lses, own)
    own_weight = jnp.exp2(own - top)
    weights = [jnp.exp2(lse - top) for lse in lses]
    inverse = 1.0 / functools.reduce(jnp.add, weights, own_weight)
    own_weight = own_weight * inverse
    weights = [weight * inverse for weight in weights]
    for h in range(heads):
        lanes = slice(h * HEAD_WIDTH, (h + 1) * HEAD_WIDTH)
        total = own_weight[:, h : h + 1] * new_head(kv_heads + h // group)
        for weight, ref in zip(weights, parts):
            total += weight[:, h : h + 1] * ref[:, lanes].astype(F32)
        out_ref[:, lanes] = total.astype(BF16)


def merge(parts, first, second, new, heads, kv_heads):
    fork_own, width = parts[0].shape
    size = len(parts) * fork_own * width
    return pl.pallas_call(
        functools.partial(merge_kernel, heads, kv_heads, len(parts)),
        out_shape=jax.ShapeDtypeStruct((fork_own, heads * HEAD_WIDTH), BF16),
        compiler_params=params(4 * size + 4 * MIB),
        cost_estimate=pl.CostEstimate(flops=4 * size, bytes_accessed=2 * size, transcendentals=0),
        name="merge",
    )(*parts, first, second, new)


def output_kernel(context_ref, weight_ref, out_ref):
    part = jnp.dot(context_ref[...], weight_ref[...], preferred_element_type=F32)

    @pl.when(pl.program_id(0) == 0)
    def _():
        out_ref[...] = part

    @pl.when(pl.program_id(0) > 0)
    def _():
        out_ref[...] += part


def output_project(context, weight, depth=1024):
    forks, rows = context.shape
    columns = weight.shape[1]
    return pl.pallas_call(
        output_kernel,
        grid=(rows // depth,),
        out_shape=jax.ShapeDtypeStruct((forks, columns), F32),
        in_specs=[
            pl.BlockSpec((forks, depth), lambda i: (0, i)),
            pl.BlockSpec((depth, columns), lambda i: (i, 0)),
        ],
        out_specs=whole((forks, columns)),
        compiler_params=params(8 * MIB, "arbitrary"),
        cost_estimate=pl.CostEstimate(
            flops=2 * forks * rows * columns, bytes_accessed=2 * rows * columns, transcendentals=0
        ),
        name="output_project",
    )(context, weight)


def shards(
    hidden,
    adapter,
    page_cache_slot,
    selection,
    query_projection_weight,
    key_projection_weight,
    value_projection_weight,
    adapter_down_weight,
    adapter_up_weight,
    output_projection_weight,
    prefix_key_cache,
    prefix_value_cache,
):
    mem_count = lax.axis_size("mem")
    mem_index = lax.axis_index("mem")
    forks = hidden.shape[0]
    fork_own = forks // mem_count
    q_width = query_projection_weight.shape[1]
    kv_width = key_projection_weight.shape[1]
    heads, kv_heads = q_width // HEAD_WIDTH, kv_width // HEAD_WIDTH
    pages = prefix_key_cache.shape[0]
    line = mem_count // 2
    index = mem_index.reshape(1)
    place, parity = mem_index // 2, mem_index % 2

    def shifted(x, shift, cross=0):
        pairs = [
            (i, 2 * ((i // 2 + shift) % line) + (i % 2 + cross) % 2) for i in range(mem_count)
        ]
        return lax.ppermute(x, "mem", pairs)

    def along(blocks, cross=0):
        return [shifted(blocks[i], i, cross) if i or cross else blocks[0] for i in range(line)]

    def gather(x):
        return jnp.concatenate([x] + [shifted(x, -i) for i in range(1, line)], axis=0)

    def pair(x):
        return shifted(x, 0, 1)

    q_weight, up, k_weight, v_weight = stage(
        query_projection_weight,
        adapter_up_weight.reshape(-1, q_width),
        key_projection_weight,
        value_projection_weight,
    )
    near_rank, far_rank = down_project(index, adapter, hidden, adapter_down_weight, mem_count)
    rank_parts = along(near_rank + pair(far_rank))

    half = q_width // 2
    project = functools.partial(
        project_queries, index, adapter, rank_parts, hidden, q_weight, up, mem_count
    )
    keep_a, send_a = project(0, half)
    keep_b, send_b = project(half, half)
    keep_new, send_new = project_kv(index, hidden, k_weight, v_weight, mem_count)

    def settle(keep, send):
        return functools.reduce(jnp.add, along(keep + pair(send))).astype(BF16)

    own_a, own_b, own_new = settle(keep_a, send_a), settle(keep_b, send_b), settle(keep_new, send_new)

    slot_ids = mem_index * pages + jnp.arange(pages, dtype=jnp.int32)
    slot_match = (page_cache_slot[None, :] == slot_ids[:, None]).astype(BF16)
    chosen = lax.dot_general(
        slot_match, (selection > 0).astype(BF16), (((1,), (1,)), ((), ())), preferred_element_type=F32
    ).reshape(pages, line, 2, fork_own)
    chosen = jnp.roll(chosen, -place, axis=1)
    even, odd = (chosen[:, :, p].reshape(pages, line * fork_own) for p in range(2))
    mask_near = jnp.tile(jnp.where(parity == 0, even, odd), (1, heads // kv_heads))
    mask_far = jnp.tile(jnp.where(parity == 0, odd, even), (1, heads // kv_heads))

    keys, values = stage(prefix_key_cache, prefix_value_cache)
    near_a, near_b = gather(own_a), gather(own_b)
    far_a, far_b = pair(near_a), pair(near_b)
    near = attend(near_a, near_b, keys, values, mask_near)
    far = attend(far_a, far_b, keys, values, mask_far)
    blocks = (line, fork_own, q_width + HEAD_WIDTH)
    parts = along(near.reshape(blocks)) + along(far.reshape(blocks), 1)
    context_own = merge(parts, own_a, own_b, own_new, heads, kv_heads)

    (out_weight,) = stage(output_projection_weight)
    near_context = gather(context_own)
    far_context = pair(near_context)
    near_out = output_project(near_context, out_weight)
    far_out = output_project(far_context, out_weight)
    tp_count = lax.axis_size("tp")
    outs = []
    for part in (near_out, far_out):
        total = part
        for shift in range(1, tp_count):
            pairs = [(i, (i + shift) % tp_count) for i in range(tp_count)]
            total = total + lax.ppermute(part, "tp", pairs)
        outs.append(jnp.roll(total.astype(BF16).reshape(line, 1, fork_own, -1), place, axis=0))
    near_out, far_out = outs
    return jnp.concatenate(
        [jnp.where(parity == 0, near_out, far_out), jnp.where(parity == 0, far_out, near_out)], axis=1
    ).reshape(forks, -1)


def solution(mesh):
    return jax.shard_map(
        shards,
        mesh=mesh,
        in_specs=(
            P("groups", "mem"),
            P("groups"),
            P("groups"),
            P("groups", None),
            P("mem", "tp"),
            P("mem", "tp"),
            P("mem", "tp"),
            P("mem", None),
            P("mem", None, "tp"),
            P("tp", "mem"),
            P(("groups", "mem"), None, "tp"),
            P(("groups", "mem"), None, "tp"),
        ),
        out_specs=P("groups", "mem"),
        check_vma=False,
    )
```

```python
import functools

import jax
import jax.numpy as jnp
from jax import lax
from jax.experimental import pallas as pl
from jax.experimental.pallas import tpu as pltpu
from jax.sharding import PartitionSpec as P

HEAD_WIDTH = 128
ADAPTER_RANK = 64
ADAPTER_COUNT = 32
LOG2E = 1.4426950408889634
SCORE_SCALE = HEAD_WIDTH ** (-0.5)
neg_floor = -1e30
MIB = 1024 * 1024
F32 = jnp.float32
BF16 = jnp.bfloat16


def params(limit, *semantics):
    return pltpu.CompilerParams(
        dimension_semantics=semantics or None, vmem_limit_bytes=int(limit)
    )


def whole(shape):
    return pl.BlockSpec(shape, lambda *_: (0,) * len(shape))


def in_hbm(x):
    return pltpu.with_memory_space_constraint(x, pltpu.HBM)


def in_vmem(x):
    return pltpu.with_memory_space_constraint(x, pltpu.VMEM)


def stage_kernel(pieces, *refs):
    count = len(refs) // 2
    sems = refs[-1]
    copies = []
    for source, target in zip(refs[:count], refs[count : 2 * count]):
        step = source.shape[0] // pieces
        for i in range(pieces):
            rows = slice(i * step, (i + 1) * step)
            copies.append(
                pltpu.make_async_copy(source.at[rows], target.at[rows], sems.at[len(copies)])
            )
    for copy in copies:
        copy.start()
    for copy in copies:
        copy.wait()


def stage(*arrays, pieces=4):
    size = sum(2 * x.size for x in arrays)
    return pl.pallas_call(
        functools.partial(stage_kernel, pieces),
        out_shape=tuple(pltpu.VMEM(x.shape, x.dtype) for x in arrays),
        in_specs=[pl.BlockSpec(memory_space=pl.ANY)] * len(arrays),
        out_specs=(pl.BlockSpec(memory_space=pl.ANY),) * len(arrays),
        scratch_shapes=[pltpu.SemaphoreType.DMA((pieces * len(arrays),))],
        compiler_params=params(MIB),
        cost_estimate=pl.CostEstimate(flops=0, bytes_accessed=size, transcendentals=0),
        name="stage",
    )(*[in_hbm(x) for x in arrays])


def take_blocks(index, blocks_ref, near_ref, far_ref):
    line = near_ref.shape[0]
    place, parity = index // 2, index % 2
    for i in range(line):
        at = 2 * lax.rem(place + i, line)
        near_ref[i] = blocks_ref[at + parity]
        far_ref[i] = blocks_ref[at + 1 - parity]


def down_kernel(
    index_ref, adapter_ref, hidden_hbm, down_ref, near_ref, far_ref, hidden_ref, held, blocks_ref, sems
):
    pieces, _, width = held.shape
    forks = hidden_ref.shape[0]
    copies = [pltpu.make_async_copy(hidden_hbm, hidden_ref, sems.at[pieces])] + [
        pltpu.make_async_copy(down_ref.at[:, i * width : (i + 1) * width], held.at[i], sems.at[i])
        for i in range(pieces)
    ]
    for copy in copies:
        copy.start()
    fork_adapter = jnp.broadcast_to(adapter_ref[...].astype(F32), (HEAD_WIDTH, forks)).T
    lane_adapter = lax.broadcasted_iota(jnp.int32, (forks, HEAD_WIDTH), 1) // ADAPTER_RANK
    wanted = fork_adapter.astype(jnp.int32) - lane_adapter
    total = jnp.zeros((forks, HEAD_WIDTH), F32)
    copies[0].wait()
    for i in range(pieces):
        copies[1 + i].wait()
        block = jnp.dot(hidden_ref[...], held[i], preferred_element_type=F32)
        for j in range(width // HEAD_WIDTH):
            first = (i * width + j * HEAD_WIDTH) // ADAPTER_RANK
            part = block[:, j * HEAD_WIDTH : (j + 1) * HEAD_WIDTH]
            total += jnp.where(wanted == first, part, 0.0)
    flipped = total.T
    flipped = flipped[:ADAPTER_RANK] + flipped[ADAPTER_RANK:]
    lanes = blocks_ref.shape[2]
    if lanes > forks:
        flipped = jnp.concatenate([flipped, jnp.zeros((ADAPTER_RANK, lanes - forks), F32)], axis=1)
    ranks = blocks_ref.shape[1]
    for i in range(blocks_ref.shape[0]):
        blocks_ref[i] = flipped[i * ranks : (i + 1) * ranks]
    take_blocks(index_ref[0], blocks_ref, near_ref, far_ref)


def down_project(index, adapter, hidden, weight, mem_count, width=256):
    forks, depth = hidden.shape
    columns = weight.shape[1]
    lanes = -(-forks // HEAD_WIDTH) * HEAD_WIDTH
    ranks = ADAPTER_RANK // mem_count
    pieces = columns // width
    out = jax.ShapeDtypeStruct((mem_count // 2, ranks, lanes), F32)
    return pl.pallas_call(
        down_kernel,
        out_shape=(out, out),
        in_specs=[
            pl.BlockSpec(memory_space=pltpu.SMEM),
            pl.BlockSpec(memory_space=pltpu.VMEM),
            pl.BlockSpec(memory_space=pl.ANY),
            pl.BlockSpec(memory_space=pl.ANY),
        ],
        out_specs=(pl.BlockSpec(memory_space=pltpu.VMEM),) * 2,
        scratch_shapes=[
            pltpu.VMEM((forks, depth), BF16),
            pltpu.VMEM((pieces, depth, width), BF16),
            pltpu.VMEM((mem_count, ranks, lanes), F32),
            pltpu.SemaphoreType.DMA((pieces + 1,)),
        ],
        compiler_params=params(2 * depth * columns + 3 * MIB),
        cost_estimate=pl.CostEstimate(
            flops=2 * forks * depth * columns, bytes_accessed=2 * depth * columns, transcendentals=0
        ),
        name="down_project",
    )(index, adapter.reshape(1, forks), in_hbm(hidden), in_hbm(weight))


def put_blocks(index, value, blocks_ref, near_ref, far_ref):
    fork_own = blocks_ref.shape[1]
    for i in range(blocks_ref.shape[0]):
        blocks_ref[i] = value[i * fork_own : (i + 1) * fork_own]
    take_blocks(index, blocks_ref, near_ref, far_ref)


def project_kernel(
    index_ref,
    hidden_hbm,
    q_hbm,
    k_hbm,
    v_hbm,
    up_hbm,
    part_ref,
    near_ref,
    far_ref,
    up_ref,
    hidden_ref,
    held,
    blocks_ref,
    sems,
):
    pieces, _, width = held.shape
    q_pieces = pieces - 2
    copies = [
        pltpu.make_async_copy(hidden_hbm, hidden_ref, sems.at[pieces]),
        pltpu.make_async_copy(k_hbm, held.at[0], sems.at[0]),
        pltpu.make_async_copy(v_hbm, held.at[1], sems.at[1]),
    ]
    for i in range(q_pieces):
        columns = q_hbm.at[:, i * width : (i + 1) * width]
        copies.append(pltpu.make_async_copy(columns, held.at[2 + i], sems.at[2 + i]))
    copies.append(pltpu.make_async_copy(up_hbm, up_ref, sems.at[pieces + 1]))
    for copy in copies:
        copy.start()
    copies[0].wait()
    for i in range(pieces):
        copies[1 + i].wait()
        part = jnp.dot(hidden_ref[...], held[i], preferred_element_type=F32)
        if i < 2:
            lanes = slice(i * width, (i + 1) * width)
            put_blocks(
                index_ref[0], part, blocks_ref, near_ref.at[:, :, lanes], far_ref.at[:, :, lanes]
            )
        else:
            part_ref[:, (i - 2) * width : (i - 1) * width] = part
    copies[-1].wait()


def project(index, hidden, q_weight, k_weight, v_weight, up, mem_count):
    forks, depth = hidden.shape
    q_width, width = q_weight.shape[1], k_weight.shape[1]
    pieces = q_width // width + 2
    line, fork_own = mem_count // 2, forks // mem_count
    out = jax.ShapeDtypeStruct((line, fork_own, 2 * width), F32)
    weights = 2 * depth * pieces * width
    return pl.pallas_call(
        project_kernel,
        out_shape=(pltpu.VMEM((forks, q_width), F32), out, out, pltpu.VMEM(up.shape, BF16)),
        in_specs=[pl.BlockSpec(memory_space=pltpu.SMEM)] + [pl.BlockSpec(memory_space=pl.ANY)] * 5,
        out_specs=(pl.BlockSpec(memory_space=pltpu.VMEM),) * 4,
        scratch_shapes=[
            pltpu.VMEM((forks, depth), BF16),
            pltpu.VMEM((pieces, depth, width), BF16),
            pltpu.VMEM((mem_count, fork_own, width), F32),
            pltpu.SemaphoreType.DMA((pieces + 2,)),
        ],
        compiler_params=params(weights + 6 * MIB),
        cost_estimate=pl.CostEstimate(
            flops=weights * forks, bytes_accessed=weights + 2 * up.size, transcendentals=0
        ),
        name="project",
    )(index, *[in_hbm(x) for x in (hidden, q_weight, k_weight, v_weight, up)])


def delta_kernel(line, start, index_ref, adapter_ref, *refs):
    rank_refs = refs[:line]
    part_ref, up_ref, near_ref, far_ref, blocks_ref = refs[line:]
    forks, width = part_ref.shape[0], blocks_ref.shape[2]
    acts = functools.reduce(jnp.add, [ref[...] for ref in rank_refs])
    acts = acts[:, :forks].astype(BF16).astype(F32)
    adapters = lax.broadcasted_iota(jnp.int32, (ADAPTER_COUNT, forks), 0)
    onehot = (adapters == adapter_ref[...]).astype(F32)
    spread = jnp.concatenate(
        [acts[r : r + 1, :] * onehot for r in range(acts.shape[0])], axis=0
    ).astype(BF16)
    for i in range(near_ref.shape[2] // width):
        at = slice(start + i * width, start + (i + 1) * width)
        delta = lax.dot_general(
            spread, up_ref[:, at], (((0,), (0,)), ((), ())), preferred_element_type=F32
        )
        lanes = slice(i * width, (i + 1) * width)
        put_blocks(
            index_ref[0],
            part_ref[:, at] + delta,
            blocks_ref,
            near_ref.at[:, :, lanes],
            far_ref.at[:, :, lanes],
        )


def add_delta(index, adapter, rank_parts, part, up, mem_count, start, columns, width=512):
    forks = part.shape[0]
    line, fork_own = mem_count // 2, forks // mem_count
    out = jax.ShapeDtypeStruct((line, fork_own, columns), F32)
    return pl.pallas_call(
        functools.partial(delta_kernel, line, start),
        out_shape=(out, out),
        in_specs=[pl.BlockSpec(memory_space=pltpu.SMEM)]
        + [pl.BlockSpec(memory_space=pltpu.VMEM)] * (line + 3),
        out_specs=(pl.BlockSpec(memory_space=pltpu.VMEM),) * 2,
        scratch_shapes=[pltpu.VMEM((mem_count, fork_own, width), F32)],
        compiler_params=params(8 * MIB),
        cost_estimate=pl.CostEstimate(
            flops=2 * forks * up.shape[0] * columns,
            bytes_accessed=2 * up.shape[0] * columns + 8 * forks * columns,
            transcendentals=0,
        ),
        name="add_delta",
    )(index, adapter.reshape(1, forks), *rank_parts, in_vmem(part), in_vmem(up))


def put_terms(lse):
    heads, forks = lse.shape
    high = lse.astype(BF16).astype(F32)
    rest = lse - high
    middle = rest.astype(BF16).astype(F32)
    low = rest - middle
    spare = jnp.zeros((HEAD_WIDTH - 3 * heads, forks), F32)
    return jnp.concatenate([high, middle, low, spare], axis=0).T.astype(BF16)


def get_terms(terms, heads):
    terms = terms.astype(F32)
    return terms[:, :heads] + terms[:, heads : 2 * heads] + terms[:, 2 * heads : 3 * heads]


def attend_kernel(q_ref, k_ref, v_ref, mask_ref, out_ref, score_ref, lse_ref):
    kv_head = pl.program_id(0)
    steps = pl.num_programs(0)
    forks = q_ref.shape[0]
    group = q_ref.shape[1] // HEAD_WIDTH
    pages = k_ref.shape[0]
    queries = jnp.concatenate(
        [q_ref[:, g * HEAD_WIDTH : (g + 1) * HEAD_WIDTH] for g in range(group)], axis=0
    )
    scale = SCORE_SCALE * LOG2E
    peaks = []
    top = None
    for p in range(pages):
        scores = lax.dot_general(
            k_ref[p], queries, (((1,), (1,)), ((), ())), preferred_element_type=F32
        )
        score_ref[p] = scores
        peak = jnp.max(scores, axis=0, keepdims=True)
        peaks.append(peak)
        chosen = jnp.where(mask_ref[p : p + 1, :] > 0, peak, neg_floor)
        top = chosen if top is None else jnp.maximum(top, chosen)
    acc = None
    mass = None
    for p in range(pages):
        weights = jnp.exp2((score_ref[p] - peaks[p]) * scale).astype(BF16)
        chosen = mask_ref[p : p + 1, :] > 0
        factor = jnp.where(
            chosen, jnp.exp2((jnp.where(chosen, peaks[p], neg_floor) - top) * scale), 0.0
        )
        page_mass = jnp.sum(weights.astype(F32), axis=0, keepdims=True) * factor
        page_acc = (
            lax.dot_general(
                v_ref[p], weights, (((0,), (0,)), ((), ())), preferred_element_type=F32
            )
            * factor
        )
        acc = page_acc if acc is None else acc + page_acc
        mass = page_mass if mass is None else mass + page_mass
    some = mass > 0
    safe = jnp.where(some, mass, 1.0)
    rows = (acc * jnp.where(some, 1.0 / safe, 0.0)).T
    lse = jnp.where(some, top * scale + jnp.log2(safe), neg_floor)
    for g in range(group):
        column = pl.multiple_of((kv_head * group + g) * HEAD_WIDTH, HEAD_WIDTH)
        out_ref[:, pl.ds(column, HEAD_WIDTH)] = rows[g * forks : (g + 1) * forks].astype(BF16)
    lse_ref[kv_head] = jnp.concatenate(
        [lse[:, g * forks : (g + 1) * forks] for g in range(group)], axis=0
    )

    @pl.when(kv_head == steps - 1)
    def _():
        heads = lse_ref.shape[0] * group
        out_ref[:, pl.ds(heads * HEAD_WIDTH, HEAD_WIDTH)] = put_terms(
            lse_ref[...].reshape(heads, forks)
        )


def attend(queries, keys, values, mask):
    forks, width = queries.shape
    pages, page_len, kv_width = keys.shape
    kv_local = kv_width // HEAD_WIDTH
    group_width = width // kv_local
    rows = mask.shape[1]
    flops = 4 * pages * page_len * kv_local * rows * HEAD_WIDTH
    return pl.pallas_call(
        attend_kernel,
        grid=(kv_local,),
        out_shape=jax.ShapeDtypeStruct((forks, width + HEAD_WIDTH), BF16),
        in_specs=[
            pl.BlockSpec((forks, group_width), lambda i: (0, i)),
            pl.BlockSpec((pages, page_len, HEAD_WIDTH), lambda i: (0, 0, i)),
            pl.BlockSpec((pages, page_len, HEAD_WIDTH), lambda i: (0, 0, i)),
            whole((pages, rows)),
        ],
        out_specs=whole((forks, width + HEAD_WIDTH)),
        scratch_shapes=[
            pltpu.VMEM((pages, page_len, rows), F32),
            pltpu.VMEM((kv_local, group_width // HEAD_WIDTH, forks), F32),
        ],
        compiler_params=params(6 * pages * page_len * rows + 8 * MIB, "arbitrary"),
        cost_estimate=pl.CostEstimate(
            flops=flops,
            bytes_accessed=4 * pages * page_len * kv_width + 4 * forks * width,
            transcendentals=pages * page_len * kv_local * rows,
        ),
        name="attend",
    )(queries, in_vmem(keys), in_vmem(values), mask)


def merge_kernel(heads, kv_heads, sources, *refs):
    parts, (q_ref, new_ref, out_ref) = refs[:sources], refs[sources:]
    group = heads // kv_heads
    width = heads * HEAD_WIDTH
    lses = [get_terms(ref[:, width : width + HEAD_WIDTH], heads) for ref in parts]

    def new_head(i):
        return new_ref[:, i * HEAD_WIDTH : (i + 1) * HEAD_WIDTH].astype(F32)

    scores = []
    for h in range(heads):
        query = q_ref[:, h * HEAD_WIDTH : (h + 1) * HEAD_WIDTH].astype(F32)
        scores.append(jnp.sum(query * new_head(h // group), axis=1, keepdims=True))
    own = jnp.concatenate(scores, axis=1) * (SCORE_SCALE * LOG2E)
    top = functools.reduce(jnp.maximum, lses, own)
    own_weight = jnp.exp2(own - top)
    weights = [jnp.exp2(lse - top) for lse in lses]
    inverse = 1.0 / functools.reduce(jnp.add, weights, own_weight)
    own_weight = own_weight * inverse
    weights = [weight * inverse for weight in weights]
    for h in range(heads):
        lanes = slice(h * HEAD_WIDTH, (h + 1) * HEAD_WIDTH)
        total = own_weight[:, h : h + 1] * new_head(kv_heads + h // group)
        for weight, ref in zip(weights, parts):
            total += weight[:, h : h + 1] * ref[:, lanes].astype(F32)
        out_ref[:, lanes] = total.astype(BF16)


def merge(parts, queries, new, heads, kv_heads):
    fork_own, width = parts[0].shape
    size = len(parts) * fork_own * width
    return pl.pallas_call(
        functools.partial(merge_kernel, heads, kv_heads, len(parts)),
        out_shape=jax.ShapeDtypeStruct((fork_own, heads * HEAD_WIDTH), BF16),
        compiler_params=params(4 * size + 4 * MIB),
        cost_estimate=pl.CostEstimate(flops=4 * size, bytes_accessed=2 * size, transcendentals=0),
        name="merge",
    )(*parts, queries, new)


def output_kernel(context_ref, weight_ref, out_ref):
    part = jnp.dot(context_ref[...], weight_ref[...], preferred_element_type=F32)

    @pl.when(pl.program_id(0) == 0)
    def _():
        out_ref[...] = part

    @pl.when(pl.program_id(0) > 0)
    def _():
        out_ref[...] += part


def output_project(context, weight, depth=1024):
    forks, rows = context.shape
    columns = weight.shape[1]
    return pl.pallas_call(
        output_kernel,
        grid=(rows // depth,),
        out_shape=jax.ShapeDtypeStruct((forks, columns), F32),
        in_specs=[
            pl.BlockSpec((forks, depth), lambda i: (0, i)),
            pl.BlockSpec((depth, columns), lambda i: (i, 0)),
        ],
        out_specs=whole((forks, columns)),
        compiler_params=params(8 * MIB, "arbitrary"),
        cost_estimate=pl.CostEstimate(
            flops=2 * forks * rows * columns, bytes_accessed=2 * rows * columns, transcendentals=0
        ),
        name="output_project",
    )(context, in_vmem(weight))


def shards(
    hidden,
    adapter,
    page_cache_slot,
    selection,
    query_projection_weight,
    key_projection_weight,
    value_projection_weight,
    adapter_down_weight,
    adapter_up_weight,
    output_projection_weight,
    prefix_key_cache,
    prefix_value_cache,
):
    mem_count = lax.axis_size("mem")
    mem_index = lax.axis_index("mem")
    forks = hidden.shape[0]
    fork_own = forks // mem_count
    q_width = query_projection_weight.shape[1]
    kv_width = key_projection_weight.shape[1]
    heads, kv_heads = q_width // HEAD_WIDTH, kv_width // HEAD_WIDTH
    pages = prefix_key_cache.shape[0]
    line = mem_count // 2
    index = mem_index.reshape(1)
    place, parity = mem_index // 2, mem_index % 2

    def shifted(x, shift, cross=0):
        pairs = [
            (i, 2 * ((i // 2 + shift) % line) + (i % 2 + cross) % 2) for i in range(mem_count)
        ]
        return lax.ppermute(x, "mem", pairs)

    def along(blocks, cross=0):
        return [shifted(blocks[i], i, cross) if i or cross else blocks[0] for i in range(line)]

    def gather(x):
        return jnp.concatenate([x] + [shifted(x, -i) for i in range(1, line)], axis=0)

    def pair(x):
        return shifted(x, 0, 1)

    near_rank, far_rank = down_project(index, adapter, hidden, adapter_down_weight, mem_count)
    rank_sum = near_rank + pair(far_rank)
    after_pair, rank_sum = lax.optimization_barrier((index, rank_sum))
    rank_parts = along(rank_sum)
    part, near_new, far_new, up = project(
        after_pair,
        hidden,
        query_projection_weight,
        key_projection_weight,
        value_projection_weight,
        adapter_up_weight.reshape(-1, q_width),
        mem_count,
    )
    new_sum = near_new + pair(far_new)

    half = q_width // 2
    near_a, far_a = add_delta(index, adapter, rank_parts, part, up, mem_count, 0, half)
    sum_a = near_a + pair(far_a)
    near_b, far_b = add_delta(index, adapter, rank_parts, part, up, mem_count, half, half)
    sum_b = jnp.concatenate([near_b + pair(far_b), new_sum], axis=2)
    own_a = functools.reduce(jnp.add, along(sum_a)).astype(BF16)
    own_b = functools.reduce(jnp.add, along(sum_b)).astype(BF16)
    own_queries = jnp.concatenate([own_a, own_b[:, :half]], axis=1)
    own_new = own_b[:, half:]

    slot_ids = mem_index * pages + jnp.arange(pages, dtype=jnp.int32)
    slot_match = (page_cache_slot[None, :] == slot_ids[:, None]).astype(BF16)
    chosen = lax.dot_general(
        slot_match, (selection > 0).astype(BF16), (((1,), (1,)), ((), ())), preferred_element_type=F32
    ).reshape(pages, line, 2, fork_own)
    chosen = jnp.roll(chosen, -place, axis=1)
    even, odd = (chosen[:, :, p].reshape(pages, line * fork_own) for p in range(2))
    mask_near = jnp.tile(jnp.where(parity == 0, even, odd), (1, heads // kv_heads))
    mask_far = jnp.tile(jnp.where(parity == 0, odd, even), (1, heads // kv_heads))

    keys, values = stage(prefix_key_cache, prefix_value_cache)
    near_queries = gather(own_queries)
    far_queries = pair(near_queries)
    near = attend(near_queries, keys, values, mask_near)
    far = attend(far_queries, keys, values, mask_far)
    blocks = (line, fork_own, q_width + HEAD_WIDTH)
    parts = along(near.reshape(blocks)) + along(far.reshape(blocks), 1)
    context_own = merge(parts, own_queries, own_new, heads, kv_heads)

    (out_weight,) = stage(output_projection_weight)
    near_context = gather(context_own)
    far_context = pair(near_context)
    near_out = output_project(near_context, out_weight)
    far_out = output_project(far_context, out_weight)
    tp_count = lax.axis_size("tp")
    outs = []
    for part in (near_out, far_out):
        total = part
        for shift in range(1, tp_count):
            pairs = [(i, (i + shift) % tp_count) for i in range(tp_count)]
            total = total + lax.ppermute(part, "tp", pairs)
        outs.append(jnp.roll(total.astype(BF16).reshape(line, 1, fork_own, -1), place, axis=0))
    near_out, far_out = outs
    return jnp.concatenate(
        [jnp.where(parity == 0, near_out, far_out), jnp.where(parity == 0, far_out, near_out)], axis=1
    ).reshape(forks, -1)


def solution(mesh):
    return jax.shard_map(
        shards,
        mesh=mesh,
        in_specs=(
            P("groups", "mem"),
            P("groups"),
            P("groups"),
            P("groups", None),
            P("mem", "tp"),
            P("mem", "tp"),
            P("mem", "tp"),
            P("mem", None),
            P("mem", None, "tp"),
            P("tp", "mem"),
            P(("groups", "mem"), None, "tp"),
            P(("groups", "mem"), None, "tp"),
        ),
        out_specs=P("groups", "mem"),
        check_vma=False,
    )
```

```python
import functools

import jax
import jax.numpy as jnp
from jax import lax
from jax.experimental import pallas as pl
from jax.experimental.pallas import tpu as pltpu
from jax.sharding import PartitionSpec as P

HEAD_WIDTH = 128
ADAPTER_RANK = 64
ADAPTER_COUNT = 32
LOG2E = 1.4426950408889634
SCORE_SCALE = HEAD_WIDTH ** (-0.5)
neg_floor = -1e30
MIB = 1024 * 1024
F32 = jnp.float32
BF16 = jnp.bfloat16


def params(limit, *semantics):
    return pltpu.CompilerParams(
        dimension_semantics=semantics or None, vmem_limit_bytes=int(limit)
    )


def whole(shape):
    return pl.BlockSpec(shape, lambda *_: (0,) * len(shape))


def in_hbm(x):
    return pltpu.with_memory_space_constraint(x, pltpu.HBM)


def in_vmem(x):
    return pltpu.with_memory_space_constraint(x, pltpu.VMEM)


def cost(flops, size, transcendentals=0):
    return pl.CostEstimate(
        flops=int(flops), bytes_accessed=int(size), transcendentals=int(transcendentals)
    )


VMEM_SPEC = pl.BlockSpec(memory_space=pltpu.VMEM)
SMEM_SPEC = pl.BlockSpec(memory_space=pltpu.SMEM)
ANY_SPEC = pl.BlockSpec(memory_space=pl.ANY)


def stage_kernel(pieces, *refs):
    count = len(refs[:-1]) // (pieces + 1)
    sources, targets, sems = refs[:count], refs[count:-1], refs[-1]
    copies = []
    for i, target in enumerate(targets):
        rows = pl.ds((i % pieces) * target.shape[0], target.shape[0])
        copies.append(
            pltpu.make_async_copy(sources[i // pieces].at[rows], target, sems.at[i])
        )
    for copy in copies:
        copy.start()
    for copy in copies:
        copy.wait()


def stage(*arrays, pieces=4):
    shapes = [(x.shape[0] // pieces,) + x.shape[1:] for x in arrays for _ in range(pieces)]
    return pl.pallas_call(
        functools.partial(stage_kernel, pieces),
        out_shape=tuple(pltpu.VMEM(shape, BF16) for shape in shapes),
        in_specs=[ANY_SPEC] * len(arrays),
        out_specs=(ANY_SPEC,) * len(shapes),
        scratch_shapes=[pltpu.SemaphoreType.DMA((len(shapes),))],
        compiler_params=params(MIB),
        cost_estimate=cost(0, sum(2 * x.size for x in arrays)),
        name="stage",
    )(*[in_hbm(x) for x in arrays])


def take_blocks(index, blocks_ref, near_ref, far_ref):
    place, parity = index // 2, index % 2
    for i in range(near_ref.shape[0]):
        at = 2 * (place ^ i)
        near_ref[i] = blocks_ref[at + parity]
        far_ref[i] = blocks_ref[at + 1 - parity]


def put_blocks(index, value, blocks_ref, near_ref, far_ref):
    count, rows, lanes = blocks_ref.shape
    own = value.shape[0] // count
    for i in range(count):
        blocks_ref[i, :own] = value[i * own : (i + 1) * own]
        if own < rows:
            blocks_ref[i, own:] = jnp.zeros((rows - own, lanes), F32)
    take_blocks(index, blocks_ref, near_ref, far_ref)


def first_kernel(
    index_ref,
    adapter_hbm,
    hidden_hbm,
    down_hbm,
    k_hbm,
    v_hbm,
    near_ref,
    far_ref,
    hidden_ref,
    adapter_ref,
    held,
    held_kv,
    rank_blocks,
    kv_blocks,
    sems,
):
    pieces, _, width = held.shape
    forks = hidden_ref.shape[0]
    kv_width = held_kv.shape[2]
    lanes = rank_blocks.shape[2]
    copies = [
        pltpu.make_async_copy(adapter_hbm, adapter_ref, sems.at[pieces + 3]),
        pltpu.make_async_copy(hidden_hbm, hidden_ref, sems.at[pieces + 2]),
        *[
            pltpu.make_async_copy(
                down_hbm.at[:, i * width : (i + 1) * width], held.at[i], sems.at[i]
            )
            for i in range(pieces)
        ],
        pltpu.make_async_copy(k_hbm, held_kv.at[0], sems.at[pieces]),
        pltpu.make_async_copy(v_hbm, held_kv.at[1], sems.at[pieces + 1]),
    ]
    for copy in copies:
        copy.start()
    copies[0].wait()
    fork_adapter = jnp.broadcast_to(adapter_ref[...].astype(F32), (HEAD_WIDTH, forks)).T
    lane_adapter = lax.broadcasted_iota(jnp.int32, (forks, HEAD_WIDTH), 1) // ADAPTER_RANK
    wanted = fork_adapter.astype(jnp.int32) - lane_adapter
    total = jnp.zeros((forks, HEAD_WIDTH), F32)
    copies[1].wait()
    for i in range(pieces):
        copies[2 + i].wait()
        block = jnp.dot(hidden_ref[...], held[i], preferred_element_type=F32)
        for j in range(width // HEAD_WIDTH):
            first = (i * width + j * HEAD_WIDTH) // ADAPTER_RANK
            part = block[:, j * HEAD_WIDTH : (j + 1) * HEAD_WIDTH]
            total += jnp.where(wanted == first, part, 0.0)
    flipped = total.T
    flipped = flipped[:ADAPTER_RANK] + flipped[ADAPTER_RANK:]
    if lanes > forks:
        flipped = jnp.concatenate([flipped, jnp.zeros((ADAPTER_RANK, lanes - forks), F32)], axis=1)
    at = slice(0, lanes)
    put_blocks(index_ref[0], flipped, rank_blocks, near_ref.at[:, :, at], far_ref.at[:, :, at])
    for i in range(2):
        copies[2 + pieces + i].wait()
        part = jnp.dot(hidden_ref[...], held_kv[i], preferred_element_type=F32)
        at = slice(lanes + i * kv_width, lanes + (i + 1) * kv_width)
        put_blocks(index_ref[0], part, kv_blocks, near_ref.at[:, :, at], far_ref.at[:, :, at])


def project_first(index, adapter, hidden, down, k_weight, v_weight, mem_count, width=256):
    forks, depth = hidden.shape
    columns, kv_width = down.shape[1], k_weight.shape[1]
    lanes = -(-forks // HEAD_WIDTH) * HEAD_WIDTH
    line, fork_own = mem_count // 2, forks // mem_count
    pieces = columns // width
    out = pltpu.VMEM((line, fork_own, lanes + 2 * kv_width), F32)
    weights = 2 * depth * (columns + 2 * kv_width)
    return pl.pallas_call(
        first_kernel,
        out_shape=(out, out, pltpu.VMEM(hidden.shape, BF16), pltpu.VMEM((1, forks), jnp.int32)),
        in_specs=[SMEM_SPEC] + [ANY_SPEC] * 5,
        out_specs=(VMEM_SPEC,) * 4,
        scratch_shapes=[
            pltpu.VMEM((pieces, depth, width), BF16),
            pltpu.VMEM((2, depth, kv_width), BF16),
            pltpu.VMEM((mem_count, fork_own, lanes), F32),
            pltpu.VMEM((mem_count, fork_own, kv_width), F32),
            pltpu.SemaphoreType.DMA((pieces + 4,)),
        ],
        compiler_params=params(weights + 4 * MIB),
        cost_estimate=cost(forks * weights, weights),
        name="project_first",
    )(index, *[in_hbm(x) for x in (adapter.reshape(1, forks), hidden, down, k_weight, v_weight)])


def project_kernel(start, extra, hidden_ref, q_hbm, *refs):
    up_hbm, part_ref, up_ref, held, sems = refs if extra else (None, refs[0], None, *refs[1:])
    pieces, _, width = held.shape
    copies = []
    for i in range(pieces):
        columns = pl.ds(start + i * width, width)
        copies.append(pltpu.make_async_copy(q_hbm.at[:, columns], held.at[i], sems.at[i]))
    if extra:
        copies.append(pltpu.make_async_copy(up_hbm, up_ref, sems.at[pieces]))
    for copy in copies:
        copy.start()
    for i in range(pieces):
        copies[i].wait()
        part_ref[:, i * width : (i + 1) * width] = jnp.dot(
            hidden_ref[...], held[i], preferred_element_type=F32
        )
    if extra:
        copies[-1].wait()


def project(hidden, q_weight, start, columns, up=None, width=512):
    forks, depth = hidden.shape
    pieces = columns // width
    weights = 2 * depth * columns
    extra = [] if up is None else [up]
    return pl.pallas_call(
        functools.partial(project_kernel, start, bool(extra)),
        out_shape=tuple(
            [pltpu.VMEM((forks, columns), F32)] + [pltpu.VMEM(x.shape, BF16) for x in extra]
        ),
        in_specs=[VMEM_SPEC] + [ANY_SPEC] * (1 + len(extra)),
        out_specs=(VMEM_SPEC,) * (1 + len(extra)),
        scratch_shapes=[
            pltpu.VMEM((pieces, depth, width), BF16),
            pltpu.SemaphoreType.DMA((pieces + 1,)),
        ],
        compiler_params=params(weights + 2 * MIB),
        cost_estimate=cost(forks * weights, weights + sum(2 * x.size for x in extra)),
        name="project",
    )(in_vmem(hidden), *[in_hbm(x) for x in [q_weight] + extra])


def delta_kernel(line, ranks, start, index_ref, adapter_ref, *refs):
    rank_refs = refs[:line]
    part_ref, up_ref, near_ref, far_ref, blocks_ref = refs[line:]
    forks, width = part_ref.shape[0], blocks_ref.shape[2]
    acts = functools.reduce(jnp.add, [ref[:ranks, :forks] for ref in rank_refs])
    acts = acts.astype(BF16).astype(F32)
    adapters = lax.broadcasted_iota(jnp.int32, (ADAPTER_COUNT, forks), 0)
    onehot = (adapters == adapter_ref[...]).astype(F32)
    spread = jnp.concatenate(
        [acts[r : r + 1, :] * onehot for r in range(ranks)], axis=0
    ).astype(BF16)
    for i in range(near_ref.shape[2] // width):
        delta = lax.dot_general(
            spread,
            up_ref[:, start + i * width : start + (i + 1) * width],
            (((0,), (0,)), ((), ())),
            preferred_element_type=F32,
        )
        at = slice(i * width, (i + 1) * width)
        put_blocks(
            index_ref[0],
            part_ref[:, at] + delta,
            blocks_ref,
            near_ref.at[:, :, at],
            far_ref.at[:, :, at],
        )


def add_delta(index, adapter, rank_parts, part, up, mem_count, start, width=512):
    forks, columns = part.shape
    line, fork_own = mem_count // 2, forks // mem_count
    ranks = ADAPTER_RANK // mem_count
    out = pltpu.VMEM((line, fork_own, columns), F32)
    return pl.pallas_call(
        functools.partial(delta_kernel, line, ranks, start),
        out_shape=(out, out),
        in_specs=[SMEM_SPEC] + [VMEM_SPEC] * (line + 3),
        out_specs=(VMEM_SPEC,) * 2,
        scratch_shapes=[pltpu.VMEM((mem_count, fork_own, width), F32)],
        compiler_params=params(4 * MIB),
        cost_estimate=cost(
            2 * forks * up.shape[0] * columns, 2 * up.shape[0] * columns + 8 * forks * columns
        ),
        name="add_delta",
    )(index, in_vmem(adapter), *rank_parts, in_vmem(part), in_vmem(up))


def put_terms(lse):
    heads, forks = lse.shape
    high = lse.astype(BF16).astype(F32)
    rest = lse - high
    middle = rest.astype(BF16).astype(F32)
    low = rest - middle
    spare = jnp.zeros((HEAD_WIDTH - 3 * heads, forks), F32)
    return jnp.concatenate([high, middle, low, spare], axis=0).T.astype(BF16)


def get_terms(terms, heads):
    terms = terms.astype(F32)
    return terms[:, :heads] + terms[:, heads : 2 * heads] + terms[:, 2 * heads : 3 * heads]


def attend_kernel(pieces, q_ref, mask_ref, *refs):
    k_refs, v_refs, (out_ref, score_ref, lse_ref) = (
        refs[:pieces],
        refs[pieces : 2 * pieces],
        refs[2 * pieces :],
    )
    forks = q_ref.shape[0]
    kv_local, group = lse_ref.shape[:2]
    pages = score_ref.shape[0]
    held = pages // pieces
    scale = SCORE_SCALE * LOG2E
    mask = jnp.concatenate([mask_ref[...]] * group, axis=1) > 0
    ones = jnp.ones((8, score_ref.shape[1]), BF16)

    @pl.loop(0, kv_local)
    def _(kv_head):
        def head(i):
            return pl.ds(pl.multiple_of((kv_head * group + i) * HEAD_WIDTH, HEAD_WIDTH), HEAD_WIDTH)

        lanes = pl.ds(pl.multiple_of(kv_head * HEAD_WIDTH, HEAD_WIDTH), HEAD_WIDTH)
        queries = jnp.concatenate([q_ref[:, head(g)] for g in range(group)], axis=0)
        peaks = []
        top = None
        for p in range(pages):
            scores = lax.dot_general(
                k_refs[p // held][p % held, :, lanes],
                queries,
                (((1,), (1,)), ((), ())),
                preferred_element_type=F32,
            )
            score_ref[p] = scores
            peak = jnp.max(scores, axis=0, keepdims=True)
            peaks.append(peak)
            chosen = jnp.where(mask[p : p + 1], peak, neg_floor)
            top = chosen if top is None else jnp.maximum(top, chosen)
        acc = None
        for p in range(pages):
            weights = jnp.exp2((score_ref[p] - peaks[p]) * scale).astype(BF16)
            chosen = jnp.where(mask[p : p + 1], peaks[p], neg_floor)
            factor = jnp.where(mask[p : p + 1], jnp.exp2((chosen - top) * scale), 0.0)
            values = jnp.concatenate([v_refs[p // held][p % held, :, lanes].T, ones], axis=0)
            term = jnp.dot(values, weights, preferred_element_type=F32) * factor
            acc = term if acc is None else acc + term
        mass = acc[HEAD_WIDTH : HEAD_WIDTH + 1]
        some = mass > 0
        safe = jnp.where(some, mass, 1.0)
        rows = (acc[:HEAD_WIDTH] * jnp.where(some, 1.0 / safe, 0.0)).T
        lse = jnp.where(some, top * scale + jnp.log2(safe), neg_floor)
        for g in range(group):
            out_ref[:, head(g)] = rows[g * forks : (g + 1) * forks].astype(BF16)
        lse_ref[kv_head] = jnp.concatenate(
            [lse[:, g * forks : (g + 1) * forks] for g in range(group)], axis=0
        )

    heads = kv_local * group
    out_ref[:, heads * HEAD_WIDTH :] = put_terms(lse_ref[...].reshape(heads, forks))


def attend(queries, keys, values, mask):
    forks, width = queries.shape
    held, page_len, kv_width = keys[0].shape
    pieces = len(keys)
    pages = held * pieces
    kv_local = kv_width // HEAD_WIDTH
    group = width // kv_width
    rows = group * forks
    return pl.pallas_call(
        functools.partial(attend_kernel, pieces),
        out_shape=pltpu.VMEM((forks, width + HEAD_WIDTH), BF16),
        in_specs=[VMEM_SPEC] * (2 + 2 * pieces),
        out_specs=VMEM_SPEC,
        scratch_shapes=[
            pltpu.VMEM((pages, page_len, rows), F32),
            pltpu.VMEM((kv_local, group, forks), F32),
        ],
        compiler_params=params(6 * pages * page_len * rows + 4 * MIB),
        cost_estimate=cost(
            4 * pages * page_len * kv_local * rows * HEAD_WIDTH,
            4 * pages * page_len * kv_width + 4 * forks * width,
            pages * page_len * kv_local * rows,
        ),
        name="attend",
    )(queries, mask, *[in_vmem(x) for x in [*keys, *values]])


def merge_kernel(heads, kv_heads, sources, *refs):
    parts, (q_ref, new_ref, out_ref) = refs[:sources], refs[sources:]
    group = heads // kv_heads
    width = heads * HEAD_WIDTH
    lses = [get_terms(ref[:, width : width + HEAD_WIDTH], heads) for ref in parts]

    def new_head(i):
        return new_ref[:, i * HEAD_WIDTH : (i + 1) * HEAD_WIDTH].astype(F32)

    scores = []
    for h in range(heads):
        query = q_ref[:, h * HEAD_WIDTH : (h + 1) * HEAD_WIDTH].astype(F32)
        scores.append(jnp.sum(query * new_head(h // group), axis=1, keepdims=True))
    own = jnp.concatenate(scores, axis=1) * (SCORE_SCALE * LOG2E)
    top = functools.reduce(jnp.maximum, lses, own)
    own_weight = jnp.exp2(own - top)
    weights = [jnp.exp2(lse - top) for lse in lses]
    inverse = 1.0 / functools.reduce(jnp.add, weights, own_weight)
    own_weight = own_weight * inverse
    weights = [weight * inverse for weight in weights]
    for h in range(heads):
        lanes = slice(h * HEAD_WIDTH, (h + 1) * HEAD_WIDTH)
        total = own_weight[:, h : h + 1] * new_head(kv_heads + h // group)
        for weight, ref in zip(weights, parts):
            total += weight[:, h : h + 1] * ref[:, lanes].astype(F32)
        out_ref[:, lanes] = total.astype(BF16)


def merge(parts, queries, new, heads, kv_heads):
    fork_own, width = parts[0].shape
    size = len(parts) * fork_own * width
    return pl.pallas_call(
        functools.partial(merge_kernel, heads, kv_heads, len(parts)),
        out_shape=jax.ShapeDtypeStruct((fork_own, heads * HEAD_WIDTH), BF16),
        compiler_params=params(4 * size + 4 * MIB),
        cost_estimate=pl.CostEstimate(flops=4 * size, bytes_accessed=2 * size, transcendentals=0),
        name="merge",
    )(*parts, queries, new)


def output_kernel(context_ref, *refs):
    weight_refs, out_ref = refs[:-1], refs[-1]
    total = None
    for i, ref in enumerate(weight_refs):
        depth = ref.shape[0]
        part = jnp.dot(
            context_ref[:, i * depth : (i + 1) * depth], ref[...], preferred_element_type=F32
        )
        total = part if total is None else total + part
    out_ref[...] = total


def output_project(context, weights):
    forks, rows = context.shape
    columns = weights[0].shape[1]
    return pl.pallas_call(
        output_kernel,
        out_shape=pltpu.VMEM((forks, columns), F32),
        in_specs=[VMEM_SPEC] * (1 + len(weights)),
        out_specs=VMEM_SPEC,
        compiler_params=params(4 * MIB),
        cost_estimate=cost(2 * forks * rows * columns, 2 * rows * columns),
        name="output_project",
    )(context, *[in_vmem(x) for x in weights])


def finish_kernel(count, line, index_ref, *refs):
    near_refs, far_refs, out_ref = refs[:count], refs[count : 2 * count], refs[-1]
    place, parity = index_ref[0] // 2, index_ref[0] % 2
    rows = out_ref.shape[1]
    for group, side in ((near_refs, parity), (far_refs, 1 - parity)):
        for i in range(line):
            total = functools.reduce(jnp.add, [ref[i * rows : (i + 1) * rows] for ref in group])
            out_ref[2 * (place ^ i) + side] = total.astype(BF16)


def finish(index, near, far, mem_count):
    rows, columns = near[0].shape
    line = mem_count // 2
    return pl.pallas_call(
        functools.partial(finish_kernel, len(near), line),
        out_shape=jax.ShapeDtypeStruct((mem_count, rows // line, columns), BF16),
        in_specs=[SMEM_SPEC] + [VMEM_SPEC] * (2 * len(near)),
        out_specs=VMEM_SPEC,
        compiler_params=params(4 * MIB),
        cost_estimate=cost(0, 8 * rows * columns * len(near)),
        name="finish",
    )(index, *near, *far)


def shards(
    hidden,
    adapter,
    page_cache_slot,
    selection,
    query_projection_weight,
    key_projection_weight,
    value_projection_weight,
    adapter_down_weight,
    adapter_up_weight,
    output_projection_weight,
    prefix_key_cache,
    prefix_value_cache,
):
    mem_count = lax.axis_size("mem")
    mem_index = lax.axis_index("mem")
    forks = hidden.shape[0]
    fork_own = forks // mem_count
    q_width = query_projection_weight.shape[1]
    kv_width = key_projection_weight.shape[1]
    heads, kv_heads = q_width // HEAD_WIDTH, kv_width // HEAD_WIDTH
    pages = prefix_key_cache.shape[0]
    line = mem_count // 2
    index = mem_index.reshape(1)
    place, parity = mem_index // 2, mem_index % 2

    def swapped(x, step, cross=0):
        pairs = [(i, i ^ (2 * step + cross)) for i in range(mem_count)]
        return lax.ppermute(x, "mem", pairs)

    def along(blocks, cross=0):
        return [swapped(blocks[i], i, cross) if i or cross else blocks[0] for i in range(line)]

    def gather(x):
        return jnp.concatenate([x] + [swapped(x, i) for i in range(1, line)], axis=0)

    def pair(x):
        return swapped(x, 0, 1)

    def by_place(x):
        x = x.reshape(line, 2, fork_own, -1)
        bit = 1
        while bit < line:
            flipped = jnp.flip(x.reshape(line // (2 * bit), 2, bit, -1), axis=1).reshape(x.shape)
            x = jnp.where((place & bit) > 0, flipped, x)
            bit *= 2
        even, odd = x[:, 0].reshape(line * fork_own, -1), x[:, 1].reshape(line * fork_own, -1)
        return jnp.where(parity == 0, even, odd), jnp.where(parity == 0, odd, even)

    near_1, far_1, hidden, adapter = project_first(
        index, adapter, hidden, adapter_down_weight, key_projection_weight, value_projection_weight, mem_count
    )
    half = q_width // 2
    (part_a,) = project(hidden, query_projection_weight, 0, half)
    first_sum, part_a, hidden = lax.optimization_barrier((near_1 + pair(far_1), part_a, hidden))
    first_parts = along(first_sum)
    part_b, up = project(
        hidden, query_projection_weight, half, half, adapter_up_weight.reshape(-1, q_width)
    )
    lanes = first_sum.shape[2] - 2 * kv_width
    rank_parts = [x[:, :lanes] for x in first_parts]
    own_new = functools.reduce(jnp.add, [x[:, lanes:] for x in first_parts]).astype(BF16)

    near_a, far_a = add_delta(index, adapter, rank_parts, part_a, up, mem_count, 0)
    got_a = pair(far_a)
    near_b, far_b = add_delta(index, adapter, rank_parts, part_b, up, mem_count, half)
    got_a, far_b = lax.optimization_barrier((got_a, far_b))
    got_b = pair(far_b)
    own_a = functools.reduce(jnp.add, along(near_a + got_a)).astype(BF16)
    own_b = functools.reduce(jnp.add, along(near_b + got_b)).astype(BF16)
    own_queries = jnp.concatenate([own_a, own_b], axis=1)

    slot_ids = mem_index * pages + jnp.arange(pages, dtype=jnp.int32)
    slot_match = (page_cache_slot[None, :] == slot_ids[:, None]).astype(BF16)
    near_mask, far_mask = [
        lax.dot_general(
            slot_match, (x > 0).astype(BF16), (((1,), (1,)), ((), ())), preferred_element_type=F32
        )
        for x in by_place(selection)
    ]

    staged = stage(prefix_key_cache, prefix_value_cache, pieces=2)
    keys, values = staged[:2], staged[2:]
    near_queries = gather(own_queries)
    far_queries = pair(near_queries)
    near = attend(near_queries, keys, values, near_mask)
    far = attend(far_queries, keys, values, far_mask)
    blocks = (line, fork_own, q_width + HEAD_WIDTH)
    parts = along(near.reshape(blocks)) + along(far.reshape(blocks), 1)
    context_own = merge(parts, own_queries, own_new, heads, kv_heads)

    out_weights = stage(output_projection_weight)
    near_context = gather(context_own)
    far_context = pair(near_context)
    tp_count = lax.axis_size("tp")
    outs = []
    for context in (near_context, far_context):
        part = output_project(context, out_weights)
        terms = [part]
        for shift in range(1, tp_count):
            pairs = [(i, (i + shift) % tp_count) for i in range(tp_count)]
            terms.append(lax.ppermute(part, "tp", pairs))
        outs.append(terms)
    return finish(index, *outs, mem_count).reshape(forks, -1)


def solution(mesh):
    return jax.shard_map(
        shards,
        mesh=mesh,
        in_specs=(
            P("groups", "mem"),
            P("groups"),
            P("groups"),
            P("groups", None),
            P("mem", "tp"),
            P("mem", "tp"),
            P("mem", "tp"),
            P("mem", None),
            P("mem", None, "tp"),
            P("tp", "mem"),
            P(("groups", "mem"), None, "tp"),
            P(("groups", "mem"), None, "tp"),
        ),
        out_specs=P("groups", "mem"),
        check_vma=False,
    )
```

```python
import functools

import jax
import jax.numpy as jnp
from jax import lax
from jax.experimental import pallas as pl
from jax.experimental.pallas import tpu as pltpu
from jax.sharding import PartitionSpec as P

HEAD_WIDTH = 128
ADAPTER_RANK = 64
ADAPTER_COUNT = 32
LOG2E = 1.4426950408889634
SCORE_SCALE = HEAD_WIDTH ** (-0.5)
neg_floor = -1e30
MIB = 1024 * 1024
F32 = jnp.float32
BF16 = jnp.bfloat16


def params(limit, *semantics):
    return pltpu.CompilerParams(
        dimension_semantics=semantics or None, vmem_limit_bytes=int(limit)
    )


def whole(shape):
    return pl.BlockSpec(shape, lambda *_: (0,) * len(shape))


def in_hbm(x):
    return pltpu.with_memory_space_constraint(x, pltpu.HBM)


def in_vmem(x):
    return pltpu.with_memory_space_constraint(x, pltpu.VMEM)


def cost(flops, size, transcendentals=0):
    return pl.CostEstimate(
        flops=int(flops), bytes_accessed=int(size), transcendentals=int(transcendentals)
    )


VMEM_SPEC = pl.BlockSpec(memory_space=pltpu.VMEM)
SMEM_SPEC = pl.BlockSpec(memory_space=pltpu.SMEM)
ANY_SPEC = pl.BlockSpec(memory_space=pl.ANY)


def stage_kernel(pieces, *refs):
    count = len(refs[:-1]) // (pieces + 1)
    sources, targets, sems = refs[:count], refs[count:-1], refs[-1]
    copies = []
    for i, target in enumerate(targets):
        rows = pl.ds((i % pieces) * target.shape[0], target.shape[0])
        copies.append(
            pltpu.make_async_copy(sources[i // pieces].at[rows], target, sems.at[i])
        )
    for copy in copies:
        copy.start()
    for copy in copies:
        copy.wait()


def stage(*arrays, pieces=4):
    shapes = [(x.shape[0] // pieces,) + x.shape[1:] for x in arrays for _ in range(pieces)]
    return pl.pallas_call(
        functools.partial(stage_kernel, pieces),
        out_shape=tuple(pltpu.VMEM(shape, BF16) for shape in shapes),
        in_specs=[ANY_SPEC] * len(arrays),
        out_specs=(ANY_SPEC,) * len(shapes),
        scratch_shapes=[pltpu.SemaphoreType.DMA((len(shapes),))],
        compiler_params=params(MIB),
        cost_estimate=cost(0, sum(2 * x.size for x in arrays)),
        name="stage",
    )(*[in_hbm(x) for x in arrays])


def cache_kernel(pieces, index_ref, slot_hbm, select_hbm, *refs):
    sources, targets = refs[:2], refs[2 : 2 + 2 * pieces]
    near_ref, far_ref, slot_ref, select_ref, blocks_ref, sems = refs[2 + 2 * pieces :]
    count = 2 * pieces
    first = [
        pltpu.make_async_copy(slot_hbm, slot_ref, sems.at[count]),
        pltpu.make_async_copy(select_hbm, select_ref, sems.at[count + 1]),
    ]
    copies = []
    for i, target in enumerate(targets):
        rows = pl.ds((i % pieces) * target.shape[0], target.shape[0])
        copies.append(
            pltpu.make_async_copy(sources[i // pieces].at[rows], target, sems.at[i])
        )
    for copy in first + copies:
        copy.start()
    for copy in first:
        copy.wait()
    pages, total = blocks_ref.shape[2], slot_ref.shape[1]
    slots = index_ref[0] * pages + lax.broadcasted_iota(jnp.int32, (pages, total), 0)
    match = (slots == slot_ref[...]).astype(BF16)
    chosen = (select_ref[...] > 0).astype(BF16)
    held = lax.dot_general(
        chosen, match, (((1,), (1,)), ((), ())), preferred_element_type=F32
    )
    put_blocks(index_ref[0], held, blocks_ref, near_ref, far_ref)
    for copy in copies:
        copy.wait()


def stage_cache(index, page_cache_slot, selection, keys, values, mem_count, pieces=2):
    forks, total = selection.shape
    pages = keys.shape[0]
    line, fork_own = mem_count // 2, forks // mem_count
    shapes = [(x.shape[0] // pieces,) + x.shape[1:] for x in (keys, values) for _ in range(pieces)]
    mask = pltpu.VMEM((line, fork_own, pages), F32)
    return pl.pallas_call(
        functools.partial(cache_kernel, pieces),
        out_shape=tuple(pltpu.VMEM(shape, BF16) for shape in shapes) + (mask, mask),
        in_specs=[SMEM_SPEC] + [ANY_SPEC] * 4,
        out_specs=(ANY_SPEC,) * len(shapes) + (VMEM_SPEC,) * 2,
        scratch_shapes=[
            pltpu.VMEM((1, total), jnp.int32),
            pltpu.VMEM((forks, total), jnp.int32),
            pltpu.VMEM((mem_count, fork_own, pages), F32),
            pltpu.SemaphoreType.DMA((2 * pieces + 2,)),
        ],
        compiler_params=params(4 * MIB),
        cost_estimate=cost(0, 4 * keys.size),
        name="stage_cache",
    )(index, *[in_hbm(x) for x in (page_cache_slot.reshape(1, total), selection, keys, values)])


def fold_kernel(one_ref, two_ref, *out_refs):
    for i, out_ref in enumerate(out_refs):
        out_ref[...] = one_ref[i] + two_ref[i]


def fold(one, two):
    out = pltpu.VMEM(one.shape[1:], F32)
    return pl.pallas_call(
        fold_kernel,
        out_shape=(out,) * one.shape[0],
        in_specs=[VMEM_SPEC] * 2,
        out_specs=(VMEM_SPEC,) * one.shape[0],
        compiler_params=params(MIB * 2 + 16 * one.size),
        cost_estimate=cost(one.size, 12 * one.size),
        name="fold",
    )(in_vmem(one), two)


def take_blocks(index, blocks_ref, near_ref, far_ref):
    place, parity = index // 2, index % 2
    for i in range(near_ref.shape[0]):
        at = 2 * (place ^ i)
        near_ref[i] = blocks_ref[at + parity]
        far_ref[i] = blocks_ref[at + 1 - parity]


def put_blocks(index, value, blocks_ref, near_ref, far_ref):
    count, rows, lanes = blocks_ref.shape
    own = value.shape[0] // count
    for i in range(count):
        blocks_ref[i, :own] = value[i * own : (i + 1) * own]
        if own < rows:
            blocks_ref[i, own:] = jnp.zeros((rows - own, lanes), F32)
    take_blocks(index, blocks_ref, near_ref, far_ref)


def first_kernel(
    index_ref,
    adapter_hbm,
    hidden_hbm,
    down_hbm,
    k_hbm,
    v_hbm,
    near_ref,
    far_ref,
    hidden_ref,
    adapter_ref,
    held,
    held_kv,
    rank_blocks,
    kv_blocks,
    sems,
):
    pieces, _, width = held.shape
    forks = hidden_ref.shape[0]
    kv_width = held_kv.shape[2]
    lanes = rank_blocks.shape[2]
    copies = [
        pltpu.make_async_copy(adapter_hbm, adapter_ref, sems.at[pieces + 3]),
        pltpu.make_async_copy(hidden_hbm, hidden_ref, sems.at[pieces + 2]),
        *[
            pltpu.make_async_copy(
                down_hbm.at[:, i * width : (i + 1) * width], held.at[i], sems.at[i]
            )
            for i in range(pieces)
        ],
        pltpu.make_async_copy(k_hbm, held_kv.at[0], sems.at[pieces]),
        pltpu.make_async_copy(v_hbm, held_kv.at[1], sems.at[pieces + 1]),
    ]
    for copy in copies:
        copy.start()
    copies[0].wait()
    fork_adapter = jnp.broadcast_to(adapter_ref[...].astype(F32), (HEAD_WIDTH, forks)).T
    lane_adapter = lax.broadcasted_iota(jnp.int32, (forks, HEAD_WIDTH), 1) // ADAPTER_RANK
    wanted = fork_adapter.astype(jnp.int32) - lane_adapter
    total = jnp.zeros((forks, HEAD_WIDTH), F32)
    copies[1].wait()
    for i in range(pieces):
        copies[2 + i].wait()
        block = jnp.dot(hidden_ref[...], held[i], preferred_element_type=F32)
        for j in range(width // HEAD_WIDTH):
            first = (i * width + j * HEAD_WIDTH) // ADAPTER_RANK
            part = block[:, j * HEAD_WIDTH : (j + 1) * HEAD_WIDTH]
            total += jnp.where(wanted == first, part, 0.0)
    flipped = total.T
    flipped = flipped[:ADAPTER_RANK] + flipped[ADAPTER_RANK:]
    if lanes > forks:
        flipped = jnp.concatenate([flipped, jnp.zeros((ADAPTER_RANK, lanes - forks), F32)], axis=1)
    at = slice(0, lanes)
    put_blocks(index_ref[0], flipped, rank_blocks, near_ref.at[:, :, at], far_ref.at[:, :, at])
    for i in range(2):
        copies[2 + pieces + i].wait()
        part = jnp.dot(hidden_ref[...], held_kv[i], preferred_element_type=F32)
        at = slice(lanes + i * kv_width, lanes + (i + 1) * kv_width)
        put_blocks(index_ref[0], part, kv_blocks, near_ref.at[:, :, at], far_ref.at[:, :, at])


def project_first(index, adapter, hidden, down, k_weight, v_weight, mem_count, width=256):
    forks, depth = hidden.shape
    columns, kv_width = down.shape[1], k_weight.shape[1]
    lanes = -(-forks // HEAD_WIDTH) * HEAD_WIDTH
    line, fork_own = mem_count // 2, forks // mem_count
    pieces = columns // width
    out = pltpu.VMEM((line, fork_own, lanes + 2 * kv_width), F32)
    weights = 2 * depth * (columns + 2 * kv_width)
    return pl.pallas_call(
        first_kernel,
        out_shape=(out, out, pltpu.VMEM(hidden.shape, BF16), pltpu.VMEM((1, forks), jnp.int32)),
        in_specs=[SMEM_SPEC] + [ANY_SPEC] * 5,
        out_specs=(VMEM_SPEC,) * 4,
        scratch_shapes=[
            pltpu.VMEM((pieces, depth, width), BF16),
            pltpu.VMEM((2, depth, kv_width), BF16),
            pltpu.VMEM((mem_count, fork_own, lanes), F32),
            pltpu.VMEM((mem_count, fork_own, kv_width), F32),
            pltpu.SemaphoreType.DMA((pieces + 4,)),
        ],
        compiler_params=params(weights + 4 * MIB),
        cost_estimate=cost(forks * weights, weights),
        name="project_first",
    )(index, *[in_hbm(x) for x in (adapter.reshape(1, forks), hidden, down, k_weight, v_weight)])


def project_kernel(start, extra, hidden_ref, q_hbm, *refs):
    up_hbm, part_ref, up_ref, held, sems = refs if extra else (None, refs[0], None, *refs[1:])
    pieces, _, width = held.shape
    copies = []
    for i in range(pieces):
        columns = pl.ds(start + i * width, width)
        copies.append(pltpu.make_async_copy(q_hbm.at[:, columns], held.at[i], sems.at[i]))
    if extra:
        copies.append(pltpu.make_async_copy(up_hbm, up_ref, sems.at[pieces]))
    for copy in copies:
        copy.start()
    for i in range(pieces):
        copies[i].wait()
        part_ref[:, i * width : (i + 1) * width] = jnp.dot(
            hidden_ref[...], held[i], preferred_element_type=F32
        )
    if extra:
        copies[-1].wait()


def project(hidden, q_weight, start, columns, up=None, width=256):
    forks, depth = hidden.shape
    pieces = columns // width
    weights = 2 * depth * columns
    extra = [] if up is None else [up]
    return pl.pallas_call(
        functools.partial(project_kernel, start, bool(extra)),
        out_shape=tuple(
            [pltpu.VMEM((forks, columns), F32)] + [pltpu.VMEM(x.shape, BF16) for x in extra]
        ),
        in_specs=[VMEM_SPEC] + [ANY_SPEC] * (1 + len(extra)),
        out_specs=(VMEM_SPEC,) * (1 + len(extra)),
        scratch_shapes=[
            pltpu.VMEM((pieces, depth, width), BF16),
            pltpu.SemaphoreType.DMA((pieces + 1,)),
        ],
        compiler_params=params(weights + 2 * MIB),
        cost_estimate=cost(forks * weights, weights + sum(2 * x.size for x in extra)),
        name="project",
    )(in_vmem(hidden), *[in_hbm(x) for x in [q_weight] + extra])


def delta_kernel(line, ranks, start, joint, index_ref, adapter_ref, *refs):
    first_refs = refs[:line]
    part_ref, up_ref, *out_refs, blocks_ref = refs[line:]
    forks, width = part_ref.shape[0], blocks_ref.shape[2]
    if joint:
        near_ref, far_ref = out_refs[0].at[:, 0], out_refs[0].at[:, 1]
        new_ref = out_refs[1]
        lanes = first_refs[0].shape[1] - new_ref.shape[1]
        total = functools.reduce(jnp.add, [ref[:, lanes:] for ref in first_refs])
        new_ref[...] = total.astype(BF16)
    else:
        near_ref, far_ref = out_refs
    acts = functools.reduce(jnp.add, [ref[:ranks, :forks] for ref in first_refs])
    acts = acts.astype(BF16).astype(F32)
    adapters = lax.broadcasted_iota(jnp.int32, (ADAPTER_COUNT, forks), 0)
    onehot = (adapters == adapter_ref[...]).astype(F32)
    spread = jnp.concatenate(
        [acts[r : r + 1, :] * onehot for r in range(ranks)], axis=0
    ).astype(BF16)
    for i in range(part_ref.shape[1] // width):
        delta = lax.dot_general(
            spread,
            up_ref[:, start + i * width : start + (i + 1) * width],
            (((0,), (0,)), ((), ())),
            preferred_element_type=F32,
        )
        at = slice(i * width, (i + 1) * width)
        put_blocks(
            index_ref[0],
            part_ref[:, at] + delta,
            blocks_ref,
            near_ref.at[:, :, at],
            far_ref.at[:, :, at],
        )


def add_delta(index, adapter, first_parts, part, up, mem_count, start, new_width=0, width=256):
    forks, columns = part.shape
    line, fork_own = mem_count // 2, forks // mem_count
    ranks = ADAPTER_RANK // mem_count
    if new_width:
        out = (
            pltpu.VMEM((line, 2, fork_own, columns), F32),
            pltpu.VMEM((fork_own, new_width), BF16),
        )
    else:
        out = (pltpu.VMEM((line, fork_own, columns), F32),) * 2
    return pl.pallas_call(
        functools.partial(delta_kernel, line, ranks, start, new_width > 0),
        out_shape=out,
        in_specs=[SMEM_SPEC] + [VMEM_SPEC] * (line + 3),
        out_specs=(VMEM_SPEC,) * 2,
        scratch_shapes=[pltpu.VMEM((mem_count, fork_own, width), F32)],
        compiler_params=params(4 * MIB),
        cost_estimate=cost(
            2 * forks * up.shape[0] * columns, 2 * up.shape[0] * columns + 8 * forks * columns
        ),
        name="add_delta",
    )(index, in_vmem(adapter), *first_parts, in_vmem(part), in_vmem(up))


def put_terms(lse):
    heads, forks = lse.shape
    high = lse.astype(BF16).astype(F32)
    rest = lse - high
    middle = rest.astype(BF16).astype(F32)
    low = rest - middle
    spare = jnp.zeros((HEAD_WIDTH - 3 * heads, forks), F32)
    return jnp.concatenate([high, middle, low, spare], axis=0).T.astype(BF16)


def get_terms(terms, heads):
    terms = terms.astype(F32)
    return terms[:, :heads] + terms[:, heads : 2 * heads] + terms[:, 2 * heads : 3 * heads]


def attend_kernel(pieces, q_ref, mask_ref, *refs):
    k_refs, v_refs, (out_ref, score_ref, lse_ref) = (
        refs[:pieces],
        refs[pieces : 2 * pieces],
        refs[2 * pieces :],
    )
    forks = q_ref.shape[0]
    kv_local, group = lse_ref.shape[:2]
    pages = score_ref.shape[0]
    held = pages // pieces
    scale = SCORE_SCALE * LOG2E
    chosen_by = mask_ref[...].reshape(forks, pages)
    spare = jnp.zeros((forks, HEAD_WIDTH - pages % HEAD_WIDTH), F32)
    chosen_by = jnp.concatenate([chosen_by, spare], axis=1).T[:pages]
    mask = jnp.concatenate([chosen_by] * group, axis=1) > 0
    ones = jnp.ones((8, score_ref.shape[1]), BF16)

    @pl.loop(0, kv_local)
    def _(kv_head):
        def head(i):
            return pl.ds(pl.multiple_of((kv_head * group + i) * HEAD_WIDTH, HEAD_WIDTH), HEAD_WIDTH)

        lanes = pl.ds(pl.multiple_of(kv_head * HEAD_WIDTH, HEAD_WIDTH), HEAD_WIDTH)
        queries = jnp.concatenate([q_ref[:, head(g)] for g in range(group)], axis=0)
        peaks = []
        top = None
        for p in range(pages):
            scores = lax.dot_general(
                k_refs[p // held][p % held, :, lanes],
                queries,
                (((1,), (1,)), ((), ())),
                preferred_element_type=F32,
            )
            score_ref[p] = scores
            peak = jnp.max(scores, axis=0, keepdims=True)
            peaks.append(peak)
            chosen = jnp.where(mask[p : p + 1], peak, neg_floor)
            top = chosen if top is None else jnp.maximum(top, chosen)
        acc = None
        for p in range(pages):
            weights = jnp.exp2((score_ref[p] - peaks[p]) * scale).astype(BF16)
            chosen = jnp.where(mask[p : p + 1], peaks[p], neg_floor)
            factor = jnp.where(mask[p : p + 1], jnp.exp2((chosen - top) * scale), 0.0)
            values = jnp.concatenate([v_refs[p // held][p % held, :, lanes].T, ones], axis=0)
            term = jnp.dot(values, weights, preferred_element_type=F32) * factor
            acc = term if acc is None else acc + term
        mass = acc[HEAD_WIDTH : HEAD_WIDTH + 1]
        some = mass > 0
        safe = jnp.where(some, mass, 1.0)
        rows = (acc[:HEAD_WIDTH] * jnp.where(some, 1.0 / safe, 0.0)).T
        lse = jnp.where(some, top * scale + jnp.log2(safe), neg_floor)
        for g in range(group):
            out_ref[:, head(g)] = rows[g * forks : (g + 1) * forks].astype(BF16)
        lse_ref[kv_head] = jnp.concatenate(
            [lse[:, g * forks : (g + 1) * forks] for g in range(group)], axis=0
        )

    heads = kv_local * group
    out_ref[:, heads * HEAD_WIDTH :] = put_terms(lse_ref[...].reshape(heads, forks))


def attend(queries, keys, values, mask):
    forks, width = queries.shape
    held, page_len, kv_width = keys[0].shape
    pieces = len(keys)
    pages = held * pieces
    kv_local = kv_width // HEAD_WIDTH
    group = width // kv_width
    rows = group * forks
    return pl.pallas_call(
        functools.partial(attend_kernel, pieces),
        out_shape=pltpu.VMEM((forks, width + HEAD_WIDTH), BF16),
        in_specs=[VMEM_SPEC] * (2 + 2 * pieces),
        out_specs=VMEM_SPEC,
        scratch_shapes=[
            pltpu.VMEM((pages, page_len, rows), F32),
            pltpu.VMEM((kv_local, group, forks), F32),
        ],
        compiler_params=params(6 * pages * page_len * rows + 4 * MIB),
        cost_estimate=cost(
            4 * pages * page_len * kv_local * rows * HEAD_WIDTH,
            4 * pages * page_len * kv_width + 4 * forks * width,
            pages * page_len * kv_local * rows,
        ),
        name="attend",
    )(queries, *[in_vmem(x) for x in [mask, *keys, *values]])


def merge_kernel(heads, kv_heads, sources, *refs):
    parts, (q_ref, new_ref, out_ref) = refs[:sources], refs[sources:]
    group = heads // kv_heads
    width = heads * HEAD_WIDTH
    lses = [get_terms(ref[:, width : width + HEAD_WIDTH], heads) for ref in parts]

    def new_head(i):
        return new_ref[:, i * HEAD_WIDTH : (i + 1) * HEAD_WIDTH].astype(F32)

    scores = []
    for h in range(heads):
        query = q_ref[:, h * HEAD_WIDTH : (h + 1) * HEAD_WIDTH].astype(F32)
        scores.append(jnp.sum(query * new_head(h // group), axis=1, keepdims=True))
    own = jnp.concatenate(scores, axis=1) * (SCORE_SCALE * LOG2E)
    top = functools.reduce(jnp.maximum, lses, own)
    own_weight = jnp.exp2(own - top)
    weights = [jnp.exp2(lse - top) for lse in lses]
    inverse = 1.0 / functools.reduce(jnp.add, weights, own_weight)
    own_weight = own_weight * inverse
    weights = [weight * inverse for weight in weights]
    for h in range(heads):
        lanes = slice(h * HEAD_WIDTH, (h + 1) * HEAD_WIDTH)
        total = own_weight[:, h : h + 1] * new_head(kv_heads + h // group)
        for weight, ref in zip(weights, parts):
            total += weight[:, h : h + 1] * ref[:, lanes].astype(F32)
        out_ref[:, lanes] = total.astype(BF16)


def merge(parts, queries, new, heads, kv_heads):
    fork_own, width = parts[0].shape
    size = len(parts) * fork_own * width
    return pl.pallas_call(
        functools.partial(merge_kernel, heads, kv_heads, len(parts)),
        out_shape=jax.ShapeDtypeStruct((fork_own, heads * HEAD_WIDTH), BF16),
        compiler_params=params(4 * size + 4 * MIB),
        cost_estimate=pl.CostEstimate(flops=4 * size, bytes_accessed=2 * size, transcendentals=0),
        name="merge",
    )(*parts, queries, new)


def output_kernel(context_ref, *refs):
    weight_refs, out_ref = refs[:-1], refs[-1]
    total = None
    for i, ref in enumerate(weight_refs):
        depth = ref.shape[0]
        part = jnp.dot(
            context_ref[:, i * depth : (i + 1) * depth], ref[...], preferred_element_type=F32
        )
        total = part if total is None else total + part
    out_ref[...] = total


def output_project(context, weights):
    forks, rows = context.shape
    columns = weights[0].shape[1]
    return pl.pallas_call(
        output_kernel,
        out_shape=pltpu.VMEM((forks, columns), F32),
        in_specs=[VMEM_SPEC] * (1 + len(weights)),
        out_specs=VMEM_SPEC,
        compiler_params=params(4 * MIB),
        cost_estimate=cost(2 * forks * rows * columns, 2 * rows * columns),
        name="output_project",
    )(context, *[in_vmem(x) for x in weights])


def finish_kernel(count, line, index_ref, *refs):
    near_refs, far_refs, out_ref = refs[:count], refs[count : 2 * count], refs[-1]
    place, parity = index_ref[0] // 2, index_ref[0] % 2
    rows = out_ref.shape[1]
    for group, side in ((near_refs, parity), (far_refs, 1 - parity)):
        for i in range(line):
            total = functools.reduce(jnp.add, [ref[i * rows : (i + 1) * rows] for ref in group])
            out_ref[2 * (place ^ i) + side] = total.astype(BF16)


def finish(index, near, far, mem_count):
    rows, columns = near[0].shape
    line = mem_count // 2
    return pl.pallas_call(
        functools.partial(finish_kernel, len(near), line),
        out_shape=jax.ShapeDtypeStruct((mem_count, rows // line, columns), BF16),
        in_specs=[SMEM_SPEC] + [VMEM_SPEC] * (2 * len(near)),
        out_specs=VMEM_SPEC,
        compiler_params=params(4 * MIB),
        cost_estimate=cost(0, 8 * rows * columns * len(near)),
        name="finish",
    )(index, *near, *far)


def shards(
    hidden,
    adapter,
    page_cache_slot,
    selection,
    query_projection_weight,
    key_projection_weight,
    value_projection_weight,
    adapter_down_weight,
    adapter_up_weight,
    output_projection_weight,
    prefix_key_cache,
    prefix_value_cache,
):
    mem_count = lax.axis_size("mem")
    mem_index = lax.axis_index("mem")
    forks = hidden.shape[0]
    fork_own = forks // mem_count
    q_width = query_projection_weight.shape[1]
    kv_width = key_projection_weight.shape[1]
    heads, kv_heads = q_width // HEAD_WIDTH, kv_width // HEAD_WIDTH
    pages = prefix_key_cache.shape[0]
    line = mem_count // 2
    index = mem_index.reshape(1)
    place, parity = mem_index // 2, mem_index % 2

    def swapped(x, step, cross=0):
        pairs = [(i, i ^ (2 * step + cross)) for i in range(mem_count)]
        return lax.ppermute(x, "mem", pairs)

    def along(blocks, cross=0):
        return [swapped(blocks[i], i, cross) if i or cross else blocks[0] for i in range(line)]

    def gather(x):
        return jnp.concatenate([x] + [swapped(x, i) for i in range(1, line)], axis=0)

    def pair(x):
        return swapped(x, 0, 1)

    near_1, far_1, hidden, adapter = project_first(
        index, adapter, hidden, adapter_down_weight, key_projection_weight, value_projection_weight, mem_count
    )
    cut = q_width * 11 // 16 // 256 * 256
    (part_a,) = project(hidden, query_projection_weight, 0, cut)
    first_parts = fold(near_1, pair(far_1))
    first_parts, part_a, hidden = lax.optimization_barrier((first_parts, part_a, hidden))
    part_b, up = project(
        hidden, query_projection_weight, cut, q_width - cut, adapter_up_weight.reshape(-1, q_width)
    )
    first_parts = along(first_parts)

    near_a, far_a = add_delta(index, adapter, first_parts, part_a, up, mem_count, 0)
    near_a, far_a, part_b = lax.optimization_barrier((near_a, far_a, part_b))
    both_b, own_new = add_delta(
        index, adapter, first_parts, part_b, up, mem_count, cut, 2 * kv_width
    )
    sums_a = fold(near_a, pair(far_a))
    sum_b = functools.reduce(jnp.add, along(both_b))
    own_a = functools.reduce(jnp.add, along(sums_a))
    own_b = sum_b[0] + pair(sum_b[1])
    own_queries = jnp.concatenate([own_a.astype(BF16), own_b.astype(BF16)], axis=1)

    *staged, near_mask, far_mask = stage_cache(
        index, page_cache_slot, selection, prefix_key_cache, prefix_value_cache, mem_count
    )
    keys, values = staged[: len(staged) // 2], staged[len(staged) // 2 :]
    near_queries = gather(own_queries)
    far_queries = pair(near_queries)
    near = attend(near_queries, keys, values, near_mask)
    far = attend(far_queries, keys, values, far_mask)
    blocks = (line, fork_own, q_width + HEAD_WIDTH)
    parts = along(near.reshape(blocks)) + along(far.reshape(blocks), 1)
    context_own = merge(parts, own_queries, own_new, heads, kv_heads)

    out_weights = stage(output_projection_weight)
    near_context = gather(context_own)
    far_context = pair(near_context)
    tp_count = lax.axis_size("tp")
    outs = []
    for context in (near_context, far_context):
        part = output_project(context, out_weights)
        terms = [part]
        for shift in range(1, tp_count):
            pairs = [(i, (i + shift) % tp_count) for i in range(tp_count)]
            terms.append(lax.ppermute(part, "tp", pairs))
        outs.append(terms)
    return finish(index, *outs, mem_count).reshape(forks, -1)


def solution(mesh):
    return jax.shard_map(
        shards,
        mesh=mesh,
        in_specs=(
            P("groups", "mem"),
            P("groups"),
            P("groups"),
            P("groups", None),
            P("mem", "tp"),
            P("mem", "tp"),
            P("mem", "tp"),
            P("mem", None),
            P("mem", None, "tp"),
            P("tp", "mem"),
            P(("groups", "mem"), None, "tp"),
            P(("groups", "mem"), None, "tp"),
        ),
        out_specs=P("groups", "mem"),
        check_vma=False,
    )
```

```python
import functools

import jax
import jax.numpy as jnp
from jax import lax
from jax.experimental import pallas as pl
from jax.experimental.pallas import tpu as pltpu
from jax.sharding import PartitionSpec as P

HEAD_WIDTH = 128
ADAPTER_RANK = 64
ADAPTER_COUNT = 32
LOG2E = 1.4426950408889634
SCORE_SCALE = HEAD_WIDTH ** (-0.5)
neg_floor = -1e30
MIB = 1024 * 1024
F32 = jnp.float32
BF16 = jnp.bfloat16


def params(limit, *semantics):
    return pltpu.CompilerParams(
        dimension_semantics=semantics or None, vmem_limit_bytes=int(limit)
    )


def whole(shape):
    return pl.BlockSpec(shape, lambda *_: (0,) * len(shape))


def in_hbm(x):
    return pltpu.with_memory_space_constraint(x, pltpu.HBM)


def in_vmem(x):
    return pltpu.with_memory_space_constraint(x, pltpu.VMEM)


def cost(flops, size, transcendentals=0):
    return pl.CostEstimate(
        flops=int(flops), bytes_accessed=int(size), transcendentals=int(transcendentals)
    )


VMEM_SPEC = pl.BlockSpec(memory_space=pltpu.VMEM)
SMEM_SPEC = pl.BlockSpec(memory_space=pltpu.SMEM)
ANY_SPEC = pl.BlockSpec(memory_space=pl.ANY)


def stage_kernel(pieces, *refs):
    count = len(refs[:-1]) // (pieces + 1)
    sources, targets, sems = refs[:count], refs[count:-1], refs[-1]
    copies = []
    for i, target in enumerate(targets):
        rows = pl.ds((i % pieces) * target.shape[0], target.shape[0])
        copies.append(
            pltpu.make_async_copy(sources[i // pieces].at[rows], target, sems.at[i])
        )
    for copy in copies:
        copy.start()
    for copy in copies:
        copy.wait()


def stage(*arrays, pieces=4):
    shapes = [(x.shape[0] // pieces,) + x.shape[1:] for x in arrays for _ in range(pieces)]
    return pl.pallas_call(
        functools.partial(stage_kernel, pieces),
        out_shape=tuple(pltpu.VMEM(shape, BF16) for shape in shapes),
        in_specs=[ANY_SPEC] * len(arrays),
        out_specs=(ANY_SPEC,) * len(shapes),
        scratch_shapes=[pltpu.SemaphoreType.DMA((len(shapes),))],
        compiler_params=params(MIB),
        cost_estimate=cost(0, sum(2 * x.size for x in arrays)),
        name="stage",
    )(*[in_hbm(x) for x in arrays])


def cache_kernel(pieces, index_ref, slot_hbm, select_hbm, *refs):
    sources, targets = refs[:2], refs[2 : 2 + 2 * pieces]
    near_ref, far_ref, slot_ref, select_ref, blocks_ref, sems = refs[2 + 2 * pieces :]
    count = 2 * pieces
    first = [
        pltpu.make_async_copy(slot_hbm, slot_ref, sems.at[count]),
        pltpu.make_async_copy(select_hbm, select_ref, sems.at[count + 1]),
    ]
    copies = []
    for i, target in enumerate(targets):
        rows = pl.ds((i % pieces) * target.shape[0], target.shape[0])
        copies.append(
            pltpu.make_async_copy(sources[i // pieces].at[rows], target, sems.at[i])
        )
    for copy in first + copies:
        copy.start()
    for copy in first:
        copy.wait()
    pages, total = blocks_ref.shape[2], slot_ref.shape[1]
    slots = index_ref[0] * pages + lax.broadcasted_iota(jnp.int32, (pages, total), 0)
    match = (slots == slot_ref[...]).astype(BF16)
    chosen = (select_ref[...] > 0).astype(BF16)
    held = lax.dot_general(
        chosen, match, (((1,), (1,)), ((), ())), preferred_element_type=F32
    )
    put_blocks(index_ref[0], held, blocks_ref, near_ref, far_ref)
    for copy in copies:
        copy.wait()


def stage_cache(index, page_cache_slot, selection, keys, values, mem_count, pieces=2):
    forks, total = selection.shape
    pages = keys.shape[0]
    line, fork_own = mem_count // 2, forks // mem_count
    shapes = [(x.shape[0] // pieces,) + x.shape[1:] for x in (keys, values) for _ in range(pieces)]
    mask = pltpu.VMEM((line, fork_own, pages), F32)
    return pl.pallas_call(
        functools.partial(cache_kernel, pieces),
        out_shape=tuple(pltpu.VMEM(shape, BF16) for shape in shapes) + (mask, mask),
        in_specs=[SMEM_SPEC] + [ANY_SPEC] * 4,
        out_specs=(ANY_SPEC,) * len(shapes) + (VMEM_SPEC,) * 2,
        scratch_shapes=[
            pltpu.VMEM((1, total), jnp.int32),
            pltpu.VMEM((forks, total), jnp.int32),
            pltpu.VMEM((mem_count, fork_own, pages), F32),
            pltpu.SemaphoreType.DMA((2 * pieces + 2,)),
        ],
        compiler_params=params(4 * MIB),
        cost_estimate=cost(0, 4 * keys.size),
        name="stage_cache",
    )(index, *[in_hbm(x) for x in (page_cache_slot.reshape(1, total), selection, keys, values)])


def fold_kernel(one_ref, two_ref, *out_refs):
    for i, out_ref in enumerate(out_refs):
        out_ref[...] = one_ref[i] + two_ref[i]


def fold(one, two):
    out = pltpu.VMEM(one.shape[1:], F32)
    return pl.pallas_call(
        fold_kernel,
        out_shape=(out,) * one.shape[0],
        in_specs=[VMEM_SPEC] * 2,
        out_specs=(VMEM_SPEC,) * one.shape[0],
        compiler_params=params(MIB * 2 + 16 * one.size),
        cost_estimate=cost(one.size, 12 * one.size),
        name="fold",
    )(in_vmem(one), two)


def take_blocks(index, blocks_ref, near_ref, far_ref):
    place, parity = index // 2, index % 2
    for i in range(near_ref.shape[0]):
        at = 2 * (place ^ i)
        near_ref[i] = blocks_ref[at + parity]
        far_ref[i] = blocks_ref[at + 1 - parity]


def put_blocks(index, value, blocks_ref, near_ref, far_ref):
    count, rows, lanes = blocks_ref.shape
    own = value.shape[0] // count
    for i in range(count):
        blocks_ref[i, :own] = value[i * own : (i + 1) * own]
        if own < rows:
            blocks_ref[i, own:] = jnp.zeros((rows - own, lanes), F32)
    take_blocks(index, blocks_ref, near_ref, far_ref)


def first_kernel(
    index_ref,
    adapter_hbm,
    hidden_hbm,
    down_hbm,
    k_hbm,
    v_hbm,
    near_ref,
    far_ref,
    hidden_ref,
    adapter_ref,
    held,
    held_kv,
    rank_blocks,
    kv_blocks,
    sems,
):
    pieces, _, width = held.shape
    forks = hidden_ref.shape[0]
    kv_width = held_kv.shape[2]
    lanes = rank_blocks.shape[2]
    copies = [
        pltpu.make_async_copy(adapter_hbm, adapter_ref, sems.at[pieces + 3]),
        pltpu.make_async_copy(hidden_hbm, hidden_ref, sems.at[pieces + 2]),
        *[
            pltpu.make_async_copy(
                down_hbm.at[:, i * width : (i + 1) * width], held.at[i], sems.at[i]
            )
            for i in range(pieces)
        ],
        pltpu.make_async_copy(k_hbm, held_kv.at[0], sems.at[pieces]),
        pltpu.make_async_copy(v_hbm, held_kv.at[1], sems.at[pieces + 1]),
    ]
    for copy in copies:
        copy.start()
    copies[0].wait()
    fork_adapter = jnp.broadcast_to(adapter_ref[...].astype(F32), (HEAD_WIDTH, forks)).T
    lane_adapter = lax.broadcasted_iota(jnp.int32, (forks, HEAD_WIDTH), 1) // ADAPTER_RANK
    wanted = fork_adapter.astype(jnp.int32) - lane_adapter
    total = jnp.zeros((forks, HEAD_WIDTH), F32)
    copies[1].wait()
    for i in range(pieces):
        copies[2 + i].wait()
        block = jnp.dot(hidden_ref[...], held[i], preferred_element_type=F32)
        for j in range(width // HEAD_WIDTH):
            first = (i * width + j * HEAD_WIDTH) // ADAPTER_RANK
            part = block[:, j * HEAD_WIDTH : (j + 1) * HEAD_WIDTH]
            total += jnp.where(wanted == first, part, 0.0)
    flipped = total.T
    flipped = flipped[:ADAPTER_RANK] + flipped[ADAPTER_RANK:]
    if lanes > forks:
        flipped = jnp.concatenate([flipped, jnp.zeros((ADAPTER_RANK, lanes - forks), F32)], axis=1)
    at = slice(0, lanes)
    put_blocks(index_ref[0], flipped, rank_blocks, near_ref.at[:, :, at], far_ref.at[:, :, at])
    for i in range(2):
        copies[2 + pieces + i].wait()
        part = jnp.dot(hidden_ref[...], held_kv[i], preferred_element_type=F32)
        at = slice(lanes + i * kv_width, lanes + (i + 1) * kv_width)
        put_blocks(index_ref[0], part, kv_blocks, near_ref.at[:, :, at], far_ref.at[:, :, at])


def project_first(index, adapter, hidden, down, k_weight, v_weight, mem_count, width=256):
    forks, depth = hidden.shape
    columns, kv_width = down.shape[1], k_weight.shape[1]
    lanes = -(-forks // HEAD_WIDTH) * HEAD_WIDTH
    line, fork_own = mem_count // 2, forks // mem_count
    pieces = columns // width
    out = pltpu.VMEM((line, fork_own, lanes + 2 * kv_width), F32)
    weights = 2 * depth * (columns + 2 * kv_width)
    return pl.pallas_call(
        first_kernel,
        out_shape=(out, out, pltpu.VMEM(hidden.shape, BF16), pltpu.VMEM((1, forks), jnp.int32)),
        in_specs=[SMEM_SPEC] + [ANY_SPEC] * 5,
        out_specs=(VMEM_SPEC,) * 4,
        scratch_shapes=[
            pltpu.VMEM((pieces, depth, width), BF16),
            pltpu.VMEM((2, depth, kv_width), BF16),
            pltpu.VMEM((mem_count, fork_own, lanes), F32),
            pltpu.VMEM((mem_count, fork_own, kv_width), F32),
            pltpu.SemaphoreType.DMA((pieces + 4,)),
        ],
        compiler_params=params(weights + 4 * MIB),
        cost_estimate=cost(forks * weights, weights),
        name="project_first",
    )(index, *[in_hbm(x) for x in (adapter.reshape(1, forks), hidden, down, k_weight, v_weight)])


def project_kernel(start, extra, hidden_ref, q_hbm, *refs):
    up_hbm, part_ref, up_ref, held, sems = refs if extra else (None, refs[0], None, *refs[1:])
    pieces, _, width = held.shape
    copies = []
    for i in range(pieces):
        columns = pl.ds(start + i * width, width)
        copies.append(pltpu.make_async_copy(q_hbm.at[:, columns], held.at[i], sems.at[i]))
    if extra:
        copies.append(pltpu.make_async_copy(up_hbm, up_ref, sems.at[pieces]))
    for copy in copies:
        copy.start()
    for i in range(pieces):
        copies[i].wait()
        part_ref[:, i * width : (i + 1) * width] = jnp.dot(
            hidden_ref[...], held[i], preferred_element_type=F32
        )
    if extra:
        copies[-1].wait()


def project(hidden, q_weight, start, columns, up=None, width=256):
    forks, depth = hidden.shape
    pieces = columns // width
    weights = 2 * depth * columns
    extra = [] if up is None else [up]
    return pl.pallas_call(
        functools.partial(project_kernel, start, bool(extra)),
        out_shape=tuple(
            [pltpu.VMEM((forks, columns), F32)] + [pltpu.VMEM(x.shape, BF16) for x in extra]
        ),
        in_specs=[VMEM_SPEC] + [ANY_SPEC] * (1 + len(extra)),
        out_specs=(VMEM_SPEC,) * (1 + len(extra)),
        scratch_shapes=[
            pltpu.VMEM((pieces, depth, width), BF16),
            pltpu.SemaphoreType.DMA((pieces + 1,)),
        ],
        compiler_params=params(weights + 2 * MIB),
        cost_estimate=cost(forks * weights, weights + sum(2 * x.size for x in extra)),
        name="project",
    )(in_vmem(hidden), *[in_hbm(x) for x in [q_weight] + extra])


def line_sum_kernel(after_ref, *refs):
    parts, (own_ref, other_ref) = refs[:-2], refs[-2:]
    own_ref[...] = functools.reduce(jnp.add, [ref[0] for ref in parts])
    other_ref[...] = functools.reduce(jnp.add, [ref[1] for ref in parts])


def line_sum(parts, after):
    out = pltpu.VMEM(parts[0].shape[1:], F32)
    size = len(parts) * parts[0].size
    return pl.pallas_call(
        line_sum_kernel,
        out_shape=(out, out),
        in_specs=[ANY_SPEC] + [VMEM_SPEC] * len(parts),
        out_specs=(VMEM_SPEC,) * 2,
        compiler_params=params(2 * MIB + 8 * size),
        cost_estimate=cost(size, 4 * size),
        name="line_sum",
    )(after, *parts)


def delta_kernel(line, ranks, start, joint, index_ref, adapter_ref, *refs):
    first_refs = refs[:line]
    part_ref, up_ref, *out_refs, blocks_ref = refs[line:]
    forks, width = part_ref.shape[0], blocks_ref.shape[2]
    if joint:
        near_ref, far_ref = out_refs[0].at[:, 0], out_refs[0].at[:, 1]
        new_ref = out_refs[1]
        lanes = first_refs[0].shape[1] - new_ref.shape[1]
        total = functools.reduce(jnp.add, [ref[:, lanes:] for ref in first_refs])
        new_ref[...] = total.astype(BF16)
    else:
        near_ref, far_ref = out_refs
    acts = functools.reduce(jnp.add, [ref[:ranks, :forks] for ref in first_refs])
    acts = acts.astype(BF16).astype(F32)
    adapters = lax.broadcasted_iota(jnp.int32, (ADAPTER_COUNT, forks), 0)
    onehot = (adapters == adapter_ref[...]).astype(F32)
    spread = jnp.concatenate(
        [acts[r : r + 1, :] * onehot for r in range(ranks)], axis=0
    ).astype(BF16)
    for i in range(part_ref.shape[1] // width):
        delta = lax.dot_general(
            spread,
            up_ref[:, start + i * width : start + (i + 1) * width],
            (((0,), (0,)), ((), ())),
            preferred_element_type=F32,
        )
        at = slice(i * width, (i + 1) * width)
        put_blocks(
            index_ref[0],
            part_ref[:, at] + delta,
            blocks_ref,
            near_ref.at[:, :, at],
            far_ref.at[:, :, at],
        )


def add_delta(index, adapter, first_parts, part, up, mem_count, start, new_width=0, width=256):
    forks, columns = part.shape
    line, fork_own = mem_count // 2, forks // mem_count
    ranks = ADAPTER_RANK // mem_count
    if new_width:
        out = (
            pltpu.VMEM((line, 2, fork_own, columns), F32),
            pltpu.VMEM((fork_own, new_width), BF16),
        )
    else:
        out = (pltpu.VMEM((line, fork_own, columns), F32),) * 2
    return pl.pallas_call(
        functools.partial(delta_kernel, line, ranks, start, new_width > 0),
        out_shape=out,
        in_specs=[SMEM_SPEC] + [VMEM_SPEC] * (line + 3),
        out_specs=(VMEM_SPEC,) * 2,
        scratch_shapes=[pltpu.VMEM((mem_count, fork_own, width), F32)],
        compiler_params=params(4 * MIB),
        cost_estimate=cost(
            2 * forks * up.shape[0] * columns, 2 * up.shape[0] * columns + 8 * forks * columns
        ),
        name="add_delta",
    )(index, in_vmem(adapter), *first_parts, in_vmem(part), in_vmem(up))


def put_terms(lse):
    heads, forks = lse.shape
    high = lse.astype(BF16).astype(F32)
    rest = lse - high
    middle = rest.astype(BF16).astype(F32)
    low = rest - middle
    spare = jnp.zeros((HEAD_WIDTH - 3 * heads, forks), F32)
    return jnp.concatenate([high, middle, low, spare], axis=0).T.astype(BF16)


def get_terms(terms, heads):
    terms = terms.astype(F32)
    return terms[:, :heads] + terms[:, heads : 2 * heads] + terms[:, 2 * heads : 3 * heads]


def attend_kernel(pieces, q_ref, mask_ref, *refs):
    k_refs, v_refs, (out_ref, score_ref, lse_ref) = (
        refs[:pieces],
        refs[pieces : 2 * pieces],
        refs[2 * pieces :],
    )
    forks = q_ref.shape[0]
    kv_local, group = lse_ref.shape[:2]
    pages = score_ref.shape[0] // 2
    held = pages // pieces
    scale = SCORE_SCALE * LOG2E
    chosen_by = mask_ref[...].reshape(forks, pages)
    spare = jnp.zeros((forks, HEAD_WIDTH - pages % HEAD_WIDTH), F32)
    chosen_by = jnp.concatenate([chosen_by, spare], axis=1).T[:pages]
    mask = jnp.concatenate([chosen_by] * group, axis=1) > 0
    ones = jnp.ones((8, score_ref.shape[1]), BF16)

    def score(kv_head, queries, p):
        lanes = slice(kv_head * HEAD_WIDTH, (kv_head + 1) * HEAD_WIDTH)
        scores = lax.dot_general(
            k_refs[p // held][p % held, :, lanes],
            queries,
            (((1,), (1,)), ((), ())),
            preferred_element_type=F32,
        )
        score_ref[kv_head % 2 * pages + p] = scores
        return jnp.max(scores, axis=0, keepdims=True)

    def term(kv_head, peaks, top, p):
        lanes = slice(kv_head * HEAD_WIDTH, (kv_head + 1) * HEAD_WIDTH)
        scores = score_ref[kv_head % 2 * pages + p]
        weights = jnp.exp2((scores - peaks[p]) * scale).astype(BF16)
        chosen = jnp.where(mask[p : p + 1], peaks[p], neg_floor)
        factor = jnp.where(mask[p : p + 1], jnp.exp2((chosen - top) * scale), 0.0)
        values = jnp.concatenate([v_refs[p // held][p % held, :, lanes].T, ones], axis=0)
        return jnp.dot(values, weights, preferred_element_type=F32) * factor

    def head_queries(kv_head):
        first = kv_head * group
        return jnp.concatenate(
            [
                q_ref[:, (first + g) * HEAD_WIDTH : (first + g + 1) * HEAD_WIDTH]
                for g in range(group)
            ],
            axis=0,
        )

    queries = head_queries(0)
    peaks = [score(0, queries, p) for p in range(pages)]
    for kv_head in range(kv_local):
        chosen = [jnp.where(mask[p : p + 1], peaks[p], neg_floor) for p in range(pages)]
        top = functools.reduce(jnp.maximum, chosen)
        if kv_head + 1 < kv_local:
            queries = head_queries(kv_head + 1)
        acc = None
        next_peaks = []
        for p in range(pages):
            if kv_head + 1 < kv_local:
                next_peaks.append(score(kv_head + 1, queries, p))
            part = term(kv_head, peaks, top, p)
            acc = part if acc is None else acc + part
        peaks = next_peaks
        mass = acc[HEAD_WIDTH : HEAD_WIDTH + 1]
        some = mass > 0
        safe = jnp.where(some, mass, 1.0)
        rows = (acc[:HEAD_WIDTH] * jnp.where(some, 1.0 / safe, 0.0)).T
        lse = jnp.where(some, top * scale + jnp.log2(safe), neg_floor)
        for g in range(group):
            at = (kv_head * group + g) * HEAD_WIDTH
            out_ref[:, at : at + HEAD_WIDTH] = rows[g * forks : (g + 1) * forks].astype(BF16)
        lse_ref[kv_head] = jnp.concatenate(
            [lse[:, g * forks : (g + 1) * forks] for g in range(group)], axis=0
        )

    heads = kv_local * group
    out_ref[:, heads * HEAD_WIDTH :] = put_terms(lse_ref[...].reshape(heads, forks))


def attend(queries, keys, values, mask):
    forks, width = queries.shape
    held, page_len, kv_width = keys[0].shape
    pieces = len(keys)
    pages = held * pieces
    kv_local = kv_width // HEAD_WIDTH
    group = width // kv_width
    rows = group * forks
    return pl.pallas_call(
        functools.partial(attend_kernel, pieces),
        out_shape=pltpu.VMEM((forks, width + HEAD_WIDTH), BF16),
        in_specs=[VMEM_SPEC] * (2 + 2 * pieces),
        out_specs=VMEM_SPEC,
        scratch_shapes=[
            pltpu.VMEM((2 * pages, page_len, rows), F32),
            pltpu.VMEM((kv_local, group, forks), F32),
        ],
        compiler_params=params(10 * pages * page_len * rows + 4 * MIB),
        cost_estimate=cost(
            4 * pages * page_len * kv_local * rows * HEAD_WIDTH,
            4 * pages * page_len * kv_width + 4 * forks * width,
            pages * page_len * kv_local * rows,
        ),
        name="attend",
    )(queries, *[in_vmem(x) for x in [mask, *keys, *values]])


def merge_kernel(heads, kv_heads, sources, *refs):
    parts, (q_ref, new_ref, out_ref) = refs[:sources], refs[sources:]
    group = heads // kv_heads
    width = heads * HEAD_WIDTH
    lses = [get_terms(ref[:, width : width + HEAD_WIDTH], heads) for ref in parts]

    def new_head(i):
        return new_ref[:, i * HEAD_WIDTH : (i + 1) * HEAD_WIDTH].astype(F32)

    scores = []
    for h in range(heads):
        query = q_ref[:, h * HEAD_WIDTH : (h + 1) * HEAD_WIDTH].astype(F32)
        scores.append(jnp.sum(query * new_head(h // group), axis=1, keepdims=True))
    own = jnp.concatenate(scores, axis=1) * (SCORE_SCALE * LOG2E)
    top = functools.reduce(jnp.maximum, lses, own)
    own_weight = jnp.exp2(own - top)
    weights = [jnp.exp2(lse - top) for lse in lses]
    inverse = 1.0 / functools.reduce(jnp.add, weights, own_weight)
    own_weight = own_weight * inverse
    weights = [weight * inverse for weight in weights]
    for h in range(heads):
        lanes = slice(h * HEAD_WIDTH, (h + 1) * HEAD_WIDTH)
        total = own_weight[:, h : h + 1] * new_head(kv_heads + h // group)
        for weight, ref in zip(weights, parts):
            total += weight[:, h : h + 1] * ref[:, lanes].astype(F32)
        out_ref[:, lanes] = total.astype(BF16)


def merge(parts, queries, new, heads, kv_heads):
    fork_own, width = parts[0].shape
    size = len(parts) * fork_own * width
    return pl.pallas_call(
        functools.partial(merge_kernel, heads, kv_heads, len(parts)),
        out_shape=jax.ShapeDtypeStruct((fork_own, heads * HEAD_WIDTH), BF16),
        compiler_params=params(4 * size + 4 * MIB),
        cost_estimate=pl.CostEstimate(flops=4 * size, bytes_accessed=2 * size, transcendentals=0),
        name="merge",
    )(*parts, queries, new)


def output_kernel(context_ref, *refs):
    weight_refs, out_ref = refs[:-1], refs[-1]
    total = None
    for i, ref in enumerate(weight_refs):
        depth = ref.shape[0]
        part = jnp.dot(
            context_ref[:, i * depth : (i + 1) * depth], ref[...], preferred_element_type=F32
        )
        total = part if total is None else total + part
    out_ref[...] = total


def output_project(context, weights):
    forks, rows = context.shape
    columns = weights[0].shape[1]
    return pl.pallas_call(
        output_kernel,
        out_shape=pltpu.VMEM((forks, columns), F32),
        in_specs=[VMEM_SPEC] * (1 + len(weights)),
        out_specs=VMEM_SPEC,
        compiler_params=params(4 * MIB),
        cost_estimate=cost(2 * forks * rows * columns, 2 * rows * columns),
        name="output_project",
    )(context, *[in_vmem(x) for x in weights])


def finish_kernel(count, line, index_ref, *refs):
    near_refs, far_refs, out_ref = refs[:count], refs[count : 2 * count], refs[-1]
    place, parity = index_ref[0] // 2, index_ref[0] % 2
    rows = out_ref.shape[1]
    for group, side in ((near_refs, parity), (far_refs, 1 - parity)):
        for i in range(line):
            total = functools.reduce(jnp.add, [ref[i * rows : (i + 1) * rows] for ref in group])
            out_ref[2 * (place ^ i) + side] = total.astype(BF16)


def finish(index, near, far, mem_count):
    rows, columns = near[0].shape
    line = mem_count // 2
    return pl.pallas_call(
        functools.partial(finish_kernel, len(near), line),
        out_shape=jax.ShapeDtypeStruct((mem_count, rows // line, columns), BF16),
        in_specs=[SMEM_SPEC] + [VMEM_SPEC] * (2 * len(near)),
        out_specs=VMEM_SPEC,
        compiler_params=params(4 * MIB),
        cost_estimate=cost(0, 8 * rows * columns * len(near)),
        name="finish",
    )(index, *near, *far)


def shards(
    hidden,
    adapter,
    page_cache_slot,
    selection,
    query_projection_weight,
    key_projection_weight,
    value_projection_weight,
    adapter_down_weight,
    adapter_up_weight,
    output_projection_weight,
    prefix_key_cache,
    prefix_value_cache,
):
    mem_count = lax.axis_size("mem")
    mem_index = lax.axis_index("mem")
    forks = hidden.shape[0]
    fork_own = forks // mem_count
    q_width = query_projection_weight.shape[1]
    kv_width = key_projection_weight.shape[1]
    heads, kv_heads = q_width // HEAD_WIDTH, kv_width // HEAD_WIDTH
    pages = prefix_key_cache.shape[0]
    line = mem_count // 2
    index = mem_index.reshape(1)
    place, parity = mem_index // 2, mem_index % 2

    def swapped(x, step, cross=0):
        pairs = [(i, i ^ (2 * step + cross)) for i in range(mem_count)]
        return lax.ppermute(x, "mem", pairs)

    def along(blocks, cross=0):
        return [swapped(blocks[i], i, cross) if i or cross else blocks[0] for i in range(line)]

    def gather(x):
        return jnp.concatenate([x] + [swapped(x, i) for i in range(1, line)], axis=0)

    def pair(x):
        return swapped(x, 0, 1)

    near_1, far_1, hidden, adapter = project_first(
        index, adapter, hidden, adapter_down_weight, key_projection_weight, value_projection_weight, mem_count
    )
    cut = q_width * 11 // 16 // 256 * 256
    (part_a,) = project(hidden, query_projection_weight, 0, cut)
    first_parts = fold(near_1, pair(far_1))
    first_parts, part_a, hidden = lax.optimization_barrier((first_parts, part_a, hidden))
    part_b, up = project(
        hidden, query_projection_weight, cut, q_width - cut, adapter_up_weight.reshape(-1, q_width)
    )
    first_parts = along(first_parts)

    near_a, far_a = add_delta(index, adapter, first_parts, part_a, up, mem_count, 0)
    near_a, far_a, part_b = lax.optimization_barrier((near_a, far_a, part_b))
    both_b, own_new = add_delta(
        index, adapter, first_parts, part_b, up, mem_count, cut, 2 * kv_width
    )
    sums_a = fold(near_a, pair(far_a))
    own_b, other_b = line_sum(along(both_b), sums_a[0])
    own_a = functools.reduce(jnp.add, along(sums_a))
    own_b = own_b + pair(other_b)
    own_queries = jnp.concatenate([own_a.astype(BF16), own_b.astype(BF16)], axis=1)

    *staged, near_mask, far_mask = stage_cache(
        index, page_cache_slot, selection, prefix_key_cache, prefix_value_cache, mem_count
    )
    keys, values = staged[: len(staged) // 2], staged[len(staged) // 2 :]
    near_queries = gather(own_queries)
    far_queries = pair(near_queries)
    near = attend(near_queries, keys, values, near_mask)
    far = attend(far_queries, keys, values, far_mask)
    blocks = (line, fork_own, q_width + HEAD_WIDTH)
    parts = along(near.reshape(blocks)) + along(far.reshape(blocks), 1)
    context_own = merge(parts, own_queries, own_new, heads, kv_heads)

    out_weights = stage(output_projection_weight)
    near_context = gather(context_own)
    far_context = pair(near_context)
    tp_count = lax.axis_size("tp")
    outs = []
    for context in (near_context, far_context):
        part = output_project(context, out_weights)
        terms = [part]
        for shift in range(1, tp_count):
            pairs = [(i, (i + shift) % tp_count) for i in range(tp_count)]
            terms.append(lax.ppermute(part, "tp", pairs))
        outs.append(terms)
    return finish(index, *outs, mem_count).reshape(forks, -1)


def solution(mesh):
    return jax.shard_map(
        shards,
        mesh=mesh,
        in_specs=(
            P("groups", "mem"),
            P("groups"),
            P("groups"),
            P("groups", None),
            P("mem", "tp"),
            P("mem", "tp"),
            P("mem", "tp"),
            P("mem", None),
            P("mem", None, "tp"),
            P("tp", "mem"),
            P(("groups", "mem"), None, "tp"),
            P(("groups", "mem"), None, "tp"),
        ),
        out_specs=P("groups", "mem"),
        check_vma=False,
    )
```

```python
import functools

import jax
import jax.numpy as jnp
from jax import lax
from jax.experimental import pallas as pl
from jax.experimental.pallas import tpu as pltpu
from jax.sharding import PartitionSpec as P

HEAD_WIDTH = 128
ADAPTER_RANK = 64
ADAPTER_COUNT = 32
LOG2E = 1.4426950408889634
SCORE_SCALE = HEAD_WIDTH ** (-0.5)
neg_floor = -1e30
MIB = 1024 * 1024
F32 = jnp.float32
BF16 = jnp.bfloat16


def params(limit, *semantics):
    return pltpu.CompilerParams(
        dimension_semantics=semantics or None, vmem_limit_bytes=int(limit)
    )


def whole(shape):
    return pl.BlockSpec(shape, lambda *_: (0,) * len(shape))


def in_hbm(x):
    return pltpu.with_memory_space_constraint(x, pltpu.HBM)


def in_vmem(x):
    return pltpu.with_memory_space_constraint(x, pltpu.VMEM)


def cost(flops, size, transcendentals=0):
    return pl.CostEstimate(
        flops=int(flops), bytes_accessed=int(size), transcendentals=int(transcendentals)
    )


VMEM_SPEC = pl.BlockSpec(memory_space=pltpu.VMEM)
SMEM_SPEC = pl.BlockSpec(memory_space=pltpu.SMEM)
ANY_SPEC = pl.BlockSpec(memory_space=pl.ANY)


def stage_kernel(pieces, *refs):
    count = len(refs[:-1]) // (pieces + 1)
    sources, targets, sems = refs[:count], refs[count:-1], refs[-1]
    copies = []
    for i, target in enumerate(targets):
        rows = pl.ds((i % pieces) * target.shape[0], target.shape[0])
        copies.append(
            pltpu.make_async_copy(sources[i // pieces].at[rows], target, sems.at[i])
        )
    for copy in copies:
        copy.start()
    for copy in copies:
        copy.wait()


def stage(*arrays, pieces=4):
    shapes = [(x.shape[0] // pieces,) + x.shape[1:] for x in arrays for _ in range(pieces)]
    return pl.pallas_call(
        functools.partial(stage_kernel, pieces),
        out_shape=tuple(pltpu.VMEM(shape, BF16) for shape in shapes),
        in_specs=[ANY_SPEC] * len(arrays),
        out_specs=(ANY_SPEC,) * len(shapes),
        scratch_shapes=[pltpu.SemaphoreType.DMA((len(shapes),))],
        compiler_params=params(MIB),
        cost_estimate=cost(0, sum(2 * x.size for x in arrays)),
        name="stage",
    )(*[in_hbm(x) for x in arrays])


def cache_kernel(pieces, index_ref, slot_hbm, select_hbm, *refs):
    sources, targets = refs[:2], refs[2 : 2 + 2 * pieces]
    near_ref, far_ref, slot_ref, select_ref, blocks_ref, sems = refs[2 + 2 * pieces :]
    count = 2 * pieces
    first = [
        pltpu.make_async_copy(slot_hbm, slot_ref, sems.at[count]),
        pltpu.make_async_copy(select_hbm, select_ref, sems.at[count + 1]),
    ]
    copies = []
    for i, target in enumerate(targets):
        rows = pl.ds((i % pieces) * target.shape[0], target.shape[0])
        copies.append(
            pltpu.make_async_copy(sources[i // pieces].at[rows], target, sems.at[i])
        )
    for copy in first + copies:
        copy.start()
    for copy in first:
        copy.wait()
    pages, total = blocks_ref.shape[2], slot_ref.shape[1]
    slots = index_ref[0] * pages + lax.broadcasted_iota(jnp.int32, (pages, total), 0)
    match = (slots == slot_ref[...]).astype(BF16)
    chosen = (select_ref[...] > 0).astype(BF16)
    held = lax.dot_general(
        chosen, match, (((1,), (1,)), ((), ())), preferred_element_type=F32
    )
    put_blocks(index_ref[0], held, blocks_ref, near_ref, far_ref)
    for copy in copies:
        copy.wait()


def stage_cache(index, page_cache_slot, selection, keys, values, mem_count, pieces=2):
    forks, total = selection.shape
    pages = keys.shape[0]
    line, fork_own = mem_count // 2, forks // mem_count
    shapes = [(x.shape[0] // pieces,) + x.shape[1:] for x in (keys, values) for _ in range(pieces)]
    mask = pltpu.VMEM((line, fork_own, pages), F32)
    return pl.pallas_call(
        functools.partial(cache_kernel, pieces),
        out_shape=tuple(pltpu.VMEM(shape, BF16) for shape in shapes) + (mask, mask),
        in_specs=[SMEM_SPEC] + [ANY_SPEC] * 4,
        out_specs=(ANY_SPEC,) * len(shapes) + (VMEM_SPEC,) * 2,
        scratch_shapes=[
            pltpu.VMEM((1, total), jnp.int32),
            pltpu.VMEM((forks, total), jnp.int32),
            pltpu.VMEM((mem_count, fork_own, pages), F32),
            pltpu.SemaphoreType.DMA((2 * pieces + 2,)),
        ],
        compiler_params=params(4 * MIB),
        cost_estimate=cost(0, 4 * keys.size),
        name="stage_cache",
    )(index, *[in_hbm(x) for x in (page_cache_slot.reshape(1, total), selection, keys, values)])


def fold_kernel(one_ref, two_ref, *out_refs):
    for i, out_ref in enumerate(out_refs):
        out_ref[...] = one_ref[i] + two_ref[i]


def fold(one, two):
    out = pltpu.VMEM(one.shape[1:], F32)
    return pl.pallas_call(
        fold_kernel,
        out_shape=(out,) * one.shape[0],
        in_specs=[VMEM_SPEC] * 2,
        out_specs=(VMEM_SPEC,) * one.shape[0],
        compiler_params=params(MIB * 2 + 16 * one.size),
        cost_estimate=cost(one.size, 12 * one.size),
        name="fold",
    )(in_vmem(one), two)


def take_blocks(index, blocks_ref, near_ref, far_ref):
    place, parity = index // 2, index % 2
    for i in range(near_ref.shape[0]):
        at = 2 * (place ^ i)
        near_ref[i] = blocks_ref[at + parity]
        far_ref[i] = blocks_ref[at + 1 - parity]


def put_blocks(index, value, blocks_ref, near_ref, far_ref):
    count, rows, lanes = blocks_ref.shape
    own = value.shape[0] // count
    for i in range(count):
        blocks_ref[i, :own] = value[i * own : (i + 1) * own]
        if own < rows:
            blocks_ref[i, own:] = jnp.zeros((rows - own, lanes), F32)
    take_blocks(index, blocks_ref, near_ref, far_ref)


def first_kernel(
    index_ref,
    adapter_hbm,
    hidden_hbm,
    down_hbm,
    k_hbm,
    v_hbm,
    near_ref,
    far_ref,
    hidden_ref,
    adapter_ref,
    held,
    held_kv,
    rank_blocks,
    kv_blocks,
    sems,
):
    pieces, _, width = held.shape
    forks = hidden_ref.shape[0]
    kv_width = held_kv.shape[2]
    lanes = rank_blocks.shape[2]
    copies = [
        pltpu.make_async_copy(adapter_hbm, adapter_ref, sems.at[pieces + 3]),
        pltpu.make_async_copy(hidden_hbm, hidden_ref, sems.at[pieces + 2]),
        *[
            pltpu.make_async_copy(
                down_hbm.at[:, i * width : (i + 1) * width], held.at[i], sems.at[i]
            )
            for i in range(pieces)
        ],
        pltpu.make_async_copy(k_hbm, held_kv.at[0], sems.at[pieces]),
        pltpu.make_async_copy(v_hbm, held_kv.at[1], sems.at[pieces + 1]),
    ]
    for copy in copies:
        copy.start()
    copies[0].wait()
    fork_adapter = jnp.broadcast_to(adapter_ref[...].astype(F32), (HEAD_WIDTH, forks)).T
    lane_adapter = lax.broadcasted_iota(jnp.int32, (forks, HEAD_WIDTH), 1) // ADAPTER_RANK
    wanted = fork_adapter.astype(jnp.int32) - lane_adapter
    total = jnp.zeros((forks, HEAD_WIDTH), F32)
    copies[1].wait()
    for i in range(pieces):
        copies[2 + i].wait()
        block = jnp.dot(hidden_ref[...], held[i], preferred_element_type=F32)
        for j in range(width // HEAD_WIDTH):
            first = (i * width + j * HEAD_WIDTH) // ADAPTER_RANK
            part = block[:, j * HEAD_WIDTH : (j + 1) * HEAD_WIDTH]
            total += jnp.where(wanted == first, part, 0.0)
    flipped = total.T
    flipped = flipped[:ADAPTER_RANK] + flipped[ADAPTER_RANK:]
    if lanes > forks:
        flipped = jnp.concatenate([flipped, jnp.zeros((ADAPTER_RANK, lanes - forks), F32)], axis=1)
    at = slice(0, lanes)
    put_blocks(index_ref[0], flipped, rank_blocks, near_ref.at[:, :, at], far_ref.at[:, :, at])
    for i in range(2):
        copies[2 + pieces + i].wait()
        part = jnp.dot(hidden_ref[...], held_kv[i], preferred_element_type=F32)
        at = slice(lanes + i * kv_width, lanes + (i + 1) * kv_width)
        put_blocks(index_ref[0], part, kv_blocks, near_ref.at[:, :, at], far_ref.at[:, :, at])


def project_first(index, adapter, hidden, down, k_weight, v_weight, mem_count, width=256):
    forks, depth = hidden.shape
    columns, kv_width = down.shape[1], k_weight.shape[1]
    lanes = -(-forks // HEAD_WIDTH) * HEAD_WIDTH
    line, fork_own = mem_count // 2, forks // mem_count
    pieces = columns // width
    out = pltpu.VMEM((line, fork_own, lanes + 2 * kv_width), F32)
    weights = 2 * depth * (columns + 2 * kv_width)
    return pl.pallas_call(
        first_kernel,
        out_shape=(out, out, pltpu.VMEM(hidden.shape, BF16), pltpu.VMEM((1, forks), jnp.int32)),
        in_specs=[SMEM_SPEC] + [ANY_SPEC] * 5,
        out_specs=(VMEM_SPEC,) * 4,
        scratch_shapes=[
            pltpu.VMEM((pieces, depth, width), BF16),
            pltpu.VMEM((2, depth, kv_width), BF16),
            pltpu.VMEM((mem_count, fork_own, lanes), F32),
            pltpu.VMEM((mem_count, fork_own, kv_width), F32),
            pltpu.SemaphoreType.DMA((pieces + 4,)),
        ],
        compiler_params=params(weights + 4 * MIB),
        cost_estimate=cost(forks * weights, weights),
        name="project_first",
    )(index, *[in_hbm(x) for x in (adapter.reshape(1, forks), hidden, down, k_weight, v_weight)])


def project_kernel(start, extra, hidden_ref, q_hbm, *refs):
    up_hbm, part_ref, up_ref, held, sems = refs if extra else (None, refs[0], None, *refs[1:])
    pieces, _, width = held.shape
    copies = []
    for i in range(pieces):
        columns = pl.ds(start + i * width, width)
        copies.append(pltpu.make_async_copy(q_hbm.at[:, columns], held.at[i], sems.at[i]))
    if extra:
        copies.append(pltpu.make_async_copy(up_hbm, up_ref, sems.at[pieces]))
    for copy in copies:
        copy.start()
    for i in range(pieces):
        copies[i].wait()
        part_ref[:, i * width : (i + 1) * width] = jnp.dot(
            hidden_ref[...], held[i], preferred_element_type=F32
        )
    if extra:
        copies[-1].wait()


def project(hidden, q_weight, start, columns, up=None, width=256):
    forks, depth = hidden.shape
    pieces = columns // width
    weights = 2 * depth * columns
    extra = [] if up is None else [up]
    return pl.pallas_call(
        functools.partial(project_kernel, start, bool(extra)),
        out_shape=tuple(
            [pltpu.VMEM((forks, columns), F32)] + [pltpu.VMEM(x.shape, BF16) for x in extra]
        ),
        in_specs=[VMEM_SPEC] + [ANY_SPEC] * (1 + len(extra)),
        out_specs=(VMEM_SPEC,) * (1 + len(extra)),
        scratch_shapes=[
            pltpu.VMEM((pieces, depth, width), BF16),
            pltpu.SemaphoreType.DMA((pieces + 1,)),
        ],
        compiler_params=params(weights + 2 * MIB),
        cost_estimate=cost(forks * weights, weights + sum(2 * x.size for x in extra)),
        name="project",
    )(in_vmem(hidden), *[in_hbm(x) for x in [q_weight] + extra])


def line_sum_kernel(after_ref, *refs):
    parts, (own_ref, other_ref) = refs[:-2], refs[-2:]
    own_ref[...] = functools.reduce(jnp.add, [ref[0] for ref in parts])
    other_ref[...] = functools.reduce(jnp.add, [ref[1] for ref in parts])


def line_sum(parts, after):
    out = pltpu.VMEM(parts[0].shape[1:], F32)
    size = len(parts) * parts[0].size
    return pl.pallas_call(
        line_sum_kernel,
        out_shape=(out, out),
        in_specs=[ANY_SPEC] + [VMEM_SPEC] * len(parts),
        out_specs=(VMEM_SPEC,) * 2,
        compiler_params=params(2 * MIB + 8 * size),
        cost_estimate=cost(size, 4 * size),
        name="line_sum",
    )(after, *parts)


def delta_kernel(line, ranks, start, joint, index_ref, adapter_ref, *refs):
    first_refs = refs[:line]
    part_ref, up_ref, *out_refs, blocks_ref = refs[line:]
    forks, width = part_ref.shape[0], blocks_ref.shape[2]
    if joint:
        near_ref, far_ref = out_refs[0].at[:, 0], out_refs[0].at[:, 1]
        new_ref = out_refs[1]
        lanes = first_refs[0].shape[1] - new_ref.shape[1]
        total = functools.reduce(jnp.add, [ref[:, lanes:] for ref in first_refs])
        new_ref[...] = total.astype(BF16)
    else:
        near_ref, far_ref = out_refs
    acts = functools.reduce(jnp.add, [ref[:ranks, :forks] for ref in first_refs])
    acts = acts.astype(BF16).astype(F32)
    adapters = lax.broadcasted_iota(jnp.int32, (ADAPTER_COUNT, forks), 0)
    onehot = (adapters == adapter_ref[...]).astype(F32)
    spread = jnp.concatenate(
        [acts[r : r + 1, :] * onehot for r in range(ranks)], axis=0
    ).astype(BF16)
    for i in range(part_ref.shape[1] // width):
        delta = lax.dot_general(
            spread,
            up_ref[:, start + i * width : start + (i + 1) * width],
            (((0,), (0,)), ((), ())),
            preferred_element_type=F32,
        )
        at = slice(i * width, (i + 1) * width)
        put_blocks(
            index_ref[0],
            part_ref[:, at] + delta,
            blocks_ref,
            near_ref.at[:, :, at],
            far_ref.at[:, :, at],
        )


def add_delta(index, adapter, first_parts, part, up, mem_count, start, new_width=0, width=256):
    forks, columns = part.shape
    line, fork_own = mem_count // 2, forks // mem_count
    ranks = ADAPTER_RANK // mem_count
    if new_width:
        out = (
            pltpu.VMEM((line, 2, fork_own, columns), F32),
            pltpu.VMEM((fork_own, new_width), BF16),
        )
    else:
        out = (pltpu.VMEM((line, fork_own, columns), F32),) * 2
    return pl.pallas_call(
        functools.partial(delta_kernel, line, ranks, start, new_width > 0),
        out_shape=out,
        in_specs=[SMEM_SPEC] + [VMEM_SPEC] * (line + 3),
        out_specs=(VMEM_SPEC,) * 2,
        scratch_shapes=[pltpu.VMEM((mem_count, fork_own, width), F32)],
        compiler_params=params(4 * MIB),
        cost_estimate=cost(
            2 * forks * up.shape[0] * columns, 2 * up.shape[0] * columns + 8 * forks * columns
        ),
        name="add_delta",
    )(index, in_vmem(adapter), *first_parts, in_vmem(part), in_vmem(up))


def put_terms(lse):
    heads, forks = lse.shape
    high = lse.astype(BF16).astype(F32)
    rest = lse - high
    middle = rest.astype(BF16).astype(F32)
    low = rest - middle
    spare = jnp.zeros((HEAD_WIDTH - 3 * heads, forks), F32)
    return jnp.concatenate([high, middle, low, spare], axis=0).T.astype(BF16)


def get_terms(terms, heads):
    terms = terms.astype(F32)
    return terms[:, :heads] + terms[:, heads : 2 * heads] + terms[:, 2 * heads : 3 * heads]


def attend_kernel(pieces, q_ref, mask_ref, *refs):
    k_refs, v_refs, (out_ref, score_ref, lse_ref) = (
        refs[:pieces],
        refs[pieces : 2 * pieces],
        refs[2 * pieces :],
    )
    forks = q_ref.shape[0]
    kv_local, group = lse_ref.shape[:2]
    pages = score_ref.shape[0] // 2
    held = pages // pieces
    scale = SCORE_SCALE * LOG2E
    chosen_by = mask_ref[...].reshape(forks, pages)
    spare = jnp.zeros((forks, HEAD_WIDTH - pages % HEAD_WIDTH), F32)
    chosen_by = jnp.concatenate([chosen_by, spare], axis=1).T[:pages]
    mask = jnp.concatenate([chosen_by] * group, axis=1) > 0
    ones = jnp.ones((8, score_ref.shape[1]), BF16)

    def score(kv_head, queries, p):
        lanes = slice(kv_head * HEAD_WIDTH, (kv_head + 1) * HEAD_WIDTH)
        scores = lax.dot_general(
            k_refs[p // held][p % held, :, lanes],
            queries,
            (((1,), (1,)), ((), ())),
            preferred_element_type=F32,
        )
        score_ref[kv_head % 2 * pages + p] = scores
        return jnp.max(scores, axis=0, keepdims=True)

    def term(kv_head, peaks, top, p):
        lanes = slice(kv_head * HEAD_WIDTH, (kv_head + 1) * HEAD_WIDTH)
        scores = score_ref[kv_head % 2 * pages + p]
        weights = jnp.exp2((scores - peaks[p]) * scale).astype(BF16)
        chosen = jnp.where(mask[p : p + 1], peaks[p], neg_floor)
        factor = jnp.where(mask[p : p + 1], jnp.exp2((chosen - top) * scale), 0.0)
        values = jnp.concatenate([v_refs[p // held][p % held, :, lanes].T, ones], axis=0)
        return jnp.dot(values, weights, preferred_element_type=F32) * factor

    def head_queries(kv_head):
        first = kv_head * group
        return jnp.concatenate(
            [
                q_ref[:, (first + g) * HEAD_WIDTH : (first + g + 1) * HEAD_WIDTH]
                for g in range(group)
            ],
            axis=0,
        )

    queries = head_queries(0)
    peaks = [score(0, queries, p) for p in range(pages)]
    for kv_head in range(kv_local):
        chosen = [jnp.where(mask[p : p + 1], peaks[p], neg_floor) for p in range(pages)]
        top = functools.reduce(jnp.maximum, chosen)
        if kv_head + 1 < kv_local:
            queries = head_queries(kv_head + 1)
        acc = None
        next_peaks = []
        for p in range(pages):
            if kv_head + 1 < kv_local:
                next_peaks.append(score(kv_head + 1, queries, p))
            part = term(kv_head, peaks, top, p)
            acc = part if acc is None else acc + part
        peaks = next_peaks
        mass = acc[HEAD_WIDTH : HEAD_WIDTH + 1]
        some = mass > 0
        safe = jnp.where(some, mass, 1.0)
        rows = (acc[:HEAD_WIDTH] * jnp.where(some, 1.0 / safe, 0.0)).T
        lse = jnp.where(some, top * scale + jnp.log2(safe), neg_floor)
        for g in range(group):
            at = (kv_head * group + g) * HEAD_WIDTH
            out_ref[:, at : at + HEAD_WIDTH] = rows[g * forks : (g + 1) * forks].astype(BF16)
        lse_ref[kv_head] = jnp.concatenate(
            [lse[:, g * forks : (g + 1) * forks] for g in range(group)], axis=0
        )

    heads = kv_local * group
    out_ref[:, heads * HEAD_WIDTH :] = put_terms(lse_ref[...].reshape(heads, forks))


def attend(queries, keys, values, mask):
    forks, width = queries.shape
    held, page_len, kv_width = keys[0].shape
    pieces = len(keys)
    pages = held * pieces
    kv_local = kv_width // HEAD_WIDTH
    group = width // kv_width
    rows = group * forks
    return pl.pallas_call(
        functools.partial(attend_kernel, pieces),
        out_shape=pltpu.VMEM((forks, width + HEAD_WIDTH), BF16),
        in_specs=[VMEM_SPEC] * (2 + 2 * pieces),
        out_specs=VMEM_SPEC,
        scratch_shapes=[
            pltpu.VMEM((2 * pages, page_len, rows), F32),
            pltpu.VMEM((kv_local, group, forks), F32),
        ],
        compiler_params=params(10 * pages * page_len * rows + 4 * MIB),
        cost_estimate=cost(
            4 * pages * page_len * kv_local * rows * HEAD_WIDTH,
            4 * pages * page_len * kv_width + 4 * forks * width,
            pages * page_len * kv_local * rows,
        ),
        name="attend",
    )(queries, *[in_vmem(x) for x in [mask, *keys, *values]])


def weigh(lses):
    top = functools.reduce(jnp.maximum, lses)
    weights = [jnp.exp2(lse - top) for lse in lses]
    mass = functools.reduce(jnp.add, weights)
    return [weight / mass for weight in weights], top + jnp.log2(mass)


def combine_kernel(heads, after_ref, *refs):
    parts, out_ref = [ref.at[1] for ref in refs[:-1]], refs[-1]
    width = heads * HEAD_WIDTH
    weights, lse = weigh([get_terms(ref[:, width:], heads) for ref in parts])
    for h in range(heads):
        lanes = slice(h * HEAD_WIDTH, (h + 1) * HEAD_WIDTH)
        out_ref[:, lanes] = functools.reduce(
            jnp.add, [w[:, h : h + 1] * ref[:, lanes].astype(F32) for w, ref in zip(weights, parts)]
        ).astype(BF16)
    lse = jnp.maximum(lse, neg_floor)
    spare = jnp.zeros((lse.shape[0], HEAD_WIDTH - heads), F32)
    out_ref[:, width:] = put_terms(jnp.concatenate([lse, spare], axis=1).T[:heads])


def combine(parts, after, heads):
    _, fork_own, width = parts[0].shape
    size = len(parts) * parts[0].size
    return pl.pallas_call(
        functools.partial(combine_kernel, heads),
        out_shape=pltpu.VMEM((fork_own, width), BF16),
        in_specs=[ANY_SPEC] + [VMEM_SPEC] * len(parts),
        out_specs=VMEM_SPEC,
        compiler_params=params(4 * size + 4 * MIB),
        cost_estimate=cost(4 * size, 2 * size),
        name="combine",
    )(after, *parts)


def merge_kernel(heads, kv_heads, *refs):
    *line_refs, more_ref, q_ref, new_ref, out_ref = refs
    parts = [ref.at[0] for ref in line_refs] + [more_ref]
    group = heads // kv_heads
    width = heads * HEAD_WIDTH

    def new_head(i):
        return new_ref[:, i * HEAD_WIDTH : (i + 1) * HEAD_WIDTH].astype(F32)

    scores = []
    for h in range(heads):
        query = q_ref[:, h * HEAD_WIDTH : (h + 1) * HEAD_WIDTH].astype(F32)
        scores.append(jnp.sum(query * new_head(h // group), axis=1, keepdims=True))
    own = jnp.concatenate(scores, axis=1) * (SCORE_SCALE * LOG2E)
    (own_weight, *weights), _ = weigh([own] + [get_terms(ref[:, width:], heads) for ref in parts])
    for h in range(heads):
        lanes = slice(h * HEAD_WIDTH, (h + 1) * HEAD_WIDTH)
        total = own_weight[:, h : h + 1] * new_head(kv_heads + h // group)
        for weight, ref in zip(weights, parts):
            total += weight[:, h : h + 1] * ref[:, lanes].astype(F32)
        out_ref[:, lanes] = total.astype(BF16)


def merge(parts, more, queries, new, heads, kv_heads):
    fork_own, width = more.shape
    size = (len(parts) + 1) * fork_own * width
    return pl.pallas_call(
        functools.partial(merge_kernel, heads, kv_heads),
        out_shape=pltpu.VMEM((fork_own, heads * HEAD_WIDTH), BF16),
        in_specs=[VMEM_SPEC] * (len(parts) + 3),
        out_specs=VMEM_SPEC,
        compiler_params=params(8 * size + 4 * MIB),
        cost_estimate=cost(4 * size, 2 * size),
        name="merge",
    )(*parts, more, queries, new)


def output_kernel(context_ref, *refs):
    weight_refs, out_ref = refs[:-1], refs[-1]
    total = None
    for i, ref in enumerate(weight_refs):
        depth = ref.shape[0]
        part = jnp.dot(
            context_ref[:, i * depth : (i + 1) * depth], ref[...], preferred_element_type=F32
        )
        total = part if total is None else total + part
    out_ref[...] = total


def output_project(context, weights):
    forks, rows = context.shape
    columns = weights[0].shape[1]
    return pl.pallas_call(
        output_kernel,
        out_shape=pltpu.VMEM((forks, columns), F32),
        in_specs=[VMEM_SPEC] * (1 + len(weights)),
        out_specs=VMEM_SPEC,
        compiler_params=params(4 * MIB),
        cost_estimate=cost(2 * forks * rows * columns, 2 * rows * columns),
        name="output_project",
    )(context, *[in_vmem(x) for x in weights])


def finish_kernel(count, line, index_ref, *refs):
    near_refs, far_refs, out_ref = refs[:count], refs[count : 2 * count], refs[-1]
    place, parity = index_ref[0] // 2, index_ref[0] % 2
    rows = out_ref.shape[1]
    for group, side in ((near_refs, parity), (far_refs, 1 - parity)):
        for i in range(line):
            total = functools.reduce(jnp.add, [ref[i * rows : (i + 1) * rows] for ref in group])
            out_ref[2 * (place ^ i) + side] = total.astype(BF16)


def finish(index, near, far, mem_count):
    rows, columns = near[0].shape
    line = mem_count // 2
    return pl.pallas_call(
        functools.partial(finish_kernel, len(near), line),
        out_shape=jax.ShapeDtypeStruct((mem_count, rows // line, columns), BF16),
        in_specs=[SMEM_SPEC] + [VMEM_SPEC] * (2 * len(near)),
        out_specs=VMEM_SPEC,
        compiler_params=params(4 * MIB),
        cost_estimate=cost(0, 8 * rows * columns * len(near)),
        name="finish",
    )(index, *near, *far)


def shards(
    hidden,
    adapter,
    page_cache_slot,
    selection,
    query_projection_weight,
    key_projection_weight,
    value_projection_weight,
    adapter_down_weight,
    adapter_up_weight,
    output_projection_weight,
    prefix_key_cache,
    prefix_value_cache,
):
    mem_count = lax.axis_size("mem")
    mem_index = lax.axis_index("mem")
    forks = hidden.shape[0]
    fork_own = forks // mem_count
    q_width = query_projection_weight.shape[1]
    kv_width = key_projection_weight.shape[1]
    heads, kv_heads = q_width // HEAD_WIDTH, kv_width // HEAD_WIDTH
    pages = prefix_key_cache.shape[0]
    line = mem_count // 2
    index = mem_index.reshape(1)
    place, parity = mem_index // 2, mem_index % 2

    def swapped(x, step, cross=0):
        pairs = [(i, i ^ (2 * step + cross)) for i in range(mem_count)]
        return lax.ppermute(x, "mem", pairs)

    def along(blocks, cross=0):
        return [swapped(blocks[i], i, cross) if i or cross else blocks[0] for i in range(line)]

    def gather(x):
        return jnp.concatenate([x] + [swapped(x, i) for i in range(1, line)], axis=0)

    def pair(x):
        return swapped(x, 0, 1)

    near_1, far_1, hidden, adapter = project_first(
        index, adapter, hidden, adapter_down_weight, key_projection_weight, value_projection_weight, mem_count
    )
    cut = q_width * 11 // 16 // 256 * 256
    (part_a,) = project(hidden, query_projection_weight, 0, cut)
    first_parts = fold(near_1, pair(far_1))
    first_parts, part_a, hidden = lax.optimization_barrier((first_parts, part_a, hidden))
    part_b, up = project(
        hidden, query_projection_weight, cut, q_width - cut, adapter_up_weight.reshape(-1, q_width)
    )
    first_parts = along(first_parts)

    near_a, far_a = add_delta(index, adapter, first_parts, part_a, up, mem_count, 0)
    near_a, far_a, part_b = lax.optimization_barrier((near_a, far_a, part_b))
    both_b, own_new = add_delta(
        index, adapter, first_parts, part_b, up, mem_count, cut, 2 * kv_width
    )
    sums_a = fold(near_a, pair(far_a))
    own_b, other_b = line_sum(along(both_b), sums_a[0])
    own_a = functools.reduce(jnp.add, along(sums_a))
    own_b = own_b + pair(other_b)
    own_queries = jnp.concatenate([own_a.astype(BF16), own_b.astype(BF16)], axis=1)

    *staged, near_mask, far_mask = stage_cache(
        index, page_cache_slot, selection, prefix_key_cache, prefix_value_cache, mem_count
    )
    keys, values = staged[: len(staged) // 2], staged[len(staged) // 2 :]
    near_queries, near_mask = lax.optimization_barrier((gather(own_queries), near_mask))
    far_queries = pair(near_queries)
    near = attend(near_queries, keys, values, near_mask)
    far = attend(far_queries, keys, values, far_mask)
    blocks = (line, 1, fork_own, q_width + HEAD_WIDTH)
    results = jnp.concatenate([near.reshape(blocks), far.reshape(blocks)], axis=1)
    results, out_weight = lax.optimization_barrier((results, output_projection_weight))
    parts = along(results)
    out_weights = stage(out_weight)
    more = pair(combine(parts, out_weights[0], heads))
    context_own = merge(parts, more, own_queries, own_new, heads, kv_heads)

    near_context = gather(context_own)
    far_context = pair(near_context)
    tp_count = lax.axis_size("tp")
    outs = []
    for context in (near_context, far_context):
        part = output_project(context, out_weights)
        terms = [part]
        for shift in range(1, tp_count):
            pairs = [(i, (i + shift) % tp_count) for i in range(tp_count)]
            terms.append(lax.ppermute(part, "tp", pairs))
        outs.append(terms)
    return finish(index, *outs, mem_count).reshape(forks, -1)


def solution(mesh):
    return jax.shard_map(
        shards,
        mesh=mesh,
        in_specs=(
            P("groups", "mem"),
            P("groups"),
            P("groups"),
            P("groups", None),
            P("mem", "tp"),
            P("mem", "tp"),
            P("mem", "tp"),
            P("mem", None),
            P("mem", None, "tp"),
            P("tp", "mem"),
            P(("groups", "mem"), None, "tp"),
            P(("groups", "mem"), None, "tp"),
        ),
        out_specs=P("groups", "mem"),
        check_vma=False,
    )
```

```python
import functools

import jax
import jax.numpy as jnp
from jax import lax
from jax.experimental import pallas as pl
from jax.experimental.pallas import tpu as pltpu
from jax.sharding import PartitionSpec as P

HEAD_WIDTH = 128
ADAPTER_RANK = 64
ADAPTER_COUNT = 32
LOG2E = 1.4426950408889634
SCORE_SCALE = HEAD_WIDTH ** (-0.5)
neg_floor = -1e30
MIB = 1024 * 1024
F32 = jnp.float32
BF16 = jnp.bfloat16


def params(limit, *semantics):
    return pltpu.CompilerParams(
        dimension_semantics=semantics or None, vmem_limit_bytes=int(limit)
    )


def whole(shape):
    return pl.BlockSpec(shape, lambda *_: (0,) * len(shape))


def in_hbm(x):
    return pltpu.with_memory_space_constraint(x, pltpu.HBM)


def in_vmem(x):
    return pltpu.with_memory_space_constraint(x, pltpu.VMEM)


def cost(flops, size, transcendentals=0):
    return pl.CostEstimate(
        flops=int(flops), bytes_accessed=int(size), transcendentals=int(transcendentals)
    )


VMEM_SPEC = pl.BlockSpec(memory_space=pltpu.VMEM)
SMEM_SPEC = pl.BlockSpec(memory_space=pltpu.SMEM)
ANY_SPEC = pl.BlockSpec(memory_space=pl.ANY)


def stage_kernel(pieces, *refs):
    count = len(refs[:-1]) // (pieces + 1)
    sources, targets, sems = refs[:count], refs[count:-1], refs[-1]
    copies = []
    for i, target in enumerate(targets):
        rows = pl.ds((i % pieces) * target.shape[0], target.shape[0])
        copies.append(
            pltpu.make_async_copy(sources[i // pieces].at[rows], target, sems.at[i])
        )
    for copy in copies:
        copy.start()
    for copy in copies:
        copy.wait()


def stage(*arrays, pieces=4):
    shapes = [(x.shape[0] // pieces,) + x.shape[1:] for x in arrays for _ in range(pieces)]
    return pl.pallas_call(
        functools.partial(stage_kernel, pieces),
        out_shape=tuple(pltpu.VMEM(shape, BF16) for shape in shapes),
        in_specs=[ANY_SPEC] * len(arrays),
        out_specs=(ANY_SPEC,) * len(shapes),
        scratch_shapes=[pltpu.SemaphoreType.DMA((len(shapes),))],
        compiler_params=params(MIB),
        cost_estimate=cost(0, sum(2 * x.size for x in arrays)),
        name="stage",
    )(*[in_hbm(x) for x in arrays])


def cache_kernel(pieces, index_ref, slot_hbm, select_hbm, *refs):
    sources, targets = refs[:2], refs[2 : 2 + 2 * pieces]
    near_ref, far_ref, slot_ref, select_ref, blocks_ref, sems = refs[2 + 2 * pieces :]
    count = 2 * pieces
    first = [
        pltpu.make_async_copy(slot_hbm, slot_ref, sems.at[count]),
        pltpu.make_async_copy(select_hbm, select_ref, sems.at[count + 1]),
    ]
    copies = []
    for i, target in enumerate(targets):
        rows = pl.ds((i % pieces) * target.shape[0], target.shape[0])
        copies.append(
            pltpu.make_async_copy(sources[i // pieces].at[rows], target, sems.at[i])
        )
    for copy in first + copies:
        copy.start()
    for copy in first:
        copy.wait()
    pages, total = blocks_ref.shape[2], slot_ref.shape[1]
    slots = index_ref[0] * pages + lax.broadcasted_iota(jnp.int32, (pages, total), 0)
    match = (slots == slot_ref[...]).astype(BF16)
    chosen = (select_ref[...] > 0).astype(BF16)
    held = lax.dot_general(
        chosen, match, (((1,), (1,)), ((), ())), preferred_element_type=F32
    )
    put_blocks(index_ref[0], held, blocks_ref, near_ref, far_ref)
    for copy in copies:
        copy.wait()


def stage_cache(index, page_cache_slot, selection, keys, values, mem_count, pieces=2):
    forks, total = selection.shape
    pages = keys.shape[0]
    line, fork_own = mem_count // 2, forks // mem_count
    shapes = [(x.shape[0] // pieces,) + x.shape[1:] for x in (keys, values) for _ in range(pieces)]
    mask = pltpu.VMEM((line, fork_own, pages), F32)
    return pl.pallas_call(
        functools.partial(cache_kernel, pieces),
        out_shape=tuple(pltpu.VMEM(shape, BF16) for shape in shapes) + (mask, mask),
        in_specs=[SMEM_SPEC] + [ANY_SPEC] * 4,
        out_specs=(ANY_SPEC,) * len(shapes) + (VMEM_SPEC,) * 2,
        scratch_shapes=[
            pltpu.VMEM((1, total), jnp.int32),
            pltpu.VMEM((forks, total), jnp.int32),
            pltpu.VMEM((mem_count, fork_own, pages), F32),
            pltpu.SemaphoreType.DMA((2 * pieces + 2,)),
        ],
        compiler_params=params(4 * MIB),
        cost_estimate=cost(0, 4 * keys.size),
        name="stage_cache",
    )(index, *[in_hbm(x) for x in (page_cache_slot.reshape(1, total), selection, keys, values)])


def fold_kernel(one_ref, two_ref, *out_refs):
    for i, out_ref in enumerate(out_refs):
        out_ref[...] = one_ref[i] + two_ref[i]


def fold(one, two):
    out = pltpu.VMEM(one.shape[1:], F32)
    return pl.pallas_call(
        fold_kernel,
        out_shape=(out,) * one.shape[0],
        in_specs=[VMEM_SPEC] * 2,
        out_specs=(VMEM_SPEC,) * one.shape[0],
        compiler_params=params(MIB * 2 + 16 * one.size),
        cost_estimate=cost(one.size, 12 * one.size),
        name="fold",
    )(in_vmem(one), two)


def take_blocks(index, blocks_ref, near_ref, far_ref):
    place, parity = index // 2, index % 2
    for i in range(near_ref.shape[0]):
        at = 2 * (place ^ i)
        near_ref[i] = blocks_ref[at + parity]
        far_ref[i] = blocks_ref[at + 1 - parity]


def put_blocks(index, value, blocks_ref, near_ref, far_ref):
    count, rows, lanes = blocks_ref.shape
    own = value.shape[0] // count
    for i in range(count):
        blocks_ref[i, :own] = value[i * own : (i + 1) * own]
        if own < rows:
            blocks_ref[i, own:] = jnp.zeros((rows - own, lanes), F32)
    take_blocks(index, blocks_ref, near_ref, far_ref)


def first_kernel(
    index_ref,
    adapter_hbm,
    hidden_hbm,
    down_hbm,
    k_hbm,
    v_hbm,
    near_ref,
    far_ref,
    hidden_ref,
    adapter_ref,
    held,
    held_kv,
    rank_blocks,
    kv_blocks,
    sems,
):
    pieces, _, width = held.shape
    forks = hidden_ref.shape[0]
    kv_width = held_kv.shape[2]
    lanes = rank_blocks.shape[2]
    copies = [
        pltpu.make_async_copy(adapter_hbm, adapter_ref, sems.at[pieces + 3]),
        pltpu.make_async_copy(hidden_hbm, hidden_ref, sems.at[pieces + 2]),
        *[
            pltpu.make_async_copy(
                down_hbm.at[:, i * width : (i + 1) * width], held.at[i], sems.at[i]
            )
            for i in range(pieces)
        ],
        pltpu.make_async_copy(k_hbm, held_kv.at[0], sems.at[pieces]),
        pltpu.make_async_copy(v_hbm, held_kv.at[1], sems.at[pieces + 1]),
    ]
    for copy in copies:
        copy.start()
    copies[0].wait()
    fork_adapter = jnp.broadcast_to(adapter_ref[...].astype(F32), (HEAD_WIDTH, forks)).T
    lane_adapter = lax.broadcasted_iota(jnp.int32, (forks, HEAD_WIDTH), 1) // ADAPTER_RANK
    wanted = fork_adapter.astype(jnp.int32) - lane_adapter
    total = jnp.zeros((forks, HEAD_WIDTH), F32)
    copies[1].wait()
    for i in range(pieces):
        copies[2 + i].wait()
        block = jnp.dot(hidden_ref[...], held[i], preferred_element_type=F32)
        for j in range(width // HEAD_WIDTH):
            first = (i * width + j * HEAD_WIDTH) // ADAPTER_RANK
            part = block[:, j * HEAD_WIDTH : (j + 1) * HEAD_WIDTH]
            total += jnp.where(wanted == first, part, 0.0)
    flipped = total.T
    flipped = flipped[:ADAPTER_RANK] + flipped[ADAPTER_RANK:]
    if lanes > forks:
        flipped = jnp.concatenate([flipped, jnp.zeros((ADAPTER_RANK, lanes - forks), F32)], axis=1)
    at = slice(0, lanes)
    put_blocks(index_ref[0], flipped, rank_blocks, near_ref.at[:, :, at], far_ref.at[:, :, at])
    for i in range(2):
        copies[2 + pieces + i].wait()
        part = jnp.dot(hidden_ref[...], held_kv[i], preferred_element_type=F32)
        at = slice(lanes + i * kv_width, lanes + (i + 1) * kv_width)
        put_blocks(index_ref[0], part, kv_blocks, near_ref.at[:, :, at], far_ref.at[:, :, at])


def project_first(index, adapter, hidden, down, k_weight, v_weight, mem_count, width=256):
    forks, depth = hidden.shape
    columns, kv_width = down.shape[1], k_weight.shape[1]
    lanes = -(-forks // HEAD_WIDTH) * HEAD_WIDTH
    line, fork_own = mem_count // 2, forks // mem_count
    pieces = columns // width
    out = pltpu.VMEM((line, fork_own, lanes + 2 * kv_width), F32)
    weights = 2 * depth * (columns + 2 * kv_width)
    return pl.pallas_call(
        first_kernel,
        out_shape=(out, out, pltpu.VMEM(hidden.shape, BF16), pltpu.VMEM((1, forks), jnp.int32)),
        in_specs=[SMEM_SPEC] + [ANY_SPEC] * 5,
        out_specs=(VMEM_SPEC,) * 4,
        scratch_shapes=[
            pltpu.VMEM((pieces, depth, width), BF16),
            pltpu.VMEM((2, depth, kv_width), BF16),
            pltpu.VMEM((mem_count, fork_own, lanes), F32),
            pltpu.VMEM((mem_count, fork_own, kv_width), F32),
            pltpu.SemaphoreType.DMA((pieces + 4,)),
        ],
        compiler_params=params(weights + 4 * MIB),
        cost_estimate=cost(forks * weights, weights),
        name="project_first",
    )(index, *[in_hbm(x) for x in (adapter.reshape(1, forks), hidden, down, k_weight, v_weight)])


def project_kernel(start, extra, hidden_ref, q_hbm, *refs):
    up_hbm, part_ref, up_ref, held, sems = refs if extra else (None, refs[0], None, *refs[1:])
    pieces, _, width = held.shape
    copies = []
    for i in range(pieces):
        columns = pl.ds(start + i * width, width)
        copies.append(pltpu.make_async_copy(q_hbm.at[:, columns], held.at[i], sems.at[i]))
    if extra:
        copies.append(pltpu.make_async_copy(up_hbm, up_ref, sems.at[pieces]))
    for copy in copies:
        copy.start()
    for i in range(pieces):
        copies[i].wait()
        part_ref[:, i * width : (i + 1) * width] = jnp.dot(
            hidden_ref[...], held[i], preferred_element_type=F32
        )
    if extra:
        copies[-1].wait()


def project(hidden, q_weight, start, columns, up=None, width=256):
    forks, depth = hidden.shape
    pieces = columns // width
    weights = 2 * depth * columns
    extra = [] if up is None else [up]
    return pl.pallas_call(
        functools.partial(project_kernel, start, bool(extra)),
        out_shape=tuple(
            [pltpu.VMEM((forks, columns), F32)] + [pltpu.VMEM(x.shape, BF16) for x in extra]
        ),
        in_specs=[VMEM_SPEC] + [ANY_SPEC] * (1 + len(extra)),
        out_specs=(VMEM_SPEC,) * (1 + len(extra)),
        scratch_shapes=[
            pltpu.VMEM((pieces, depth, width), BF16),
            pltpu.SemaphoreType.DMA((pieces + 1,)),
        ],
        compiler_params=params(weights + 2 * MIB),
        cost_estimate=cost(forks * weights, weights + sum(2 * x.size for x in extra)),
        name="project",
    )(in_vmem(hidden), *[in_hbm(x) for x in [q_weight] + extra])


def line_sum_kernel(after_ref, *refs):
    parts, (own_ref, other_ref) = refs[:-2], refs[-2:]
    own_ref[...] = functools.reduce(jnp.add, [ref[0] for ref in parts])
    other_ref[...] = functools.reduce(jnp.add, [ref[1] for ref in parts])


def line_sum(parts, after):
    out = pltpu.VMEM(parts[0].shape[1:], F32)
    size = len(parts) * parts[0].size
    return pl.pallas_call(
        line_sum_kernel,
        out_shape=(out, out),
        in_specs=[ANY_SPEC] + [VMEM_SPEC] * len(parts),
        out_specs=(VMEM_SPEC,) * 2,
        compiler_params=params(2 * MIB + 8 * size),
        cost_estimate=cost(size, 4 * size),
        name="line_sum",
    )(after, *parts)


def delta_kernel(line, ranks, start, joint, index_ref, adapter_ref, *refs):
    first_refs = refs[:line]
    part_ref, up_ref, *out_refs, blocks_ref = refs[line:]
    forks, width = part_ref.shape[0], blocks_ref.shape[2]
    if joint:
        near_ref, far_ref = out_refs[0].at[:, 0], out_refs[0].at[:, 1]
        new_ref = out_refs[1]
        lanes = first_refs[0].shape[1] - new_ref.shape[1]
        total = functools.reduce(jnp.add, [ref[:, lanes:] for ref in first_refs])
        new_ref[...] = total.astype(BF16)
    else:
        near_ref, far_ref = out_refs
    acts = functools.reduce(jnp.add, [ref[:ranks, :forks] for ref in first_refs])
    acts = acts.astype(BF16).astype(F32)
    adapters = lax.broadcasted_iota(jnp.int32, (ADAPTER_COUNT, forks), 0)
    onehot = (adapters == adapter_ref[...]).astype(F32)
    spread = jnp.concatenate(
        [acts[r : r + 1, :] * onehot for r in range(ranks)], axis=0
    ).astype(BF16)
    for i in range(part_ref.shape[1] // width):
        delta = lax.dot_general(
            spread,
            up_ref[:, start + i * width : start + (i + 1) * width],
            (((0,), (0,)), ((), ())),
            preferred_element_type=F32,
        )
        at = slice(i * width, (i + 1) * width)
        put_blocks(
            index_ref[0],
            part_ref[:, at] + delta,
            blocks_ref,
            near_ref.at[:, :, at],
            far_ref.at[:, :, at],
        )


def add_delta(index, adapter, first_parts, part, up, mem_count, start, new_width=0, width=256):
    forks, columns = part.shape
    line, fork_own = mem_count // 2, forks // mem_count
    ranks = ADAPTER_RANK // mem_count
    if new_width:
        out = (
            pltpu.VMEM((line, 2, fork_own, columns), F32),
            pltpu.VMEM((fork_own, new_width), BF16),
        )
    else:
        out = (pltpu.VMEM((line, fork_own, columns), F32),) * 2
    return pl.pallas_call(
        functools.partial(delta_kernel, line, ranks, start, new_width > 0),
        out_shape=out,
        in_specs=[SMEM_SPEC] + [VMEM_SPEC] * (line + 3),
        out_specs=(VMEM_SPEC,) * 2,
        scratch_shapes=[pltpu.VMEM((mem_count, fork_own, width), F32)],
        compiler_params=params(4 * MIB),
        cost_estimate=cost(
            2 * forks * up.shape[0] * columns, 2 * up.shape[0] * columns + 8 * forks * columns
        ),
        name="add_delta",
    )(index, in_vmem(adapter), *first_parts, in_vmem(part), in_vmem(up))


def put_terms(lse):
    heads, forks = lse.shape
    high = lse.astype(BF16).astype(F32)
    rest = lse - high
    middle = rest.astype(BF16).astype(F32)
    low = rest - middle
    spare = jnp.zeros((HEAD_WIDTH - 3 * heads, forks), F32)
    return jnp.concatenate([high, middle, low, spare], axis=0).T.astype(BF16)


def get_terms(terms, heads):
    terms = terms.astype(F32)
    return terms[:, :heads] + terms[:, heads : 2 * heads] + terms[:, 2 * heads : 3 * heads]


def attend_kernel(pieces, q_ref, mask_ref, *refs):
    k_refs, v_refs, (out_ref, score_ref, lse_ref) = (
        refs[:pieces],
        refs[pieces : 2 * pieces],
        refs[2 * pieces :],
    )
    forks = q_ref.shape[0]
    kv_local, group = lse_ref.shape[:2]
    pages = score_ref.shape[0] // 2
    held = pages // pieces
    scale = SCORE_SCALE * LOG2E
    chosen_by = mask_ref[...].reshape(forks, pages)
    spare = jnp.zeros((forks, HEAD_WIDTH - pages % HEAD_WIDTH), F32)
    chosen_by = jnp.concatenate([chosen_by, spare], axis=1).T[:pages]
    mask = jnp.concatenate([chosen_by] * group, axis=1) > 0
    ones = jnp.ones((8, score_ref.shape[1]), BF16)

    def score(kv_head, queries, p):
        lanes = slice(kv_head * HEAD_WIDTH, (kv_head + 1) * HEAD_WIDTH)
        scores = lax.dot_general(
            k_refs[p // held][p % held, :, lanes],
            queries,
            (((1,), (1,)), ((), ())),
            preferred_element_type=F32,
        )
        score_ref[kv_head % 2 * pages + p] = scores
        return jnp.max(scores, axis=0, keepdims=True)

    def term(kv_head, peaks, top, p):
        lanes = slice(kv_head * HEAD_WIDTH, (kv_head + 1) * HEAD_WIDTH)
        scores = score_ref[kv_head % 2 * pages + p]
        weights = jnp.exp2((scores - peaks[p]) * scale).astype(BF16)
        chosen = jnp.where(mask[p : p + 1], peaks[p], neg_floor)
        factor = jnp.where(mask[p : p + 1], jnp.exp2((chosen - top) * scale), 0.0)
        values = jnp.concatenate([v_refs[p // held][p % held, :, lanes].T, ones], axis=0)
        return jnp.dot(values, weights, preferred_element_type=F32) * factor

    def head_queries(kv_head):
        first = kv_head * group
        return jnp.concatenate(
            [
                q_ref[:, (first + g) * HEAD_WIDTH : (first + g + 1) * HEAD_WIDTH]
                for g in range(group)
            ],
            axis=0,
        )

    queries = head_queries(0)
    peaks = [score(0, queries, p) for p in range(pages)]
    for kv_head in range(kv_local):
        chosen = [jnp.where(mask[p : p + 1], peaks[p], neg_floor) for p in range(pages)]
        top = functools.reduce(jnp.maximum, chosen)
        if kv_head + 1 < kv_local:
            queries = head_queries(kv_head + 1)
        acc = None
        next_peaks = []
        for p in range(pages):
            if kv_head + 1 < kv_local:
                next_peaks.append(score(kv_head + 1, queries, p))
            part = term(kv_head, peaks, top, p)
            acc = part if acc is None else acc + part
        peaks = next_peaks
        mass = acc[HEAD_WIDTH : HEAD_WIDTH + 1]
        some = mass > 0
        safe = jnp.where(some, mass, 1.0)
        rows = (acc[:HEAD_WIDTH] * jnp.where(some, 1.0 / safe, 0.0)).T
        lse = jnp.where(some, top * scale + jnp.log2(safe), neg_floor)
        for g in range(group):
            at = (kv_head * group + g) * HEAD_WIDTH
            out_ref[:, at : at + HEAD_WIDTH] = rows[g * forks : (g + 1) * forks].astype(BF16)
        lse_ref[kv_head] = jnp.concatenate(
            [lse[:, g * forks : (g + 1) * forks] for g in range(group)], axis=0
        )

    heads = kv_local * group
    out_ref[:, heads * HEAD_WIDTH :] = put_terms(lse_ref[...].reshape(heads, forks))


def attend(queries, keys, values, mask):
    forks, width = queries.shape
    held, page_len, kv_width = keys[0].shape
    pieces = len(keys)
    pages = held * pieces
    kv_local = kv_width // HEAD_WIDTH
    group = width // kv_width
    rows = group * forks
    return pl.pallas_call(
        functools.partial(attend_kernel, pieces),
        out_shape=pltpu.VMEM((forks, width + HEAD_WIDTH), BF16),
        in_specs=[VMEM_SPEC] * (2 + 2 * pieces),
        out_specs=VMEM_SPEC,
        scratch_shapes=[
            pltpu.VMEM((2 * pages, page_len, rows), F32),
            pltpu.VMEM((kv_local, group, forks), F32),
        ],
        compiler_params=params(10 * pages * page_len * rows + 4 * MIB),
        cost_estimate=cost(
            4 * pages * page_len * kv_local * rows * HEAD_WIDTH,
            4 * pages * page_len * kv_width + 4 * forks * width,
            pages * page_len * kv_local * rows,
        ),
        name="attend",
    )(queries, *[in_vmem(x) for x in [mask, *keys, *values]])


def merge_kernel(heads, kv_heads, sources, *refs):
    parts, (q_ref, new_ref, _, out_ref) = refs[:sources], refs[sources:]
    group = heads // kv_heads
    width = heads * HEAD_WIDTH
    lses = [get_terms(ref[:, width : width + HEAD_WIDTH], heads) for ref in parts]

    def new_head(i):
        return new_ref[:, i * HEAD_WIDTH : (i + 1) * HEAD_WIDTH].astype(F32)

    scores = []
    for h in range(heads):
        query = q_ref[:, h * HEAD_WIDTH : (h + 1) * HEAD_WIDTH].astype(F32)
        scores.append(jnp.sum(query * new_head(h // group), axis=1, keepdims=True))
    own = jnp.concatenate(scores, axis=1) * (SCORE_SCALE * LOG2E)
    top = functools.reduce(jnp.maximum, lses, own)
    own_weight = jnp.exp2(own - top)
    weights = [jnp.exp2(lse - top) for lse in lses]
    inverse = 1.0 / functools.reduce(jnp.add, weights, own_weight)
    own_weight = own_weight * inverse
    weights = [weight * inverse for weight in weights]
    for h in range(heads):
        lanes = slice(h * HEAD_WIDTH, (h + 1) * HEAD_WIDTH)
        total = own_weight[:, h : h + 1] * new_head(kv_heads + h // group)
        for weight, ref in zip(weights, parts):
            total += weight[:, h : h + 1] * ref[:, lanes].astype(F32)
        out_ref[:, lanes] = total.astype(BF16)


def merge(parts, queries, new, after, heads, kv_heads):
    fork_own, width = parts[0].shape
    size = len(parts) * fork_own * width
    return pl.pallas_call(
        functools.partial(merge_kernel, heads, kv_heads, len(parts)),
        out_shape=pltpu.VMEM((fork_own, heads * HEAD_WIDTH), BF16),
        in_specs=[VMEM_SPEC] * (len(parts) + 2) + [ANY_SPEC],
        out_specs=VMEM_SPEC,
        compiler_params=params(4 * size + 4 * MIB),
        cost_estimate=pl.CostEstimate(flops=4 * size, bytes_accessed=2 * size, transcendentals=0),
        name="merge",
    )(*parts, queries, new, after)


def output_kernel(context_ref, *refs):
    weight_refs, out_ref = refs[:-1], refs[-1]
    total = None
    for i, ref in enumerate(weight_refs):
        depth = ref.shape[0]
        part = jnp.dot(
            context_ref[:, i * depth : (i + 1) * depth], ref[...], preferred_element_type=F32
        )
        total = part if total is None else total + part
    out_ref[...] = total


def output_project(context, weights):
    forks, rows = context.shape
    columns = weights[0].shape[1]
    return pl.pallas_call(
        output_kernel,
        out_shape=pltpu.VMEM((forks, columns), F32),
        in_specs=[VMEM_SPEC] * (1 + len(weights)),
        out_specs=VMEM_SPEC,
        compiler_params=params(4 * MIB),
        cost_estimate=cost(2 * forks * rows * columns, 2 * rows * columns),
        name="output_project",
    )(context, *[in_vmem(x) for x in weights])


def finish_kernel(count, line, index_ref, *refs):
    near_refs, far_refs, out_ref = refs[:count], refs[count : 2 * count], refs[-1]
    place, parity = index_ref[0] // 2, index_ref[0] % 2
    rows = out_ref.shape[1]
    for group, side in ((near_refs, parity), (far_refs, 1 - parity)):
        for i in range(line):
            total = functools.reduce(jnp.add, [ref[i * rows : (i + 1) * rows] for ref in group])
            out_ref[2 * (place ^ i) + side] = total.astype(BF16)


def finish(index, near, far, mem_count):
    rows, columns = near[0].shape
    line = mem_count // 2
    return pl.pallas_call(
        functools.partial(finish_kernel, len(near), line),
        out_shape=jax.ShapeDtypeStruct((mem_count, rows // line, columns), BF16),
        in_specs=[SMEM_SPEC] + [VMEM_SPEC] * (2 * len(near)),
        out_specs=VMEM_SPEC,
        compiler_params=params(4 * MIB),
        cost_estimate=cost(0, 8 * rows * columns * len(near)),
        name="finish",
    )(index, *near, *far)


def shards(
    hidden,
    adapter,
    page_cache_slot,
    selection,
    query_projection_weight,
    key_projection_weight,
    value_projection_weight,
    adapter_down_weight,
    adapter_up_weight,
    output_projection_weight,
    prefix_key_cache,
    prefix_value_cache,
):
    mem_count = lax.axis_size("mem")
    mem_index = lax.axis_index("mem")
    forks = hidden.shape[0]
    fork_own = forks // mem_count
    q_width = query_projection_weight.shape[1]
    kv_width = key_projection_weight.shape[1]
    heads, kv_heads = q_width // HEAD_WIDTH, kv_width // HEAD_WIDTH
    pages = prefix_key_cache.shape[0]
    line = mem_count // 2
    index = mem_index.reshape(1)
    place, parity = mem_index // 2, mem_index % 2

    def swapped(x, step, cross=0):
        pairs = [(i, i ^ (2 * step + cross)) for i in range(mem_count)]
        return lax.ppermute(x, "mem", pairs)

    def along(blocks, cross=0):
        return [swapped(blocks[i], i, cross) if i or cross else blocks[0] for i in range(line)]

    def gather(x):
        return jnp.concatenate([x] + [swapped(x, i) for i in range(1, line)], axis=0)

    def pair(x, pieces=1):
        step = x.shape[0] // pieces
        got = [swapped(x[i * step : (i + 1) * step], 0, 1) for i in range(pieces)]
        return jnp.concatenate(got, axis=0)

    near_1, far_1, hidden, adapter = project_first(
        index, adapter, hidden, adapter_down_weight, key_projection_weight, value_projection_weight, mem_count
    )
    cut = q_width * 11 // 16 // 256 * 256
    (part_a,) = project(hidden, query_projection_weight, 0, cut)
    first_parts = fold(near_1, pair(far_1))
    first_parts, part_a, hidden = lax.optimization_barrier((first_parts, part_a, hidden))
    part_b, up = project(
        hidden, query_projection_weight, cut, q_width - cut, adapter_up_weight.reshape(-1, q_width)
    )
    first_parts = along(first_parts)

    near_a, far_a = add_delta(index, adapter, first_parts, part_a, up, mem_count, 0)
    near_a, far_a, part_b = lax.optimization_barrier((near_a, far_a, part_b))
    both_b, own_new = add_delta(
        index, adapter, first_parts, part_b, up, mem_count, cut, 2 * kv_width
    )
    sums_a = fold(near_a, pair(far_a, 2))
    own_b, other_b = line_sum(along(both_b), sums_a[0])
    own_a = functools.reduce(jnp.add, along(sums_a))
    own_b = own_b + pair(other_b)
    own_queries = jnp.concatenate([own_a.astype(BF16), own_b.astype(BF16)], axis=1)

    *staged, near_mask, far_mask = stage_cache(
        index, page_cache_slot, selection, prefix_key_cache, prefix_value_cache, mem_count
    )
    keys, values = staged[: len(staged) // 2], staged[len(staged) // 2 :]
    near_queries, near_mask = lax.optimization_barrier((gather(own_queries), near_mask))
    far_queries = pair(near_queries, 2)
    near = attend(near_queries, keys, values, near_mask)
    far = attend(far_queries, keys, values, far_mask)
    blocks = (line, fork_own, q_width + HEAD_WIDTH)
    far, out_weight = lax.optimization_barrier((far, output_projection_weight))
    parts = along(near.reshape(blocks)) + along(far.reshape(blocks), 1)
    out_weights = stage(out_weight)
    context_own = merge(parts, own_queries, own_new, out_weights[0], heads, kv_heads)

    near_context = gather(context_own)
    far_context = pair(near_context, 2)
    tp_count = lax.axis_size("tp")
    outs = []
    for context in (near_context, far_context):
        part = output_project(context, out_weights)
        terms = [part]
        for shift in range(1, tp_count):
            pairs = [(i, (i + shift) % tp_count) for i in range(tp_count)]
            terms.append(lax.ppermute(part, "tp", pairs))
        outs.append(terms)
    return finish(index, *outs, mem_count).reshape(forks, -1)


def solution(mesh):
    return jax.shard_map(
        shards,
        mesh=mesh,
        in_specs=(
            P("groups", "mem"),
            P("groups"),
            P("groups"),
            P("groups", None),
            P("mem", "tp"),
            P("mem", "tp"),
            P("mem", "tp"),
            P("mem", None),
            P("mem", None, "tp"),
            P("tp", "mem"),
            P(("groups", "mem"), None, "tp"),
            P(("groups", "mem"), None, "tp"),
        ),
        out_specs=P("groups", "mem"),
        check_vma=False,
    )
```

```python
import functools

import jax
import jax.numpy as jnp
from jax import lax
from jax.experimental import pallas as pl
from jax.experimental.pallas import tpu as pltpu
from jax.sharding import PartitionSpec as P

HEAD_WIDTH = 128
ADAPTER_RANK = 64
ADAPTER_COUNT = 32
LOG2E = 1.4426950408889634
SCORE_SCALE = HEAD_WIDTH ** (-0.5)
neg_floor = -1e30
MIB = 1024 * 1024
F32 = jnp.float32
BF16 = jnp.bfloat16


def params(limit, *semantics):
    return pltpu.CompilerParams(
        dimension_semantics=semantics or None, vmem_limit_bytes=int(limit)
    )


def whole(shape):
    return pl.BlockSpec(shape, lambda *_: (0,) * len(shape))


def in_hbm(x):
    return pltpu.with_memory_space_constraint(x, pltpu.HBM)


def in_vmem(x):
    return pltpu.with_memory_space_constraint(x, pltpu.VMEM)


def cost(flops, size, transcendentals=0):
    return pl.CostEstimate(
        flops=int(flops), bytes_accessed=int(size), transcendentals=int(transcendentals)
    )


VMEM_SPEC = pl.BlockSpec(memory_space=pltpu.VMEM)
SMEM_SPEC = pl.BlockSpec(memory_space=pltpu.SMEM)
ANY_SPEC = pl.BlockSpec(memory_space=pl.ANY)


def stage_kernel(pieces, *refs):
    count = len(refs[:-1]) // (pieces + 1)
    sources, targets, sems = refs[:count], refs[count:-1], refs[-1]
    copies = []
    for i, target in enumerate(targets):
        rows = pl.ds((i % pieces) * target.shape[0], target.shape[0])
        copies.append(
            pltpu.make_async_copy(sources[i // pieces].at[rows], target, sems.at[i])
        )
    for copy in copies:
        copy.start()
    for copy in copies:
        copy.wait()


def stage(*arrays, pieces=4):
    shapes = [(x.shape[0] // pieces,) + x.shape[1:] for x in arrays for _ in range(pieces)]
    return pl.pallas_call(
        functools.partial(stage_kernel, pieces),
        out_shape=tuple(pltpu.VMEM(shape, BF16) for shape in shapes),
        in_specs=[ANY_SPEC] * len(arrays),
        out_specs=(ANY_SPEC,) * len(shapes),
        scratch_shapes=[pltpu.SemaphoreType.DMA((len(shapes),))],
        compiler_params=params(MIB),
        cost_estimate=cost(0, sum(2 * x.size for x in arrays)),
        name="stage",
    )(*[in_hbm(x) for x in arrays])


def cache_kernel(pieces, index_ref, slot_hbm, select_hbm, *refs):
    sources, targets = refs[:2], refs[2 : 2 + 2 * pieces]
    near_ref, far_ref, slot_ref, select_ref, blocks_ref, sems = refs[2 + 2 * pieces :]
    count = 2 * pieces
    first = [
        pltpu.make_async_copy(slot_hbm, slot_ref, sems.at[count]),
        pltpu.make_async_copy(select_hbm, select_ref, sems.at[count + 1]),
    ]
    copies = []
    for i, target in enumerate(targets):
        rows = pl.ds((i % pieces) * target.shape[0], target.shape[0])
        copies.append(
            pltpu.make_async_copy(sources[i // pieces].at[rows], target, sems.at[i])
        )
    for copy in first + copies:
        copy.start()
    for copy in first:
        copy.wait()
    pages, total = blocks_ref.shape[2], slot_ref.shape[1]
    slots = index_ref[0] * pages + lax.broadcasted_iota(jnp.int32, (pages, total), 0)
    match = (slots == slot_ref[...]).astype(BF16)
    chosen = (select_ref[...] > 0).astype(BF16)
    held = lax.dot_general(
        chosen, match, (((1,), (1,)), ((), ())), preferred_element_type=F32
    )
    put_blocks(index_ref[0], held, blocks_ref, near_ref, far_ref)
    for copy in copies:
        copy.wait()


def stage_cache(index, page_cache_slot, selection, keys, values, mem_count, pieces=2):
    forks, total = selection.shape
    pages = keys.shape[0]
    line, fork_own = mem_count // 2, forks // mem_count
    shapes = [(x.shape[0] // pieces,) + x.shape[1:] for x in (keys, values) for _ in range(pieces)]
    mask = pltpu.VMEM((line, fork_own, pages), F32)
    return pl.pallas_call(
        functools.partial(cache_kernel, pieces),
        out_shape=tuple(pltpu.VMEM(shape, BF16) for shape in shapes) + (mask, mask),
        in_specs=[SMEM_SPEC] + [ANY_SPEC] * 4,
        out_specs=(ANY_SPEC,) * len(shapes) + (VMEM_SPEC,) * 2,
        scratch_shapes=[
            pltpu.VMEM((1, total), jnp.int32),
            pltpu.VMEM((forks, total), jnp.int32),
            pltpu.VMEM((mem_count, fork_own, pages), F32),
            pltpu.SemaphoreType.DMA((2 * pieces + 2,)),
        ],
        compiler_params=params(4 * MIB),
        cost_estimate=cost(0, 4 * keys.size),
        name="stage_cache",
    )(index, *[in_hbm(x) for x in (page_cache_slot.reshape(1, total), selection, keys, values)])


def fold_kernel(one_ref, two_ref, *out_refs):
    for i, out_ref in enumerate(out_refs):
        out_ref[...] = one_ref[i] + two_ref[i]


def fold(one, two):
    out = pltpu.VMEM(one.shape[1:], F32)
    return pl.pallas_call(
        fold_kernel,
        out_shape=(out,) * one.shape[0],
        in_specs=[VMEM_SPEC] * 2,
        out_specs=(VMEM_SPEC,) * one.shape[0],
        compiler_params=params(MIB * 2 + 16 * one.size),
        cost_estimate=cost(one.size, 12 * one.size),
        name="fold",
    )(in_vmem(one), two)


def take_blocks(index, blocks_ref, near_ref, far_ref):
    place, parity = index // 2, index % 2
    for i in range(near_ref.shape[0]):
        at = 2 * (place ^ i)
        near_ref[i] = blocks_ref[at + parity]
        far_ref[i] = blocks_ref[at + 1 - parity]


def put_blocks(index, value, blocks_ref, near_ref, far_ref):
    count, rows, lanes = blocks_ref.shape
    own = value.shape[0] // count
    for i in range(count):
        blocks_ref[i, :own] = value[i * own : (i + 1) * own]
        if own < rows:
            blocks_ref[i, own:] = jnp.zeros((rows - own, lanes), F32)
    take_blocks(index, blocks_ref, near_ref, far_ref)


def first_kernel(
    index_ref,
    adapter_hbm,
    hidden_hbm,
    down_hbm,
    k_hbm,
    v_hbm,
    near_ref,
    far_ref,
    hidden_ref,
    adapter_ref,
    held,
    held_kv,
    rank_blocks,
    kv_blocks,
    sems,
):
    pieces, _, width = held.shape
    forks = hidden_ref.shape[0]
    kv_width = held_kv.shape[2]
    lanes = rank_blocks.shape[2]
    copies = [
        pltpu.make_async_copy(adapter_hbm, adapter_ref, sems.at[pieces + 3]),
        pltpu.make_async_copy(hidden_hbm, hidden_ref, sems.at[pieces + 2]),
        *[
            pltpu.make_async_copy(
                down_hbm.at[:, i * width : (i + 1) * width], held.at[i], sems.at[i]
            )
            for i in range(pieces)
        ],
        pltpu.make_async_copy(k_hbm, held_kv.at[0], sems.at[pieces]),
        pltpu.make_async_copy(v_hbm, held_kv.at[1], sems.at[pieces + 1]),
    ]
    for copy in copies:
        copy.start()
    copies[0].wait()
    fork_adapter = jnp.broadcast_to(adapter_ref[...].astype(F32), (HEAD_WIDTH, forks)).T
    lane_adapter = lax.broadcasted_iota(jnp.int32, (forks, HEAD_WIDTH), 1) // ADAPTER_RANK
    wanted = fork_adapter.astype(jnp.int32) - lane_adapter
    total = jnp.zeros((forks, HEAD_WIDTH), F32)
    copies[1].wait()
    for i in range(pieces):
        copies[2 + i].wait()
        block = jnp.dot(hidden_ref[...], held[i], preferred_element_type=F32)
        for j in range(width // HEAD_WIDTH):
            first = (i * width + j * HEAD_WIDTH) // ADAPTER_RANK
            part = block[:, j * HEAD_WIDTH : (j + 1) * HEAD_WIDTH]
            total += jnp.where(wanted == first, part, 0.0)
    flipped = total.T
    flipped = flipped[:ADAPTER_RANK] + flipped[ADAPTER_RANK:]
    if lanes > forks:
        flipped = jnp.concatenate([flipped, jnp.zeros((ADAPTER_RANK, lanes - forks), F32)], axis=1)
    at = slice(0, lanes)
    put_blocks(index_ref[0], flipped, rank_blocks, near_ref.at[:, :, at], far_ref.at[:, :, at])
    for i in range(2):
        copies[2 + pieces + i].wait()
        part = jnp.dot(hidden_ref[...], held_kv[i], preferred_element_type=F32)
        at = slice(lanes + i * kv_width, lanes + (i + 1) * kv_width)
        put_blocks(index_ref[0], part, kv_blocks, near_ref.at[:, :, at], far_ref.at[:, :, at])


def project_first(index, adapter, hidden, down, k_weight, v_weight, mem_count, width=256):
    forks, depth = hidden.shape
    columns, kv_width = down.shape[1], k_weight.shape[1]
    lanes = -(-forks // HEAD_WIDTH) * HEAD_WIDTH
    line, fork_own = mem_count // 2, forks // mem_count
    pieces = columns // width
    out = pltpu.VMEM((line, fork_own, lanes + 2 * kv_width), F32)
    weights = 2 * depth * (columns + 2 * kv_width)
    return pl.pallas_call(
        first_kernel,
        out_shape=(out, out, pltpu.VMEM(hidden.shape, BF16), pltpu.VMEM((1, forks), jnp.int32)),
        in_specs=[SMEM_SPEC] + [ANY_SPEC] * 5,
        out_specs=(VMEM_SPEC,) * 4,
        scratch_shapes=[
            pltpu.VMEM((pieces, depth, width), BF16),
            pltpu.VMEM((2, depth, kv_width), BF16),
            pltpu.VMEM((mem_count, fork_own, lanes), F32),
            pltpu.VMEM((mem_count, fork_own, kv_width), F32),
            pltpu.SemaphoreType.DMA((pieces + 4,)),
        ],
        compiler_params=params(weights + 4 * MIB),
        cost_estimate=cost(forks * weights, weights),
        name="project_first",
    )(index, *[in_hbm(x) for x in (adapter.reshape(1, forks), hidden, down, k_weight, v_weight)])


def project_kernel(start, extra, hidden_ref, q_hbm, *refs):
    up_hbm, part_ref, up_ref, held, sems = refs if extra else (None, refs[0], None, *refs[1:])
    pieces, _, width = held.shape
    copies = []
    for i in range(pieces):
        columns = pl.ds(start + i * width, width)
        copies.append(pltpu.make_async_copy(q_hbm.at[:, columns], held.at[i], sems.at[i]))
    if extra:
        copies.append(pltpu.make_async_copy(up_hbm, up_ref, sems.at[pieces]))
    for copy in copies:
        copy.start()
    for i in range(pieces):
        copies[i].wait()
        part_ref[:, i * width : (i + 1) * width] = jnp.dot(
            hidden_ref[...], held[i], preferred_element_type=F32
        )
    if extra:
        copies[-1].wait()


def project(hidden, q_weight, start, columns, up=None, width=256):
    forks, depth = hidden.shape
    pieces = columns // width
    weights = 2 * depth * columns
    extra = [] if up is None else [up]
    return pl.pallas_call(
        functools.partial(project_kernel, start, bool(extra)),
        out_shape=tuple(
            [pltpu.VMEM((forks, columns), F32)] + [pltpu.VMEM(x.shape, BF16) for x in extra]
        ),
        in_specs=[VMEM_SPEC] + [ANY_SPEC] * (1 + len(extra)),
        out_specs=(VMEM_SPEC,) * (1 + len(extra)),
        scratch_shapes=[
            pltpu.VMEM((pieces, depth, width), BF16),
            pltpu.SemaphoreType.DMA((pieces + 1,)),
        ],
        compiler_params=params(weights + 2 * MIB),
        cost_estimate=cost(forks * weights, weights + sum(2 * x.size for x in extra)),
        name="project",
    )(in_vmem(hidden), *[in_hbm(x) for x in [q_weight] + extra])


def line_sum_kernel(after_ref, *refs):
    parts, (own_ref, other_ref) = refs[:-2], refs[-2:]
    own_ref[...] = functools.reduce(jnp.add, [ref[0] for ref in parts])
    other_ref[...] = functools.reduce(jnp.add, [ref[1] for ref in parts])


def line_sum(parts, after):
    out = pltpu.VMEM(parts[0].shape[1:], F32)
    size = len(parts) * parts[0].size
    return pl.pallas_call(
        line_sum_kernel,
        out_shape=(out, out),
        in_specs=[ANY_SPEC] + [VMEM_SPEC] * len(parts),
        out_specs=(VMEM_SPEC,) * 2,
        compiler_params=params(2 * MIB + 8 * size),
        cost_estimate=cost(size, 4 * size),
        name="line_sum",
    )(after, *parts)


def join_kernel(first_ref, one_ref, two_ref, out_ref):
    cut = first_ref.shape[1]
    out_ref[:, :cut] = first_ref[...]
    out_ref[:, cut:] = (one_ref[...] + two_ref[...]).astype(BF16)


def join(first, one, two):
    rows, columns = first.shape[0], first.shape[1] + one.shape[1]
    return pl.pallas_call(
        join_kernel,
        out_shape=pltpu.VMEM((rows, columns), BF16),
        in_specs=[VMEM_SPEC] * 3,
        out_specs=VMEM_SPEC,
        compiler_params=params(MIB + 16 * rows * columns),
        cost_estimate=cost(one.size, 4 * rows * columns),
        name="join",
    )(first, in_vmem(one), two)


def delta_kernel(line, ranks, start, joint, index_ref, adapter_ref, *refs):
    first_refs = refs[:line]
    part_ref, up_ref, *out_refs, blocks_ref = refs[line:]
    forks, width = part_ref.shape[0], blocks_ref.shape[2]
    if joint:
        near_ref, far_ref = out_refs[0].at[:, 0], out_refs[0].at[:, 1]
        new_ref = out_refs[1]
        lanes = first_refs[0].shape[1] - new_ref.shape[1]
        total = functools.reduce(jnp.add, [ref[:, lanes:] for ref in first_refs])
        new_ref[...] = total.astype(BF16)
    else:
        near_ref, far_ref = out_refs
    acts = functools.reduce(jnp.add, [ref[:ranks, :forks] for ref in first_refs])
    acts = acts.astype(BF16).astype(F32)
    adapters = lax.broadcasted_iota(jnp.int32, (ADAPTER_COUNT, forks), 0)
    onehot = (adapters == adapter_ref[...]).astype(F32)
    spread = jnp.concatenate(
        [acts[r : r + 1, :] * onehot for r in range(ranks)], axis=0
    ).astype(BF16)
    for i in range(part_ref.shape[1] // width):
        delta = lax.dot_general(
            spread,
            up_ref[:, start + i * width : start + (i + 1) * width],
            (((0,), (0,)), ((), ())),
            preferred_element_type=F32,
        )
        at = slice(i * width, (i + 1) * width)
        put_blocks(
            index_ref[0],
            part_ref[:, at] + delta,
            blocks_ref,
            near_ref.at[:, :, at],
            far_ref.at[:, :, at],
        )


def add_delta(index, adapter, first_parts, part, up, mem_count, start, new_width=0, width=256):
    forks, columns = part.shape
    line, fork_own = mem_count // 2, forks // mem_count
    ranks = ADAPTER_RANK // mem_count
    if new_width:
        out = (
            pltpu.VMEM((line, 2, fork_own, columns), F32),
            pltpu.VMEM((fork_own, new_width), BF16),
        )
    else:
        out = (pltpu.VMEM((line, fork_own, columns), F32),) * 2
    return pl.pallas_call(
        functools.partial(delta_kernel, line, ranks, start, new_width > 0),
        out_shape=out,
        in_specs=[SMEM_SPEC] + [VMEM_SPEC] * (line + 3),
        out_specs=(VMEM_SPEC,) * 2,
        scratch_shapes=[pltpu.VMEM((mem_count, fork_own, width), F32)],
        compiler_params=params(4 * MIB),
        cost_estimate=cost(
            2 * forks * up.shape[0] * columns, 2 * up.shape[0] * columns + 8 * forks * columns
        ),
        name="add_delta",
    )(index, in_vmem(adapter), *first_parts, in_vmem(part), in_vmem(up))


def put_terms(lse):
    heads, forks = lse.shape
    high = lse.astype(BF16).astype(F32)
    rest = lse - high
    middle = rest.astype(BF16).astype(F32)
    low = rest - middle
    spare = jnp.zeros((HEAD_WIDTH - 3 * heads, forks), F32)
    return jnp.concatenate([high, middle, low, spare], axis=0).T.astype(BF16)


def get_terms(terms, heads):
    terms = terms.astype(F32)
    return terms[:, :heads] + terms[:, heads : 2 * heads] + terms[:, 2 * heads : 3 * heads]


def attend_kernel(pieces, q_ref, mask_ref, *refs):
    k_refs, v_refs, (out_ref, score_ref, lse_ref) = (
        refs[:pieces],
        refs[pieces : 2 * pieces],
        refs[2 * pieces :],
    )
    forks = q_ref.shape[0]
    kv_local, group = lse_ref.shape[:2]
    pages = score_ref.shape[0] // 2
    held = pages // pieces
    scale = SCORE_SCALE * LOG2E
    chosen_by = mask_ref[...].reshape(forks, pages)
    spare = jnp.zeros((forks, HEAD_WIDTH - pages % HEAD_WIDTH), F32)
    chosen_by = jnp.concatenate([chosen_by, spare], axis=1).T[:pages]
    mask = jnp.concatenate([chosen_by] * group, axis=1) > 0
    ones = jnp.ones((8, score_ref.shape[1]), BF16)

    def score(kv_head, queries, p):
        lanes = slice(kv_head * HEAD_WIDTH, (kv_head + 1) * HEAD_WIDTH)
        scores = lax.dot_general(
            k_refs[p // held][p % held, :, lanes],
            queries,
            (((1,), (1,)), ((), ())),
            preferred_element_type=F32,
        )
        score_ref[kv_head % 2 * pages + p] = scores
        return jnp.max(scores, axis=0, keepdims=True)

    def term(kv_head, peaks, top, p):
        lanes = slice(kv_head * HEAD_WIDTH, (kv_head + 1) * HEAD_WIDTH)
        scores = score_ref[kv_head % 2 * pages + p]
        weights = jnp.exp2((scores - peaks[p]) * scale).astype(BF16)
        chosen = jnp.where(mask[p : p + 1], peaks[p], neg_floor)
        factor = jnp.where(mask[p : p + 1], jnp.exp2((chosen - top) * scale), 0.0)
        values = jnp.concatenate([v_refs[p // held][p % held, :, lanes].T, ones], axis=0)
        return jnp.dot(values, weights, preferred_element_type=F32) * factor

    def head_queries(kv_head):
        first = kv_head * group
        return jnp.concatenate(
            [
                q_ref[:, (first + g) * HEAD_WIDTH : (first + g + 1) * HEAD_WIDTH]
                for g in range(group)
            ],
            axis=0,
        )

    queries = head_queries(0)
    peaks = [score(0, queries, p) for p in range(pages)]
    for kv_head in range(kv_local):
        chosen = [jnp.where(mask[p : p + 1], peaks[p], neg_floor) for p in range(pages)]
        top = functools.reduce(jnp.maximum, chosen)
        if kv_head + 1 < kv_local:
            queries = head_queries(kv_head + 1)
        acc = None
        next_peaks = []
        for p in range(pages):
            if kv_head + 1 < kv_local:
                next_peaks.append(score(kv_head + 1, queries, p))
            part = term(kv_head, peaks, top, p)
            acc = part if acc is None else acc + part
        peaks = next_peaks
        mass = acc[HEAD_WIDTH : HEAD_WIDTH + 1]
        some = mass > 0
        safe = jnp.where(some, mass, 1.0)
        rows = (acc[:HEAD_WIDTH] * jnp.where(some, 1.0 / safe, 0.0)).T
        lse = jnp.where(some, top * scale + jnp.log2(safe), neg_floor)
        for g in range(group):
            at = (kv_head * group + g) * HEAD_WIDTH
            out_ref[:, at : at + HEAD_WIDTH] = rows[g * forks : (g + 1) * forks].astype(BF16)
        lse_ref[kv_head] = jnp.concatenate(
            [lse[:, g * forks : (g + 1) * forks] for g in range(group)], axis=0
        )

    heads = kv_local * group
    out_ref[:, heads * HEAD_WIDTH :] = put_terms(lse_ref[...].reshape(heads, forks))


def attend(queries, keys, values, mask):
    forks, width = queries.shape
    held, page_len, kv_width = keys[0].shape
    pieces = len(keys)
    pages = held * pieces
    kv_local = kv_width // HEAD_WIDTH
    group = width // kv_width
    rows = group * forks
    return pl.pallas_call(
        functools.partial(attend_kernel, pieces),
        out_shape=pltpu.VMEM((forks, width + HEAD_WIDTH), BF16),
        in_specs=[VMEM_SPEC] * (2 + 2 * pieces),
        out_specs=VMEM_SPEC,
        scratch_shapes=[
            pltpu.VMEM((2 * pages, page_len, rows), F32),
            pltpu.VMEM((kv_local, group, forks), F32),
        ],
        compiler_params=params(10 * pages * page_len * rows + 4 * MIB),
        cost_estimate=cost(
            4 * pages * page_len * kv_local * rows * HEAD_WIDTH,
            4 * pages * page_len * kv_width + 4 * forks * width,
            pages * page_len * kv_local * rows,
        ),
        name="attend",
    )(queries, *[in_vmem(x) for x in [mask, *keys, *values]])


def merge_kernel(heads, kv_heads, sources, *refs):
    parts, (q_ref, new_ref, out_ref) = refs[:sources], refs[sources:]
    group = heads // kv_heads
    width = heads * HEAD_WIDTH
    lses = [get_terms(ref[:, width : width + HEAD_WIDTH], heads) for ref in parts]

    def new_head(i):
        return new_ref[:, i * HEAD_WIDTH : (i + 1) * HEAD_WIDTH].astype(F32)

    scores = []
    for h in range(heads):
        query = q_ref[:, h * HEAD_WIDTH : (h + 1) * HEAD_WIDTH].astype(F32)
        scores.append(jnp.sum(query * new_head(h // group), axis=1, keepdims=True))
    own = jnp.concatenate(scores, axis=1) * (SCORE_SCALE * LOG2E)
    top = functools.reduce(jnp.maximum, lses, own)
    own_weight = jnp.exp2(own - top)
    weights = [jnp.exp2(lse - top) for lse in lses]
    inverse = 1.0 / functools.reduce(jnp.add, weights, own_weight)
    own_weight = own_weight * inverse
    weights = [weight * inverse for weight in weights]
    for h in range(heads):
        lanes = slice(h * HEAD_WIDTH, (h + 1) * HEAD_WIDTH)
        total = own_weight[:, h : h + 1] * new_head(kv_heads + h // group)
        for weight, ref in zip(weights, parts):
            total += weight[:, h : h + 1] * ref[:, lanes].astype(F32)
        out_ref[:, lanes] = total.astype(BF16)


def merge(parts, queries, new, heads, kv_heads):
    fork_own, width = parts[0].shape
    size = len(parts) * fork_own * width
    return pl.pallas_call(
        functools.partial(merge_kernel, heads, kv_heads, len(parts)),
        out_shape=jax.ShapeDtypeStruct((fork_own, heads * HEAD_WIDTH), BF16),
        compiler_params=params(4 * size + 4 * MIB),
        cost_estimate=pl.CostEstimate(flops=4 * size, bytes_accessed=2 * size, transcendentals=0),
        name="merge",
    )(*parts, queries, new)


def output_kernel(context_ref, *refs):
    weight_refs, out_ref = refs[:-1], refs[-1]
    total = None
    for i, ref in enumerate(weight_refs):
        depth = ref.shape[0]
        part = jnp.dot(
            context_ref[:, i * depth : (i + 1) * depth], ref[...], preferred_element_type=F32
        )
        total = part if total is None else total + part
    out_ref[...] = total


def output_project(context, weights):
    forks, rows = context.shape
    columns = weights[0].shape[1]
    return pl.pallas_call(
        output_kernel,
        out_shape=pltpu.VMEM((forks, columns), F32),
        in_specs=[VMEM_SPEC] * (1 + len(weights)),
        out_specs=VMEM_SPEC,
        compiler_params=params(4 * MIB),
        cost_estimate=cost(2 * forks * rows * columns, 2 * rows * columns),
        name="output_project",
    )(context, *[in_vmem(x) for x in weights])


def finish_kernel(count, line, index_ref, *refs):
    near_refs, far_refs, out_ref = refs[:count], refs[count : 2 * count], refs[-1]
    place, parity = index_ref[0] // 2, index_ref[0] % 2
    rows = out_ref.shape[1]
    for group, side in ((near_refs, parity), (far_refs, 1 - parity)):
        for i in range(line):
            total = functools.reduce(jnp.add, [ref[i * rows : (i + 1) * rows] for ref in group])
            out_ref[2 * (place ^ i) + side] = total.astype(BF16)


def finish(index, near, far, mem_count):
    rows, columns = near[0].shape
    line = mem_count // 2
    return pl.pallas_call(
        functools.partial(finish_kernel, len(near), line),
        out_shape=jax.ShapeDtypeStruct((mem_count, rows // line, columns), BF16),
        in_specs=[SMEM_SPEC] + [VMEM_SPEC] * (2 * len(near)),
        out_specs=VMEM_SPEC,
        compiler_params=params(4 * MIB),
        cost_estimate=cost(0, 8 * rows * columns * len(near)),
        name="finish",
    )(index, *near, *far)


def shards(
    hidden,
    adapter,
    page_cache_slot,
    selection,
    query_projection_weight,
    key_projection_weight,
    value_projection_weight,
    adapter_down_weight,
    adapter_up_weight,
    output_projection_weight,
    prefix_key_cache,
    prefix_value_cache,
):
    mem_count = lax.axis_size("mem")
    mem_index = lax.axis_index("mem")
    forks = hidden.shape[0]
    fork_own = forks // mem_count
    q_width = query_projection_weight.shape[1]
    kv_width = key_projection_weight.shape[1]
    heads, kv_heads = q_width // HEAD_WIDTH, kv_width // HEAD_WIDTH
    pages = prefix_key_cache.shape[0]
    line = mem_count // 2
    index = mem_index.reshape(1)
    place, parity = mem_index // 2, mem_index % 2

    def swapped(x, step, cross=0):
        pairs = [(i, i ^ (2 * step + cross)) for i in range(mem_count)]
        return lax.ppermute(x, "mem", pairs)

    def along(blocks, cross=0):
        return [swapped(blocks[i], i, cross) if i or cross else blocks[0] for i in range(line)]

    def gather(x):
        return jnp.concatenate([x] + [swapped(x, i) for i in range(1, line)], axis=0)

    def pair(x):
        return swapped(x, 0, 1)

    near_1, far_1, hidden, adapter = project_first(
        index, adapter, hidden, adapter_down_weight, key_projection_weight, value_projection_weight, mem_count
    )
    cut = q_width * 10 // 16 // 256 * 256
    (part_a,) = project(hidden, query_projection_weight, 0, cut)
    first_parts = fold(near_1, pair(far_1))
    first_parts, part_a, hidden = lax.optimization_barrier((first_parts, part_a, hidden))
    part_b, up = project(
        hidden, query_projection_weight, cut, q_width - cut, adapter_up_weight.reshape(-1, q_width)
    )
    first_parts = along(first_parts)

    near_a, far_a = add_delta(index, adapter, first_parts, part_a, up, mem_count, 0)
    near_a, far_a, part_b = lax.optimization_barrier((near_a, far_a, part_b))
    both_b, own_new = add_delta(
        index, adapter, first_parts, part_b, up, mem_count, cut, 2 * kv_width
    )
    sums_a = fold(near_a, pair(far_a))
    own_b, other_b = line_sum(along(both_b), sums_a[0])
    own_a = functools.reduce(jnp.add, along(sums_a)[::-1]).astype(BF16)
    own_queries = join(own_a, own_b, pair(other_b))

    *staged, near_mask, far_mask = stage_cache(
        index, page_cache_slot, selection, prefix_key_cache, prefix_value_cache, mem_count
    )
    keys, values = staged[: len(staged) // 2], staged[len(staged) // 2 :]
    near_queries = gather(own_queries)
    far_queries = pair(near_queries)
    near = attend(near_queries, keys, values, near_mask)
    far = attend(far_queries, keys, values, far_mask)
    blocks = (line, fork_own, q_width + HEAD_WIDTH)
    parts = along(near.reshape(blocks)) + along(far.reshape(blocks), 1)
    context_own = merge(parts, own_queries, own_new, heads, kv_heads)

    out_weights = stage(output_projection_weight)
    near_context = gather(context_own)
    far_context = pair(near_context)
    tp_count = lax.axis_size("tp")
    outs = []
    for context in (near_context, far_context):
        part = output_project(context, out_weights)
        terms = [part]
        for shift in range(1, tp_count):
            pairs = [(i, (i + shift) % tp_count) for i in range(tp_count)]
            terms.append(lax.ppermute(part, "tp", pairs))
        outs.append(terms)
    return finish(index, *outs, mem_count).reshape(forks, -1)


def solution(mesh):
    return jax.shard_map(
        shards,
        mesh=mesh,
        in_specs=(
            P("groups", "mem"),
            P("groups"),
            P("groups"),
            P("groups", None),
            P("mem", "tp"),
            P("mem", "tp"),
            P("mem", "tp"),
            P("mem", None),
            P("mem", None, "tp"),
            P("tp", "mem"),
            P(("groups", "mem"), None, "tp"),
            P(("groups", "mem"), None, "tp"),
        ),
        out_specs=P("groups", "mem"),
        check_vma=False,
    )
```

```python
import functools

import jax
import jax.numpy as jnp
from jax import lax
from jax.experimental import pallas as pl
from jax.experimental.pallas import tpu as pltpu
from jax.sharding import PartitionSpec as P

HEAD_WIDTH = 128
ADAPTER_RANK = 64
ADAPTER_COUNT = 32
LOG2E = 1.4426950408889634
SCORE_SCALE = HEAD_WIDTH ** (-0.5)
neg_floor = -1e30
MIB = 1024 * 1024
F32 = jnp.float32
BF16 = jnp.bfloat16


def params(limit, *semantics):
    return pltpu.CompilerParams(
        dimension_semantics=semantics or None, vmem_limit_bytes=int(limit)
    )


def whole(shape):
    return pl.BlockSpec(shape, lambda *_: (0,) * len(shape))


def in_hbm(x):
    return pltpu.with_memory_space_constraint(x, pltpu.HBM)


def in_vmem(x):
    return pltpu.with_memory_space_constraint(x, pltpu.VMEM)


def cost(flops, size, transcendentals=0):
    return pl.CostEstimate(
        flops=int(flops), bytes_accessed=int(size), transcendentals=int(transcendentals)
    )


VMEM_SPEC = pl.BlockSpec(memory_space=pltpu.VMEM)
SMEM_SPEC = pl.BlockSpec(memory_space=pltpu.SMEM)
ANY_SPEC = pl.BlockSpec(memory_space=pl.ANY)


def stage_kernel(pieces, *refs):
    count = len(refs[:-1]) // (pieces + 1)
    sources, targets, sems = refs[:count], refs[count:-1], refs[-1]
    copies = []
    for i, target in enumerate(targets):
        rows = pl.ds((i % pieces) * target.shape[0], target.shape[0])
        copies.append(
            pltpu.make_async_copy(sources[i // pieces].at[rows], target, sems.at[i])
        )
    for copy in copies:
        copy.start()
    for copy in copies:
        copy.wait()


def stage(*arrays, pieces=4):
    shapes = [(x.shape[0] // pieces,) + x.shape[1:] for x in arrays for _ in range(pieces)]
    return pl.pallas_call(
        functools.partial(stage_kernel, pieces),
        out_shape=tuple(pltpu.VMEM(shape, BF16) for shape in shapes),
        in_specs=[ANY_SPEC] * len(arrays),
        out_specs=(ANY_SPEC,) * len(shapes),
        scratch_shapes=[pltpu.SemaphoreType.DMA((len(shapes),))],
        compiler_params=params(MIB),
        cost_estimate=cost(0, sum(2 * x.size for x in arrays)),
        name="stage",
    )(*[in_hbm(x) for x in arrays])


def cache_kernel(pieces, index_ref, slot_hbm, select_hbm, *refs):
    sources, targets = refs[:2], refs[2 : 2 + 2 * pieces]
    near_ref, far_ref, slot_ref, select_ref, blocks_ref, sems = refs[2 + 2 * pieces :]
    count = 2 * pieces
    first = [
        pltpu.make_async_copy(slot_hbm, slot_ref, sems.at[count]),
        pltpu.make_async_copy(select_hbm, select_ref, sems.at[count + 1]),
    ]
    copies = []
    for i, target in enumerate(targets):
        rows = pl.ds((i % pieces) * target.shape[0], target.shape[0])
        copies.append(
            pltpu.make_async_copy(sources[i // pieces].at[rows], target, sems.at[i])
        )
    for copy in first + copies:
        copy.start()
    for copy in first:
        copy.wait()
    pages, total = blocks_ref.shape[2], slot_ref.shape[1]
    slots = index_ref[0] * pages + lax.broadcasted_iota(jnp.int32, (pages, total), 0)
    match = (slots == slot_ref[...]).astype(BF16)
    chosen = (select_ref[...] > 0).astype(BF16)
    held = lax.dot_general(
        chosen, match, (((1,), (1,)), ((), ())), preferred_element_type=F32
    )
    put_blocks(index_ref[0], held, blocks_ref, near_ref, far_ref)
    for copy in copies:
        copy.wait()


def stage_cache(index, page_cache_slot, selection, keys, values, mem_count, pieces=2):
    forks, total = selection.shape
    pages = keys.shape[0]
    line, fork_own = mem_count // 2, forks // mem_count
    shapes = [(x.shape[0] // pieces,) + x.shape[1:] for x in (keys, values) for _ in range(pieces)]
    mask = pltpu.VMEM((line, fork_own, pages), F32)
    return pl.pallas_call(
        functools.partial(cache_kernel, pieces),
        out_shape=tuple(pltpu.VMEM(shape, BF16) for shape in shapes) + (mask, mask),
        in_specs=[SMEM_SPEC] + [ANY_SPEC] * 4,
        out_specs=(ANY_SPEC,) * len(shapes) + (VMEM_SPEC,) * 2,
        scratch_shapes=[
            pltpu.VMEM((1, total), jnp.int32),
            pltpu.VMEM((forks, total), jnp.int32),
            pltpu.VMEM((mem_count, fork_own, pages), F32),
            pltpu.SemaphoreType.DMA((2 * pieces + 2,)),
        ],
        compiler_params=params(4 * MIB),
        cost_estimate=cost(0, 4 * keys.size),
        name="stage_cache",
    )(index, *[in_hbm(x) for x in (page_cache_slot.reshape(1, total), selection, keys, values)])


def fold_kernel(one_ref, two_ref, *out_refs):
    for i, out_ref in enumerate(out_refs):
        out_ref[...] = one_ref[i] + two_ref[i]


def fold(one, two):
    out = pltpu.VMEM(one.shape[1:], F32)
    return pl.pallas_call(
        fold_kernel,
        out_shape=(out,) * one.shape[0],
        in_specs=[VMEM_SPEC] * 2,
        out_specs=(VMEM_SPEC,) * one.shape[0],
        compiler_params=params(MIB * 2 + 16 * one.size),
        cost_estimate=cost(one.size, 12 * one.size),
        name="fold",
    )(in_vmem(one), two)


def step_of(i):
    return i ^ (i >> 1)


def take_blocks(index, blocks_ref, near_ref, far_ref):
    place, parity = index // 2, index % 2
    for i in range(near_ref.shape[0]):
        at = 2 * (place ^ step_of(i))
        near_ref[i] = blocks_ref[at + parity]
        far_ref[i] = blocks_ref[at + 1 - parity]


def put_blocks(index, value, blocks_ref, near_ref, far_ref):
    count, rows, lanes = blocks_ref.shape
    own = value.shape[0] // count
    for i in range(count):
        blocks_ref[i, :own] = value[i * own : (i + 1) * own]
        if own < rows:
            blocks_ref[i, own:] = jnp.zeros((rows - own, lanes), F32)
    take_blocks(index, blocks_ref, near_ref, far_ref)


def first_kernel(
    index_ref,
    adapter_hbm,
    hidden_hbm,
    down_hbm,
    k_hbm,
    v_hbm,
    near_ref,
    far_ref,
    hidden_ref,
    adapter_ref,
    held,
    held_kv,
    rank_blocks,
    kv_blocks,
    sems,
):
    pieces, _, width = held.shape
    forks = hidden_ref.shape[0]
    kv_width = held_kv.shape[2]
    lanes = rank_blocks.shape[2]
    copies = [
        pltpu.make_async_copy(adapter_hbm, adapter_ref, sems.at[pieces + 3]),
        pltpu.make_async_copy(hidden_hbm, hidden_ref, sems.at[pieces + 2]),
        *[
            pltpu.make_async_copy(
                down_hbm.at[:, i * width : (i + 1) * width], held.at[i], sems.at[i]
            )
            for i in range(pieces)
        ],
        pltpu.make_async_copy(k_hbm, held_kv.at[0], sems.at[pieces]),
        pltpu.make_async_copy(v_hbm, held_kv.at[1], sems.at[pieces + 1]),
    ]
    for copy in copies:
        copy.start()
    copies[0].wait()
    fork_adapter = jnp.broadcast_to(adapter_ref[...].astype(F32), (HEAD_WIDTH, forks)).T
    lane_adapter = lax.broadcasted_iota(jnp.int32, (forks, HEAD_WIDTH), 1) // ADAPTER_RANK
    wanted = fork_adapter.astype(jnp.int32) - lane_adapter
    total = jnp.zeros((forks, HEAD_WIDTH), F32)
    copies[1].wait()
    for i in range(pieces):
        copies[2 + i].wait()
        block = jnp.dot(hidden_ref[...], held[i], preferred_element_type=F32)
        for j in range(width // HEAD_WIDTH):
            first = (i * width + j * HEAD_WIDTH) // ADAPTER_RANK
            part = block[:, j * HEAD_WIDTH : (j + 1) * HEAD_WIDTH]
            total += jnp.where(wanted == first, part, 0.0)
    flipped = total.T
    flipped = flipped[:ADAPTER_RANK] + flipped[ADAPTER_RANK:]
    if lanes > forks:
        flipped = jnp.concatenate([flipped, jnp.zeros((ADAPTER_RANK, lanes - forks), F32)], axis=1)
    at = slice(0, lanes)
    put_blocks(index_ref[0], flipped, rank_blocks, near_ref.at[:, :, at], far_ref.at[:, :, at])
    for i in range(2):
        copies[2 + pieces + i].wait()
        part = jnp.dot(hidden_ref[...], held_kv[i], preferred_element_type=F32)
        at = slice(lanes + i * kv_width, lanes + (i + 1) * kv_width)
        put_blocks(index_ref[0], part, kv_blocks, near_ref.at[:, :, at], far_ref.at[:, :, at])


def project_first(index, adapter, hidden, down, k_weight, v_weight, mem_count, width=256):
    forks, depth = hidden.shape
    columns, kv_width = down.shape[1], k_weight.shape[1]
    lanes = -(-forks // HEAD_WIDTH) * HEAD_WIDTH
    line, fork_own = mem_count // 2, forks // mem_count
    pieces = columns // width
    out = pltpu.VMEM((line, fork_own, lanes + 2 * kv_width), F32)
    weights = 2 * depth * (columns + 2 * kv_width)
    return pl.pallas_call(
        first_kernel,
        out_shape=(out, out, pltpu.VMEM(hidden.shape, BF16), pltpu.VMEM((1, forks), jnp.int32)),
        in_specs=[SMEM_SPEC] + [ANY_SPEC] * 5,
        out_specs=(VMEM_SPEC,) * 4,
        scratch_shapes=[
            pltpu.VMEM((pieces, depth, width), BF16),
            pltpu.VMEM((2, depth, kv_width), BF16),
            pltpu.VMEM((mem_count, fork_own, lanes), F32),
            pltpu.VMEM((mem_count, fork_own, kv_width), F32),
            pltpu.SemaphoreType.DMA((pieces + 4,)),
        ],
        compiler_params=params(weights + 4 * MIB),
        cost_estimate=cost(forks * weights, weights),
        name="project_first",
    )(index, *[in_hbm(x) for x in (adapter.reshape(1, forks), hidden, down, k_weight, v_weight)])


def project_kernel(start, extra, hidden_ref, q_hbm, *refs):
    up_hbm, part_ref, up_ref, held, sems = refs if extra else (None, refs[0], None, *refs[1:])
    pieces, _, width = held.shape
    copies = []
    for i in range(pieces):
        columns = pl.ds(start + i * width, width)
        copies.append(pltpu.make_async_copy(q_hbm.at[:, columns], held.at[i], sems.at[i]))
    if extra:
        copies.append(pltpu.make_async_copy(up_hbm, up_ref, sems.at[pieces]))
    for copy in copies:
        copy.start()
    for i in range(pieces):
        copies[i].wait()
        part_ref[:, i * width : (i + 1) * width] = jnp.dot(
            hidden_ref[...], held[i], preferred_element_type=F32
        )
    if extra:
        copies[-1].wait()


def project(hidden, q_weight, start, columns, up=None, width=256):
    forks, depth = hidden.shape
    pieces = columns // width
    weights = 2 * depth * columns
    extra = [] if up is None else [up]
    return pl.pallas_call(
        functools.partial(project_kernel, start, bool(extra)),
        out_shape=tuple(
            [pltpu.VMEM((forks, columns), F32)] + [pltpu.VMEM(x.shape, BF16) for x in extra]
        ),
        in_specs=[VMEM_SPEC] + [ANY_SPEC] * (1 + len(extra)),
        out_specs=(VMEM_SPEC,) * (1 + len(extra)),
        scratch_shapes=[
            pltpu.VMEM((pieces, depth, width), BF16),
            pltpu.SemaphoreType.DMA((pieces + 1,)),
        ],
        compiler_params=params(weights + 2 * MIB),
        cost_estimate=cost(forks * weights, weights + sum(2 * x.size for x in extra)),
        name="project",
    )(in_vmem(hidden), *[in_hbm(x) for x in [q_weight] + extra])


def line_sum_kernel(after_ref, *refs):
    parts, (own_ref, other_ref) = refs[:-2], refs[-2:]
    own_ref[...] = functools.reduce(jnp.add, [ref[0] for ref in parts])
    other_ref[...] = functools.reduce(jnp.add, [ref[1] for ref in parts])


def line_sum(parts, after):
    out = pltpu.VMEM(parts[0].shape[1:], F32)
    size = len(parts) * parts[0].size
    return pl.pallas_call(
        line_sum_kernel,
        out_shape=(out, out),
        in_specs=[ANY_SPEC] + [VMEM_SPEC] * len(parts),
        out_specs=(VMEM_SPEC,) * 2,
        compiler_params=params(2 * MIB + 8 * size),
        cost_estimate=cost(size, 4 * size),
        name="line_sum",
    )(after, *parts)


def join_kernel(first_ref, one_ref, two_ref, out_ref):
    cut = first_ref.shape[1]
    out_ref[:, :cut] = first_ref[...]
    out_ref[:, cut:] = (one_ref[...] + two_ref[...]).astype(BF16)


def join(first, one, two):
    rows, columns = first.shape[0], first.shape[1] + one.shape[1]
    return pl.pallas_call(
        join_kernel,
        out_shape=pltpu.VMEM((rows, columns), BF16),
        in_specs=[VMEM_SPEC] * 3,
        out_specs=VMEM_SPEC,
        compiler_params=params(MIB + 16 * rows * columns),
        cost_estimate=cost(one.size, 4 * rows * columns),
        name="join",
    )(first, in_vmem(one), two)


def delta_kernel(line, ranks, start, joint, index_ref, adapter_ref, *refs):
    first_refs = refs[:line]
    part_ref, up_ref, *out_refs, blocks_ref = refs[line:]
    forks, width = part_ref.shape[0], blocks_ref.shape[2]
    if joint:
        near_ref, far_ref = out_refs[0].at[:, 0], out_refs[0].at[:, 1]
        new_ref = out_refs[1]
        lanes = first_refs[0].shape[1] - new_ref.shape[1]
        total = functools.reduce(jnp.add, [ref[:, lanes:] for ref in first_refs])
        new_ref[...] = total.astype(BF16)
    else:
        near_ref, far_ref = out_refs
    acts = functools.reduce(jnp.add, [ref[:ranks, :forks] for ref in first_refs])
    acts = acts.astype(BF16).astype(F32)
    adapters = lax.broadcasted_iota(jnp.int32, (ADAPTER_COUNT, forks), 0)
    onehot = (adapters == adapter_ref[...]).astype(F32)
    spread = jnp.concatenate(
        [acts[r : r + 1, :] * onehot for r in range(ranks)], axis=0
    ).astype(BF16)
    for i in range(part_ref.shape[1] // width):
        delta = lax.dot_general(
            spread,
            up_ref[:, start + i * width : start + (i + 1) * width],
            (((0,), (0,)), ((), ())),
            preferred_element_type=F32,
        )
        at = slice(i * width, (i + 1) * width)
        put_blocks(
            index_ref[0],
            part_ref[:, at] + delta,
            blocks_ref,
            near_ref.at[:, :, at],
            far_ref.at[:, :, at],
        )


def add_delta(index, adapter, first_parts, part, up, mem_count, start, new_width=0, width=256):
    forks, columns = part.shape
    line, fork_own = mem_count // 2, forks // mem_count
    ranks = ADAPTER_RANK // mem_count
    if new_width:
        out = (
            pltpu.VMEM((line, 2, fork_own, columns), F32),
            pltpu.VMEM((fork_own, new_width), BF16),
        )
    else:
        out = (pltpu.VMEM((line, fork_own, columns), F32),) * 2
    return pl.pallas_call(
        functools.partial(delta_kernel, line, ranks, start, new_width > 0),
        out_shape=out,
        in_specs=[SMEM_SPEC] + [VMEM_SPEC] * (line + 3),
        out_specs=(VMEM_SPEC,) * 2,
        scratch_shapes=[pltpu.VMEM((mem_count, fork_own, width), F32)],
        compiler_params=params(4 * MIB),
        cost_estimate=cost(
            2 * forks * up.shape[0] * columns, 2 * up.shape[0] * columns + 8 * forks * columns
        ),
        name="add_delta",
    )(index, in_vmem(adapter), *first_parts, in_vmem(part), in_vmem(up))


def put_terms(lse):
    heads, forks = lse.shape
    high = lse.astype(BF16).astype(F32)
    rest = lse - high
    middle = rest.astype(BF16).astype(F32)
    low = rest - middle
    spare = jnp.zeros((HEAD_WIDTH - 3 * heads, forks), F32)
    return jnp.concatenate([high, middle, low, spare], axis=0).T.astype(BF16)


def get_terms(terms, heads):
    terms = terms.astype(F32)
    return terms[:, :heads] + terms[:, heads : 2 * heads] + terms[:, 2 * heads : 3 * heads]


def attend_kernel(pieces, q_ref, mask_ref, *refs):
    k_refs, v_refs, (out_ref, score_ref, lse_ref) = (
        refs[:pieces],
        refs[pieces : 2 * pieces],
        refs[2 * pieces :],
    )
    forks = q_ref.shape[0]
    kv_local, group = lse_ref.shape[:2]
    pages = score_ref.shape[0] // 2
    held = pages // pieces
    scale = SCORE_SCALE * LOG2E
    chosen_by = mask_ref[...].reshape(forks, pages)
    spare = jnp.zeros((forks, HEAD_WIDTH - pages % HEAD_WIDTH), F32)
    chosen_by = jnp.concatenate([chosen_by, spare], axis=1).T[:pages]
    mask = jnp.concatenate([chosen_by] * group, axis=1) > 0
    ones = jnp.ones((8, score_ref.shape[1]), BF16)

    def score(kv_head, queries, p):
        lanes = slice(kv_head * HEAD_WIDTH, (kv_head + 1) * HEAD_WIDTH)
        scores = lax.dot_general(
            k_refs[p // held][p % held, :, lanes],
            queries,
            (((1,), (1,)), ((), ())),
            preferred_element_type=F32,
        )
        score_ref[kv_head % 2 * pages + p] = scores
        return jnp.max(scores, axis=0, keepdims=True)

    def term(kv_head, peaks, top, p):
        lanes = slice(kv_head * HEAD_WIDTH, (kv_head + 1) * HEAD_WIDTH)
        scores = score_ref[kv_head % 2 * pages + p]
        weights = jnp.exp2((scores - peaks[p]) * scale).astype(BF16)
        chosen = jnp.where(mask[p : p + 1], peaks[p], neg_floor)
        factor = jnp.where(mask[p : p + 1], jnp.exp2((chosen - top) * scale), 0.0)
        values = jnp.concatenate([v_refs[p // held][p % held, :, lanes].T, ones], axis=0)
        return jnp.dot(values, weights, preferred_element_type=F32) * factor

    def head_queries(kv_head):
        first = kv_head * group
        return jnp.concatenate(
            [
                q_ref[:, (first + g) * HEAD_WIDTH : (first + g + 1) * HEAD_WIDTH]
                for g in range(group)
            ],
            axis=0,
        )

    queries = head_queries(0)
    peaks = [score(0, queries, p) for p in range(pages)]
    for kv_head in range(kv_local):
        chosen = [jnp.where(mask[p : p + 1], peaks[p], neg_floor) for p in range(pages)]
        top = functools.reduce(jnp.maximum, chosen)
        if kv_head + 1 < kv_local:
            queries = head_queries(kv_head + 1)
        acc = None
        next_peaks = []
        for p in range(pages):
            if kv_head + 1 < kv_local:
                next_peaks.append(score(kv_head + 1, queries, p))
            part = term(kv_head, peaks, top, p)
            acc = part if acc is None else acc + part
        peaks = next_peaks
        mass = acc[HEAD_WIDTH : HEAD_WIDTH + 1]
        some = mass > 0
        safe = jnp.where(some, mass, 1.0)
        rows = (acc[:HEAD_WIDTH] * jnp.where(some, 1.0 / safe, 0.0)).T
        lse = jnp.where(some, top * scale + jnp.log2(safe), neg_floor)
        for g in range(group):
            at = (kv_head * group + g) * HEAD_WIDTH
            out_ref[:, at : at + HEAD_WIDTH] = rows[g * forks : (g + 1) * forks].astype(BF16)
        lse_ref[kv_head] = jnp.concatenate(
            [lse[:, g * forks : (g + 1) * forks] for g in range(group)], axis=0
        )

    heads = kv_local * group
    out_ref[:, heads * HEAD_WIDTH :] = put_terms(lse_ref[...].reshape(heads, forks))


def attend(queries, keys, values, mask):
    forks, width = queries.shape
    held, page_len, kv_width = keys[0].shape
    pieces = len(keys)
    pages = held * pieces
    kv_local = kv_width // HEAD_WIDTH
    group = width // kv_width
    rows = group * forks
    return pl.pallas_call(
        functools.partial(attend_kernel, pieces),
        out_shape=pltpu.VMEM((forks, width + HEAD_WIDTH), BF16),
        in_specs=[VMEM_SPEC] * (2 + 2 * pieces),
        out_specs=VMEM_SPEC,
        scratch_shapes=[
            pltpu.VMEM((2 * pages, page_len, rows), F32),
            pltpu.VMEM((kv_local, group, forks), F32),
        ],
        compiler_params=params(10 * pages * page_len * rows + 4 * MIB),
        cost_estimate=cost(
            4 * pages * page_len * kv_local * rows * HEAD_WIDTH,
            4 * pages * page_len * kv_width + 4 * forks * width,
            pages * page_len * kv_local * rows,
        ),
        name="attend",
    )(queries, *[in_vmem(x) for x in [mask, *keys, *values]])


def merge_kernel(heads, kv_heads, sources, *refs):
    parts, (q_ref, new_ref, out_ref) = refs[:sources], refs[sources:]
    group = heads // kv_heads
    width = heads * HEAD_WIDTH
    lses = [get_terms(ref[:, width : width + HEAD_WIDTH], heads) for ref in parts]

    def new_head(i):
        return new_ref[:, i * HEAD_WIDTH : (i + 1) * HEAD_WIDTH].astype(F32)

    scores = []
    for h in range(heads):
        query = q_ref[:, h * HEAD_WIDTH : (h + 1) * HEAD_WIDTH].astype(F32)
        scores.append(jnp.sum(query * new_head(h // group), axis=1, keepdims=True))
    own = jnp.concatenate(scores, axis=1) * (SCORE_SCALE * LOG2E)
    top = functools.reduce(jnp.maximum, lses, own)
    own_weight = jnp.exp2(own - top)
    weights = [jnp.exp2(lse - top) for lse in lses]
    inverse = 1.0 / functools.reduce(jnp.add, weights, own_weight)
    own_weight = own_weight * inverse
    weights = [weight * inverse for weight in weights]
    for h in range(heads):
        lanes = slice(h * HEAD_WIDTH, (h + 1) * HEAD_WIDTH)
        total = own_weight[:, h : h + 1] * new_head(kv_heads + h // group)
        for weight, ref in zip(weights, parts):
            total += weight[:, h : h + 1] * ref[:, lanes].astype(F32)
        out_ref[:, lanes] = total.astype(BF16)


def merge(parts, queries, new, heads, kv_heads):
    fork_own, width = parts[0].shape
    size = len(parts) * fork_own * width
    return pl.pallas_call(
        functools.partial(merge_kernel, heads, kv_heads, len(parts)),
        out_shape=jax.ShapeDtypeStruct((fork_own, heads * HEAD_WIDTH), BF16),
        compiler_params=params(4 * size + 4 * MIB),
        cost_estimate=pl.CostEstimate(flops=4 * size, bytes_accessed=2 * size, transcendentals=0),
        name="merge",
    )(*parts, queries, new)


def output_kernel(context_ref, *refs):
    weight_refs, out_ref = refs[:-1], refs[-1]
    total = None
    for i, ref in enumerate(weight_refs):
        depth = ref.shape[0]
        part = jnp.dot(
            context_ref[:, i * depth : (i + 1) * depth], ref[...], preferred_element_type=F32
        )
        total = part if total is None else total + part
    out_ref[...] = total


def output_project(context, weights):
    forks, rows = context.shape
    columns = weights[0].shape[1]
    return pl.pallas_call(
        output_kernel,
        out_shape=pltpu.VMEM((forks, columns), F32),
        in_specs=[VMEM_SPEC] * (1 + len(weights)),
        out_specs=VMEM_SPEC,
        compiler_params=params(4 * MIB),
        cost_estimate=cost(2 * forks * rows * columns, 2 * rows * columns),
        name="output_project",
    )(context, *[in_vmem(x) for x in weights])


def finish_kernel(count, line, index_ref, *refs):
    near_refs, far_refs, out_ref = refs[:count], refs[count : 2 * count], refs[-1]
    place, parity = index_ref[0] // 2, index_ref[0] % 2
    rows = out_ref.shape[1]
    for group, side in ((near_refs, parity), (far_refs, 1 - parity)):
        for i in range(line):
            total = functools.reduce(jnp.add, [ref[i * rows : (i + 1) * rows] for ref in group])
            out_ref[2 * (place ^ step_of(i)) + side] = total.astype(BF16)


def finish(index, near, far, mem_count):
    rows, columns = near[0].shape
    line = mem_count // 2
    return pl.pallas_call(
        functools.partial(finish_kernel, len(near), line),
        out_shape=jax.ShapeDtypeStruct((mem_count, rows // line, columns), BF16),
        in_specs=[SMEM_SPEC] + [VMEM_SPEC] * (2 * len(near)),
        out_specs=VMEM_SPEC,
        compiler_params=params(4 * MIB),
        cost_estimate=cost(0, 8 * rows * columns * len(near)),
        name="finish",
    )(index, *near, *far)


def shards(
    hidden,
    adapter,
    page_cache_slot,
    selection,
    query_projection_weight,
    key_projection_weight,
    value_projection_weight,
    adapter_down_weight,
    adapter_up_weight,
    output_projection_weight,
    prefix_key_cache,
    prefix_value_cache,
):
    mem_count = lax.axis_size("mem")
    mem_index = lax.axis_index("mem")
    forks = hidden.shape[0]
    fork_own = forks // mem_count
    q_width = query_projection_weight.shape[1]
    kv_width = key_projection_weight.shape[1]
    heads, kv_heads = q_width // HEAD_WIDTH, kv_width // HEAD_WIDTH
    pages = prefix_key_cache.shape[0]
    line = mem_count // 2
    index = mem_index.reshape(1)
    place, parity = mem_index // 2, mem_index % 2

    def swapped(x, step, cross=0):
        pairs = [(i, i ^ (2 * step + cross)) for i in range(mem_count)]
        return lax.ppermute(x, "mem", pairs)

    def along(blocks, cross=0):
        return [
            swapped(blocks[i], step_of(i), cross) if i or cross else blocks[0] for i in range(line)
        ]

    def gather(x):
        return jnp.concatenate([x] + [swapped(x, step_of(i)) for i in range(1, line)], axis=0)

    def pair(x):
        return swapped(x, 0, 1)

    near_1, far_1, hidden, adapter = project_first(
        index, adapter, hidden, adapter_down_weight, key_projection_weight, value_projection_weight, mem_count
    )
    cut = q_width * 10 // 16 // 256 * 256
    (part_a,) = project(hidden, query_projection_weight, 0, cut)
    first_parts = fold(near_1, pair(far_1))
    first_parts, part_a, hidden = lax.optimization_barrier((first_parts, part_a, hidden))
    part_b, up = project(
        hidden, query_projection_weight, cut, q_width - cut, adapter_up_weight.reshape(-1, q_width)
    )
    first_parts = along(first_parts)[::-1]

    near_a, far_a = add_delta(index, adapter, first_parts, part_a, up, mem_count, 0)
    near_a, far_a, part_b = lax.optimization_barrier((near_a, far_a, part_b))
    both_b, own_new = add_delta(
        index, adapter, first_parts, part_b, up, mem_count, cut, 2 * kv_width
    )
    sums_a = fold(near_a, pair(far_a))
    own_b, other_b = line_sum(along(both_b), sums_a[0])
    own_a = functools.reduce(jnp.add, along(sums_a)[::-1]).astype(BF16)
    own_queries = join(own_a, own_b, pair(other_b))

    *staged, near_mask, far_mask = stage_cache(
        index, page_cache_slot, selection, prefix_key_cache, prefix_value_cache, mem_count
    )
    keys, values = staged[: len(staged) // 2], staged[len(staged) // 2 :]
    near_queries = gather(own_queries)
    far_queries = pair(near_queries)
    near = attend(near_queries, keys, values, near_mask)
    far = attend(far_queries, keys, values, far_mask)
    blocks = (line, fork_own, q_width + HEAD_WIDTH)
    parts = along(near.reshape(blocks)) + along(far.reshape(blocks), 1)
    context_own = merge(parts, own_queries, own_new, heads, kv_heads)

    out_weights = stage(output_projection_weight)
    near_context = gather(context_own)
    far_context = pair(near_context)
    tp_count = lax.axis_size("tp")
    outs = []
    for context in (near_context, far_context):
        part = output_project(context, out_weights)
        terms = [part]
        for shift in range(1, tp_count):
            pairs = [(i, (i + shift) % tp_count) for i in range(tp_count)]
            terms.append(lax.ppermute(part, "tp", pairs))
        outs.append(terms)
    return finish(index, *outs, mem_count).reshape(forks, -1)


def solution(mesh):
    return jax.shard_map(
        shards,
        mesh=mesh,
        in_specs=(
            P("groups", "mem"),
            P("groups"),
            P("groups"),
            P("groups", None),
            P("mem", "tp"),
            P("mem", "tp"),
            P("mem", "tp"),
            P("mem", None),
            P("mem", None, "tp"),
            P("tp", "mem"),
            P(("groups", "mem"), None, "tp"),
            P(("groups", "mem"), None, "tp"),
        ),
        out_specs=P("groups", "mem"),
        check_vma=False,
    )
```

```python
import functools

import jax
import jax.numpy as jnp
from jax import lax
from jax.experimental import pallas as pl
from jax.experimental.pallas import tpu as pltpu
from jax.sharding import PartitionSpec as P

HEAD_WIDTH = 128
ADAPTER_RANK = 64
ADAPTER_COUNT = 32
LOG2E = 1.4426950408889634
SCORE_SCALE = HEAD_WIDTH ** (-0.5)
neg_floor = -1e30
MIB = 1024 * 1024
F32 = jnp.float32
BF16 = jnp.bfloat16


def params(limit, *semantics):
    return pltpu.CompilerParams(
        dimension_semantics=semantics or None, vmem_limit_bytes=int(limit)
    )


def whole(shape):
    return pl.BlockSpec(shape, lambda *_: (0,) * len(shape))


def in_hbm(x):
    return pltpu.with_memory_space_constraint(x, pltpu.HBM)


def in_vmem(x):
    return pltpu.with_memory_space_constraint(x, pltpu.VMEM)


def cost(flops, size, transcendentals=0):
    return pl.CostEstimate(
        flops=int(flops), bytes_accessed=int(size), transcendentals=int(transcendentals)
    )


VMEM_SPEC = pl.BlockSpec(memory_space=pltpu.VMEM)
SMEM_SPEC = pl.BlockSpec(memory_space=pltpu.SMEM)
ANY_SPEC = pl.BlockSpec(memory_space=pl.ANY)


def stage_kernel(pieces, *refs):
    count = len(refs[:-1]) // (pieces + 1)
    sources, targets, sems = refs[:count], refs[count:-1], refs[-1]
    copies = []
    for i, target in enumerate(targets):
        rows = pl.ds((i % pieces) * target.shape[0], target.shape[0])
        copies.append(
            pltpu.make_async_copy(sources[i // pieces].at[rows], target, sems.at[i])
        )
    for copy in copies:
        copy.start()
    for copy in copies:
        copy.wait()


def stage(*arrays, pieces=4):
    shapes = [(x.shape[0] // pieces,) + x.shape[1:] for x in arrays for _ in range(pieces)]
    return pl.pallas_call(
        functools.partial(stage_kernel, pieces),
        out_shape=tuple(pltpu.VMEM(shape, BF16) for shape in shapes),
        in_specs=[ANY_SPEC] * len(arrays),
        out_specs=(ANY_SPEC,) * len(shapes),
        scratch_shapes=[pltpu.SemaphoreType.DMA((len(shapes),))],
        compiler_params=params(MIB),
        cost_estimate=cost(0, sum(2 * x.size for x in arrays)),
        name="stage",
    )(*[in_hbm(x) for x in arrays])


def cache_kernel(pieces, index_ref, slot_hbm, select_hbm, *refs):
    sources, targets = refs[:2], refs[2 : 2 + 2 * pieces]
    near_ref, far_ref, slot_ref, select_ref, blocks_ref, sems = refs[2 + 2 * pieces :]
    count = 2 * pieces
    first = [
        pltpu.make_async_copy(slot_hbm, slot_ref, sems.at[count]),
        pltpu.make_async_copy(select_hbm, select_ref, sems.at[count + 1]),
    ]
    copies = []
    for i, target in enumerate(targets):
        rows = pl.ds((i % pieces) * target.shape[0], target.shape[0])
        copies.append(
            pltpu.make_async_copy(sources[i // pieces].at[rows], target, sems.at[i])
        )
    for copy in first + copies:
        copy.start()
    for copy in first:
        copy.wait()
    pages, total = blocks_ref.shape[2], slot_ref.shape[1]
    slots = index_ref[0] * pages + lax.broadcasted_iota(jnp.int32, (pages, total), 0)
    match = (slots == slot_ref[...]).astype(BF16)
    chosen = (select_ref[...] > 0).astype(BF16)
    held = lax.dot_general(
        chosen, match, (((1,), (1,)), ((), ())), preferred_element_type=F32
    )
    put_blocks(index_ref[0], held, blocks_ref, near_ref, far_ref)
    for copy in copies:
        copy.wait()


def stage_cache(index, page_cache_slot, selection, keys, values, mem_count, pieces=2):
    forks, total = selection.shape
    pages = keys.shape[0]
    line, fork_own = mem_count // 2, forks // mem_count
    shapes = [(x.shape[0] // pieces,) + x.shape[1:] for x in (keys, values) for _ in range(pieces)]
    mask = pltpu.VMEM((line, fork_own, pages), F32)
    return pl.pallas_call(
        functools.partial(cache_kernel, pieces),
        out_shape=tuple(pltpu.VMEM(shape, BF16) for shape in shapes) + (mask, mask),
        in_specs=[SMEM_SPEC] + [ANY_SPEC] * 4,
        out_specs=(ANY_SPEC,) * len(shapes) + (VMEM_SPEC,) * 2,
        scratch_shapes=[
            pltpu.VMEM((1, total), jnp.int32),
            pltpu.VMEM((forks, total), jnp.int32),
            pltpu.VMEM((mem_count, fork_own, pages), F32),
            pltpu.SemaphoreType.DMA((2 * pieces + 2,)),
        ],
        compiler_params=params(4 * MIB),
        cost_estimate=cost(0, 4 * keys.size),
        name="stage_cache",
    )(index, *[in_hbm(x) for x in (page_cache_slot.reshape(1, total), selection, keys, values)])


def fold_kernel(one_ref, two_ref, *out_refs):
    for i, out_ref in enumerate(out_refs):
        out_ref[...] = one_ref[i] + two_ref[i]


def fold(one, two):
    out = pltpu.VMEM(one.shape[1:], F32)
    return pl.pallas_call(
        fold_kernel,
        out_shape=(out,) * one.shape[0],
        in_specs=[VMEM_SPEC] * 2,
        out_specs=(VMEM_SPEC,) * one.shape[0],
        compiler_params=params(MIB * 2 + 16 * one.size),
        cost_estimate=cost(one.size, 12 * one.size),
        name="fold",
    )(in_vmem(one), two)


def take_blocks(index, blocks_ref, near_ref, far_ref):
    place, parity = index // 2, index % 2
    for i in range(near_ref.shape[0]):
        at = 2 * (place ^ i)
        near_ref[i] = blocks_ref[at + parity]
        far_ref[i] = blocks_ref[at + 1 - parity]


def put_blocks(index, value, blocks_ref, near_ref, far_ref):
    count, rows, lanes = blocks_ref.shape
    own = value.shape[0] // count
    for i in range(count):
        blocks_ref[i, :own] = value[i * own : (i + 1) * own]
        if own < rows:
            blocks_ref[i, own:] = jnp.zeros((rows - own, lanes), F32)
    take_blocks(index, blocks_ref, near_ref, far_ref)


def first_kernel(
    index_ref,
    adapter_hbm,
    hidden_hbm,
    down_hbm,
    k_hbm,
    v_hbm,
    near_ref,
    far_ref,
    hidden_ref,
    adapter_ref,
    held,
    held_kv,
    rank_blocks,
    kv_blocks,
    sems,
):
    pieces, _, width = held.shape
    forks = hidden_ref.shape[0]
    kv_width = held_kv.shape[2]
    lanes = rank_blocks.shape[2]
    copies = [
        pltpu.make_async_copy(adapter_hbm, adapter_ref, sems.at[pieces + 3]),
        pltpu.make_async_copy(hidden_hbm, hidden_ref, sems.at[pieces + 2]),
        *[
            pltpu.make_async_copy(
                down_hbm.at[:, i * width : (i + 1) * width], held.at[i], sems.at[i]
            )
            for i in range(pieces)
        ],
        pltpu.make_async_copy(k_hbm, held_kv.at[0], sems.at[pieces]),
        pltpu.make_async_copy(v_hbm, held_kv.at[1], sems.at[pieces + 1]),
    ]
    for copy in copies:
        copy.start()
    copies[0].wait()
    fork_adapter = jnp.broadcast_to(adapter_ref[...].astype(F32), (HEAD_WIDTH, forks)).T
    lane_adapter = lax.broadcasted_iota(jnp.int32, (forks, HEAD_WIDTH), 1) // ADAPTER_RANK
    wanted = fork_adapter.astype(jnp.int32) - lane_adapter
    total = jnp.zeros((forks, HEAD_WIDTH), F32)
    copies[1].wait()
    for i in range(pieces):
        copies[2 + i].wait()
        block = jnp.dot(hidden_ref[...], held[i], preferred_element_type=F32)
        for j in range(width // HEAD_WIDTH):
            first = (i * width + j * HEAD_WIDTH) // ADAPTER_RANK
            part = block[:, j * HEAD_WIDTH : (j + 1) * HEAD_WIDTH]
            total += jnp.where(wanted == first, part, 0.0)
    flipped = total.T
    flipped = flipped[:ADAPTER_RANK] + flipped[ADAPTER_RANK:]
    if lanes > forks:
        flipped = jnp.concatenate([flipped, jnp.zeros((ADAPTER_RANK, lanes - forks), F32)], axis=1)
    at = slice(0, lanes)
    put_blocks(index_ref[0], flipped, rank_blocks, near_ref.at[:, :, at], far_ref.at[:, :, at])
    for i in range(2):
        copies[2 + pieces + i].wait()
        part = jnp.dot(hidden_ref[...], held_kv[i], preferred_element_type=F32)
        at = slice(lanes + i * kv_width, lanes + (i + 1) * kv_width)
        put_blocks(index_ref[0], part, kv_blocks, near_ref.at[:, :, at], far_ref.at[:, :, at])


def project_first(index, adapter, hidden, down, k_weight, v_weight, mem_count, width=256):
    forks, depth = hidden.shape
    columns, kv_width = down.shape[1], k_weight.shape[1]
    lanes = -(-forks // HEAD_WIDTH) * HEAD_WIDTH
    line, fork_own = mem_count // 2, forks // mem_count
    pieces = columns // width
    out = pltpu.VMEM((line, fork_own, lanes + 2 * kv_width), F32)
    weights = 2 * depth * (columns + 2 * kv_width)
    return pl.pallas_call(
        first_kernel,
        out_shape=(out, out, pltpu.VMEM(hidden.shape, BF16), pltpu.VMEM((1, forks), jnp.int32)),
        in_specs=[SMEM_SPEC] + [ANY_SPEC] * 5,
        out_specs=(VMEM_SPEC,) * 4,
        scratch_shapes=[
            pltpu.VMEM((pieces, depth, width), BF16),
            pltpu.VMEM((2, depth, kv_width), BF16),
            pltpu.VMEM((mem_count, fork_own, lanes), F32),
            pltpu.VMEM((mem_count, fork_own, kv_width), F32),
            pltpu.SemaphoreType.DMA((pieces + 4,)),
        ],
        compiler_params=params(weights + 4 * MIB),
        cost_estimate=cost(forks * weights, weights),
        name="project_first",
    )(index, *[in_hbm(x) for x in (adapter.reshape(1, forks), hidden, down, k_weight, v_weight)])


def project_kernel(start, extra, hidden_ref, q_hbm, *refs):
    up_hbm, part_ref, up_ref, held, sems = refs if extra else (None, refs[0], None, *refs[1:])
    pieces, _, width = held.shape
    copies = []
    for i in range(pieces):
        columns = pl.ds(start + i * width, width)
        copies.append(pltpu.make_async_copy(q_hbm.at[:, columns], held.at[i], sems.at[i]))
    if extra:
        copies.append(pltpu.make_async_copy(up_hbm, up_ref, sems.at[pieces]))
    for copy in copies:
        copy.start()
    for i in range(pieces):
        copies[i].wait()
        part_ref[:, i * width : (i + 1) * width] = jnp.dot(
            hidden_ref[...], held[i], preferred_element_type=F32
        )
    if extra:
        copies[-1].wait()


def project(hidden, q_weight, start, columns, up=None, width=256):
    forks, depth = hidden.shape
    pieces = columns // width
    weights = 2 * depth * columns
    extra = [] if up is None else [up]
    return pl.pallas_call(
        functools.partial(project_kernel, start, bool(extra)),
        out_shape=tuple(
            [pltpu.VMEM((forks, columns), F32)] + [pltpu.VMEM(x.shape, BF16) for x in extra]
        ),
        in_specs=[VMEM_SPEC] + [ANY_SPEC] * (1 + len(extra)),
        out_specs=(VMEM_SPEC,) * (1 + len(extra)),
        scratch_shapes=[
            pltpu.VMEM((pieces, depth, width), BF16),
            pltpu.SemaphoreType.DMA((pieces + 1,)),
        ],
        compiler_params=params(weights + 2 * MIB),
        cost_estimate=cost(forks * weights, weights + sum(2 * x.size for x in extra)),
        name="project",
    )(in_vmem(hidden), *[in_hbm(x) for x in [q_weight] + extra])


def line_sum_kernel(after_ref, *refs):
    parts, (own_ref, other_ref) = refs[:-2], refs[-2:]
    own_ref[...] = functools.reduce(jnp.add, [ref[0] for ref in parts])
    other_ref[...] = functools.reduce(jnp.add, [ref[1] for ref in parts])


def line_sum(parts, after):
    out = pltpu.VMEM(parts[0].shape[1:], F32)
    size = len(parts) * parts[0].size
    return pl.pallas_call(
        line_sum_kernel,
        out_shape=(out, out),
        in_specs=[ANY_SPEC] + [VMEM_SPEC] * len(parts),
        out_specs=(VMEM_SPEC,) * 2,
        compiler_params=params(2 * MIB + 8 * size),
        cost_estimate=cost(size, 4 * size),
        name="line_sum",
    )(after, *parts)


def join_kernel(first_ref, one_ref, two_ref, out_ref):
    cut = first_ref.shape[1]
    out_ref[:, :cut] = first_ref[...]
    out_ref[:, cut:] = (one_ref[...] + two_ref[...]).astype(BF16)


def join(first, one, two):
    rows, columns = first.shape[0], first.shape[1] + one.shape[1]
    return pl.pallas_call(
        join_kernel,
        out_shape=pltpu.VMEM((rows, columns), BF16),
        in_specs=[VMEM_SPEC] * 3,
        out_specs=VMEM_SPEC,
        compiler_params=params(MIB + 16 * rows * columns),
        cost_estimate=cost(one.size, 4 * rows * columns),
        name="join",
    )(first, in_vmem(one), two)


def delta_kernel(line, ranks, start, joint, index_ref, adapter_ref, *refs):
    first_refs = refs[:line]
    part_ref, up_ref, *out_refs, blocks_ref = refs[line:]
    forks, width = part_ref.shape[0], blocks_ref.shape[2]
    if joint:
        near_ref, far_ref = out_refs[0].at[:, 0], out_refs[0].at[:, 1]
        new_ref = out_refs[1]
        lanes = first_refs[0].shape[1] - new_ref.shape[1]
        total = functools.reduce(jnp.add, [ref[:, lanes:] for ref in first_refs])
        new_ref[...] = total.astype(BF16)
    else:
        near_ref, far_ref = out_refs
    acts = functools.reduce(jnp.add, [ref[:ranks, :forks] for ref in first_refs])
    acts = acts.astype(BF16).astype(F32)
    adapters = lax.broadcasted_iota(jnp.int32, (ADAPTER_COUNT, forks), 0)
    onehot = (adapters == adapter_ref[...]).astype(F32)
    spread = jnp.concatenate(
        [acts[r : r + 1, :] * onehot for r in range(ranks)], axis=0
    ).astype(BF16)
    for i in range(part_ref.shape[1] // width):
        delta = lax.dot_general(
            spread,
            up_ref[:, start + i * width : start + (i + 1) * width],
            (((0,), (0,)), ((), ())),
            preferred_element_type=F32,
        )
        at = slice(i * width, (i + 1) * width)
        put_blocks(
            index_ref[0],
            part_ref[:, at] + delta,
            blocks_ref,
            near_ref.at[:, :, at],
            far_ref.at[:, :, at],
        )


def add_delta(index, adapter, first_parts, part, up, mem_count, start, new_width=0, width=256):
    forks, columns = part.shape
    line, fork_own = mem_count // 2, forks // mem_count
    ranks = ADAPTER_RANK // mem_count
    if new_width:
        out = (
            pltpu.VMEM((line, 2, fork_own, columns), F32),
            pltpu.VMEM((fork_own, new_width), BF16),
        )
    else:
        out = (pltpu.VMEM((line, fork_own, columns), F32),) * 2
    return pl.pallas_call(
        functools.partial(delta_kernel, line, ranks, start, new_width > 0),
        out_shape=out,
        in_specs=[SMEM_SPEC] + [VMEM_SPEC] * (line + 3),
        out_specs=(VMEM_SPEC,) * 2,
        scratch_shapes=[pltpu.VMEM((mem_count, fork_own, width), F32)],
        compiler_params=params(4 * MIB),
        cost_estimate=cost(
            2 * forks * up.shape[0] * columns, 2 * up.shape[0] * columns + 8 * forks * columns
        ),
        name="add_delta",
    )(index, in_vmem(adapter), *first_parts, in_vmem(part), in_vmem(up))


def put_terms(lse):
    heads, forks = lse.shape
    high = lse.astype(BF16).astype(F32)
    rest = lse - high
    middle = rest.astype(BF16).astype(F32)
    low = rest - middle
    spare = jnp.zeros((HEAD_WIDTH - 3 * heads, forks), F32)
    return jnp.concatenate([high, middle, low, spare], axis=0).T.astype(BF16)


def get_terms(terms, heads):
    terms = terms.astype(F32)
    return terms[:, :heads] + terms[:, heads : 2 * heads] + terms[:, 2 * heads : 3 * heads]


def attend_kernel(pieces, q_ref, mask_ref, *refs):
    k_refs, v_refs, (out_ref, score_ref, lse_ref) = (
        refs[:pieces],
        refs[pieces : 2 * pieces],
        refs[2 * pieces :],
    )
    forks = q_ref.shape[0]
    kv_local, group = lse_ref.shape[:2]
    pages = score_ref.shape[0] // 2
    held = pages // pieces
    scale = SCORE_SCALE * LOG2E
    chosen_by = mask_ref[...].reshape(forks, pages)
    spare = jnp.zeros((forks, HEAD_WIDTH - pages % HEAD_WIDTH), F32)
    chosen_by = jnp.concatenate([chosen_by, spare], axis=1).T[:pages]
    mask = jnp.concatenate([chosen_by] * group, axis=1) > 0
    ones = jnp.ones((8, score_ref.shape[1]), BF16)

    def score(kv_head, queries, p):
        lanes = slice(kv_head * HEAD_WIDTH, (kv_head + 1) * HEAD_WIDTH)
        scores = lax.dot_general(
            k_refs[p // held][p % held, :, lanes],
            queries,
            (((1,), (1,)), ((), ())),
            preferred_element_type=F32,
        )
        score_ref[kv_head % 2 * pages + p] = scores
        return jnp.max(scores, axis=0, keepdims=True)

    def term(kv_head, peaks, top, p):
        lanes = slice(kv_head * HEAD_WIDTH, (kv_head + 1) * HEAD_WIDTH)
        scores = score_ref[kv_head % 2 * pages + p]
        weights = jnp.exp2((scores - peaks[p]) * scale).astype(BF16)
        chosen = jnp.where(mask[p : p + 1], peaks[p], neg_floor)
        factor = jnp.where(mask[p : p + 1], jnp.exp2((chosen - top) * scale), 0.0)
        values = jnp.concatenate([v_refs[p // held][p % held, :, lanes].T, ones], axis=0)
        return jnp.dot(values, weights, preferred_element_type=F32) * factor

    def head_queries(kv_head):
        first = kv_head * group
        return jnp.concatenate(
            [
                q_ref[:, (first + g) * HEAD_WIDTH : (first + g + 1) * HEAD_WIDTH]
                for g in range(group)
            ],
            axis=0,
        )

    queries = head_queries(0)
    peaks = [score(0, queries, p) for p in range(pages)]
    for kv_head in range(kv_local):
        chosen = [jnp.where(mask[p : p + 1], peaks[p], neg_floor) for p in range(pages)]
        top = functools.reduce(jnp.maximum, chosen)
        if kv_head + 1 < kv_local:
            queries = head_queries(kv_head + 1)
        acc = None
        next_peaks = []
        for p in range(pages):
            if kv_head + 1 < kv_local:
                next_peaks.append(score(kv_head + 1, queries, p))
            part = term(kv_head, peaks, top, p)
            acc = part if acc is None else acc + part
        peaks = next_peaks
        mass = acc[HEAD_WIDTH : HEAD_WIDTH + 1]
        some = mass > 0
        safe = jnp.where(some, mass, 1.0)
        rows = (acc[:HEAD_WIDTH] * jnp.where(some, 1.0 / safe, 0.0)).T
        lse = jnp.where(some, top * scale + jnp.log2(safe), neg_floor)
        for g in range(group):
            at = (kv_head * group + g) * HEAD_WIDTH
            out_ref[:, at : at + HEAD_WIDTH] = rows[g * forks : (g + 1) * forks].astype(BF16)
        lse_ref[kv_head] = jnp.concatenate(
            [lse[:, g * forks : (g + 1) * forks] for g in range(group)], axis=0
        )

    heads = kv_local * group
    out_ref[:, heads * HEAD_WIDTH :] = put_terms(lse_ref[...].reshape(heads, forks))


def attend(queries, keys, values, mask):
    forks, width = queries.shape
    held, page_len, kv_width = keys[0].shape
    pieces = len(keys)
    pages = held * pieces
    kv_local = kv_width // HEAD_WIDTH
    group = width // kv_width
    rows = group * forks
    return pl.pallas_call(
        functools.partial(attend_kernel, pieces),
        out_shape=pltpu.VMEM((forks, width + HEAD_WIDTH), BF16),
        in_specs=[VMEM_SPEC] * (2 + 2 * pieces),
        out_specs=VMEM_SPEC,
        scratch_shapes=[
            pltpu.VMEM((2 * pages, page_len, rows), F32),
            pltpu.VMEM((kv_local, group, forks), F32),
        ],
        compiler_params=params(10 * pages * page_len * rows + 4 * MIB),
        cost_estimate=cost(
            4 * pages * page_len * kv_local * rows * HEAD_WIDTH,
            4 * pages * page_len * kv_width + 4 * forks * width,
            pages * page_len * kv_local * rows,
        ),
        name="attend",
    )(queries, *[in_vmem(x) for x in [mask, *keys, *values]])


def merge_kernel(heads, kv_heads, sources, *refs):
    parts, (q_ref, new_ref, out_ref) = refs[:sources], refs[sources:]
    group = heads // kv_heads
    width = heads * HEAD_WIDTH
    lses = [get_terms(ref[:, width : width + HEAD_WIDTH], heads) for ref in parts]

    def new_head(i):
        return new_ref[:, i * HEAD_WIDTH : (i + 1) * HEAD_WIDTH].astype(F32)

    scores = []
    for h in range(heads):
        query = q_ref[:, h * HEAD_WIDTH : (h + 1) * HEAD_WIDTH].astype(F32)
        scores.append(jnp.sum(query * new_head(h // group), axis=1, keepdims=True))
    own = jnp.concatenate(scores, axis=1) * (SCORE_SCALE * LOG2E)
    top = functools.reduce(jnp.maximum, lses, own)
    own_weight = jnp.exp2(own - top)
    weights = [jnp.exp2(lse - top) for lse in lses]
    inverse = 1.0 / functools.reduce(jnp.add, weights, own_weight)
    own_weight = own_weight * inverse
    weights = [weight * inverse for weight in weights]
    for h in range(heads):
        lanes = slice(h * HEAD_WIDTH, (h + 1) * HEAD_WIDTH)
        total = own_weight[:, h : h + 1] * new_head(kv_heads + h // group)
        for weight, ref in zip(weights, parts):
            total += weight[:, h : h + 1] * ref[:, lanes].astype(F32)
        out_ref[:, lanes] = total.astype(BF16)


def merge(parts, queries, new, heads, kv_heads):
    fork_own, width = parts[0].shape
    size = len(parts) * fork_own * width
    return pl.pallas_call(
        functools.partial(merge_kernel, heads, kv_heads, len(parts)),
        out_shape=jax.ShapeDtypeStruct((fork_own, heads * HEAD_WIDTH), BF16),
        compiler_params=params(4 * size + 4 * MIB),
        cost_estimate=pl.CostEstimate(flops=4 * size, bytes_accessed=2 * size, transcendentals=0),
        name="merge",
    )(*parts, queries, new)


def output_kernel(context_ref, *refs):
    weight_refs, out_ref = refs[:-1], refs[-1]
    total = None
    for i, ref in enumerate(weight_refs):
        depth = ref.shape[0]
        part = jnp.dot(
            context_ref[:, i * depth : (i + 1) * depth], ref[...], preferred_element_type=F32
        )
        total = part if total is None else total + part
    out_ref[...] = total


def output_project(context, weights):
    forks, rows = context.shape
    columns = weights[0].shape[1]
    return pl.pallas_call(
        output_kernel,
        out_shape=pltpu.VMEM((forks, columns), F32),
        in_specs=[VMEM_SPEC] * (1 + len(weights)),
        out_specs=VMEM_SPEC,
        compiler_params=params(4 * MIB),
        cost_estimate=cost(2 * forks * rows * columns, 2 * rows * columns),
        name="output_project",
    )(context, *[in_vmem(x) for x in weights])


def finish_kernel(count, line, index_ref, *refs):
    near_refs, far_refs, out_ref = refs[:count], refs[count : 2 * count], refs[-1]
    place, parity = index_ref[0] // 2, index_ref[0] % 2
    rows = out_ref.shape[1]
    for group, side in ((near_refs, parity), (far_refs, 1 - parity)):
        for i in range(line):
            total = functools.reduce(jnp.add, [ref[i * rows : (i + 1) * rows] for ref in group])
            out_ref[2 * (place ^ i) + side] = total.astype(BF16)


def finish(index, near, far, mem_count):
    rows, columns = near[0].shape
    line = mem_count // 2
    return pl.pallas_call(
        functools.partial(finish_kernel, len(near), line),
        out_shape=jax.ShapeDtypeStruct((mem_count, rows // line, columns), BF16),
        in_specs=[SMEM_SPEC] + [VMEM_SPEC] * (2 * len(near)),
        out_specs=VMEM_SPEC,
        compiler_params=params(4 * MIB),
        cost_estimate=cost(0, 8 * rows * columns * len(near)),
        name="finish",
    )(index, *near, *far)


def shards(
    hidden,
    adapter,
    page_cache_slot,
    selection,
    query_projection_weight,
    key_projection_weight,
    value_projection_weight,
    adapter_down_weight,
    adapter_up_weight,
    output_projection_weight,
    prefix_key_cache,
    prefix_value_cache,
):
    mem_count = lax.axis_size("mem")
    mem_index = lax.axis_index("mem")
    forks = hidden.shape[0]
    fork_own = forks // mem_count
    q_width = query_projection_weight.shape[1]
    kv_width = key_projection_weight.shape[1]
    heads, kv_heads = q_width // HEAD_WIDTH, kv_width // HEAD_WIDTH
    pages = prefix_key_cache.shape[0]
    line = mem_count // 2
    index = mem_index.reshape(1)
    place, parity = mem_index // 2, mem_index % 2

    def swapped(x, step, cross=0):
        pairs = [(i, i ^ (2 * step + cross)) for i in range(mem_count)]
        return lax.ppermute(x, "mem", pairs)

    def along(blocks, cross=0):
        return [swapped(blocks[i], i, cross) if i or cross else blocks[0] for i in range(line)]

    def gather(x):
        pieces = [x]
        for i in range(1, line):
            high = 1 << (i.bit_length() - 1)
            pieces.append(swapped(pieces[high], i ^ high) if i ^ high else swapped(x, i))
        return jnp.concatenate(pieces, axis=0)

    def pair(x):
        return swapped(x, 0, 1)

    near_1, far_1, hidden, adapter = project_first(
        index, adapter, hidden, adapter_down_weight, key_projection_weight, value_projection_weight, mem_count
    )
    cut = q_width * 10 // 16 // 256 * 256
    (part_a,) = project(hidden, query_projection_weight, 0, cut)
    first_parts = fold(near_1, pair(far_1))
    first_parts, part_a, hidden = lax.optimization_barrier((first_parts, part_a, hidden))
    part_b, up = project(
        hidden, query_projection_weight, cut, q_width - cut, adapter_up_weight.reshape(-1, q_width)
    )
    first_parts = along(first_parts)

    near_a, far_a = add_delta(index, adapter, first_parts, part_a, up, mem_count, 0)
    near_a, far_a, part_b = lax.optimization_barrier((near_a, far_a, part_b))
    both_b, own_new = add_delta(
        index, adapter, first_parts, part_b, up, mem_count, cut, 2 * kv_width
    )
    sums_a = fold(near_a, pair(far_a))
    own_b, other_b = line_sum(along(both_b), sums_a[0])
    own_a = functools.reduce(jnp.add, along(sums_a)[::-1]).astype(BF16)
    own_queries = join(own_a, own_b, pair(other_b))

    *staged, near_mask, far_mask = stage_cache(
        index, page_cache_slot, selection, prefix_key_cache, prefix_value_cache, mem_count
    )
    keys, values = staged[: len(staged) // 2], staged[len(staged) // 2 :]
    near_queries = gather(own_queries)
    far_queries = pair(near_queries)
    near = attend(near_queries, keys, values, near_mask)
    far = attend(far_queries, keys, values, far_mask)
    blocks = (line, fork_own, q_width + HEAD_WIDTH)
    parts = along(near.reshape(blocks)) + along(far.reshape(blocks), 1)
    context_own = merge(parts, own_queries, own_new, heads, kv_heads)

    out_weights = stage(output_projection_weight)
    near_context = gather(context_own)
    far_context = pair(near_context)
    tp_count = lax.axis_size("tp")
    outs = []
    for context in (near_context, far_context):
        part = output_project(context, out_weights)
        terms = [part]
        for shift in range(1, tp_count):
            pairs = [(i, (i + shift) % tp_count) for i in range(tp_count)]
            terms.append(lax.ppermute(part, "tp", pairs))
        outs.append(terms)
    return finish(index, *outs, mem_count).reshape(forks, -1)


def solution(mesh):
    return jax.shard_map(
        shards,
        mesh=mesh,
        in_specs=(
            P("groups", "mem"),
            P("groups"),
            P("groups"),
            P("groups", None),
            P("mem", "tp"),
            P("mem", "tp"),
            P("mem", "tp"),
            P("mem", None),
            P("mem", None, "tp"),
            P("tp", "mem"),
            P(("groups", "mem"), None, "tp"),
            P(("groups", "mem"), None, "tp"),
        ),
        out_specs=P("groups", "mem"),
        check_vma=False,
    )
```

```python
import functools

import jax
import jax.numpy as jnp
from jax import lax
from jax.experimental import pallas as pl
from jax.experimental.pallas import tpu as pltpu
from jax.sharding import PartitionSpec as P

HEAD_WIDTH = 128
ADAPTER_RANK = 64
ADAPTER_COUNT = 32
LOG2E = 1.4426950408889634
SCORE_SCALE = HEAD_WIDTH ** (-0.5)
neg_floor = -1e30
MIB = 1024 * 1024
F32 = jnp.float32
BF16 = jnp.bfloat16


def params(limit, *semantics):
    return pltpu.CompilerParams(
        dimension_semantics=semantics or None, vmem_limit_bytes=int(limit)
    )


def whole(shape):
    return pl.BlockSpec(shape, lambda *_: (0,) * len(shape))


def in_hbm(x):
    return pltpu.with_memory_space_constraint(x, pltpu.HBM)


def in_vmem(x):
    return pltpu.with_memory_space_constraint(x, pltpu.VMEM)


def cost(flops, size, transcendentals=0):
    return pl.CostEstimate(
        flops=int(flops), bytes_accessed=int(size), transcendentals=int(transcendentals)
    )


VMEM_SPEC = pl.BlockSpec(memory_space=pltpu.VMEM)
SMEM_SPEC = pl.BlockSpec(memory_space=pltpu.SMEM)
ANY_SPEC = pl.BlockSpec(memory_space=pl.ANY)


def stage_kernel(pieces, *refs):
    count = len(refs[:-1]) // (pieces + 1)
    sources, targets, sems = refs[:count], refs[count:-1], refs[-1]
    copies = []
    for i, target in enumerate(targets):
        rows = pl.ds((i % pieces) * target.shape[0], target.shape[0])
        copies.append(
            pltpu.make_async_copy(sources[i // pieces].at[rows], target, sems.at[i])
        )
    for copy in copies:
        copy.start()
    for copy in copies:
        copy.wait()


def stage(*arrays, pieces=4):
    shapes = [(x.shape[0] // pieces,) + x.shape[1:] for x in arrays for _ in range(pieces)]
    return pl.pallas_call(
        functools.partial(stage_kernel, pieces),
        out_shape=tuple(pltpu.VMEM(shape, BF16) for shape in shapes),
        in_specs=[ANY_SPEC] * len(arrays),
        out_specs=(ANY_SPEC,) * len(shapes),
        scratch_shapes=[pltpu.SemaphoreType.DMA((len(shapes),))],
        compiler_params=params(MIB),
        cost_estimate=cost(0, sum(2 * x.size for x in arrays)),
        name="stage",
    )(*[in_hbm(x) for x in arrays])


def cache_kernel(pieces, index_ref, slot_hbm, select_hbm, *refs):
    sources, targets = refs[:2], refs[2 : 2 + 2 * pieces]
    near_ref, far_ref, slot_ref, select_ref, blocks_ref, sems = refs[2 + 2 * pieces :]
    count = 2 * pieces
    first = [
        pltpu.make_async_copy(slot_hbm, slot_ref, sems.at[count]),
        pltpu.make_async_copy(select_hbm, select_ref, sems.at[count + 1]),
    ]
    copies = []
    for i, target in enumerate(targets):
        rows = pl.ds((i % pieces) * target.shape[0], target.shape[0])
        copies.append(
            pltpu.make_async_copy(sources[i // pieces].at[rows], target, sems.at[i])
        )
    for copy in first + copies:
        copy.start()
    for copy in first:
        copy.wait()
    pages, total = blocks_ref.shape[2], slot_ref.shape[1]
    slots = index_ref[0] * pages + lax.broadcasted_iota(jnp.int32, (pages, total), 0)
    match = (slots == slot_ref[...]).astype(BF16)
    chosen = (select_ref[...] > 0).astype(BF16)
    held = lax.dot_general(
        chosen, match, (((1,), (1,)), ((), ())), preferred_element_type=F32
    )
    put_blocks(index_ref[0], held, blocks_ref, near_ref, far_ref)
    for copy in copies:
        copy.wait()


def stage_cache(index, page_cache_slot, selection, keys, values, mem_count, pieces=2):
    forks, total = selection.shape
    pages = keys.shape[0]
    line, fork_own = mem_count // 2, forks // mem_count
    shapes = [(x.shape[0] // pieces,) + x.shape[1:] for x in (keys, values) for _ in range(pieces)]
    mask = pltpu.VMEM((line, fork_own, pages), F32)
    return pl.pallas_call(
        functools.partial(cache_kernel, pieces),
        out_shape=tuple(pltpu.VMEM(shape, BF16) for shape in shapes) + (mask, mask),
        in_specs=[SMEM_SPEC] + [ANY_SPEC] * 4,
        out_specs=(ANY_SPEC,) * len(shapes) + (VMEM_SPEC,) * 2,
        scratch_shapes=[
            pltpu.VMEM((1, total), jnp.int32),
            pltpu.VMEM((forks, total), jnp.int32),
            pltpu.VMEM((mem_count, fork_own, pages), F32),
            pltpu.SemaphoreType.DMA((2 * pieces + 2,)),
        ],
        compiler_params=params(4 * MIB),
        cost_estimate=cost(0, 4 * keys.size),
        name="stage_cache",
    )(index, *[in_hbm(x) for x in (page_cache_slot.reshape(1, total), selection, keys, values)])


def fold_kernel(one_ref, two_ref, *out_refs):
    for i, out_ref in enumerate(out_refs):
        out_ref[...] = one_ref[i] + two_ref[i]


def fold(one, two):
    out = pltpu.VMEM(one.shape[1:], F32)
    return pl.pallas_call(
        fold_kernel,
        out_shape=(out,) * one.shape[0],
        in_specs=[VMEM_SPEC] * 2,
        out_specs=(VMEM_SPEC,) * one.shape[0],
        compiler_params=params(MIB * 2 + 16 * one.size),
        cost_estimate=cost(one.size, 12 * one.size),
        name="fold",
    )(in_vmem(one), two)


def step_of(i):
    return i ^ (i >> 1)


def take_blocks(index, blocks_ref, near_ref, far_ref):
    place, parity = index // 2, index % 2
    for i in range(near_ref.shape[0]):
        at = 2 * (place ^ step_of(i))
        near_ref[i] = blocks_ref[at + parity]
        far_ref[i] = blocks_ref[at + 1 - parity]


def put_blocks(index, value, blocks_ref, near_ref, far_ref):
    count, rows, lanes = blocks_ref.shape
    own = value.shape[0] // count
    for i in range(count):
        blocks_ref[i, :own] = value[i * own : (i + 1) * own]
        if own < rows:
            blocks_ref[i, own:] = jnp.zeros((rows - own, lanes), F32)
    take_blocks(index, blocks_ref, near_ref, far_ref)


def first_kernel(
    index_ref,
    adapter_hbm,
    hidden_hbm,
    down_hbm,
    k_hbm,
    v_hbm,
    near_ref,
    far_ref,
    hidden_ref,
    adapter_ref,
    held,
    held_kv,
    rank_blocks,
    kv_blocks,
    sems,
):
    pieces, _, width = held.shape
    forks = hidden_ref.shape[0]
    kv_width = held_kv.shape[2]
    lanes = rank_blocks.shape[2]
    copies = [
        pltpu.make_async_copy(adapter_hbm, adapter_ref, sems.at[pieces + 3]),
        pltpu.make_async_copy(hidden_hbm, hidden_ref, sems.at[pieces + 2]),
        *[
            pltpu.make_async_copy(
                down_hbm.at[:, i * width : (i + 1) * width], held.at[i], sems.at[i]
            )
            for i in range(pieces)
        ],
        pltpu.make_async_copy(k_hbm, held_kv.at[0], sems.at[pieces]),
        pltpu.make_async_copy(v_hbm, held_kv.at[1], sems.at[pieces + 1]),
    ]
    ahead = 6
    for copy in copies[:ahead]:
        copy.start()

    def take(i):
        copies[i].wait()
        if i >= 2 and i - 2 + ahead < len(copies):
            copies[i - 2 + ahead].start()

    take(0)
    fork_adapter = jnp.broadcast_to(adapter_ref[...].astype(F32), (HEAD_WIDTH, forks)).T
    lane_adapter = lax.broadcasted_iota(jnp.int32, (forks, HEAD_WIDTH), 1) // ADAPTER_RANK
    wanted = fork_adapter.astype(jnp.int32) - lane_adapter
    total = jnp.zeros((forks, HEAD_WIDTH), F32)
    take(1)
    for i in range(pieces):
        take(2 + i)
        block = jnp.dot(hidden_ref[...], held[i], preferred_element_type=F32)
        for j in range(width // HEAD_WIDTH):
            first = (i * width + j * HEAD_WIDTH) // ADAPTER_RANK
            part = block[:, j * HEAD_WIDTH : (j + 1) * HEAD_WIDTH]
            total += jnp.where(wanted == first, part, 0.0)
    flipped = total.T
    flipped = flipped[:ADAPTER_RANK] + flipped[ADAPTER_RANK:]
    if lanes > forks:
        flipped = jnp.concatenate([flipped, jnp.zeros((ADAPTER_RANK, lanes - forks), F32)], axis=1)
    at = slice(0, lanes)
    put_blocks(index_ref[0], flipped, rank_blocks, near_ref.at[:, :, at], far_ref.at[:, :, at])
    for i in range(2):
        take(2 + pieces + i)
        part = jnp.dot(hidden_ref[...], held_kv[i], preferred_element_type=F32)
        at = slice(lanes + i * kv_width, lanes + (i + 1) * kv_width)
        put_blocks(index_ref[0], part, kv_blocks, near_ref.at[:, :, at], far_ref.at[:, :, at])


def project_first(index, adapter, hidden, down, k_weight, v_weight, mem_count, width=256):
    forks, depth = hidden.shape
    columns, kv_width = down.shape[1], k_weight.shape[1]
    lanes = -(-forks // HEAD_WIDTH) * HEAD_WIDTH
    line, fork_own = mem_count // 2, forks // mem_count
    pieces = columns // width
    out = pltpu.VMEM((line, fork_own, lanes + 2 * kv_width), F32)
    weights = 2 * depth * (columns + 2 * kv_width)
    return pl.pallas_call(
        first_kernel,
        out_shape=(out, out, pltpu.VMEM(hidden.shape, BF16), pltpu.VMEM((1, forks), jnp.int32)),
        in_specs=[SMEM_SPEC] + [ANY_SPEC] * 5,
        out_specs=(VMEM_SPEC,) * 4,
        scratch_shapes=[
            pltpu.VMEM((pieces, depth, width), BF16),
            pltpu.VMEM((2, depth, kv_width), BF16),
            pltpu.VMEM((mem_count, fork_own, lanes), F32),
            pltpu.VMEM((mem_count, fork_own, kv_width), F32),
            pltpu.SemaphoreType.DMA((pieces + 4,)),
        ],
        compiler_params=params(weights + 4 * MIB),
        cost_estimate=cost(forks * weights, weights),
        name="project_first",
    )(index, *[in_hbm(x) for x in (adapter.reshape(1, forks), hidden, down, k_weight, v_weight)])


def project_kernel(start, extra, hidden_ref, q_hbm, *refs):
    up_hbm, part_ref, up_ref, held, sems = refs if extra else (None, refs[0], None, *refs[1:])
    pieces, _, width = held.shape
    copies = []
    for i in range(pieces):
        columns = pl.ds(start + i * width, width)
        copies.append(pltpu.make_async_copy(q_hbm.at[:, columns], held.at[i], sems.at[i]))
    if extra:
        copies.append(pltpu.make_async_copy(up_hbm, up_ref, sems.at[pieces]))
    for copy in copies:
        copy.start()
    for i in range(pieces):
        copies[i].wait()
        part_ref[:, i * width : (i + 1) * width] = jnp.dot(
            hidden_ref[...], held[i], preferred_element_type=F32
        )
    if extra:
        copies[-1].wait()


def project(hidden, q_weight, start, columns, up=None, width=256):
    forks, depth = hidden.shape
    pieces = columns // width
    weights = 2 * depth * columns
    extra = [] if up is None else [up]
    return pl.pallas_call(
        functools.partial(project_kernel, start, bool(extra)),
        out_shape=tuple(
            [pltpu.VMEM((forks, columns), F32)] + [pltpu.VMEM(x.shape, BF16) for x in extra]
        ),
        in_specs=[VMEM_SPEC] + [ANY_SPEC] * (1 + len(extra)),
        out_specs=(VMEM_SPEC,) * (1 + len(extra)),
        scratch_shapes=[
            pltpu.VMEM((pieces, depth, width), BF16),
            pltpu.SemaphoreType.DMA((pieces + 1,)),
        ],
        compiler_params=params(weights + 2 * MIB),
        cost_estimate=cost(forks * weights, weights + sum(2 * x.size for x in extra)),
        name="project",
    )(in_vmem(hidden), *[in_hbm(x) for x in [q_weight] + extra])


def line_sum_kernel(after_ref, *refs):
    parts, (own_ref, other_ref) = refs[:-2], refs[-2:]
    own_ref[...] = functools.reduce(jnp.add, [ref[0] for ref in parts])
    other_ref[...] = functools.reduce(jnp.add, [ref[1] for ref in parts])


def line_sum(parts, after):
    out = pltpu.VMEM(parts[0].shape[1:], F32)
    size = len(parts) * parts[0].size
    return pl.pallas_call(
        line_sum_kernel,
        out_shape=(out, out),
        in_specs=[ANY_SPEC] + [VMEM_SPEC] * len(parts),
        out_specs=(VMEM_SPEC,) * 2,
        compiler_params=params(2 * MIB + 8 * size),
        cost_estimate=cost(size, 4 * size),
        name="line_sum",
    )(after, *parts)


def join_kernel(first_ref, one_ref, two_ref, out_ref):
    cut = first_ref.shape[1]
    out_ref[:, :cut] = first_ref[...]
    out_ref[:, cut:] = (one_ref[...] + two_ref[...]).astype(BF16)


def join(first, one, two):
    rows, columns = first.shape[0], first.shape[1] + one.shape[1]
    return pl.pallas_call(
        join_kernel,
        out_shape=pltpu.VMEM((rows, columns), BF16),
        in_specs=[VMEM_SPEC] * 3,
        out_specs=VMEM_SPEC,
        compiler_params=params(MIB + 16 * rows * columns),
        cost_estimate=cost(one.size, 4 * rows * columns),
        name="join",
    )(first, in_vmem(one), two)


def delta_kernel(line, ranks, start, joint, index_ref, adapter_ref, *refs):
    first_refs = refs[:line]
    part_ref, up_ref, *out_refs, blocks_ref = refs[line:]
    forks, width = part_ref.shape[0], blocks_ref.shape[2]
    if joint:
        near_ref, far_ref = out_refs[0].at[:, 0], out_refs[0].at[:, 1]
        new_ref = out_refs[1]
        lanes = first_refs[0].shape[1] - new_ref.shape[1]
        total = functools.reduce(jnp.add, [ref[:, lanes:] for ref in first_refs])
        new_ref[...] = total.astype(BF16)
    else:
        near_ref, far_ref = out_refs
    acts = functools.reduce(jnp.add, [ref[:ranks, :forks] for ref in first_refs])
    acts = acts.astype(BF16).astype(F32)
    adapters = lax.broadcasted_iota(jnp.int32, (ADAPTER_COUNT, forks), 0)
    onehot = (adapters == adapter_ref[...]).astype(F32)
    spread = jnp.concatenate(
        [acts[r : r + 1, :] * onehot for r in range(ranks)], axis=0
    ).astype(BF16)
    for i in range(part_ref.shape[1] // width):
        delta = lax.dot_general(
            spread,
            up_ref[:, start + i * width : start + (i + 1) * width],
            (((0,), (0,)), ((), ())),
            preferred_element_type=F32,
        )
        at = slice(i * width, (i + 1) * width)
        put_blocks(
            index_ref[0],
            part_ref[:, at] + delta,
            blocks_ref,
            near_ref.at[:, :, at],
            far_ref.at[:, :, at],
        )


def add_delta(index, adapter, first_parts, part, up, mem_count, start, new_width=0, width=256):
    forks, columns = part.shape
    line, fork_own = mem_count // 2, forks // mem_count
    ranks = ADAPTER_RANK // mem_count
    if new_width:
        out = (
            pltpu.VMEM((line, 2, fork_own, columns), F32),
            pltpu.VMEM((fork_own, new_width), BF16),
        )
    else:
        out = (pltpu.VMEM((line, fork_own, columns), F32),) * 2
    return pl.pallas_call(
        functools.partial(delta_kernel, line, ranks, start, new_width > 0),
        out_shape=out,
        in_specs=[SMEM_SPEC] + [VMEM_SPEC] * (line + 3),
        out_specs=(VMEM_SPEC,) * 2,
        scratch_shapes=[pltpu.VMEM((mem_count, fork_own, width), F32)],
        compiler_params=params(4 * MIB),
        cost_estimate=cost(
            2 * forks * up.shape[0] * columns, 2 * up.shape[0] * columns + 8 * forks * columns
        ),
        name="add_delta",
    )(index, in_vmem(adapter), *first_parts, in_vmem(part), in_vmem(up))


def put_terms(lse):
    heads, forks = lse.shape
    high = lse.astype(BF16).astype(F32)
    rest = lse - high
    middle = rest.astype(BF16).astype(F32)
    low = rest - middle
    spare = jnp.zeros((HEAD_WIDTH - 3 * heads, forks), F32)
    return jnp.concatenate([high, middle, low, spare], axis=0).T.astype(BF16)


def get_terms(terms, heads):
    terms = terms.astype(F32)
    return terms[:, :heads] + terms[:, heads : 2 * heads] + terms[:, 2 * heads : 3 * heads]


def attend_kernel(pieces, q_ref, mask_ref, *refs):
    k_refs, v_refs, (out_ref, score_ref, lse_ref) = (
        refs[:pieces],
        refs[pieces : 2 * pieces],
        refs[2 * pieces :],
    )
    forks = q_ref.shape[0]
    kv_local, group = lse_ref.shape[:2]
    pages = score_ref.shape[0] // 2
    held = pages // pieces
    scale = SCORE_SCALE * LOG2E
    chosen_by = mask_ref[...].reshape(forks, pages)
    spare = jnp.zeros((forks, HEAD_WIDTH - pages % HEAD_WIDTH), F32)
    chosen_by = jnp.concatenate([chosen_by, spare], axis=1).T[:pages]
    mask = jnp.concatenate([chosen_by] * group, axis=1) > 0
    ones = jnp.ones((8, score_ref.shape[1]), BF16)

    def score(kv_head, queries, p):
        lanes = slice(kv_head * HEAD_WIDTH, (kv_head + 1) * HEAD_WIDTH)
        scores = lax.dot_general(
            k_refs[p // held][p % held, :, lanes],
            queries,
            (((1,), (1,)), ((), ())),
            preferred_element_type=F32,
        )
        score_ref[kv_head % 2 * pages + p] = scores
        return jnp.max(scores, axis=0, keepdims=True)

    def term(kv_head, peaks, top, p):
        lanes = slice(kv_head * HEAD_WIDTH, (kv_head + 1) * HEAD_WIDTH)
        scores = score_ref[kv_head % 2 * pages + p]
        weights = jnp.exp2((scores - peaks[p]) * scale).astype(BF16)
        chosen = jnp.where(mask[p : p + 1], peaks[p], neg_floor)
        factor = jnp.where(mask[p : p + 1], jnp.exp2((chosen - top) * scale), 0.0)
        values = jnp.concatenate([v_refs[p // held][p % held, :, lanes].T, ones], axis=0)
        return jnp.dot(values, weights, preferred_element_type=F32) * factor

    def head_queries(kv_head):
        first = kv_head * group
        return jnp.concatenate(
            [
                q_ref[:, (first + g) * HEAD_WIDTH : (first + g + 1) * HEAD_WIDTH]
                for g in range(group)
            ],
            axis=0,
        )

    queries = head_queries(0)
    peaks = [score(0, queries, p) for p in range(pages)]
    for kv_head in range(kv_local):
        chosen = [jnp.where(mask[p : p + 1], peaks[p], neg_floor) for p in range(pages)]
        top = functools.reduce(jnp.maximum, chosen)
        if kv_head + 1 < kv_local:
            queries = head_queries(kv_head + 1)
        acc = None
        next_peaks = []
        for p in range(pages):
            if kv_head + 1 < kv_local:
                next_peaks.append(score(kv_head + 1, queries, p))
            part = term(kv_head, peaks, top, p)
            acc = part if acc is None else acc + part
        peaks = next_peaks
        mass = acc[HEAD_WIDTH : HEAD_WIDTH + 1]
        some = mass > 0
        safe = jnp.where(some, mass, 1.0)
        rows = (acc[:HEAD_WIDTH] * jnp.where(some, 1.0 / safe, 0.0)).T
        lse = jnp.where(some, top * scale + jnp.log2(safe), neg_floor)
        for g in range(group):
            at = (kv_head * group + g) * HEAD_WIDTH
            out_ref[:, at : at + HEAD_WIDTH] = rows[g * forks : (g + 1) * forks].astype(BF16)
        lse_ref[kv_head] = jnp.concatenate(
            [lse[:, g * forks : (g + 1) * forks] for g in range(group)], axis=0
        )

    heads = kv_local * group
    out_ref[:, heads * HEAD_WIDTH :] = put_terms(lse_ref[...].reshape(heads, forks))


def attend(queries, keys, values, mask):
    forks, width = queries.shape
    held, page_len, kv_width = keys[0].shape
    pieces = len(keys)
    pages = held * pieces
    kv_local = kv_width // HEAD_WIDTH
    group = width // kv_width
    rows = group * forks
    return pl.pallas_call(
        functools.partial(attend_kernel, pieces),
        out_shape=pltpu.VMEM((forks, width + HEAD_WIDTH), BF16),
        in_specs=[VMEM_SPEC] * (2 + 2 * pieces),
        out_specs=VMEM_SPEC,
        scratch_shapes=[
            pltpu.VMEM((2 * pages, page_len, rows), F32),
            pltpu.VMEM((kv_local, group, forks), F32),
        ],
        compiler_params=params(10 * pages * page_len * rows + 4 * MIB),
        cost_estimate=cost(
            4 * pages * page_len * kv_local * rows * HEAD_WIDTH,
            4 * pages * page_len * kv_width + 4 * forks * width,
            pages * page_len * kv_local * rows,
        ),
        name="attend",
    )(queries, *[in_vmem(x) for x in [mask, *keys, *values]])


def merge_kernel(heads, kv_heads, sources, *refs):
    parts, (q_ref, new_ref, out_ref) = refs[:sources], refs[sources:]
    group = heads // kv_heads
    width = heads * HEAD_WIDTH
    lses = [get_terms(ref[:, width : width + HEAD_WIDTH], heads) for ref in parts]

    def new_head(i):
        return new_ref[:, i * HEAD_WIDTH : (i + 1) * HEAD_WIDTH].astype(F32)

    scores = []
    for h in range(heads):
        query = q_ref[:, h * HEAD_WIDTH : (h + 1) * HEAD_WIDTH].astype(F32)
        scores.append(jnp.sum(query * new_head(h // group), axis=1, keepdims=True))
    own = jnp.concatenate(scores, axis=1) * (SCORE_SCALE * LOG2E)
    top = functools.reduce(jnp.maximum, lses, own)
    own_weight = jnp.exp2(own - top)
    weights = [jnp.exp2(lse - top) for lse in lses]
    inverse = 1.0 / functools.reduce(jnp.add, weights, own_weight)
    own_weight = own_weight * inverse
    weights = [weight * inverse for weight in weights]
    for h in range(heads):
        lanes = slice(h * HEAD_WIDTH, (h + 1) * HEAD_WIDTH)
        total = own_weight[:, h : h + 1] * new_head(kv_heads + h // group)
        for weight, ref in zip(weights, parts):
            total += weight[:, h : h + 1] * ref[:, lanes].astype(F32)
        out_ref[:, lanes] = total.astype(BF16)


def merge(parts, queries, new, heads, kv_heads):
    fork_own, width = parts[0].shape
    size = len(parts) * fork_own * width
    return pl.pallas_call(
        functools.partial(merge_kernel, heads, kv_heads, len(parts)),
        out_shape=jax.ShapeDtypeStruct((fork_own, heads * HEAD_WIDTH), BF16),
        compiler_params=params(4 * size + 4 * MIB),
        cost_estimate=pl.CostEstimate(flops=4 * size, bytes_accessed=2 * size, transcendentals=0),
        name="merge",
    )(*parts, queries, new)


def output_kernel(context_ref, *refs):
    weight_refs, out_ref = refs[:-1], refs[-1]
    total = None
    for i, ref in enumerate(weight_refs):
        depth = ref.shape[0]
        part = jnp.dot(
            context_ref[:, i * depth : (i + 1) * depth], ref[...], preferred_element_type=F32
        )
        total = part if total is None else total + part
    out_ref[...] = total


def output_project(context, weights):
    forks, rows = context.shape
    columns = weights[0].shape[1]
    return pl.pallas_call(
        output_kernel,
        out_shape=pltpu.VMEM((forks, columns), F32),
        in_specs=[VMEM_SPEC] * (1 + len(weights)),
        out_specs=VMEM_SPEC,
        compiler_params=params(4 * MIB),
        cost_estimate=cost(2 * forks * rows * columns, 2 * rows * columns),
        name="output_project",
    )(context, *[in_vmem(x) for x in weights])


def finish_kernel(count, line, index_ref, *refs):
    near_refs, far_refs, out_ref = refs[:count], refs[count : 2 * count], refs[-1]
    place, parity = index_ref[0] // 2, index_ref[0] % 2
    rows = out_ref.shape[1]
    for group, side in ((near_refs, parity), (far_refs, 1 - parity)):
        for i in range(line):
            total = functools.reduce(jnp.add, [ref[i * rows : (i + 1) * rows] for ref in group])
            out_ref[2 * (place ^ step_of(i)) + side] = total.astype(BF16)


def finish(index, near, far, mem_count):
    rows, columns = near[0].shape
    line = mem_count // 2
    return pl.pallas_call(
        functools.partial(finish_kernel, len(near), line),
        out_shape=jax.ShapeDtypeStruct((mem_count, rows // line, columns), BF16),
        in_specs=[SMEM_SPEC] + [VMEM_SPEC] * (2 * len(near)),
        out_specs=VMEM_SPEC,
        compiler_params=params(4 * MIB),
        cost_estimate=cost(0, 8 * rows * columns * len(near)),
        name="finish",
    )(index, *near, *far)


def shards(
    hidden,
    adapter,
    page_cache_slot,
    selection,
    query_projection_weight,
    key_projection_weight,
    value_projection_weight,
    adapter_down_weight,
    adapter_up_weight,
    output_projection_weight,
    prefix_key_cache,
    prefix_value_cache,
):
    mem_count = lax.axis_size("mem")
    mem_index = lax.axis_index("mem")
    forks = hidden.shape[0]
    fork_own = forks // mem_count
    q_width = query_projection_weight.shape[1]
    kv_width = key_projection_weight.shape[1]
    heads, kv_heads = q_width // HEAD_WIDTH, kv_width // HEAD_WIDTH
    pages = prefix_key_cache.shape[0]
    line = mem_count // 2
    index = mem_index.reshape(1)
    place, parity = mem_index // 2, mem_index % 2

    def swapped(x, step, cross=0):
        pairs = [(i, i ^ (2 * step + cross)) for i in range(mem_count)]
        return lax.ppermute(x, "mem", pairs)

    def along(blocks, cross=0):
        return [
            swapped(blocks[i], step_of(i), cross) if i or cross else blocks[0] for i in range(line)
        ]

    def gather(x):
        return jnp.concatenate([x] + [swapped(x, step_of(i)) for i in range(1, line)], axis=0)

    def pair(x):
        return swapped(x, 0, 1)

    near_1, far_1, hidden, adapter = project_first(
        index, adapter, hidden, adapter_down_weight, key_projection_weight, value_projection_weight, mem_count
    )
    cut = q_width * 10 // 16 // 256 * 256
    (part_a,) = project(hidden, query_projection_weight, 0, cut)
    first_parts = fold(near_1, pair(far_1))
    first_parts, part_a, hidden = lax.optimization_barrier((first_parts, part_a, hidden))
    part_b, up = project(
        hidden, query_projection_weight, cut, q_width - cut, adapter_up_weight.reshape(-1, q_width)
    )
    first_parts = along(first_parts)[::-1]

    near_a, far_a = add_delta(index, adapter, first_parts, part_a, up, mem_count, 0)
    near_a, far_a, part_b = lax.optimization_barrier((near_a, far_a, part_b))
    both_b, own_new = add_delta(
        index, adapter, first_parts, part_b, up, mem_count, cut, 2 * kv_width
    )
    sums_a = fold(near_a, pair(far_a))
    own_b, other_b = line_sum(along(both_b), sums_a[0])
    terms_a = along(sums_a)[1:]
    terms_a = sorted(zip(range(1, line), terms_a), key=lambda item: -step_of(item[0]))
    own_a = functools.reduce(jnp.add, [term for _, term in terms_a] + [sums_a[0]]).astype(BF16)
    own_queries = join(own_a, own_b, pair(other_b))

    *staged, near_mask, far_mask = stage_cache(
        index, page_cache_slot, selection, prefix_key_cache, prefix_value_cache, mem_count
    )
    keys, values = staged[: len(staged) // 2], staged[len(staged) // 2 :]
    near_queries = gather(own_queries)
    far_queries = pair(near_queries)
    near = attend(near_queries, keys, values, near_mask)
    far = attend(far_queries, keys, values, far_mask)
    blocks = (line, fork_own, q_width + HEAD_WIDTH)
    parts = along(near.reshape(blocks)) + along(far.reshape(blocks), 1)
    context_own = merge(parts, own_queries, own_new, heads, kv_heads)

    out_weights = stage(output_projection_weight)
    near_context = gather(context_own)
    far_context = pair(near_context)
    tp_count = lax.axis_size("tp")
    outs = []
    for context in (near_context, far_context):
        part = output_project(context, out_weights)
        terms = [part]
        for shift in range(1, tp_count):
            pairs = [(i, (i + shift) % tp_count) for i in range(tp_count)]
            terms.append(lax.ppermute(part, "tp", pairs))
        outs.append(terms)
    return finish(index, *outs, mem_count).reshape(forks, -1)


def solution(mesh):
    return jax.shard_map(
        shards,
        mesh=mesh,
        in_specs=(
            P("groups", "mem"),
            P("groups"),
            P("groups"),
            P("groups", None),
            P("mem", "tp"),
            P("mem", "tp"),
            P("mem", "tp"),
            P("mem", None),
            P("mem", None, "tp"),
            P("tp", "mem"),
            P(("groups", "mem"), None, "tp"),
            P(("groups", "mem"), None, "tp"),
        ),
        out_specs=P("groups", "mem"),
        check_vma=False,
    )
```

```python
import functools

import jax
import jax.numpy as jnp
from jax import lax
from jax.experimental import pallas as pl
from jax.experimental.pallas import tpu as pltpu
from jax.sharding import PartitionSpec as P

HEAD_WIDTH = 128
ADAPTER_RANK = 64
ADAPTER_COUNT = 32
LOG2E = 1.4426950408889634
SCORE_SCALE = HEAD_WIDTH ** (-0.5)
neg_floor = -1e30
MIB = 1024 * 1024
F32 = jnp.float32
BF16 = jnp.bfloat16


def params(limit, *semantics):
    return pltpu.CompilerParams(
        dimension_semantics=semantics or None, vmem_limit_bytes=int(limit)
    )


def whole(shape):
    return pl.BlockSpec(shape, lambda *_: (0,) * len(shape))


def in_hbm(x):
    return pltpu.with_memory_space_constraint(x, pltpu.HBM)


def in_vmem(x):
    return pltpu.with_memory_space_constraint(x, pltpu.VMEM)


def cost(flops, size, transcendentals=0):
    return pl.CostEstimate(
        flops=int(flops), bytes_accessed=int(size), transcendentals=int(transcendentals)
    )


VMEM_SPEC = pl.BlockSpec(memory_space=pltpu.VMEM)
SMEM_SPEC = pl.BlockSpec(memory_space=pltpu.SMEM)
ANY_SPEC = pl.BlockSpec(memory_space=pl.ANY)


def stage_kernel(pieces, *refs):
    count = len(refs[:-1]) // (pieces + 1)
    sources, targets, sems = refs[:count], refs[count:-1], refs[-1]
    copies = []
    for i, target in enumerate(targets):
        rows = pl.ds((i % pieces) * target.shape[0], target.shape[0])
        copies.append(
            pltpu.make_async_copy(sources[i // pieces].at[rows], target, sems.at[i])
        )
    for copy in copies:
        copy.start()
    for copy in copies:
        copy.wait()


def stage(*arrays, pieces=4):
    shapes = [(x.shape[0] // pieces,) + x.shape[1:] for x in arrays for _ in range(pieces)]
    return pl.pallas_call(
        functools.partial(stage_kernel, pieces),
        out_shape=tuple(pltpu.VMEM(shape, BF16) for shape in shapes),
        in_specs=[ANY_SPEC] * len(arrays),
        out_specs=(ANY_SPEC,) * len(shapes),
        scratch_shapes=[pltpu.SemaphoreType.DMA((len(shapes),))],
        compiler_params=params(MIB),
        cost_estimate=cost(0, sum(2 * x.size for x in arrays)),
        name="stage",
    )(*[in_hbm(x) for x in arrays])


def cache_kernel(pieces, index_ref, slot_hbm, select_hbm, *refs):
    sources, targets = refs[:2], refs[2 : 2 + 2 * pieces]
    near_ref, far_ref, slot_ref, select_ref, blocks_ref, sems = refs[2 + 2 * pieces :]
    count = 2 * pieces
    first = [
        pltpu.make_async_copy(slot_hbm, slot_ref, sems.at[count]),
        pltpu.make_async_copy(select_hbm, select_ref, sems.at[count + 1]),
    ]
    copies = []
    for i, target in enumerate(targets):
        rows = pl.ds((i % pieces) * target.shape[0], target.shape[0])
        copies.append(
            pltpu.make_async_copy(sources[i // pieces].at[rows], target, sems.at[i])
        )
    for copy in first + copies:
        copy.start()
    for copy in first:
        copy.wait()
    pages, total = blocks_ref.shape[2], slot_ref.shape[1]
    slots = index_ref[0] * pages + lax.broadcasted_iota(jnp.int32, (pages, total), 0)
    match = (slots == slot_ref[...]).astype(BF16)
    chosen = (select_ref[...] > 0).astype(BF16)
    held = lax.dot_general(
        chosen, match, (((1,), (1,)), ((), ())), preferred_element_type=F32
    )
    put_blocks(index_ref[0], held, blocks_ref, near_ref, far_ref)
    for copy in copies:
        copy.wait()


def stage_cache(index, page_cache_slot, selection, keys, values, mem_count, pieces=2):
    forks, total = selection.shape
    pages = keys.shape[0]
    line, fork_own = mem_count // 2, forks // mem_count
    shapes = [(x.shape[0] // pieces,) + x.shape[1:] for x in (keys, values) for _ in range(pieces)]
    mask = pltpu.VMEM((line, fork_own, pages), F32)
    return pl.pallas_call(
        functools.partial(cache_kernel, pieces),
        out_shape=tuple(pltpu.VMEM(shape, BF16) for shape in shapes) + (mask, mask),
        in_specs=[SMEM_SPEC] + [ANY_SPEC] * 4,
        out_specs=(ANY_SPEC,) * len(shapes) + (VMEM_SPEC,) * 2,
        scratch_shapes=[
            pltpu.VMEM((1, total), jnp.int32),
            pltpu.VMEM((forks, total), jnp.int32),
            pltpu.VMEM((mem_count, fork_own, pages), F32),
            pltpu.SemaphoreType.DMA((2 * pieces + 2,)),
        ],
        compiler_params=params(4 * MIB),
        cost_estimate=cost(0, 4 * keys.size),
        name="stage_cache",
    )(index, *[in_hbm(x) for x in (page_cache_slot.reshape(1, total), selection, keys, values)])


def fold_kernel(one_ref, two_ref, *out_refs):
    for i, out_ref in enumerate(out_refs):
        out_ref[...] = one_ref[i] + two_ref[i]


def fold(one, two):
    out = pltpu.VMEM(one.shape[1:], F32)
    return pl.pallas_call(
        fold_kernel,
        out_shape=(out,) * one.shape[0],
        in_specs=[VMEM_SPEC] * 2,
        out_specs=(VMEM_SPEC,) * one.shape[0],
        compiler_params=params(MIB * 2 + 16 * one.size),
        cost_estimate=cost(one.size, 12 * one.size),
        name="fold",
    )(in_vmem(one), two)


def step_of(i):
    return i ^ (i >> 1)


def take_blocks(index, blocks_ref, near_ref, far_ref):
    place, parity = index // 2, index % 2
    for i in range(near_ref.shape[0]):
        at = 2 * (place ^ step_of(i))
        near_ref[i] = blocks_ref[at + parity]
        far_ref[i] = blocks_ref[at + 1 - parity]


def put_blocks(index, value, blocks_ref, near_ref, far_ref):
    count, rows, lanes = blocks_ref.shape
    own = value.shape[0] // count
    for i in range(count):
        blocks_ref[i, :own] = value[i * own : (i + 1) * own]
        if own < rows:
            blocks_ref[i, own:] = jnp.zeros((rows - own, lanes), F32)
    take_blocks(index, blocks_ref, near_ref, far_ref)


def first_kernel(
    index_ref,
    adapter_hbm,
    hidden_hbm,
    down_hbm,
    k_hbm,
    v_hbm,
    near_ref,
    far_ref,
    hidden_ref,
    adapter_ref,
    held,
    held_kv,
    rank_blocks,
    kv_blocks,
    sems,
):
    pieces, _, width = held.shape
    forks = hidden_ref.shape[0]
    kv_width = held_kv.shape[2]
    lanes = rank_blocks.shape[2]
    copies = [
        pltpu.make_async_copy(adapter_hbm, adapter_ref, sems.at[pieces + 3]),
        pltpu.make_async_copy(hidden_hbm, hidden_ref, sems.at[pieces + 2]),
        *[
            pltpu.make_async_copy(
                down_hbm.at[:, i * width : (i + 1) * width], held.at[i], sems.at[i]
            )
            for i in range(pieces)
        ],
        pltpu.make_async_copy(k_hbm, held_kv.at[0], sems.at[pieces]),
        pltpu.make_async_copy(v_hbm, held_kv.at[1], sems.at[pieces + 1]),
    ]
    for copy in copies:
        copy.start()
    copies[0].wait()
    fork_adapter = jnp.broadcast_to(adapter_ref[...].astype(F32), (HEAD_WIDTH, forks)).T
    lane_adapter = lax.broadcasted_iota(jnp.int32, (forks, HEAD_WIDTH), 1) // ADAPTER_RANK
    wanted = fork_adapter.astype(jnp.int32) - lane_adapter
    total = jnp.zeros((forks, HEAD_WIDTH), F32)
    copies[1].wait()
    for i in range(pieces):
        copies[2 + i].wait()
        block = jnp.dot(hidden_ref[...], held[i], preferred_element_type=F32)
        for j in range(width // HEAD_WIDTH):
            first = (i * width + j * HEAD_WIDTH) // ADAPTER_RANK
            part = block[:, j * HEAD_WIDTH : (j + 1) * HEAD_WIDTH]
            total += jnp.where(wanted == first, part, 0.0)
    flipped = total.T
    flipped = flipped[:ADAPTER_RANK] + flipped[ADAPTER_RANK:]
    if lanes > forks:
        flipped = jnp.concatenate([flipped, jnp.zeros((ADAPTER_RANK, lanes - forks), F32)], axis=1)
    at = slice(0, lanes)
    put_blocks(index_ref[0], flipped, rank_blocks, near_ref.at[:, :, at], far_ref.at[:, :, at])
    for i in range(2):
        copies[2 + pieces + i].wait()
        part = jnp.dot(hidden_ref[...], held_kv[i], preferred_element_type=F32)
        at = slice(lanes + i * kv_width, lanes + (i + 1) * kv_width)
        put_blocks(index_ref[0], part, kv_blocks, near_ref.at[:, :, at], far_ref.at[:, :, at])


def project_first(index, adapter, hidden, down, k_weight, v_weight, mem_count, width=256):
    forks, depth = hidden.shape
    columns, kv_width = down.shape[1], k_weight.shape[1]
    lanes = -(-forks // HEAD_WIDTH) * HEAD_WIDTH
    line, fork_own = mem_count // 2, forks // mem_count
    pieces = columns // width
    out = pltpu.VMEM((line, fork_own, lanes + 2 * kv_width), F32)
    weights = 2 * depth * (columns + 2 * kv_width)
    return pl.pallas_call(
        first_kernel,
        out_shape=(out, out, pltpu.VMEM(hidden.shape, BF16), pltpu.VMEM((1, forks), jnp.int32)),
        in_specs=[SMEM_SPEC] + [ANY_SPEC] * 5,
        out_specs=(VMEM_SPEC,) * 4,
        scratch_shapes=[
            pltpu.VMEM((pieces, depth, width), BF16),
            pltpu.VMEM((2, depth, kv_width), BF16),
            pltpu.VMEM((mem_count, fork_own, lanes), F32),
            pltpu.VMEM((mem_count, fork_own, kv_width), F32),
            pltpu.SemaphoreType.DMA((pieces + 4,)),
        ],
        compiler_params=params(weights + 4 * MIB),
        cost_estimate=cost(forks * weights, weights),
        name="project_first",
    )(index, *[in_hbm(x) for x in (adapter.reshape(1, forks), hidden, down, k_weight, v_weight)])


def project_kernel(start, extra, hidden_ref, q_hbm, *refs):
    up_hbm, part_ref, up_ref, held, sems = refs if extra else (None, refs[0], None, *refs[1:])
    pieces, _, width = held.shape
    copies = []
    for i in range(pieces):
        columns = pl.ds(start + i * width, width)
        copies.append(pltpu.make_async_copy(q_hbm.at[:, columns], held.at[i], sems.at[i]))
    if extra:
        copies.append(pltpu.make_async_copy(up_hbm, up_ref, sems.at[pieces]))
    for copy in copies:
        copy.start()
    for i in range(pieces):
        copies[i].wait()
        part_ref[:, i * width : (i + 1) * width] = jnp.dot(
            hidden_ref[...], held[i], preferred_element_type=F32
        )
    if extra:
        copies[-1].wait()


def project(hidden, q_weight, start, columns, up=None, width=256):
    forks, depth = hidden.shape
    pieces = columns // width
    weights = 2 * depth * columns
    extra = [] if up is None else [up]
    return pl.pallas_call(
        functools.partial(project_kernel, start, bool(extra)),
        out_shape=tuple(
            [pltpu.VMEM((forks, columns), F32)] + [pltpu.VMEM(x.shape, BF16) for x in extra]
        ),
        in_specs=[VMEM_SPEC] + [ANY_SPEC] * (1 + len(extra)),
        out_specs=(VMEM_SPEC,) * (1 + len(extra)),
        scratch_shapes=[
            pltpu.VMEM((pieces, depth, width), BF16),
            pltpu.SemaphoreType.DMA((pieces + 1,)),
        ],
        compiler_params=params(weights + 2 * MIB),
        cost_estimate=cost(forks * weights, weights + sum(2 * x.size for x in extra)),
        name="project",
    )(in_vmem(hidden), *[in_hbm(x) for x in [q_weight] + extra])


def line_sum_kernel(after_ref, *refs):
    parts, (own_ref, other_ref) = refs[:-2], refs[-2:]
    own_ref[...] = functools.reduce(jnp.add, [ref[0] for ref in parts])
    other_ref[...] = functools.reduce(jnp.add, [ref[1] for ref in parts])


def line_sum(parts, after):
    out = pltpu.VMEM(parts[0].shape[1:], F32)
    size = len(parts) * parts[0].size
    return pl.pallas_call(
        line_sum_kernel,
        out_shape=(out, out),
        in_specs=[ANY_SPEC] + [VMEM_SPEC] * len(parts),
        out_specs=(VMEM_SPEC,) * 2,
        compiler_params=params(2 * MIB + 8 * size),
        cost_estimate=cost(size, 4 * size),
        name="line_sum",
    )(after, *parts)


def join_kernel(first_ref, one_ref, two_ref, out_ref):
    cut = first_ref.shape[1]
    out_ref[:, :cut] = first_ref[...]
    out_ref[:, cut:] = (one_ref[...] + two_ref[...]).astype(BF16)


def join(first, one, two):
    rows, columns = first.shape[0], first.shape[1] + one.shape[1]
    return pl.pallas_call(
        join_kernel,
        out_shape=pltpu.VMEM((rows, columns), BF16),
        in_specs=[VMEM_SPEC] * 3,
        out_specs=VMEM_SPEC,
        compiler_params=params(MIB + 16 * rows * columns),
        cost_estimate=cost(one.size, 4 * rows * columns),
        name="join",
    )(first, in_vmem(one), two)


def delta_kernel(line, ranks, start, joint, index_ref, adapter_ref, *refs):
    first_refs = refs[:line]
    part_ref, up_ref, *out_refs, blocks_ref = refs[line:]
    forks, width = part_ref.shape[0], blocks_ref.shape[2]
    if joint:
        near_ref, far_ref = out_refs[0].at[:, 0], out_refs[0].at[:, 1]
        new_ref = out_refs[1]
        lanes = first_refs[0].shape[1] - new_ref.shape[1]
        total = functools.reduce(jnp.add, [ref[:, lanes:] for ref in first_refs])
        new_ref[...] = total.astype(BF16)
    else:
        near_ref, far_ref = out_refs
    acts = functools.reduce(jnp.add, [ref[:ranks, :forks] for ref in first_refs])
    acts = acts.astype(BF16).astype(F32)
    adapters = lax.broadcasted_iota(jnp.int32, (ADAPTER_COUNT, forks), 0)
    onehot = (adapters == adapter_ref[...]).astype(F32)
    spread = jnp.concatenate(
        [acts[r : r + 1, :] * onehot for r in range(ranks)], axis=0
    ).astype(BF16)
    for i in range(part_ref.shape[1] // width):
        delta = lax.dot_general(
            spread,
            up_ref[:, start + i * width : start + (i + 1) * width],
            (((0,), (0,)), ((), ())),
            preferred_element_type=F32,
        )
        at = slice(i * width, (i + 1) * width)
        put_blocks(
            index_ref[0],
            part_ref[:, at] + delta,
            blocks_ref,
            near_ref.at[:, :, at],
            far_ref.at[:, :, at],
        )


def add_delta(index, adapter, first_parts, part, up, mem_count, start, new_width=0, width=256):
    forks, columns = part.shape
    line, fork_own = mem_count // 2, forks // mem_count
    ranks = ADAPTER_RANK // mem_count
    if new_width:
        out = (
            pltpu.VMEM((line, 2, fork_own, columns), F32),
            pltpu.VMEM((fork_own, new_width), BF16),
        )
    else:
        out = (pltpu.VMEM((line, fork_own, columns), F32),) * 2
    return pl.pallas_call(
        functools.partial(delta_kernel, line, ranks, start, new_width > 0),
        out_shape=out,
        in_specs=[SMEM_SPEC] + [VMEM_SPEC] * (line + 3),
        out_specs=(VMEM_SPEC,) * 2,
        scratch_shapes=[pltpu.VMEM((mem_count, fork_own, width), F32)],
        compiler_params=params(4 * MIB),
        cost_estimate=cost(
            2 * forks * up.shape[0] * columns, 2 * up.shape[0] * columns + 8 * forks * columns
        ),
        name="add_delta",
    )(index, in_vmem(adapter), *first_parts, in_vmem(part), in_vmem(up))


def put_terms(lse):
    heads, forks = lse.shape
    high = lse.astype(BF16).astype(F32)
    rest = lse - high
    middle = rest.astype(BF16).astype(F32)
    low = rest - middle
    spare = jnp.zeros((HEAD_WIDTH - 3 * heads, forks), F32)
    return jnp.concatenate([high, middle, low, spare], axis=0).T.astype(BF16)


def get_terms(terms, heads):
    terms = terms.astype(F32)
    return terms[:, :heads] + terms[:, heads : 2 * heads] + terms[:, 2 * heads : 3 * heads]


def attend_kernel(pieces, q_ref, mask_ref, *refs):
    k_refs, v_refs, (out_ref, score_ref, lse_ref) = (
        refs[:pieces],
        refs[pieces : 2 * pieces],
        refs[2 * pieces :],
    )
    forks = q_ref.shape[0]
    kv_local, group = lse_ref.shape[:2]
    pages = score_ref.shape[0] // 2
    held = pages // pieces
    scale = SCORE_SCALE * LOG2E
    chosen_by = mask_ref[...].reshape(forks, pages)
    spare = jnp.zeros((forks, HEAD_WIDTH - pages % HEAD_WIDTH), F32)
    chosen_by = jnp.concatenate([chosen_by, spare], axis=1).T[:pages]
    mask = jnp.concatenate([chosen_by] * group, axis=1) > 0
    ones = jnp.ones((8, score_ref.shape[1]), BF16)

    def score(kv_head, queries, p):
        lanes = slice(kv_head * HEAD_WIDTH, (kv_head + 1) * HEAD_WIDTH)
        scores = lax.dot_general(
            k_refs[p // held][p % held, :, lanes],
            queries,
            (((1,), (1,)), ((), ())),
            preferred_element_type=F32,
        )
        score_ref[kv_head % 2 * pages + p] = scores
        return jnp.max(scores, axis=0, keepdims=True)

    def term(kv_head, peaks, top, p):
        lanes = slice(kv_head * HEAD_WIDTH, (kv_head + 1) * HEAD_WIDTH)
        scores = score_ref[kv_head % 2 * pages + p]
        weights = jnp.exp2((scores - peaks[p]) * scale).astype(BF16)
        chosen = jnp.where(mask[p : p + 1], peaks[p], neg_floor)
        factor = jnp.where(mask[p : p + 1], jnp.exp2((chosen - top) * scale), 0.0)
        values = jnp.concatenate([v_refs[p // held][p % held, :, lanes].T, ones], axis=0)
        return jnp.dot(values, weights, preferred_element_type=F32) * factor

    def head_queries(kv_head):
        first = kv_head * group
        return jnp.concatenate(
            [
                q_ref[:, (first + g) * HEAD_WIDTH : (first + g + 1) * HEAD_WIDTH]
                for g in range(group)
            ],
            axis=0,
        )

    queries = head_queries(0)
    peaks = [score(0, queries, p) for p in range(pages)]
    for kv_head in range(kv_local):
        chosen = [jnp.where(mask[p : p + 1], peaks[p], neg_floor) for p in range(pages)]
        top = functools.reduce(jnp.maximum, chosen)
        if kv_head + 1 < kv_local:
            queries = head_queries(kv_head + 1)
        acc = None
        next_peaks = []
        for p in range(pages):
            if kv_head + 1 < kv_local:
                next_peaks.append(score(kv_head + 1, queries, p))
            part = term(kv_head, peaks, top, p)
            acc = part if acc is None else acc + part
        peaks = next_peaks
        mass = acc[HEAD_WIDTH : HEAD_WIDTH + 1]
        some = mass > 0
        safe = jnp.where(some, mass, 1.0)
        rows = (acc[:HEAD_WIDTH] * jnp.where(some, 1.0 / safe, 0.0)).T
        lse = jnp.where(some, top * scale + jnp.log2(safe), neg_floor)
        for g in range(group):
            at = (kv_head * group + g) * HEAD_WIDTH
            out_ref[:, at : at + HEAD_WIDTH] = rows[g * forks : (g + 1) * forks].astype(BF16)
        lse_ref[kv_head] = jnp.concatenate(
            [lse[:, g * forks : (g + 1) * forks] for g in range(group)], axis=0
        )

    heads = kv_local * group
    out_ref[:, heads * HEAD_WIDTH :] = put_terms(lse_ref[...].reshape(heads, forks))


def attend(queries, keys, values, mask):
    forks, width = queries.shape
    held, page_len, kv_width = keys[0].shape
    pieces = len(keys)
    pages = held * pieces
    kv_local = kv_width // HEAD_WIDTH
    group = width // kv_width
    rows = group * forks
    return pl.pallas_call(
        functools.partial(attend_kernel, pieces),
        out_shape=pltpu.VMEM((forks, width + HEAD_WIDTH), BF16),
        in_specs=[VMEM_SPEC] * (2 + 2 * pieces),
        out_specs=VMEM_SPEC,
        scratch_shapes=[
            pltpu.VMEM((2 * pages, page_len, rows), F32),
            pltpu.VMEM((kv_local, group, forks), F32),
        ],
        compiler_params=params(10 * pages * page_len * rows + 4 * MIB),
        cost_estimate=cost(
            4 * pages * page_len * kv_local * rows * HEAD_WIDTH,
            4 * pages * page_len * kv_width + 4 * forks * width,
            pages * page_len * kv_local * rows,
        ),
        name="attend",
    )(queries, *[in_vmem(x) for x in [mask, *keys, *values]])


def merge_kernel(heads, kv_heads, sources, *refs):
    parts, (q_ref, new_ref, out_ref) = refs[:sources], refs[sources:]
    group = heads // kv_heads
    width = heads * HEAD_WIDTH
    lses = [get_terms(ref[:, width : width + HEAD_WIDTH], heads) for ref in parts]

    def new_head(i):
        return new_ref[:, i * HEAD_WIDTH : (i + 1) * HEAD_WIDTH].astype(F32)

    scores = []
    for h in range(heads):
        query = q_ref[:, h * HEAD_WIDTH : (h + 1) * HEAD_WIDTH].astype(F32)
        scores.append(jnp.sum(query * new_head(h // group), axis=1, keepdims=True))
    own = jnp.concatenate(scores, axis=1) * (SCORE_SCALE * LOG2E)
    top = functools.reduce(jnp.maximum, lses, own)
    own_weight = jnp.exp2(own - top)
    weights = [jnp.exp2(lse - top) for lse in lses]
    inverse = 1.0 / functools.reduce(jnp.add, weights, own_weight)
    own_weight = own_weight * inverse
    weights = [weight * inverse for weight in weights]
    for h in range(heads):
        lanes = slice(h * HEAD_WIDTH, (h + 1) * HEAD_WIDTH)
        total = own_weight[:, h : h + 1] * new_head(kv_heads + h // group)
        for weight, ref in zip(weights, parts):
            total += weight[:, h : h + 1] * ref[:, lanes].astype(F32)
        out_ref[:, lanes] = total.astype(BF16)


def merge(parts, queries, new, heads, kv_heads):
    fork_own, width = parts[0].shape
    size = len(parts) * fork_own * width
    return pl.pallas_call(
        functools.partial(merge_kernel, heads, kv_heads, len(parts)),
        out_shape=jax.ShapeDtypeStruct((fork_own, heads * HEAD_WIDTH), BF16),
        compiler_params=params(4 * size + 4 * MIB),
        cost_estimate=pl.CostEstimate(flops=4 * size, bytes_accessed=2 * size, transcendentals=0),
        name="merge",
    )(*parts, queries, new)


def output_kernel(context_ref, *refs):
    weight_refs, out_ref = refs[:-1], refs[-1]
    total = None
    for i, ref in enumerate(weight_refs):
        depth = ref.shape[0]
        part = jnp.dot(
            context_ref[:, i * depth : (i + 1) * depth], ref[...], preferred_element_type=F32
        )
        total = part if total is None else total + part
    out_ref[...] = total


def output_project(context, weights):
    forks, rows = context.shape
    columns = weights[0].shape[1]
    return pl.pallas_call(
        output_kernel,
        out_shape=pltpu.VMEM((forks, columns), F32),
        in_specs=[VMEM_SPEC] * (1 + len(weights)),
        out_specs=VMEM_SPEC,
        compiler_params=params(4 * MIB),
        cost_estimate=cost(2 * forks * rows * columns, 2 * rows * columns),
        name="output_project",
    )(context, *[in_vmem(x) for x in weights])


def finish_kernel(count, line, index_ref, *refs):
    near_refs, far_refs, out_ref = refs[:count], refs[count : 2 * count], refs[-1]
    place, parity = index_ref[0] // 2, index_ref[0] % 2
    rows = out_ref.shape[1]
    for group, side in ((near_refs, parity), (far_refs, 1 - parity)):
        for i in range(line):
            total = functools.reduce(jnp.add, [ref[i * rows : (i + 1) * rows] for ref in group])
            out_ref[2 * (place ^ step_of(i)) + side] = total.astype(BF16)


def finish(index, near, far, mem_count):
    rows, columns = near[0].shape
    line = mem_count // 2
    return pl.pallas_call(
        functools.partial(finish_kernel, len(near), line),
        out_shape=jax.ShapeDtypeStruct((mem_count, rows // line, columns), BF16),
        in_specs=[SMEM_SPEC] + [VMEM_SPEC] * (2 * len(near)),
        out_specs=VMEM_SPEC,
        compiler_params=params(4 * MIB),
        cost_estimate=cost(0, 8 * rows * columns * len(near)),
        name="finish",
    )(index, *near, *far)


def shards(
    hidden,
    adapter,
    page_cache_slot,
    selection,
    query_projection_weight,
    key_projection_weight,
    value_projection_weight,
    adapter_down_weight,
    adapter_up_weight,
    output_projection_weight,
    prefix_key_cache,
    prefix_value_cache,
):
    mem_count = lax.axis_size("mem")
    mem_index = lax.axis_index("mem")
    forks = hidden.shape[0]
    fork_own = forks // mem_count
    q_width = query_projection_weight.shape[1]
    kv_width = key_projection_weight.shape[1]
    heads, kv_heads = q_width // HEAD_WIDTH, kv_width // HEAD_WIDTH
    pages = prefix_key_cache.shape[0]
    line = mem_count // 2
    index = mem_index.reshape(1)
    place, parity = mem_index // 2, mem_index % 2

    def swapped(x, step, cross=0):
        pairs = [(i, i ^ (2 * step + cross)) for i in range(mem_count)]
        return lax.ppermute(x, "mem", pairs)

    def along(blocks, cross=0):
        return [
            swapped(blocks[i], step_of(i), cross) if i or cross else blocks[0] for i in range(line)
        ]

    def gather(x):
        return jnp.concatenate([x] + [swapped(x, step_of(i)) for i in range(1, line)], axis=0)

    def pair(x):
        return swapped(x, 0, 1)

    near_1, far_1, hidden, adapter = project_first(
        index, adapter, hidden, adapter_down_weight, key_projection_weight, value_projection_weight, mem_count
    )
    cut = q_width * 10 // 16 // 256 * 256
    part_a, up = project(
        hidden, query_projection_weight, 0, cut, adapter_up_weight.reshape(-1, q_width)
    )
    first_parts = fold(near_1, pair(far_1))
    first_parts, part_a, hidden = lax.optimization_barrier((first_parts, part_a, hidden))
    (part_b,) = project(hidden, query_projection_weight, cut, q_width - cut)
    first_parts = along(first_parts)[::-1]

    near_a, far_a = add_delta(index, adapter, first_parts, part_a, up, mem_count, 0)
    near_a, far_a, part_b = lax.optimization_barrier((near_a, far_a, part_b))
    both_b, own_new = add_delta(
        index, adapter, first_parts, part_b, up, mem_count, cut, 2 * kv_width
    )
    sums_a = fold(near_a, pair(far_a))
    own_b, other_b = line_sum(along(both_b), sums_a[0])
    terms_a = along(sums_a)[1:]
    terms_a = sorted(zip(range(1, line), terms_a), key=lambda item: -step_of(item[0]))
    own_a = functools.reduce(jnp.add, [term for _, term in terms_a] + [sums_a[0]]).astype(BF16)
    own_queries = join(own_a, own_b, pair(other_b))

    *staged, near_mask, far_mask = stage_cache(
        index, page_cache_slot, selection, prefix_key_cache, prefix_value_cache, mem_count
    )
    keys, values = staged[: len(staged) // 2], staged[len(staged) // 2 :]
    near_queries = gather(own_queries)
    far_queries = pair(near_queries)
    near = attend(near_queries, keys, values, near_mask)
    far = attend(far_queries, keys, values, far_mask)
    blocks = (line, fork_own, q_width + HEAD_WIDTH)
    parts = along(near.reshape(blocks)) + along(far.reshape(blocks), 1)
    context_own = merge(parts, own_queries, own_new, heads, kv_heads)

    out_weights = stage(output_projection_weight)
    near_context = gather(context_own)
    far_context = pair(near_context)
    tp_count = lax.axis_size("tp")
    outs = []
    for context in (near_context, far_context):
        part = output_project(context, out_weights)
        terms = [part]
        for shift in range(1, tp_count):
            pairs = [(i, (i + shift) % tp_count) for i in range(tp_count)]
            terms.append(lax.ppermute(part, "tp", pairs))
        outs.append(terms)
    return finish(index, *outs, mem_count).reshape(forks, -1)


def solution(mesh):
    return jax.shard_map(
        shards,
        mesh=mesh,
        in_specs=(
            P("groups", "mem"),
            P("groups"),
            P("groups"),
            P("groups", None),
            P("mem", "tp"),
            P("mem", "tp"),
            P("mem", "tp"),
            P("mem", None),
            P("mem", None, "tp"),
            P("tp", "mem"),
            P(("groups", "mem"), None, "tp"),
            P(("groups", "mem"), None, "tp"),
        ),
        out_specs=P("groups", "mem"),
        check_vma=False,
    )
```

```python
import functools

import jax
import jax.numpy as jnp
from jax import lax
from jax.experimental import pallas as pl
from jax.experimental.pallas import tpu as pltpu
from jax.sharding import PartitionSpec as P

HEAD_WIDTH = 128
ADAPTER_RANK = 64
ADAPTER_COUNT = 32
LOG2E = 1.4426950408889634
SCORE_SCALE = HEAD_WIDTH ** (-0.5)
neg_floor = -1e30
MIB = 1024 * 1024
F32 = jnp.float32
BF16 = jnp.bfloat16


def params(limit, *semantics):
    return pltpu.CompilerParams(
        dimension_semantics=semantics or None, vmem_limit_bytes=int(limit)
    )


def whole(shape):
    return pl.BlockSpec(shape, lambda *_: (0,) * len(shape))


def in_hbm(x):
    return pltpu.with_memory_space_constraint(x, pltpu.HBM)


def in_vmem(x):
    return pltpu.with_memory_space_constraint(x, pltpu.VMEM)


def cost(flops, size, transcendentals=0):
    return pl.CostEstimate(
        flops=int(flops), bytes_accessed=int(size), transcendentals=int(transcendentals)
    )


VMEM_SPEC = pl.BlockSpec(memory_space=pltpu.VMEM)
SMEM_SPEC = pl.BlockSpec(memory_space=pltpu.SMEM)
ANY_SPEC = pl.BlockSpec(memory_space=pl.ANY)


def stage_kernel(pieces, *refs):
    count = len(refs[:-1]) // (pieces + 1)
    sources, targets, sems = refs[:count], refs[count:-1], refs[-1]
    copies = []
    for i, target in enumerate(targets):
        rows = pl.ds((i % pieces) * target.shape[0], target.shape[0])
        copies.append(
            pltpu.make_async_copy(sources[i // pieces].at[rows], target, sems.at[i])
        )
    for copy in copies:
        copy.start()
    for copy in copies:
        copy.wait()


def stage(*arrays, pieces=4):
    shapes = [(x.shape[0] // pieces,) + x.shape[1:] for x in arrays for _ in range(pieces)]
    return pl.pallas_call(
        functools.partial(stage_kernel, pieces),
        out_shape=tuple(pltpu.VMEM(shape, BF16) for shape in shapes),
        in_specs=[ANY_SPEC] * len(arrays),
        out_specs=(ANY_SPEC,) * len(shapes),
        scratch_shapes=[pltpu.SemaphoreType.DMA((len(shapes),))],
        compiler_params=params(MIB),
        cost_estimate=cost(0, sum(2 * x.size for x in arrays)),
        name="stage",
    )(*[in_hbm(x) for x in arrays])


def cache_kernel(pieces, index_ref, slot_hbm, select_hbm, *refs):
    sources, targets = refs[:2], refs[2 : 2 + 2 * pieces]
    near_ref, far_ref, slot_ref, select_ref, blocks_ref, sems = refs[2 + 2 * pieces :]
    count = 2 * pieces
    first = [
        pltpu.make_async_copy(slot_hbm, slot_ref, sems.at[count]),
        pltpu.make_async_copy(select_hbm, select_ref, sems.at[count + 1]),
    ]
    copies = []
    for i, target in enumerate(targets):
        rows = pl.ds((i % pieces) * target.shape[0], target.shape[0])
        copies.append(
            pltpu.make_async_copy(sources[i // pieces].at[rows], target, sems.at[i])
        )
    for copy in first + copies:
        copy.start()
    for copy in first:
        copy.wait()
    pages, total = blocks_ref.shape[2], slot_ref.shape[1]
    slots = index_ref[0] * pages + lax.broadcasted_iota(jnp.int32, (pages, total), 0)
    match = (slots == slot_ref[...]).astype(BF16)
    chosen = (select_ref[...] > 0).astype(BF16)
    held = lax.dot_general(
        chosen, match, (((1,), (1,)), ((), ())), preferred_element_type=F32
    )
    put_blocks(index_ref[0], held, blocks_ref, near_ref, far_ref)
    for copy in copies:
        copy.wait()


def stage_cache(index, page_cache_slot, selection, keys, values, mem_count, pieces=2):
    forks, total = selection.shape
    pages = keys.shape[0]
    line, fork_own = mem_count // 2, forks // mem_count
    shapes = [(x.shape[0] // pieces,) + x.shape[1:] for x in (keys, values) for _ in range(pieces)]
    mask = pltpu.VMEM((line, fork_own, pages), F32)
    return pl.pallas_call(
        functools.partial(cache_kernel, pieces),
        out_shape=tuple(pltpu.VMEM(shape, BF16) for shape in shapes) + (mask, mask),
        in_specs=[SMEM_SPEC] + [ANY_SPEC] * 4,
        out_specs=(ANY_SPEC,) * len(shapes) + (VMEM_SPEC,) * 2,
        scratch_shapes=[
            pltpu.VMEM((1, total), jnp.int32),
            pltpu.VMEM((forks, total), jnp.int32),
            pltpu.VMEM((mem_count, fork_own, pages), F32),
            pltpu.SemaphoreType.DMA((2 * pieces + 2,)),
        ],
        compiler_params=params(4 * MIB),
        cost_estimate=cost(0, 4 * keys.size),
        name="stage_cache",
    )(index, *[in_hbm(x) for x in (page_cache_slot.reshape(1, total), selection, keys, values)])


def fold_kernel(one_ref, two_ref, *out_refs):
    for i, out_ref in enumerate(out_refs):
        out_ref[...] = one_ref[i] + two_ref[i]


def fold(one, two):
    out = pltpu.VMEM(one.shape[1:], F32)
    return pl.pallas_call(
        fold_kernel,
        out_shape=(out,) * one.shape[0],
        in_specs=[VMEM_SPEC] * 2,
        out_specs=(VMEM_SPEC,) * one.shape[0],
        compiler_params=params(MIB * 2 + 16 * one.size),
        cost_estimate=cost(one.size, 12 * one.size),
        name="fold",
    )(in_vmem(one), two)


def two_first(terms):
    return [terms[i ^ (i >> 1)] for i in range(len(terms))]


def take_blocks(index, blocks_ref, near_ref, far_ref):
    place, parity = index // 2, index % 2
    for i in range(near_ref.shape[0]):
        at = 2 * (place ^ i)
        near_ref[i] = blocks_ref[at + parity]
        far_ref[i] = blocks_ref[at + 1 - parity]


def put_blocks(index, value, blocks_ref, near_ref, far_ref):
    count, rows, lanes = blocks_ref.shape
    own = value.shape[0] // count
    for i in range(count):
        blocks_ref[i, :own] = value[i * own : (i + 1) * own]
        if own < rows:
            blocks_ref[i, own:] = jnp.zeros((rows - own, lanes), F32)
    take_blocks(index, blocks_ref, near_ref, far_ref)


def first_kernel(
    index_ref,
    adapter_hbm,
    hidden_hbm,
    down_hbm,
    k_hbm,
    v_hbm,
    near_ref,
    far_ref,
    hidden_ref,
    adapter_ref,
    held,
    held_kv,
    rank_blocks,
    kv_blocks,
    sems,
):
    pieces, _, width = held.shape
    forks = hidden_ref.shape[0]
    kv_width = held_kv.shape[2]
    lanes = rank_blocks.shape[2]
    copies = [
        pltpu.make_async_copy(adapter_hbm, adapter_ref, sems.at[pieces + 3]),
        pltpu.make_async_copy(hidden_hbm, hidden_ref, sems.at[pieces + 2]),
        *[
            pltpu.make_async_copy(
                down_hbm.at[:, i * width : (i + 1) * width], held.at[i], sems.at[i]
            )
            for i in range(pieces)
        ],
        pltpu.make_async_copy(k_hbm, held_kv.at[0], sems.at[pieces]),
        pltpu.make_async_copy(v_hbm, held_kv.at[1], sems.at[pieces + 1]),
    ]
    for copy in copies:
        copy.start()
    copies[0].wait()
    fork_adapter = jnp.broadcast_to(adapter_ref[...].astype(F32), (HEAD_WIDTH, forks)).T
    lane_adapter = lax.broadcasted_iota(jnp.int32, (forks, HEAD_WIDTH), 1) // ADAPTER_RANK
    wanted = fork_adapter.astype(jnp.int32) - lane_adapter
    total = jnp.zeros((forks, HEAD_WIDTH), F32)
    copies[1].wait()
    for i in range(pieces):
        copies[2 + i].wait()
        block = jnp.dot(hidden_ref[...], held[i], preferred_element_type=F32)
        for j in range(width // HEAD_WIDTH):
            first = (i * width + j * HEAD_WIDTH) // ADAPTER_RANK
            part = block[:, j * HEAD_WIDTH : (j + 1) * HEAD_WIDTH]
            total += jnp.where(wanted == first, part, 0.0)
    flipped = total.T
    flipped = flipped[:ADAPTER_RANK] + flipped[ADAPTER_RANK:]
    if lanes > forks:
        flipped = jnp.concatenate([flipped, jnp.zeros((ADAPTER_RANK, lanes - forks), F32)], axis=1)
    at = slice(0, lanes)
    put_blocks(index_ref[0], flipped, rank_blocks, near_ref.at[:, :, at], far_ref.at[:, :, at])
    for i in range(2):
        copies[2 + pieces + i].wait()
        part = jnp.dot(hidden_ref[...], held_kv[i], preferred_element_type=F32)
        at = slice(lanes + i * kv_width, lanes + (i + 1) * kv_width)
        put_blocks(index_ref[0], part, kv_blocks, near_ref.at[:, :, at], far_ref.at[:, :, at])


def project_first(index, adapter, hidden, down, k_weight, v_weight, mem_count, width=256):
    forks, depth = hidden.shape
    columns, kv_width = down.shape[1], k_weight.shape[1]
    lanes = -(-forks // HEAD_WIDTH) * HEAD_WIDTH
    line, fork_own = mem_count // 2, forks // mem_count
    pieces = columns // width
    out = pltpu.VMEM((line, fork_own, lanes + 2 * kv_width), F32)
    weights = 2 * depth * (columns + 2 * kv_width)
    return pl.pallas_call(
        first_kernel,
        out_shape=(out, out, pltpu.VMEM(hidden.shape, BF16), pltpu.VMEM((1, forks), jnp.int32)),
        in_specs=[SMEM_SPEC] + [ANY_SPEC] * 5,
        out_specs=(VMEM_SPEC,) * 4,
        scratch_shapes=[
            pltpu.VMEM((pieces, depth, width), BF16),
            pltpu.VMEM((2, depth, kv_width), BF16),
            pltpu.VMEM((mem_count, fork_own, lanes), F32),
            pltpu.VMEM((mem_count, fork_own, kv_width), F32),
            pltpu.SemaphoreType.DMA((pieces + 4,)),
        ],
        compiler_params=params(weights + 4 * MIB),
        cost_estimate=cost(forks * weights, weights),
        name="project_first",
    )(index, *[in_hbm(x) for x in (adapter.reshape(1, forks), hidden, down, k_weight, v_weight)])


def project_kernel(start, extra, hidden_ref, q_hbm, *refs):
    up_hbm, part_ref, up_ref, held, sems = refs if extra else (None, refs[0], None, *refs[1:])
    pieces, _, width = held.shape
    copies = []
    for i in range(pieces):
        columns = pl.ds(start + i * width, width)
        copies.append(pltpu.make_async_copy(q_hbm.at[:, columns], held.at[i], sems.at[i]))
    if extra:
        copies.append(pltpu.make_async_copy(up_hbm, up_ref, sems.at[pieces]))
    for copy in copies:
        copy.start()
    for i in range(pieces):
        copies[i].wait()
        part_ref[:, i * width : (i + 1) * width] = jnp.dot(
            hidden_ref[...], held[i], preferred_element_type=F32
        )
    if extra:
        copies[-1].wait()


def project(hidden, q_weight, start, columns, up=None, width=256):
    forks, depth = hidden.shape
    pieces = columns // width
    weights = 2 * depth * columns
    extra = [] if up is None else [up]
    return pl.pallas_call(
        functools.partial(project_kernel, start, bool(extra)),
        out_shape=tuple(
            [pltpu.VMEM((forks, columns), F32)] + [pltpu.VMEM(x.shape, BF16) for x in extra]
        ),
        in_specs=[VMEM_SPEC] + [ANY_SPEC] * (1 + len(extra)),
        out_specs=(VMEM_SPEC,) * (1 + len(extra)),
        scratch_shapes=[
            pltpu.VMEM((pieces, depth, width), BF16),
            pltpu.SemaphoreType.DMA((pieces + 1,)),
        ],
        compiler_params=params(weights + 2 * MIB),
        cost_estimate=cost(forks * weights, weights + sum(2 * x.size for x in extra)),
        name="project",
    )(in_vmem(hidden), *[in_hbm(x) for x in [q_weight] + extra])


def line_sum_kernel(after_ref, *refs):
    parts, (own_ref, other_ref) = refs[:-2], refs[-2:]
    own_ref[...] = functools.reduce(jnp.add, [ref[0] for ref in parts])
    other_ref[...] = functools.reduce(jnp.add, [ref[1] for ref in parts])


def line_sum(parts, after):
    out = pltpu.VMEM(parts[0].shape[1:], F32)
    size = len(parts) * parts[0].size
    return pl.pallas_call(
        line_sum_kernel,
        out_shape=(out, out),
        in_specs=[ANY_SPEC] + [VMEM_SPEC] * len(parts),
        out_specs=(VMEM_SPEC,) * 2,
        compiler_params=params(2 * MIB + 8 * size),
        cost_estimate=cost(size, 4 * size),
        name="line_sum",
    )(after, *parts)


def join_kernel(first_ref, one_ref, two_ref, out_ref):
    cut = first_ref.shape[1]
    out_ref[:, :cut] = first_ref[...]
    out_ref[:, cut:] = (one_ref[...] + two_ref[...]).astype(BF16)


def join(first, one, two):
    rows, columns = first.shape[0], first.shape[1] + one.shape[1]
    return pl.pallas_call(
        join_kernel,
        out_shape=pltpu.VMEM((rows, columns), BF16),
        in_specs=[VMEM_SPEC] * 3,
        out_specs=VMEM_SPEC,
        compiler_params=params(MIB + 16 * rows * columns),
        cost_estimate=cost(one.size, 4 * rows * columns),
        name="join",
    )(first, in_vmem(one), two)


def delta_kernel(line, ranks, start, joint, index_ref, adapter_ref, *refs):
    first_refs = refs[:line]
    part_ref, up_ref, *out_refs, blocks_ref = refs[line:]
    forks, width = part_ref.shape[0], blocks_ref.shape[2]
    if joint:
        near_ref, far_ref = out_refs[0].at[:, 0], out_refs[0].at[:, 1]
        new_ref = out_refs[1]
        lanes = first_refs[0].shape[1] - new_ref.shape[1]
        total = functools.reduce(jnp.add, [ref[:, lanes:] for ref in first_refs])
        new_ref[...] = total.astype(BF16)
    else:
        near_ref, far_ref = out_refs
    acts = functools.reduce(jnp.add, [ref[:ranks, :forks] for ref in first_refs])
    acts = acts.astype(BF16).astype(F32)
    adapters = lax.broadcasted_iota(jnp.int32, (ADAPTER_COUNT, forks), 0)
    onehot = (adapters == adapter_ref[...]).astype(F32)
    spread = jnp.concatenate(
        [acts[r : r + 1, :] * onehot for r in range(ranks)], axis=0
    ).astype(BF16)
    for i in range(part_ref.shape[1] // width):
        delta = lax.dot_general(
            spread,
            up_ref[:, start + i * width : start + (i + 1) * width],
            (((0,), (0,)), ((), ())),
            preferred_element_type=F32,
        )
        at = slice(i * width, (i + 1) * width)
        put_blocks(
            index_ref[0],
            part_ref[:, at] + delta,
            blocks_ref,
            near_ref.at[:, :, at],
            far_ref.at[:, :, at],
        )


def add_delta(index, adapter, first_parts, part, up, mem_count, start, new_width=0, width=256):
    forks, columns = part.shape
    line, fork_own = mem_count // 2, forks // mem_count
    ranks = ADAPTER_RANK // mem_count
    if new_width:
        out = (
            pltpu.VMEM((line, 2, fork_own, columns), F32),
            pltpu.VMEM((fork_own, new_width), BF16),
        )
    else:
        out = (pltpu.VMEM((line, fork_own, columns), F32),) * 2
    return pl.pallas_call(
        functools.partial(delta_kernel, line, ranks, start, new_width > 0),
        out_shape=out,
        in_specs=[SMEM_SPEC] + [VMEM_SPEC] * (line + 3),
        out_specs=(VMEM_SPEC,) * 2,
        scratch_shapes=[pltpu.VMEM((mem_count, fork_own, width), F32)],
        compiler_params=params(4 * MIB),
        cost_estimate=cost(
            2 * forks * up.shape[0] * columns, 2 * up.shape[0] * columns + 8 * forks * columns
        ),
        name="add_delta",
    )(index, in_vmem(adapter), *first_parts, in_vmem(part), in_vmem(up))


def put_terms(lse):
    heads, forks = lse.shape
    high = lse.astype(BF16).astype(F32)
    rest = lse - high
    middle = rest.astype(BF16).astype(F32)
    low = rest - middle
    spare = jnp.zeros((HEAD_WIDTH - 3 * heads, forks), F32)
    return jnp.concatenate([high, middle, low, spare], axis=0).T.astype(BF16)


def get_terms(terms, heads):
    terms = terms.astype(F32)
    return terms[:, :heads] + terms[:, heads : 2 * heads] + terms[:, 2 * heads : 3 * heads]


def attend_kernel(pieces, q_ref, mask_ref, *refs):
    k_refs, v_refs, (out_ref, score_ref, lse_ref) = (
        refs[:pieces],
        refs[pieces : 2 * pieces],
        refs[2 * pieces :],
    )
    forks = q_ref.shape[0]
    kv_local, group = lse_ref.shape[:2]
    pages = score_ref.shape[0] // 2
    held = pages // pieces
    scale = SCORE_SCALE * LOG2E
    chosen_by = mask_ref[...].reshape(forks, pages)
    spare = jnp.zeros((forks, HEAD_WIDTH - pages % HEAD_WIDTH), F32)
    chosen_by = jnp.concatenate([chosen_by, spare], axis=1).T[:pages]
    mask = jnp.concatenate([chosen_by] * group, axis=1) > 0
    ones = jnp.ones((8, score_ref.shape[1]), BF16)

    def score(kv_head, queries, p):
        lanes = slice(kv_head * HEAD_WIDTH, (kv_head + 1) * HEAD_WIDTH)
        scores = lax.dot_general(
            k_refs[p // held][p % held, :, lanes],
            queries,
            (((1,), (1,)), ((), ())),
            preferred_element_type=F32,
        )
        score_ref[kv_head % 2 * pages + p] = scores
        return jnp.max(scores, axis=0, keepdims=True)

    def term(kv_head, peaks, top, p):
        lanes = slice(kv_head * HEAD_WIDTH, (kv_head + 1) * HEAD_WIDTH)
        scores = score_ref[kv_head % 2 * pages + p]
        weights = jnp.exp2((scores - peaks[p]) * scale).astype(BF16)
        chosen = jnp.where(mask[p : p + 1], peaks[p], neg_floor)
        factor = jnp.where(mask[p : p + 1], jnp.exp2((chosen - top) * scale), 0.0)
        values = jnp.concatenate([v_refs[p // held][p % held, :, lanes].T, ones], axis=0)
        return jnp.dot(values, weights, preferred_element_type=F32) * factor

    def head_queries(kv_head):
        first = kv_head * group
        return jnp.concatenate(
            [
                q_ref[:, (first + g) * HEAD_WIDTH : (first + g + 1) * HEAD_WIDTH]
                for g in range(group)
            ],
            axis=0,
        )

    queries = head_queries(0)
    peaks = [score(0, queries, p) for p in range(pages)]
    for kv_head in range(kv_local):
        chosen = [jnp.where(mask[p : p + 1], peaks[p], neg_floor) for p in range(pages)]
        top = functools.reduce(jnp.maximum, chosen)
        if kv_head + 1 < kv_local:
            queries = head_queries(kv_head + 1)
        acc = None
        next_peaks = []
        for p in range(pages):
            if kv_head + 1 < kv_local:
                next_peaks.append(score(kv_head + 1, queries, p))
            part = term(kv_head, peaks, top, p)
            acc = part if acc is None else acc + part
        peaks = next_peaks
        mass = acc[HEAD_WIDTH : HEAD_WIDTH + 1]
        some = mass > 0
        safe = jnp.where(some, mass, 1.0)
        rows = (acc[:HEAD_WIDTH] * jnp.where(some, 1.0 / safe, 0.0)).T
        lse = jnp.where(some, top * scale + jnp.log2(safe), neg_floor)
        for g in range(group):
            at = (kv_head * group + g) * HEAD_WIDTH
            out_ref[:, at : at + HEAD_WIDTH] = rows[g * forks : (g + 1) * forks].astype(BF16)
        lse_ref[kv_head] = jnp.concatenate(
            [lse[:, g * forks : (g + 1) * forks] for g in range(group)], axis=0
        )

    heads = kv_local * group
    out_ref[:, heads * HEAD_WIDTH :] = put_terms(lse_ref[...].reshape(heads, forks))


def attend(queries, keys, values, mask):
    forks, width = queries.shape
    held, page_len, kv_width = keys[0].shape
    pieces = len(keys)
    pages = held * pieces
    kv_local = kv_width // HEAD_WIDTH
    group = width // kv_width
    rows = group * forks
    return pl.pallas_call(
        functools.partial(attend_kernel, pieces),
        out_shape=pltpu.VMEM((forks, width + HEAD_WIDTH), BF16),
        in_specs=[VMEM_SPEC] * (2 + 2 * pieces),
        out_specs=VMEM_SPEC,
        scratch_shapes=[
            pltpu.VMEM((2 * pages, page_len, rows), F32),
            pltpu.VMEM((kv_local, group, forks), F32),
        ],
        compiler_params=params(10 * pages * page_len * rows + 4 * MIB),
        cost_estimate=cost(
            4 * pages * page_len * kv_local * rows * HEAD_WIDTH,
            4 * pages * page_len * kv_width + 4 * forks * width,
            pages * page_len * kv_local * rows,
        ),
        name="attend",
    )(queries, *[in_vmem(x) for x in [mask, *keys, *values]])


def merge_kernel(heads, kv_heads, sources, *refs):
    parts, (q_ref, new_ref, out_ref) = refs[:sources], refs[sources:]
    group = heads // kv_heads
    width = heads * HEAD_WIDTH
    lses = [get_terms(ref[:, width : width + HEAD_WIDTH], heads) for ref in parts]

    def new_head(i):
        return new_ref[:, i * HEAD_WIDTH : (i + 1) * HEAD_WIDTH].astype(F32)

    scores = []
    for h in range(heads):
        query = q_ref[:, h * HEAD_WIDTH : (h + 1) * HEAD_WIDTH].astype(F32)
        scores.append(jnp.sum(query * new_head(h // group), axis=1, keepdims=True))
    own = jnp.concatenate(scores, axis=1) * (SCORE_SCALE * LOG2E)
    top = functools.reduce(jnp.maximum, lses, own)
    own_weight = jnp.exp2(own - top)
    weights = [jnp.exp2(lse - top) for lse in lses]
    inverse = 1.0 / functools.reduce(jnp.add, weights, own_weight)
    own_weight = own_weight * inverse
    weights = [weight * inverse for weight in weights]
    for h in range(heads):
        lanes = slice(h * HEAD_WIDTH, (h + 1) * HEAD_WIDTH)
        total = own_weight[:, h : h + 1] * new_head(kv_heads + h // group)
        for weight, ref in zip(weights, parts):
            total += weight[:, h : h + 1] * ref[:, lanes].astype(F32)
        out_ref[:, lanes] = total.astype(BF16)


def merge(parts, queries, new, heads, kv_heads):
    fork_own, width = parts[0].shape
    size = len(parts) * fork_own * width
    return pl.pallas_call(
        functools.partial(merge_kernel, heads, kv_heads, len(parts)),
        out_shape=jax.ShapeDtypeStruct((fork_own, heads * HEAD_WIDTH), BF16),
        compiler_params=params(4 * size + 4 * MIB),
        cost_estimate=pl.CostEstimate(flops=4 * size, bytes_accessed=2 * size, transcendentals=0),
        name="merge",
    )(*parts, queries, new)


def output_kernel(context_ref, *refs):
    weight_refs, out_ref = refs[:-1], refs[-1]
    total = None
    for i, ref in enumerate(weight_refs):
        depth = ref.shape[0]
        part = jnp.dot(
            context_ref[:, i * depth : (i + 1) * depth], ref[...], preferred_element_type=F32
        )
        total = part if total is None else total + part
    out_ref[...] = total


def output_project(context, weights):
    forks, rows = context.shape
    columns = weights[0].shape[1]
    return pl.pallas_call(
        output_kernel,
        out_shape=pltpu.VMEM((forks, columns), F32),
        in_specs=[VMEM_SPEC] * (1 + len(weights)),
        out_specs=VMEM_SPEC,
        compiler_params=params(4 * MIB),
        cost_estimate=cost(2 * forks * rows * columns, 2 * rows * columns),
        name="output_project",
    )(context, *[in_vmem(x) for x in weights])


def finish_kernel(count, line, index_ref, *refs):
    near_refs, far_refs, out_ref = refs[:count], refs[count : 2 * count], refs[-1]
    place, parity = index_ref[0] // 2, index_ref[0] % 2
    rows = out_ref.shape[1]
    for group, side in ((near_refs, parity), (far_refs, 1 - parity)):
        for i in range(line):
            total = functools.reduce(jnp.add, [ref[i * rows : (i + 1) * rows] for ref in group])
            out_ref[2 * (place ^ i) + side] = total.astype(BF16)


def finish(index, near, far, mem_count):
    rows, columns = near[0].shape
    line = mem_count // 2
    return pl.pallas_call(
        functools.partial(finish_kernel, len(near), line),
        out_shape=jax.ShapeDtypeStruct((mem_count, rows // line, columns), BF16),
        in_specs=[SMEM_SPEC] + [VMEM_SPEC] * (2 * len(near)),
        out_specs=VMEM_SPEC,
        compiler_params=params(4 * MIB),
        cost_estimate=cost(0, 8 * rows * columns * len(near)),
        name="finish",
    )(index, *near, *far)


def shards(
    hidden,
    adapter,
    page_cache_slot,
    selection,
    query_projection_weight,
    key_projection_weight,
    value_projection_weight,
    adapter_down_weight,
    adapter_up_weight,
    output_projection_weight,
    prefix_key_cache,
    prefix_value_cache,
):
    mem_count = lax.axis_size("mem")
    mem_index = lax.axis_index("mem")
    forks = hidden.shape[0]
    fork_own = forks // mem_count
    q_width = query_projection_weight.shape[1]
    kv_width = key_projection_weight.shape[1]
    heads, kv_heads = q_width // HEAD_WIDTH, kv_width // HEAD_WIDTH
    pages = prefix_key_cache.shape[0]
    line = mem_count // 2
    index = mem_index.reshape(1)
    place, parity = mem_index // 2, mem_index % 2

    def swapped(x, step, cross=0):
        pairs = [(i, i ^ (2 * step + cross)) for i in range(mem_count)]
        return lax.ppermute(x, "mem", pairs)

    def along(blocks, cross=0):
        return [
            swapped(blocks[i], i, cross) if i or cross else blocks[0] for i in range(line)
        ]

    def gather(x):
        return jnp.concatenate([x] + [swapped(x, i) for i in range(1, line)], axis=0)

    def pair(x):
        return swapped(x, 0, 1)

    near_1, far_1, hidden, adapter = project_first(
        index, adapter, hidden, adapter_down_weight, key_projection_weight, value_projection_weight, mem_count
    )
    cut = q_width * 10 // 16 // 256 * 256
    part_a, up = project(
        hidden, query_projection_weight, 0, cut, adapter_up_weight.reshape(-1, q_width)
    )
    first_parts = fold(near_1, pair(far_1))
    first_parts, part_a, hidden = lax.optimization_barrier((first_parts, part_a, hidden))
    (part_b,) = project(hidden, query_projection_weight, cut, q_width - cut)
    first_parts = two_first(along(first_parts))[::-1]

    near_a, far_a = add_delta(index, adapter, first_parts, part_a, up, mem_count, 0)
    near_a, far_a, part_b = lax.optimization_barrier((near_a, far_a, part_b))
    both_b, own_new = add_delta(
        index, adapter, first_parts, part_b, up, mem_count, cut, 2 * kv_width
    )
    sums_a = fold(near_a, pair(far_a))
    own_b, other_b = line_sum(two_first(along(both_b)), sums_a[0])
    own_a = functools.reduce(jnp.add, along(sums_a)[::-1]).astype(BF16)
    own_queries = join(own_a, own_b, pair(other_b))

    *staged, near_mask, far_mask = stage_cache(
        index, page_cache_slot, selection, prefix_key_cache, prefix_value_cache, mem_count
    )
    keys, values = staged[: len(staged) // 2], staged[len(staged) // 2 :]
    near_queries = gather(own_queries)
    far_queries = pair(near_queries)
    near = attend(near_queries, keys, values, near_mask)
    far = attend(far_queries, keys, values, far_mask)
    blocks = (line, fork_own, q_width + HEAD_WIDTH)
    parts = along(near.reshape(blocks)) + along(far.reshape(blocks), 1)
    context_own = merge(parts, own_queries, own_new, heads, kv_heads)

    out_weights = stage(output_projection_weight)
    near_context = gather(context_own)
    far_context = pair(near_context)
    tp_count = lax.axis_size("tp")
    outs = []
    for context in (near_context, far_context):
        part = output_project(context, out_weights)
        terms = [part]
        for shift in range(1, tp_count):
            pairs = [(i, (i + shift) % tp_count) for i in range(tp_count)]
            terms.append(lax.ppermute(part, "tp", pairs))
        outs.append(terms)
    return finish(index, *outs, mem_count).reshape(forks, -1)


def solution(mesh):
    return jax.shard_map(
        shards,
        mesh=mesh,
        in_specs=(
            P("groups", "mem"),
            P("groups"),
            P("groups"),
            P("groups", None),
            P("mem", "tp"),
            P("mem", "tp"),
            P("mem", "tp"),
            P("mem", None),
            P("mem", None, "tp"),
            P("tp", "mem"),
            P(("groups", "mem"), None, "tp"),
            P(("groups", "mem"), None, "tp"),
        ),
        out_specs=P("groups", "mem"),
        check_vma=False,
    )
```

```python
import functools

import jax
import jax.numpy as jnp
from jax import lax
from jax.experimental import pallas as pl
from jax.experimental.pallas import tpu as pltpu
from jax.sharding import PartitionSpec as P

HEAD_WIDTH = 128
ADAPTER_RANK = 64
ADAPTER_COUNT = 32
LOG2E = 1.4426950408889634
SCORE_SCALE = HEAD_WIDTH ** (-0.5)
neg_floor = -1e30
MIB = 1024 * 1024
F32 = jnp.float32
BF16 = jnp.bfloat16


def params(limit, *semantics):
    return pltpu.CompilerParams(
        dimension_semantics=semantics or None, vmem_limit_bytes=int(limit)
    )


def whole(shape):
    return pl.BlockSpec(shape, lambda *_: (0,) * len(shape))


def in_hbm(x):
    return pltpu.with_memory_space_constraint(x, pltpu.HBM)


def in_vmem(x):
    return pltpu.with_memory_space_constraint(x, pltpu.VMEM)


def cost(flops, size, transcendentals=0):
    return pl.CostEstimate(
        flops=int(flops), bytes_accessed=int(size), transcendentals=int(transcendentals)
    )


VMEM_SPEC = pl.BlockSpec(memory_space=pltpu.VMEM)
SMEM_SPEC = pl.BlockSpec(memory_space=pltpu.SMEM)
ANY_SPEC = pl.BlockSpec(memory_space=pl.ANY)


def stage_kernel(pieces, *refs):
    count = len(refs[:-1]) // (pieces + 1)
    sources, targets, sems = refs[:count], refs[count:-1], refs[-1]
    copies = []
    for i, target in enumerate(targets):
        rows = pl.ds((i % pieces) * target.shape[0], target.shape[0])
        copies.append(
            pltpu.make_async_copy(sources[i // pieces].at[rows], target, sems.at[i])
        )
    for copy in copies:
        copy.start()
    for copy in copies:
        copy.wait()


def stage(*arrays, pieces=4):
    shapes = [(x.shape[0] // pieces,) + x.shape[1:] for x in arrays for _ in range(pieces)]
    return pl.pallas_call(
        functools.partial(stage_kernel, pieces),
        out_shape=tuple(pltpu.VMEM(shape, BF16) for shape in shapes),
        in_specs=[ANY_SPEC] * len(arrays),
        out_specs=(ANY_SPEC,) * len(shapes),
        scratch_shapes=[pltpu.SemaphoreType.DMA((len(shapes),))],
        compiler_params=params(MIB),
        cost_estimate=cost(0, sum(2 * x.size for x in arrays)),
        name="stage",
    )(*[in_hbm(x) for x in arrays])


def cache_kernel(pieces, index_ref, slot_hbm, select_hbm, *refs):
    sources, targets = refs[:2], refs[2 : 2 + 2 * pieces]
    near_ref, far_ref, slot_ref, select_ref, blocks_ref, sems = refs[2 + 2 * pieces :]
    count = 2 * pieces
    first = [
        pltpu.make_async_copy(slot_hbm, slot_ref, sems.at[count]),
        pltpu.make_async_copy(select_hbm, select_ref, sems.at[count + 1]),
    ]
    copies = []
    for i, target in enumerate(targets):
        rows = pl.ds((i % pieces) * target.shape[0], target.shape[0])
        copies.append(
            pltpu.make_async_copy(sources[i // pieces].at[rows], target, sems.at[i])
        )
    for copy in first + copies:
        copy.start()
    for copy in first:
        copy.wait()
    pages, total = blocks_ref.shape[2], slot_ref.shape[1]
    slots = index_ref[0] * pages + lax.broadcasted_iota(jnp.int32, (pages, total), 0)
    match = (slots == slot_ref[...]).astype(BF16)
    chosen = (select_ref[...] > 0).astype(BF16)
    held = lax.dot_general(
        chosen, match, (((1,), (1,)), ((), ())), preferred_element_type=F32
    )
    put_blocks(index_ref[0], held, blocks_ref, near_ref, far_ref)
    for copy in copies:
        copy.wait()


def stage_cache(index, page_cache_slot, selection, keys, values, mem_count, pieces=2):
    forks, total = selection.shape
    pages = keys.shape[0]
    line, fork_own = mem_count // 2, forks // mem_count
    shapes = [(x.shape[0] // pieces,) + x.shape[1:] for x in (keys, values) for _ in range(pieces)]
    mask = pltpu.VMEM((line, fork_own, pages), F32)
    return pl.pallas_call(
        functools.partial(cache_kernel, pieces),
        out_shape=tuple(pltpu.VMEM(shape, BF16) for shape in shapes) + (mask, mask),
        in_specs=[SMEM_SPEC] + [ANY_SPEC] * 4,
        out_specs=(ANY_SPEC,) * len(shapes) + (VMEM_SPEC,) * 2,
        scratch_shapes=[
            pltpu.VMEM((1, total), jnp.int32),
            pltpu.VMEM((forks, total), jnp.int32),
            pltpu.VMEM((mem_count, fork_own, pages), F32),
            pltpu.SemaphoreType.DMA((2 * pieces + 2,)),
        ],
        compiler_params=params(4 * MIB),
        cost_estimate=cost(0, 4 * keys.size),
        name="stage_cache",
    )(index, *[in_hbm(x) for x in (page_cache_slot.reshape(1, total), selection, keys, values)])


def fold_kernel(one_ref, two_ref, *out_refs):
    for i, out_ref in enumerate(out_refs):
        out_ref[...] = one_ref[i] + two_ref[i]


def fold(one, two):
    out = pltpu.VMEM(one.shape[1:], F32)
    return pl.pallas_call(
        fold_kernel,
        out_shape=(out,) * one.shape[0],
        in_specs=[VMEM_SPEC] * 2,
        out_specs=(VMEM_SPEC,) * one.shape[0],
        compiler_params=params(MIB * 2 + 16 * one.size),
        cost_estimate=cost(one.size, 12 * one.size),
        name="fold",
    )(in_vmem(one), two)


def two_first(terms):
    return [terms[i ^ (i >> 1)] for i in range(len(terms))]


def take_blocks(index, blocks_ref, near_ref, far_ref):
    place, parity = index // 2, index % 2
    for i in range(near_ref.shape[0]):
        at = 2 * (place ^ i)
        near_ref[i] = blocks_ref[at + parity]
        far_ref[i] = blocks_ref[at + 1 - parity]


def put_blocks(index, value, blocks_ref, near_ref, far_ref):
    count, rows, lanes = blocks_ref.shape
    own = value.shape[0] // count
    for i in range(count):
        blocks_ref[i, :own] = value[i * own : (i + 1) * own]
        if own < rows:
            blocks_ref[i, own:] = jnp.zeros((rows - own, lanes), F32)
    take_blocks(index, blocks_ref, near_ref, far_ref)


def first_kernel(
    index_ref,
    adapter_hbm,
    hidden_hbm,
    down_hbm,
    k_hbm,
    v_hbm,
    near_ref,
    far_ref,
    hidden_ref,
    adapter_ref,
    held,
    held_kv,
    rank_blocks,
    kv_blocks,
    sems,
):
    pieces, _, width = held.shape
    forks = hidden_ref.shape[0]
    kv_width = held_kv.shape[2]
    lanes = rank_blocks.shape[2]
    copies = [
        pltpu.make_async_copy(adapter_hbm, adapter_ref, sems.at[pieces + 3]),
        pltpu.make_async_copy(hidden_hbm, hidden_ref, sems.at[pieces + 2]),
        *[
            pltpu.make_async_copy(
                down_hbm.at[:, i * width : (i + 1) * width], held.at[i], sems.at[i]
            )
            for i in range(pieces)
        ],
        pltpu.make_async_copy(k_hbm, held_kv.at[0], sems.at[pieces]),
        pltpu.make_async_copy(v_hbm, held_kv.at[1], sems.at[pieces + 1]),
    ]
    for copy in copies:
        copy.start()
    copies[0].wait()
    fork_adapter = jnp.broadcast_to(adapter_ref[...].astype(F32), (HEAD_WIDTH, forks)).T
    lane_adapter = lax.broadcasted_iota(jnp.int32, (forks, HEAD_WIDTH), 1) // ADAPTER_RANK
    wanted = fork_adapter.astype(jnp.int32) - lane_adapter
    total = jnp.zeros((forks, HEAD_WIDTH), F32)
    copies[1].wait()
    for i in range(pieces):
        copies[2 + i].wait()
        block = jnp.dot(hidden_ref[...], held[i], preferred_element_type=F32)
        for j in range(width // HEAD_WIDTH):
            first = (i * width + j * HEAD_WIDTH) // ADAPTER_RANK
            part = block[:, j * HEAD_WIDTH : (j + 1) * HEAD_WIDTH]
            total += jnp.where(wanted == first, part, 0.0)
    flipped = total.T
    flipped = flipped[:ADAPTER_RANK] + flipped[ADAPTER_RANK:]
    if lanes > forks:
        flipped = jnp.concatenate([flipped, jnp.zeros((ADAPTER_RANK, lanes - forks), F32)], axis=1)
    at = slice(0, lanes)
    put_blocks(index_ref[0], flipped, rank_blocks, near_ref.at[:, :, at], far_ref.at[:, :, at])
    for i in range(2):
        copies[2 + pieces + i].wait()
        part = jnp.dot(hidden_ref[...], held_kv[i], preferred_element_type=F32)
        at = slice(lanes + i * kv_width, lanes + (i + 1) * kv_width)
        put_blocks(index_ref[0], part, kv_blocks, near_ref.at[:, :, at], far_ref.at[:, :, at])


def project_first(index, adapter, hidden, down, k_weight, v_weight, mem_count, width=256):
    forks, depth = hidden.shape
    columns, kv_width = down.shape[1], k_weight.shape[1]
    lanes = -(-forks // HEAD_WIDTH) * HEAD_WIDTH
    line, fork_own = mem_count // 2, forks // mem_count
    pieces = columns // width
    out = pltpu.VMEM((line, fork_own, lanes + 2 * kv_width), F32)
    weights = 2 * depth * (columns + 2 * kv_width)
    return pl.pallas_call(
        first_kernel,
        out_shape=(out, out, pltpu.VMEM(hidden.shape, BF16), pltpu.VMEM((1, forks), jnp.int32)),
        in_specs=[SMEM_SPEC] + [ANY_SPEC] * 5,
        out_specs=(VMEM_SPEC,) * 4,
        scratch_shapes=[
            pltpu.VMEM((pieces, depth, width), BF16),
            pltpu.VMEM((2, depth, kv_width), BF16),
            pltpu.VMEM((mem_count, fork_own, lanes), F32),
            pltpu.VMEM((mem_count, fork_own, kv_width), F32),
            pltpu.SemaphoreType.DMA((pieces + 4,)),
        ],
        compiler_params=params(weights + 4 * MIB),
        cost_estimate=cost(forks * weights, weights),
        name="project_first",
    )(index, *[in_hbm(x) for x in (adapter.reshape(1, forks), hidden, down, k_weight, v_weight)])


def project_kernel(start, extra, hidden_ref, q_hbm, *refs):
    up_hbm, part_ref, up_ref, held, sems = refs if extra else (None, refs[0], None, *refs[1:])
    pieces, _, width = held.shape
    copies = []
    for i in range(pieces):
        columns = pl.ds(start + i * width, width)
        copies.append(pltpu.make_async_copy(q_hbm.at[:, columns], held.at[i], sems.at[i]))
    if extra:
        copies.append(pltpu.make_async_copy(up_hbm, up_ref, sems.at[pieces]))
    for copy in copies:
        copy.start()
    for i in range(pieces):
        copies[i].wait()
        part_ref[:, i * width : (i + 1) * width] = jnp.dot(
            hidden_ref[...], held[i], preferred_element_type=F32
        )
    if extra:
        copies[-1].wait()


def project(hidden, q_weight, start, columns, up=None, width=256):
    forks, depth = hidden.shape
    pieces = columns // width
    weights = 2 * depth * columns
    extra = [] if up is None else [up]
    return pl.pallas_call(
        functools.partial(project_kernel, start, bool(extra)),
        out_shape=tuple(
            [pltpu.VMEM((forks, columns), F32)] + [pltpu.VMEM(x.shape, BF16) for x in extra]
        ),
        in_specs=[VMEM_SPEC] + [ANY_SPEC] * (1 + len(extra)),
        out_specs=(VMEM_SPEC,) * (1 + len(extra)),
        scratch_shapes=[
            pltpu.VMEM((pieces, depth, width), BF16),
            pltpu.SemaphoreType.DMA((pieces + 1,)),
        ],
        compiler_params=params(weights + 2 * MIB),
        cost_estimate=cost(forks * weights, weights + sum(2 * x.size for x in extra)),
        name="project",
    )(in_vmem(hidden), *[in_hbm(x) for x in [q_weight] + extra])


def line_sum_kernel(after_ref, *refs):
    parts, (own_ref, other_ref) = refs[:-2], refs[-2:]
    own_ref[...] = functools.reduce(jnp.add, [ref[0] for ref in parts])
    other_ref[...] = functools.reduce(jnp.add, [ref[1] for ref in parts])


def line_sum(parts, after):
    out = pltpu.VMEM(parts[0].shape[1:], F32)
    size = len(parts) * parts[0].size
    return pl.pallas_call(
        line_sum_kernel,
        out_shape=(out, out),
        in_specs=[ANY_SPEC] + [VMEM_SPEC] * len(parts),
        out_specs=(VMEM_SPEC,) * 2,
        compiler_params=params(2 * MIB + 8 * size),
        cost_estimate=cost(size, 4 * size),
        name="line_sum",
    )(after, *parts)


def join_kernel(first_ref, one_ref, two_ref, out_ref):
    cut = first_ref.shape[1]
    out_ref[:, :cut] = first_ref[...]
    out_ref[:, cut:] = (one_ref[...] + two_ref[...]).astype(BF16)


def join(first, one, two):
    rows, columns = first.shape[0], first.shape[1] + one.shape[1]
    return pl.pallas_call(
        join_kernel,
        out_shape=pltpu.VMEM((rows, columns), BF16),
        in_specs=[VMEM_SPEC] * 3,
        out_specs=VMEM_SPEC,
        compiler_params=params(MIB + 16 * rows * columns),
        cost_estimate=cost(one.size, 4 * rows * columns),
        name="join",
    )(first, in_vmem(one), two)


def delta_kernel(line, ranks, start, joint, index_ref, adapter_ref, *refs):
    first_refs = refs[:line]
    part_ref, up_ref, *out_refs, blocks_ref = refs[line:]
    forks, width = part_ref.shape[0], blocks_ref.shape[2]
    if joint:
        near_ref, far_ref = out_refs[0].at[:, 0], out_refs[0].at[:, 1]
        new_ref = out_refs[1]
        lanes = first_refs[0].shape[1] - new_ref.shape[1]
        total = functools.reduce(jnp.add, [ref[:, lanes:] for ref in first_refs])
        new_ref[...] = total.astype(BF16)
    else:
        near_ref, far_ref = out_refs
    acts = functools.reduce(jnp.add, [ref[:ranks, :forks] for ref in first_refs])
    acts = acts.astype(BF16).astype(F32)
    adapters = lax.broadcasted_iota(jnp.int32, (ADAPTER_COUNT, forks), 0)
    onehot = (adapters == adapter_ref[...]).astype(F32)
    spread = jnp.concatenate(
        [acts[r : r + 1, :] * onehot for r in range(ranks)], axis=0
    ).astype(BF16)
    for i in range(part_ref.shape[1] // width):
        delta = lax.dot_general(
            spread,
            up_ref[:, start + i * width : start + (i + 1) * width],
            (((0,), (0,)), ((), ())),
            preferred_element_type=F32,
        )
        at = slice(i * width, (i + 1) * width)
        put_blocks(
            index_ref[0],
            part_ref[:, at] + delta,
            blocks_ref,
            near_ref.at[:, :, at],
            far_ref.at[:, :, at],
        )


def add_delta(index, adapter, first_parts, part, up, mem_count, start, new_width=0, width=256):
    forks, columns = part.shape
    line, fork_own = mem_count // 2, forks // mem_count
    ranks = ADAPTER_RANK // mem_count
    if new_width:
        out = (
            pltpu.VMEM((line, 2, fork_own, columns), F32),
            pltpu.VMEM((fork_own, new_width), BF16),
        )
    else:
        out = (pltpu.VMEM((line, fork_own, columns), F32),) * 2
    return pl.pallas_call(
        functools.partial(delta_kernel, line, ranks, start, new_width > 0),
        out_shape=out,
        in_specs=[SMEM_SPEC] + [VMEM_SPEC] * (line + 3),
        out_specs=(VMEM_SPEC,) * 2,
        scratch_shapes=[pltpu.VMEM((mem_count, fork_own, width), F32)],
        compiler_params=params(4 * MIB),
        cost_estimate=cost(
            2 * forks * up.shape[0] * columns, 2 * up.shape[0] * columns + 8 * forks * columns
        ),
        name="add_delta",
    )(index, in_vmem(adapter), *first_parts, in_vmem(part), in_vmem(up))


def put_terms(lse):
    heads, forks = lse.shape
    high = lse.astype(BF16).astype(F32)
    rest = lse - high
    middle = rest.astype(BF16).astype(F32)
    low = rest - middle
    spare = jnp.zeros((HEAD_WIDTH - 3 * heads, forks), F32)
    return jnp.concatenate([high, middle, low, spare], axis=0).T.astype(BF16)


def get_terms(terms, heads):
    terms = terms.astype(F32)
    return terms[:, :heads] + terms[:, heads : 2 * heads] + terms[:, 2 * heads : 3 * heads]


def attend_kernel(pieces, q_ref, mask_ref, *refs):
    k_refs, v_refs, (out_ref, score_ref, lse_ref) = (
        refs[:pieces],
        refs[pieces : 2 * pieces],
        refs[2 * pieces :],
    )
    forks = q_ref.shape[0]
    kv_local, group = lse_ref.shape[:2]
    pages = score_ref.shape[0] // 2
    held = pages // pieces
    scale = SCORE_SCALE * LOG2E
    chosen_by = mask_ref[...].reshape(forks, pages)
    spare = jnp.zeros((forks, HEAD_WIDTH - pages % HEAD_WIDTH), F32)
    chosen_by = jnp.concatenate([chosen_by, spare], axis=1).T[:pages]
    mask = jnp.concatenate([chosen_by] * group, axis=1) > 0
    ones = jnp.ones((8, score_ref.shape[1]), BF16)

    def score(kv_head, queries, p):
        lanes = slice(kv_head * HEAD_WIDTH, (kv_head + 1) * HEAD_WIDTH)
        scores = lax.dot_general(
            k_refs[p // held][p % held, :, lanes],
            queries,
            (((1,), (1,)), ((), ())),
            preferred_element_type=F32,
        )
        score_ref[kv_head % 2 * pages + p] = scores
        return jnp.max(scores, axis=0, keepdims=True)

    def term(kv_head, peaks, top, p):
        lanes = slice(kv_head * HEAD_WIDTH, (kv_head + 1) * HEAD_WIDTH)
        scores = score_ref[kv_head % 2 * pages + p]
        weights = jnp.exp2((scores - peaks[p]) * scale).astype(BF16)
        chosen = jnp.where(mask[p : p + 1], peaks[p], neg_floor)
        factor = jnp.where(mask[p : p + 1], jnp.exp2((chosen - top) * scale), 0.0)
        values = jnp.concatenate([v_refs[p // held][p % held, :, lanes].T, ones], axis=0)
        return jnp.dot(values, weights, preferred_element_type=F32) * factor

    def head_queries(kv_head):
        first = kv_head * group
        return jnp.concatenate(
            [
                q_ref[:, (first + g) * HEAD_WIDTH : (first + g + 1) * HEAD_WIDTH]
                for g in range(group)
            ],
            axis=0,
        )

    queries = head_queries(0)
    peaks = [score(0, queries, p) for p in range(pages)]
    for kv_head in range(kv_local):
        chosen = [jnp.where(mask[p : p + 1], peaks[p], neg_floor) for p in range(pages)]
        top = functools.reduce(jnp.maximum, chosen)
        if kv_head + 1 < kv_local:
            queries = head_queries(kv_head + 1)
        acc = None
        next_peaks = []
        for p in range(pages):
            if kv_head + 1 < kv_local:
                next_peaks.append(score(kv_head + 1, queries, p))
            part = term(kv_head, peaks, top, p)
            acc = part if acc is None else acc + part
        peaks = next_peaks
        mass = acc[HEAD_WIDTH : HEAD_WIDTH + 1]
        some = mass > 0
        safe = jnp.where(some, mass, 1.0)
        rows = (acc[:HEAD_WIDTH] * jnp.where(some, 1.0 / safe, 0.0)).T
        lse = jnp.where(some, top * scale + jnp.log2(safe), neg_floor)
        for g in range(group):
            at = (kv_head * group + g) * HEAD_WIDTH
            out_ref[:, at : at + HEAD_WIDTH] = rows[g * forks : (g + 1) * forks].astype(BF16)
        lse_ref[kv_head] = jnp.concatenate(
            [lse[:, g * forks : (g + 1) * forks] for g in range(group)], axis=0
        )

    heads = kv_local * group
    out_ref[:, heads * HEAD_WIDTH :] = put_terms(lse_ref[...].reshape(heads, forks))


def attend(queries, keys, values, mask):
    forks, width = queries.shape
    held, page_len, kv_width = keys[0].shape
    pieces = len(keys)
    pages = held * pieces
    kv_local = kv_width // HEAD_WIDTH
    group = width // kv_width
    rows = group * forks
    return pl.pallas_call(
        functools.partial(attend_kernel, pieces),
        out_shape=pltpu.VMEM((forks, width + HEAD_WIDTH), BF16),
        in_specs=[VMEM_SPEC] * (2 + 2 * pieces),
        out_specs=VMEM_SPEC,
        scratch_shapes=[
            pltpu.VMEM((2 * pages, page_len, rows), F32),
            pltpu.VMEM((kv_local, group, forks), F32),
        ],
        compiler_params=params(10 * pages * page_len * rows + 4 * MIB),
        cost_estimate=cost(
            4 * pages * page_len * kv_local * rows * HEAD_WIDTH,
            4 * pages * page_len * kv_width + 4 * forks * width,
            pages * page_len * kv_local * rows,
        ),
        name="attend",
    )(queries, *[in_vmem(x) for x in [mask, *keys, *values]])


def merge_kernel(heads, kv_heads, sources, *refs):
    parts, (q_ref, new_ref, out_ref) = refs[:sources], refs[sources:]
    group = heads // kv_heads
    width = heads * HEAD_WIDTH
    lses = [get_terms(ref[:, width : width + HEAD_WIDTH], heads) for ref in parts]

    def new_head(i):
        return new_ref[:, i * HEAD_WIDTH : (i + 1) * HEAD_WIDTH].astype(F32)

    scores = []
    for h in range(heads):
        query = q_ref[:, h * HEAD_WIDTH : (h + 1) * HEAD_WIDTH].astype(F32)
        scores.append(jnp.sum(query * new_head(h // group), axis=1, keepdims=True))
    own = jnp.concatenate(scores, axis=1) * (SCORE_SCALE * LOG2E)
    top = functools.reduce(jnp.maximum, lses, own)
    own_weight = jnp.exp2(own - top)
    weights = [jnp.exp2(lse - top) for lse in lses]
    inverse = 1.0 / functools.reduce(jnp.add, weights, own_weight)
    own_weight = own_weight * inverse
    weights = [weight * inverse for weight in weights]
    for h in range(heads):
        lanes = slice(h * HEAD_WIDTH, (h + 1) * HEAD_WIDTH)
        total = own_weight[:, h : h + 1] * new_head(kv_heads + h // group)
        for weight, ref in zip(weights, parts):
            total += weight[:, h : h + 1] * ref[:, lanes].astype(F32)
        out_ref[:, lanes] = total.astype(BF16)


def merge(parts, queries, new, heads, kv_heads):
    fork_own, width = parts[0].shape
    size = len(parts) * fork_own * width
    return pl.pallas_call(
        functools.partial(merge_kernel, heads, kv_heads, len(parts)),
        out_shape=jax.ShapeDtypeStruct((fork_own, heads * HEAD_WIDTH), BF16),
        compiler_params=params(4 * size + 4 * MIB),
        cost_estimate=pl.CostEstimate(flops=4 * size, bytes_accessed=2 * size, transcendentals=0),
        name="merge",
    )(*parts, queries, new)


def output_kernel(context_ref, *refs):
    weight_refs, out_ref = refs[:-1], refs[-1]
    total = None
    for i, ref in enumerate(weight_refs):
        depth = ref.shape[0]
        part = jnp.dot(
            context_ref[:, i * depth : (i + 1) * depth], ref[...], preferred_element_type=F32
        )
        total = part if total is None else total + part
    out_ref[...] = total


def output_project(context, weights):
    forks, rows = context.shape
    columns = weights[0].shape[1]
    return pl.pallas_call(
        output_kernel,
        out_shape=pltpu.VMEM((forks, columns), F32),
        in_specs=[VMEM_SPEC] * (1 + len(weights)),
        out_specs=VMEM_SPEC,
        compiler_params=params(4 * MIB),
        cost_estimate=cost(2 * forks * rows * columns, 2 * rows * columns),
        name="output_project",
    )(context, *[in_vmem(x) for x in weights])


def finish_kernel(count, line, index_ref, *refs):
    near_refs, far_refs, out_ref = refs[:count], refs[count : 2 * count], refs[-1]
    place, parity = index_ref[0] // 2, index_ref[0] % 2
    rows = out_ref.shape[1]
    for group, side in ((near_refs, parity), (far_refs, 1 - parity)):
        for i in range(line):
            total = functools.reduce(jnp.add, [ref[i * rows : (i + 1) * rows] for ref in group])
            out_ref[2 * (place ^ i) + side] = total.astype(BF16)


def finish(index, near, far, mem_count):
    rows, columns = near[0].shape
    line = mem_count // 2
    return pl.pallas_call(
        functools.partial(finish_kernel, len(near), line),
        out_shape=jax.ShapeDtypeStruct((mem_count, rows // line, columns), BF16),
        in_specs=[SMEM_SPEC] + [VMEM_SPEC] * (2 * len(near)),
        out_specs=VMEM_SPEC,
        compiler_params=params(4 * MIB),
        cost_estimate=cost(0, 8 * rows * columns * len(near)),
        name="finish",
    )(index, *near, *far)


def shards(
    hidden,
    adapter,
    page_cache_slot,
    selection,
    query_projection_weight,
    key_projection_weight,
    value_projection_weight,
    adapter_down_weight,
    adapter_up_weight,
    output_projection_weight,
    prefix_key_cache,
    prefix_value_cache,
):
    mem_count = lax.axis_size("mem")
    mem_index = lax.axis_index("mem")
    forks = hidden.shape[0]
    fork_own = forks // mem_count
    q_width = query_projection_weight.shape[1]
    kv_width = key_projection_weight.shape[1]
    heads, kv_heads = q_width // HEAD_WIDTH, kv_width // HEAD_WIDTH
    pages = prefix_key_cache.shape[0]
    line = mem_count // 2
    index = mem_index.reshape(1)
    place, parity = mem_index // 2, mem_index % 2

    def swapped(x, step, cross=0):
        pairs = [(i, i ^ (2 * step + cross)) for i in range(mem_count)]
        return lax.ppermute(x, "mem", pairs)

    def along(blocks, cross=0):
        return [
            swapped(blocks[i], i, cross) if i or cross else blocks[0] for i in range(line)
        ]

    def gather(x):
        return jnp.concatenate([x] + [swapped(x, i) for i in range(1, line)], axis=0)

    def pair(x):
        return swapped(x, 0, 1)

    near_1, far_1, hidden, adapter = project_first(
        index, adapter, hidden, adapter_down_weight, key_projection_weight, value_projection_weight, mem_count
    )
    cut = q_width * 10 // 16 // 256 * 256
    part_a, up = project(
        hidden, query_projection_weight, 0, cut, adapter_up_weight.reshape(-1, q_width)
    )
    first_parts = fold(near_1, pair(far_1))
    first_parts, part_a, hidden = lax.optimization_barrier((first_parts, part_a, hidden))
    (part_b,) = project(hidden, query_projection_weight, cut, q_width - cut)
    first_parts = two_first(along(first_parts))[::-1]

    near_a, far_a = add_delta(index, adapter, first_parts, part_a, up, mem_count, 0)
    near_a, far_a, part_b = lax.optimization_barrier((near_a, far_a, part_b))
    both_b, own_new = add_delta(
        index, adapter, first_parts, part_b, up, mem_count, cut, 2 * kv_width
    )
    sums_a = fold(near_a, pair(far_a))
    own_b, other_b = line_sum(along(both_b), sums_a[0])
    own_a = functools.reduce(jnp.add, along(sums_a)[::-1]).astype(BF16)
    own_queries = join(own_a, own_b, pair(other_b))

    *staged, near_mask, far_mask = stage_cache(
        index, page_cache_slot, selection, prefix_key_cache, prefix_value_cache, mem_count
    )
    keys, values = staged[: len(staged) // 2], staged[len(staged) // 2 :]
    near_queries = gather(own_queries)
    far_queries = pair(near_queries)
    near = attend(near_queries, keys, values, near_mask)
    far = attend(far_queries, keys, values, far_mask)
    blocks = (line, fork_own, q_width + HEAD_WIDTH)
    parts = two_first(along(near.reshape(blocks))) + along(far.reshape(blocks), 1)
    context_own = merge(parts, own_queries, own_new, heads, kv_heads)

    out_weights = stage(output_projection_weight)
    near_context = gather(context_own)
    far_context = pair(near_context)
    tp_count = lax.axis_size("tp")
    outs = []
    for context in (near_context, far_context):
        part = output_project(context, out_weights)
        terms = [part]
        for shift in range(1, tp_count):
            pairs = [(i, (i + shift) % tp_count) for i in range(tp_count)]
            terms.append(lax.ppermute(part, "tp", pairs))
        outs.append(terms)
    return finish(index, *outs, mem_count).reshape(forks, -1)


def solution(mesh):
    return jax.shard_map(
        shards,
        mesh=mesh,
        in_specs=(
            P("groups", "mem"),
            P("groups"),
            P("groups"),
            P("groups", None),
            P("mem", "tp"),
            P("mem", "tp"),
            P("mem", "tp"),
            P("mem", None),
            P("mem", None, "tp"),
            P("tp", "mem"),
            P(("groups", "mem"), None, "tp"),
            P(("groups", "mem"), None, "tp"),
        ),
        out_specs=P("groups", "mem"),
        check_vma=False,
    )
```

```python
import functools

import jax
import jax.numpy as jnp
from jax import lax
from jax.experimental import pallas as pl
from jax.experimental.pallas import tpu as pltpu
from jax.sharding import PartitionSpec as P

HEAD_WIDTH = 128
ADAPTER_RANK = 64
ADAPTER_COUNT = 32
LOG2E = 1.4426950408889634
SCORE_SCALE = HEAD_WIDTH ** (-0.5)
neg_floor = -1e30
MIB = 1024 * 1024
F32 = jnp.float32
BF16 = jnp.bfloat16


def params(limit, *semantics):
    return pltpu.CompilerParams(
        dimension_semantics=semantics or None, vmem_limit_bytes=int(limit)
    )


def whole(shape):
    return pl.BlockSpec(shape, lambda *_: (0,) * len(shape))


def in_hbm(x):
    return pltpu.with_memory_space_constraint(x, pltpu.HBM)


def in_vmem(x):
    return pltpu.with_memory_space_constraint(x, pltpu.VMEM)


def cost(flops, size, transcendentals=0):
    return pl.CostEstimate(
        flops=int(flops), bytes_accessed=int(size), transcendentals=int(transcendentals)
    )


VMEM_SPEC = pl.BlockSpec(memory_space=pltpu.VMEM)
SMEM_SPEC = pl.BlockSpec(memory_space=pltpu.SMEM)
ANY_SPEC = pl.BlockSpec(memory_space=pl.ANY)


def stage_kernel(pieces, *refs):
    count = len(refs[:-1]) // (pieces + 1)
    sources, targets, sems = refs[:count], refs[count:-1], refs[-1]
    copies = []
    for i, target in enumerate(targets):
        rows = pl.ds((i % pieces) * target.shape[0], target.shape[0])
        copies.append(
            pltpu.make_async_copy(sources[i // pieces].at[rows], target, sems.at[i])
        )
    for copy in copies:
        copy.start()
    for copy in copies:
        copy.wait()


def stage(*arrays, pieces=4):
    shapes = [(x.shape[0] // pieces,) + x.shape[1:] for x in arrays for _ in range(pieces)]
    return pl.pallas_call(
        functools.partial(stage_kernel, pieces),
        out_shape=tuple(pltpu.VMEM(shape, BF16) for shape in shapes),
        in_specs=[ANY_SPEC] * len(arrays),
        out_specs=(ANY_SPEC,) * len(shapes),
        scratch_shapes=[pltpu.SemaphoreType.DMA((len(shapes),))],
        compiler_params=params(MIB),
        cost_estimate=cost(0, sum(2 * x.size for x in arrays)),
        name="stage",
    )(*[in_hbm(x) for x in arrays])


def cache_kernel(pieces, index_ref, slot_hbm, select_hbm, *refs):
    sources, targets = refs[:2], refs[2 : 2 + 2 * pieces]
    near_ref, far_ref, slot_ref, select_ref, blocks_ref, sems = refs[2 + 2 * pieces :]
    count = 2 * pieces
    first = [
        pltpu.make_async_copy(slot_hbm, slot_ref, sems.at[count]),
        pltpu.make_async_copy(select_hbm, select_ref, sems.at[count + 1]),
    ]
    copies = []
    for i, target in enumerate(targets):
        rows = pl.ds((i % pieces) * target.shape[0], target.shape[0])
        copies.append(
            pltpu.make_async_copy(sources[i // pieces].at[rows], target, sems.at[i])
        )
    for copy in first + copies:
        copy.start()
    for copy in first:
        copy.wait()
    pages, total = blocks_ref.shape[2], slot_ref.shape[1]
    slots = index_ref[0] * pages + lax.broadcasted_iota(jnp.int32, (pages, total), 0)
    match = (slots == slot_ref[...]).astype(BF16)
    chosen = (select_ref[...] > 0).astype(BF16)
    held = lax.dot_general(
        chosen, match, (((1,), (1,)), ((), ())), preferred_element_type=F32
    )
    put_blocks(index_ref[0], held, blocks_ref, near_ref, far_ref)
    for copy in copies:
        copy.wait()


def stage_cache(index, page_cache_slot, selection, keys, values, mem_count, pieces=2):
    forks, total = selection.shape
    pages = keys.shape[0]
    line, fork_own = mem_count // 2, forks // mem_count
    shapes = [(x.shape[0] // pieces,) + x.shape[1:] for x in (keys, values) for _ in range(pieces)]
    mask = pltpu.VMEM((line, fork_own, pages), F32)
    return pl.pallas_call(
        functools.partial(cache_kernel, pieces),
        out_shape=tuple(pltpu.VMEM(shape, BF16) for shape in shapes) + (mask, mask),
        in_specs=[SMEM_SPEC] + [ANY_SPEC] * 4,
        out_specs=(ANY_SPEC,) * len(shapes) + (VMEM_SPEC,) * 2,
        scratch_shapes=[
            pltpu.VMEM((1, total), jnp.int32),
            pltpu.VMEM((forks, total), jnp.int32),
            pltpu.VMEM((mem_count, fork_own, pages), F32),
            pltpu.SemaphoreType.DMA((2 * pieces + 2,)),
        ],
        compiler_params=params(4 * MIB),
        cost_estimate=cost(0, 4 * keys.size),
        name="stage_cache",
    )(index, *[in_hbm(x) for x in (page_cache_slot.reshape(1, total), selection, keys, values)])


def fold_kernel(one_ref, two_ref, *out_refs):
    for i, out_ref in enumerate(out_refs):
        out_ref[...] = one_ref[i] + two_ref[i]


def fold(one, two):
    out = pltpu.VMEM(one.shape[1:], F32)
    return pl.pallas_call(
        fold_kernel,
        out_shape=(out,) * one.shape[0],
        in_specs=[VMEM_SPEC] * 2,
        out_specs=(VMEM_SPEC,) * one.shape[0],
        compiler_params=params(MIB * 2 + 16 * one.size),
        cost_estimate=cost(one.size, 12 * one.size),
        name="fold",
    )(in_vmem(one), two)


def step_of(i):
    return i ^ (i >> 1)


def by_step(terms):
    return [terms[step_of(i)] for i in range(len(terms))] if len(terms) < 5 else terms


def take_blocks(index, blocks_ref, near_ref, far_ref):
    place, parity = index // 2, index % 2
    for i in range(near_ref.shape[0]):
        at = 2 * (place ^ step_of(i))
        near_ref[i] = blocks_ref[at + parity]
        far_ref[i] = blocks_ref[at + 1 - parity]


def put_blocks(index, value, blocks_ref, near_ref, far_ref):
    count, rows, lanes = blocks_ref.shape
    own = value.shape[0] // count
    for i in range(count):
        blocks_ref[i, :own] = value[i * own : (i + 1) * own]
        if own < rows:
            blocks_ref[i, own:] = jnp.zeros((rows - own, lanes), F32)
    take_blocks(index, blocks_ref, near_ref, far_ref)


def first_kernel(
    index_ref,
    adapter_hbm,
    hidden_hbm,
    down_hbm,
    k_hbm,
    v_hbm,
    near_ref,
    far_ref,
    hidden_ref,
    adapter_ref,
    held,
    held_kv,
    rank_blocks,
    kv_blocks,
    sems,
):
    pieces, _, width = held.shape
    forks = hidden_ref.shape[0]
    kv_width = held_kv.shape[2]
    lanes = rank_blocks.shape[2]
    copies = [
        pltpu.make_async_copy(adapter_hbm, adapter_ref, sems.at[pieces + 3]),
        pltpu.make_async_copy(hidden_hbm, hidden_ref, sems.at[pieces + 2]),
        *[
            pltpu.make_async_copy(
                down_hbm.at[:, i * width : (i + 1) * width], held.at[i], sems.at[i]
            )
            for i in range(pieces)
        ],
        pltpu.make_async_copy(k_hbm, held_kv.at[0], sems.at[pieces]),
        pltpu.make_async_copy(v_hbm, held_kv.at[1], sems.at[pieces + 1]),
    ]
    for copy in copies:
        copy.start()
    copies[0].wait()
    fork_adapter = jnp.broadcast_to(adapter_ref[...].astype(F32), (HEAD_WIDTH, forks)).T
    lane_adapter = lax.broadcasted_iota(jnp.int32, (forks, HEAD_WIDTH), 1) // ADAPTER_RANK
    wanted = fork_adapter.astype(jnp.int32) - lane_adapter
    total = jnp.zeros((forks, HEAD_WIDTH), F32)
    copies[1].wait()
    for i in range(pieces):
        copies[2 + i].wait()
        block = jnp.dot(hidden_ref[...], held[i], preferred_element_type=F32)
        for j in range(width // HEAD_WIDTH):
            first = (i * width + j * HEAD_WIDTH) // ADAPTER_RANK
            part = block[:, j * HEAD_WIDTH : (j + 1) * HEAD_WIDTH]
            total += jnp.where(wanted == first, part, 0.0)
    flipped = total.T
    flipped = flipped[:ADAPTER_RANK] + flipped[ADAPTER_RANK:]
    if lanes > forks:
        flipped = jnp.concatenate([flipped, jnp.zeros((ADAPTER_RANK, lanes - forks), F32)], axis=1)
    at = slice(0, lanes)
    put_blocks(index_ref[0], flipped, rank_blocks, near_ref.at[:, :, at], far_ref.at[:, :, at])
    for i in range(2):
        copies[2 + pieces + i].wait()
        part = jnp.dot(hidden_ref[...], held_kv[i], preferred_element_type=F32)
        at = slice(lanes + i * kv_width, lanes + (i + 1) * kv_width)
        put_blocks(index_ref[0], part, kv_blocks, near_ref.at[:, :, at], far_ref.at[:, :, at])


def project_first(index, adapter, hidden, down, k_weight, v_weight, mem_count, width=256):
    forks, depth = hidden.shape
    columns, kv_width = down.shape[1], k_weight.shape[1]
    lanes = -(-forks // HEAD_WIDTH) * HEAD_WIDTH
    line, fork_own = mem_count // 2, forks // mem_count
    pieces = columns // width
    out = pltpu.VMEM((line, fork_own, lanes + 2 * kv_width), F32)
    weights = 2 * depth * (columns + 2 * kv_width)
    return pl.pallas_call(
        first_kernel,
        out_shape=(out, out, pltpu.VMEM(hidden.shape, BF16), pltpu.VMEM((1, forks), jnp.int32)),
        in_specs=[SMEM_SPEC] + [ANY_SPEC] * 5,
        out_specs=(VMEM_SPEC,) * 4,
        scratch_shapes=[
            pltpu.VMEM((pieces, depth, width), BF16),
            pltpu.VMEM((2, depth, kv_width), BF16),
            pltpu.VMEM((mem_count, fork_own, lanes), F32),
            pltpu.VMEM((mem_count, fork_own, kv_width), F32),
            pltpu.SemaphoreType.DMA((pieces + 4,)),
        ],
        compiler_params=params(weights + 4 * MIB),
        cost_estimate=cost(forks * weights, weights),
        name="project_first",
    )(index, *[in_hbm(x) for x in (adapter.reshape(1, forks), hidden, down, k_weight, v_weight)])


def project_kernel(start, extra, hidden_ref, q_hbm, *refs):
    up_hbm, part_ref, up_ref, held, sems = refs if extra else (None, refs[0], None, *refs[1:])
    pieces, _, width = held.shape
    copies = []
    for i in range(pieces):
        columns = pl.ds(start + i * width, width)
        copies.append(pltpu.make_async_copy(q_hbm.at[:, columns], held.at[i], sems.at[i]))
    if extra:
        copies.append(pltpu.make_async_copy(up_hbm, up_ref, sems.at[pieces]))
    for copy in copies:
        copy.start()
    for i in range(pieces):
        copies[i].wait()
        part_ref[:, i * width : (i + 1) * width] = jnp.dot(
            hidden_ref[...], held[i], preferred_element_type=F32
        )
    if extra:
        copies[-1].wait()


def project(hidden, q_weight, start, columns, up=None, width=256):
    forks, depth = hidden.shape
    pieces = columns // width
    weights = 2 * depth * columns
    extra = [] if up is None else [up]
    return pl.pallas_call(
        functools.partial(project_kernel, start, bool(extra)),
        out_shape=tuple(
            [pltpu.VMEM((forks, columns), F32)] + [pltpu.VMEM(x.shape, BF16) for x in extra]
        ),
        in_specs=[VMEM_SPEC] + [ANY_SPEC] * (1 + len(extra)),
        out_specs=(VMEM_SPEC,) * (1 + len(extra)),
        scratch_shapes=[
            pltpu.VMEM((pieces, depth, width), BF16),
            pltpu.SemaphoreType.DMA((pieces + 1,)),
        ],
        compiler_params=params(weights + 2 * MIB),
        cost_estimate=cost(forks * weights, weights + sum(2 * x.size for x in extra)),
        name="project",
    )(in_vmem(hidden), *[in_hbm(x) for x in [q_weight] + extra])


def line_sum_kernel(after_ref, *refs):
    parts, (own_ref, other_ref) = refs[:-2], refs[-2:]
    own_ref[...] = functools.reduce(jnp.add, [ref[0] for ref in parts])
    other_ref[...] = functools.reduce(jnp.add, [ref[1] for ref in parts])


def line_sum(parts, after):
    out = pltpu.VMEM(parts[0].shape[1:], F32)
    size = len(parts) * parts[0].size
    return pl.pallas_call(
        line_sum_kernel,
        out_shape=(out, out),
        in_specs=[ANY_SPEC] + [VMEM_SPEC] * len(parts),
        out_specs=(VMEM_SPEC,) * 2,
        compiler_params=params(2 * MIB + 8 * size),
        cost_estimate=cost(size, 4 * size),
        name="line_sum",
    )(after, *parts)


def join_kernel(first_ref, one_ref, two_ref, out_ref):
    cut = first_ref.shape[1]
    out_ref[:, :cut] = first_ref[...]
    out_ref[:, cut:] = (one_ref[...] + two_ref[...]).astype(BF16)


def join(first, one, two):
    rows, columns = first.shape[0], first.shape[1] + one.shape[1]
    return pl.pallas_call(
        join_kernel,
        out_shape=pltpu.VMEM((rows, columns), BF16),
        in_specs=[VMEM_SPEC] * 3,
        out_specs=VMEM_SPEC,
        compiler_params=params(MIB + 16 * rows * columns),
        cost_estimate=cost(one.size, 4 * rows * columns),
        name="join",
    )(first, in_vmem(one), two)


def delta_kernel(line, ranks, start, joint, index_ref, adapter_ref, *refs):
    first_refs = refs[:line]
    part_ref, up_ref, *out_refs, blocks_ref = refs[line:]
    forks, width = part_ref.shape[0], blocks_ref.shape[2]
    if joint:
        near_ref, far_ref = out_refs[0].at[:, 0], out_refs[0].at[:, 1]
        new_ref = out_refs[1]
        lanes = first_refs[0].shape[1] - new_ref.shape[1]
        total = functools.reduce(jnp.add, [ref[:, lanes:] for ref in first_refs])
        new_ref[...] = total.astype(BF16)
    else:
        near_ref, far_ref = out_refs
    acts = functools.reduce(jnp.add, [ref[:ranks, :forks] for ref in first_refs])
    acts = acts.astype(BF16).astype(F32)
    adapters = lax.broadcasted_iota(jnp.int32, (ADAPTER_COUNT, forks), 0)
    onehot = (adapters == adapter_ref[...]).astype(F32)
    spread = jnp.concatenate(
        [acts[r : r + 1, :] * onehot for r in range(ranks)], axis=0
    ).astype(BF16)
    for i in range(part_ref.shape[1] // width):
        delta = lax.dot_general(
            spread,
            up_ref[:, start + i * width : start + (i + 1) * width],
            (((0,), (0,)), ((), ())),
            preferred_element_type=F32,
        )
        at = slice(i * width, (i + 1) * width)
        put_blocks(
            index_ref[0],
            part_ref[:, at] + delta,
            blocks_ref,
            near_ref.at[:, :, at],
            far_ref.at[:, :, at],
        )


def add_delta(index, adapter, first_parts, part, up, mem_count, start, new_width=0, width=256):
    forks, columns = part.shape
    line, fork_own = mem_count // 2, forks // mem_count
    ranks = ADAPTER_RANK // mem_count
    if new_width:
        out = (
            pltpu.VMEM((line, 2, fork_own, columns), F32),
            pltpu.VMEM((fork_own, new_width), BF16),
        )
    else:
        out = (pltpu.VMEM((line, fork_own, columns), F32),) * 2
    return pl.pallas_call(
        functools.partial(delta_kernel, line, ranks, start, new_width > 0),
        out_shape=out,
        in_specs=[SMEM_SPEC] + [VMEM_SPEC] * (line + 3),
        out_specs=(VMEM_SPEC,) * 2,
        scratch_shapes=[pltpu.VMEM((mem_count, fork_own, width), F32)],
        compiler_params=params(4 * MIB),
        cost_estimate=cost(
            2 * forks * up.shape[0] * columns, 2 * up.shape[0] * columns + 8 * forks * columns
        ),
        name="add_delta",
    )(index, in_vmem(adapter), *first_parts, in_vmem(part), in_vmem(up))


def put_terms(lse):
    heads, forks = lse.shape
    high = lse.astype(BF16).astype(F32)
    rest = lse - high
    middle = rest.astype(BF16).astype(F32)
    low = rest - middle
    spare = jnp.zeros((HEAD_WIDTH - 3 * heads, forks), F32)
    return jnp.concatenate([high, middle, low, spare], axis=0).T.astype(BF16)


def get_terms(terms, heads):
    terms = terms.astype(F32)
    return terms[:, :heads] + terms[:, heads : 2 * heads] + terms[:, 2 * heads : 3 * heads]


def attend_kernel(pieces, q_ref, mask_ref, *refs):
    k_refs, v_refs, (out_ref, score_ref, lse_ref) = (
        refs[:pieces],
        refs[pieces : 2 * pieces],
        refs[2 * pieces :],
    )
    forks = q_ref.shape[0]
    kv_local, group = lse_ref.shape[:2]
    pages = score_ref.shape[0] // 2
    held = pages // pieces
    scale = SCORE_SCALE * LOG2E
    chosen_by = mask_ref[...].reshape(forks, pages)
    spare = jnp.zeros((forks, HEAD_WIDTH - pages % HEAD_WIDTH), F32)
    chosen_by = jnp.concatenate([chosen_by, spare], axis=1).T[:pages]
    mask = jnp.concatenate([chosen_by] * group, axis=1) > 0
    ones = jnp.ones((8, score_ref.shape[1]), BF16)

    def score(kv_head, queries, p):
        lanes = slice(kv_head * HEAD_WIDTH, (kv_head + 1) * HEAD_WIDTH)
        scores = lax.dot_general(
            k_refs[p // held][p % held, :, lanes],
            queries,
            (((1,), (1,)), ((), ())),
            preferred_element_type=F32,
        )
        score_ref[kv_head % 2 * pages + p] = scores
        return jnp.max(scores, axis=0, keepdims=True)

    def term(kv_head, peaks, top, p):
        lanes = slice(kv_head * HEAD_WIDTH, (kv_head + 1) * HEAD_WIDTH)
        scores = score_ref[kv_head % 2 * pages + p]
        weights = jnp.exp2((scores - peaks[p]) * scale).astype(BF16)
        chosen = jnp.where(mask[p : p + 1], peaks[p], neg_floor)
        factor = jnp.where(mask[p : p + 1], jnp.exp2((chosen - top) * scale), 0.0)
        values = jnp.concatenate([v_refs[p // held][p % held, :, lanes].T, ones], axis=0)
        return jnp.dot(values, weights, preferred_element_type=F32) * factor

    def head_queries(kv_head):
        first = kv_head * group
        return jnp.concatenate(
            [
                q_ref[:, (first + g) * HEAD_WIDTH : (first + g + 1) * HEAD_WIDTH]
                for g in range(group)
            ],
            axis=0,
        )

    queries = head_queries(0)
    peaks = [score(0, queries, p) for p in range(pages)]
    for kv_head in range(kv_local):
        chosen = [jnp.where(mask[p : p + 1], peaks[p], neg_floor) for p in range(pages)]
        top = functools.reduce(jnp.maximum, chosen)
        if kv_head + 1 < kv_local:
            queries = head_queries(kv_head + 1)
        acc = None
        next_peaks = []
        for p in range(pages):
            if kv_head + 1 < kv_local:
                next_peaks.append(score(kv_head + 1, queries, p))
            part = term(kv_head, peaks, top, p)
            acc = part if acc is None else acc + part
        peaks = next_peaks
        mass = acc[HEAD_WIDTH : HEAD_WIDTH + 1]
        some = mass > 0
        safe = jnp.where(some, mass, 1.0)
        rows = (acc[:HEAD_WIDTH] * jnp.where(some, 1.0 / safe, 0.0)).T
        lse = jnp.where(some, top * scale + jnp.log2(safe), neg_floor)
        for g in range(group):
            at = (kv_head * group + g) * HEAD_WIDTH
            out_ref[:, at : at + HEAD_WIDTH] = rows[g * forks : (g + 1) * forks].astype(BF16)
        lse_ref[kv_head] = jnp.concatenate(
            [lse[:, g * forks : (g + 1) * forks] for g in range(group)], axis=0
        )

    heads = kv_local * group
    out_ref[:, heads * HEAD_WIDTH :] = put_terms(lse_ref[...].reshape(heads, forks))


def attend(queries, keys, values, mask):
    forks, width = queries.shape
    held, page_len, kv_width = keys[0].shape
    pieces = len(keys)
    pages = held * pieces
    kv_local = kv_width // HEAD_WIDTH
    group = width // kv_width
    rows = group * forks
    return pl.pallas_call(
        functools.partial(attend_kernel, pieces),
        out_shape=pltpu.VMEM((forks, width + HEAD_WIDTH), BF16),
        in_specs=[VMEM_SPEC] * (2 + 2 * pieces),
        out_specs=VMEM_SPEC,
        scratch_shapes=[
            pltpu.VMEM((2 * pages, page_len, rows), F32),
            pltpu.VMEM((kv_local, group, forks), F32),
        ],
        compiler_params=params(10 * pages * page_len * rows + 4 * MIB),
        cost_estimate=cost(
            4 * pages * page_len * kv_local * rows * HEAD_WIDTH,
            4 * pages * page_len * kv_width + 4 * forks * width,
            pages * page_len * kv_local * rows,
        ),
        name="attend",
    )(queries, *[in_vmem(x) for x in [mask, *keys, *values]])


def merge_kernel(heads, kv_heads, sources, *refs):
    parts, (q_ref, new_ref, out_ref) = refs[:sources], refs[sources:]
    group = heads // kv_heads
    width = heads * HEAD_WIDTH
    lses = [get_terms(ref[:, width : width + HEAD_WIDTH], heads) for ref in parts]

    def new_head(i):
        return new_ref[:, i * HEAD_WIDTH : (i + 1) * HEAD_WIDTH].astype(F32)

    scores = []
    for h in range(heads):
        query = q_ref[:, h * HEAD_WIDTH : (h + 1) * HEAD_WIDTH].astype(F32)
        scores.append(jnp.sum(query * new_head(h // group), axis=1, keepdims=True))
    own = jnp.concatenate(scores, axis=1) * (SCORE_SCALE * LOG2E)
    top = functools.reduce(jnp.maximum, lses, own)
    own_weight = jnp.exp2(own - top)
    weights = [jnp.exp2(lse - top) for lse in lses]
    inverse = 1.0 / functools.reduce(jnp.add, weights, own_weight)
    own_weight = own_weight * inverse
    weights = [weight * inverse for weight in weights]
    for h in range(heads):
        lanes = slice(h * HEAD_WIDTH, (h + 1) * HEAD_WIDTH)
        total = own_weight[:, h : h + 1] * new_head(kv_heads + h // group)
        for weight, ref in zip(weights, parts):
            total += weight[:, h : h + 1] * ref[:, lanes].astype(F32)
        out_ref[:, lanes] = total.astype(BF16)


def merge(parts, queries, new, heads, kv_heads):
    fork_own, width = parts[0].shape
    size = len(parts) * fork_own * width
    return pl.pallas_call(
        functools.partial(merge_kernel, heads, kv_heads, len(parts)),
        out_shape=jax.ShapeDtypeStruct((fork_own, heads * HEAD_WIDTH), BF16),
        compiler_params=params(4 * size + 4 * MIB),
        cost_estimate=pl.CostEstimate(flops=4 * size, bytes_accessed=2 * size, transcendentals=0),
        name="merge",
    )(*parts, queries, new)


def output_kernel(context_ref, *refs):
    weight_refs, out_ref = refs[:-1], refs[-1]
    total = None
    for i, ref in enumerate(weight_refs):
        depth = ref.shape[0]
        part = jnp.dot(
            context_ref[:, i * depth : (i + 1) * depth], ref[...], preferred_element_type=F32
        )
        total = part if total is None else total + part
    out_ref[...] = total


def output_project(context, weights):
    forks, rows = context.shape
    columns = weights[0].shape[1]
    return pl.pallas_call(
        output_kernel,
        out_shape=pltpu.VMEM((forks, columns), F32),
        in_specs=[VMEM_SPEC] * (1 + len(weights)),
        out_specs=VMEM_SPEC,
        compiler_params=params(4 * MIB),
        cost_estimate=cost(2 * forks * rows * columns, 2 * rows * columns),
        name="output_project",
    )(context, *[in_vmem(x) for x in weights])


def finish_kernel(count, line, index_ref, *refs):
    near_refs, far_refs, out_ref = refs[:count], refs[count : 2 * count], refs[-1]
    place, parity = index_ref[0] // 2, index_ref[0] % 2
    rows = out_ref.shape[1]
    for group, side in ((near_refs, parity), (far_refs, 1 - parity)):
        for i in range(line):
            total = functools.reduce(jnp.add, [ref[i * rows : (i + 1) * rows] for ref in group])
            out_ref[2 * (place ^ step_of(i)) + side] = total.astype(BF16)


def finish(index, near, far, mem_count):
    rows, columns = near[0].shape
    line = mem_count // 2
    return pl.pallas_call(
        functools.partial(finish_kernel, len(near), line),
        out_shape=jax.ShapeDtypeStruct((mem_count, rows // line, columns), BF16),
        in_specs=[SMEM_SPEC] + [VMEM_SPEC] * (2 * len(near)),
        out_specs=VMEM_SPEC,
        compiler_params=params(4 * MIB),
        cost_estimate=cost(0, 8 * rows * columns * len(near)),
        name="finish",
    )(index, *near, *far)


def shards(
    hidden,
    adapter,
    page_cache_slot,
    selection,
    query_projection_weight,
    key_projection_weight,
    value_projection_weight,
    adapter_down_weight,
    adapter_up_weight,
    output_projection_weight,
    prefix_key_cache,
    prefix_value_cache,
):
    mem_count = lax.axis_size("mem")
    mem_index = lax.axis_index("mem")
    forks = hidden.shape[0]
    fork_own = forks // mem_count
    q_width = query_projection_weight.shape[1]
    kv_width = key_projection_weight.shape[1]
    heads, kv_heads = q_width // HEAD_WIDTH, kv_width // HEAD_WIDTH
    pages = prefix_key_cache.shape[0]
    line = mem_count // 2
    index = mem_index.reshape(1)
    place, parity = mem_index // 2, mem_index % 2

    def swapped(x, step, cross=0):
        pairs = [(i, i ^ (2 * step + cross)) for i in range(mem_count)]
        return lax.ppermute(x, "mem", pairs)

    def along(blocks, cross=0):
        return [
            swapped(blocks[i], step_of(i), cross) if i or cross else blocks[0] for i in range(line)
        ]

    def gather(x):
        return jnp.concatenate([x] + [swapped(x, step_of(i)) for i in range(1, line)], axis=0)

    def pair(x):
        return swapped(x, 0, 1)

    near_1, far_1, hidden, adapter = project_first(
        index, adapter, hidden, adapter_down_weight, key_projection_weight, value_projection_weight, mem_count
    )
    cut = q_width * 10 // 16 // 256 * 256
    part_a, up = project(
        hidden, query_projection_weight, 0, cut, adapter_up_weight.reshape(-1, q_width)
    )
    first_parts = fold(near_1, pair(far_1))
    first_parts, part_a, hidden = lax.optimization_barrier((first_parts, part_a, hidden))
    (part_b,) = project(hidden, query_projection_weight, cut, q_width - cut)
    first_parts = along(first_parts)[::-1]

    near_a, far_a = add_delta(index, adapter, first_parts, part_a, up, mem_count, 0)
    near_a, far_a, part_b = lax.optimization_barrier((near_a, far_a, part_b))
    both_b, own_new = add_delta(
        index, adapter, first_parts, part_b, up, mem_count, cut, 2 * kv_width
    )
    sums_a = fold(near_a, pair(far_a))
    own_b, other_b = line_sum(by_step(along(both_b)), sums_a[0])
    own_a = functools.reduce(jnp.add, by_step(along(sums_a))[::-1]).astype(BF16)
    own_queries = join(own_a, own_b, pair(other_b))

    *staged, near_mask, far_mask = stage_cache(
        index, page_cache_slot, selection, prefix_key_cache, prefix_value_cache, mem_count
    )
    keys, values = staged[: len(staged) // 2], staged[len(staged) // 2 :]
    near_queries = gather(own_queries)
    far_queries = pair(near_queries)
    near = attend(near_queries, keys, values, near_mask)
    far = attend(far_queries, keys, values, far_mask)
    blocks = (line, fork_own, q_width + HEAD_WIDTH)
    parts = along(near.reshape(blocks)) + by_step(along(far.reshape(blocks), 1))
    context_own = merge(parts, own_queries, own_new, heads, kv_heads)

    out_weights = stage(output_projection_weight)
    near_context = gather(context_own)
    far_context = pair(near_context)
    tp_count = lax.axis_size("tp")
    outs = []
    for context in (near_context, far_context):
        part = output_project(context, out_weights)
        terms = [part]
        for shift in range(1, tp_count):
            pairs = [(i, (i + shift) % tp_count) for i in range(tp_count)]
            terms.append(lax.ppermute(part, "tp", pairs))
        outs.append(terms)
    return finish(index, *outs, mem_count).reshape(forks, -1)


def solution(mesh):
    return jax.shard_map(
        shards,
        mesh=mesh,
        in_specs=(
            P("groups", "mem"),
            P("groups"),
            P("groups"),
            P("groups", None),
            P("mem", "tp"),
            P("mem", "tp"),
            P("mem", "tp"),
            P("mem", None),
            P("mem", None, "tp"),
            P("tp", "mem"),
            P(("groups", "mem"), None, "tp"),
            P(("groups", "mem"), None, "tp"),
        ),
        out_specs=P("groups", "mem"),
        check_vma=False,
    )
```

```python
import functools

import jax
import jax.numpy as jnp
from jax import lax
from jax.experimental import pallas as pl
from jax.experimental.pallas import tpu as pltpu
from jax.sharding import PartitionSpec as P

HEAD_WIDTH = 128
ADAPTER_RANK = 64
ADAPTER_COUNT = 32
LOG2E = 1.4426950408889634
SCORE_SCALE = HEAD_WIDTH ** (-0.5)
neg_floor = -1e30
MIB = 1024 * 1024
F32 = jnp.float32
BF16 = jnp.bfloat16


def params(limit, *semantics):
    return pltpu.CompilerParams(
        dimension_semantics=semantics or None, vmem_limit_bytes=int(limit)
    )


def whole(shape):
    return pl.BlockSpec(shape, lambda *_: (0,) * len(shape))


def in_hbm(x):
    return pltpu.with_memory_space_constraint(x, pltpu.HBM)


def in_vmem(x):
    return pltpu.with_memory_space_constraint(x, pltpu.VMEM)


def cost(flops, size, transcendentals=0):
    return pl.CostEstimate(
        flops=int(flops), bytes_accessed=int(size), transcendentals=int(transcendentals)
    )


VMEM_SPEC = pl.BlockSpec(memory_space=pltpu.VMEM)
SMEM_SPEC = pl.BlockSpec(memory_space=pltpu.SMEM)
ANY_SPEC = pl.BlockSpec(memory_space=pl.ANY)


def stage_kernel(pieces, *refs):
    count = len(refs[:-1]) // (pieces + 1)
    sources, targets, sems = refs[:count], refs[count:-1], refs[-1]
    copies = []
    for i, target in enumerate(targets):
        rows = pl.ds((i % pieces) * target.shape[0], target.shape[0])
        copies.append(
            pltpu.make_async_copy(sources[i // pieces].at[rows], target, sems.at[i])
        )
    for copy in copies:
        copy.start()
    for copy in copies:
        copy.wait()


def stage(*arrays, pieces=4):
    shapes = [(x.shape[0] // pieces,) + x.shape[1:] for x in arrays for _ in range(pieces)]
    return pl.pallas_call(
        functools.partial(stage_kernel, pieces),
        out_shape=tuple(pltpu.VMEM(shape, BF16) for shape in shapes),
        in_specs=[ANY_SPEC] * len(arrays),
        out_specs=(ANY_SPEC,) * len(shapes),
        scratch_shapes=[pltpu.SemaphoreType.DMA((len(shapes),))],
        compiler_params=params(MIB),
        cost_estimate=cost(0, sum(2 * x.size for x in arrays)),
        name="stage",
    )(*[in_hbm(x) for x in arrays])


def cache_kernel(pieces, index_ref, slot_hbm, select_hbm, *refs):
    sources, targets = refs[:2], refs[2 : 2 + 2 * pieces]
    near_ref, far_ref, slot_ref, select_ref, blocks_ref, sems = refs[2 + 2 * pieces :]
    count = 2 * pieces
    first = [
        pltpu.make_async_copy(slot_hbm, slot_ref, sems.at[count]),
        pltpu.make_async_copy(select_hbm, select_ref, sems.at[count + 1]),
    ]
    copies = []
    for i, target in enumerate(targets):
        rows = pl.ds((i % pieces) * target.shape[0], target.shape[0])
        copies.append(
            pltpu.make_async_copy(sources[i // pieces].at[rows], target, sems.at[i])
        )
    for copy in first + copies:
        copy.start()
    for copy in first:
        copy.wait()
    pages, total = blocks_ref.shape[2], slot_ref.shape[1]
    slots = index_ref[0] * pages + lax.broadcasted_iota(jnp.int32, (pages, total), 0)
    match = (slots == slot_ref[...]).astype(BF16)
    chosen = (select_ref[...] > 0).astype(BF16)
    held = lax.dot_general(
        chosen, match, (((1,), (1,)), ((), ())), preferred_element_type=F32
    )
    put_blocks(index_ref[0], held, blocks_ref, near_ref, far_ref)
    for copy in copies:
        copy.wait()


def stage_cache(index, page_cache_slot, selection, keys, values, mem_count, pieces=2):
    forks, total = selection.shape
    pages = keys.shape[0]
    line, fork_own = mem_count // 2, forks // mem_count
    shapes = [(x.shape[0] // pieces,) + x.shape[1:] for x in (keys, values) for _ in range(pieces)]
    mask = pltpu.VMEM((line, fork_own, pages), F32)
    return pl.pallas_call(
        functools.partial(cache_kernel, pieces),
        out_shape=tuple(pltpu.VMEM(shape, BF16) for shape in shapes) + (mask, mask),
        in_specs=[SMEM_SPEC] + [ANY_SPEC] * 4,
        out_specs=(ANY_SPEC,) * len(shapes) + (VMEM_SPEC,) * 2,
        scratch_shapes=[
            pltpu.VMEM((1, total), jnp.int32),
            pltpu.VMEM((forks, total), jnp.int32),
            pltpu.VMEM((mem_count, fork_own, pages), F32),
            pltpu.SemaphoreType.DMA((2 * pieces + 2,)),
        ],
        compiler_params=params(4 * MIB),
        cost_estimate=cost(0, 4 * keys.size),
        name="stage_cache",
    )(index, *[in_hbm(x) for x in (page_cache_slot.reshape(1, total), selection, keys, values)])


def fold_kernel(one_ref, two_ref, *out_refs):
    for i, out_ref in enumerate(out_refs):
        out_ref[...] = one_ref[i] + two_ref[i]


def fold(one, two):
    out = pltpu.VMEM(one.shape[1:], F32)
    return pl.pallas_call(
        fold_kernel,
        out_shape=(out,) * one.shape[0],
        in_specs=[VMEM_SPEC] * 2,
        out_specs=(VMEM_SPEC,) * one.shape[0],
        compiler_params=params(MIB * 2 + 16 * one.size),
        cost_estimate=cost(one.size, 12 * one.size),
        name="fold",
    )(in_vmem(one), two)


def two_first(terms):
    return [terms[i ^ (i >> 1)] for i in range(len(terms))]


def take_blocks(index, blocks_ref, near_ref, far_ref):
    place, parity = index // 2, index % 2
    for i in range(near_ref.shape[0]):
        at = 2 * (place ^ i)
        near_ref[i] = blocks_ref[at + parity]
        far_ref[i] = blocks_ref[at + 1 - parity]


def put_blocks(index, value, blocks_ref, near_ref, far_ref):
    count, rows, lanes = blocks_ref.shape
    own = value.shape[0] // count
    for i in range(count):
        blocks_ref[i, :own] = value[i * own : (i + 1) * own]
        if own < rows:
            blocks_ref[i, own:] = jnp.zeros((rows - own, lanes), F32)
    take_blocks(index, blocks_ref, near_ref, far_ref)


def first_kernel(
    index_ref,
    adapter_hbm,
    hidden_hbm,
    down_hbm,
    k_hbm,
    v_hbm,
    near_ref,
    far_ref,
    hidden_ref,
    adapter_ref,
    held,
    held_kv,
    rank_blocks,
    kv_blocks,
    sems,
):
    pieces, _, width = held.shape
    forks = hidden_ref.shape[0]
    kv_width = held_kv.shape[2]
    lanes = rank_blocks.shape[2]
    copies = [
        pltpu.make_async_copy(adapter_hbm, adapter_ref, sems.at[pieces + 3]),
        pltpu.make_async_copy(hidden_hbm, hidden_ref, sems.at[pieces + 2]),
        *[
            pltpu.make_async_copy(
                down_hbm.at[:, i * width : (i + 1) * width], held.at[i], sems.at[i]
            )
            for i in range(pieces)
        ],
        pltpu.make_async_copy(k_hbm, held_kv.at[0], sems.at[pieces]),
        pltpu.make_async_copy(v_hbm, held_kv.at[1], sems.at[pieces + 1]),
    ]
    for copy in copies:
        copy.start()
    copies[0].wait()
    fork_adapter = jnp.broadcast_to(adapter_ref[...].astype(F32), (HEAD_WIDTH, forks)).T
    lane_adapter = lax.broadcasted_iota(jnp.int32, (forks, HEAD_WIDTH), 1) // ADAPTER_RANK
    wanted = fork_adapter.astype(jnp.int32) - lane_adapter
    total = jnp.zeros((forks, HEAD_WIDTH), F32)
    copies[1].wait()
    for i in range(pieces):
        copies[2 + i].wait()
        block = jnp.dot(hidden_ref[...], held[i], preferred_element_type=F32)
        for j in range(width // HEAD_WIDTH):
            first = (i * width + j * HEAD_WIDTH) // ADAPTER_RANK
            part = block[:, j * HEAD_WIDTH : (j + 1) * HEAD_WIDTH]
            total += jnp.where(wanted == first, part, 0.0)
    flipped = total.T
    flipped = flipped[:ADAPTER_RANK] + flipped[ADAPTER_RANK:]
    if lanes > forks:
        flipped = jnp.concatenate([flipped, jnp.zeros((ADAPTER_RANK, lanes - forks), F32)], axis=1)
    at = slice(0, lanes)
    put_blocks(index_ref[0], flipped, rank_blocks, near_ref.at[:, :, at], far_ref.at[:, :, at])
    for i in range(2):
        copies[2 + pieces + i].wait()
        part = jnp.dot(hidden_ref[...], held_kv[i], preferred_element_type=F32)
        at = slice(lanes + i * kv_width, lanes + (i + 1) * kv_width)
        put_blocks(index_ref[0], part, kv_blocks, near_ref.at[:, :, at], far_ref.at[:, :, at])


def project_first(index, adapter, hidden, down, k_weight, v_weight, mem_count, width=256):
    forks, depth = hidden.shape
    columns, kv_width = down.shape[1], k_weight.shape[1]
    lanes = -(-forks // HEAD_WIDTH) * HEAD_WIDTH
    line, fork_own = mem_count // 2, forks // mem_count
    pieces = columns // width
    out = pltpu.VMEM((line, fork_own, lanes + 2 * kv_width), F32)
    weights = 2 * depth * (columns + 2 * kv_width)
    return pl.pallas_call(
        first_kernel,
        out_shape=(out, out, pltpu.VMEM(hidden.shape, BF16), pltpu.VMEM((1, forks), jnp.int32)),
        in_specs=[SMEM_SPEC] + [ANY_SPEC] * 5,
        out_specs=(VMEM_SPEC,) * 4,
        scratch_shapes=[
            pltpu.VMEM((pieces, depth, width), BF16),
            pltpu.VMEM((2, depth, kv_width), BF16),
            pltpu.VMEM((mem_count, fork_own, lanes), F32),
            pltpu.VMEM((mem_count, fork_own, kv_width), F32),
            pltpu.SemaphoreType.DMA((pieces + 4,)),
        ],
        compiler_params=params(weights + 4 * MIB),
        cost_estimate=cost(forks * weights, weights),
        name="project_first",
    )(index, *[in_hbm(x) for x in (adapter.reshape(1, forks), hidden, down, k_weight, v_weight)])


def project_kernel(start, extra, hidden_ref, q_hbm, *refs):
    up_hbm, part_ref, up_ref, held, sems = refs if extra else (None, refs[0], None, *refs[1:])
    pieces, _, width = held.shape
    copies = []
    for i in range(pieces):
        columns = pl.ds(start + i * width, width)
        copies.append(pltpu.make_async_copy(q_hbm.at[:, columns], held.at[i], sems.at[i]))
    if extra:
        copies.append(pltpu.make_async_copy(up_hbm, up_ref, sems.at[pieces]))
    for copy in copies:
        copy.start()
    for i in range(pieces):
        copies[i].wait()
        part_ref[:, i * width : (i + 1) * width] = jnp.dot(
            hidden_ref[...], held[i], preferred_element_type=F32
        )
    if extra:
        copies[-1].wait()


def project(hidden, q_weight, start, columns, up=None, width=256):
    forks, depth = hidden.shape
    pieces = columns // width
    weights = 2 * depth * columns
    extra = [] if up is None else [up]
    return pl.pallas_call(
        functools.partial(project_kernel, start, bool(extra)),
        out_shape=tuple(
            [pltpu.VMEM((forks, columns), F32)] + [pltpu.VMEM(x.shape, BF16) for x in extra]
        ),
        in_specs=[VMEM_SPEC] + [ANY_SPEC] * (1 + len(extra)),
        out_specs=(VMEM_SPEC,) * (1 + len(extra)),
        scratch_shapes=[
            pltpu.VMEM((pieces, depth, width), BF16),
            pltpu.SemaphoreType.DMA((pieces + 1,)),
        ],
        compiler_params=params(weights + 2 * MIB),
        cost_estimate=cost(forks * weights, weights + sum(2 * x.size for x in extra)),
        name="project",
    )(in_vmem(hidden), *[in_hbm(x) for x in [q_weight] + extra])


def line_sum_kernel(after_ref, *refs):
    parts, (own_ref, other_ref) = refs[:-2], refs[-2:]
    own_ref[...] = functools.reduce(jnp.add, [ref[0] for ref in parts])
    other_ref[...] = functools.reduce(jnp.add, [ref[1] for ref in parts])


def line_sum(parts, after):
    out = pltpu.VMEM(parts[0].shape[1:], F32)
    size = len(parts) * parts[0].size
    return pl.pallas_call(
        line_sum_kernel,
        out_shape=(out, out),
        in_specs=[ANY_SPEC] + [VMEM_SPEC] * len(parts),
        out_specs=(VMEM_SPEC,) * 2,
        compiler_params=params(2 * MIB + 8 * size),
        cost_estimate=cost(size, 4 * size),
        name="line_sum",
    )(after, *parts)


def join_kernel(first_ref, one_ref, two_ref, out_ref):
    cut = first_ref.shape[1]
    out_ref[:, :cut] = first_ref[...]
    out_ref[:, cut:] = (one_ref[...] + two_ref[...]).astype(BF16)


def join(first, one, two):
    rows, columns = first.shape[0], first.shape[1] + one.shape[1]
    return pl.pallas_call(
        join_kernel,
        out_shape=pltpu.VMEM((rows, columns), BF16),
        in_specs=[VMEM_SPEC] * 3,
        out_specs=VMEM_SPEC,
        compiler_params=params(MIB + 16 * rows * columns),
        cost_estimate=cost(one.size, 4 * rows * columns),
        name="join",
    )(first, in_vmem(one), two)


def delta_kernel(line, ranks, start, joint, index_ref, adapter_ref, *refs):
    first_refs = refs[:line]
    part_ref, up_ref, *out_refs, blocks_ref = refs[line:]
    forks, width = part_ref.shape[0], blocks_ref.shape[2]
    if joint:
        near_ref, far_ref = out_refs[0].at[:, 0], out_refs[0].at[:, 1]
        new_ref = out_refs[1]
        lanes = first_refs[0].shape[1] - new_ref.shape[1]
        total = functools.reduce(jnp.add, [ref[:, lanes:] for ref in first_refs])
        new_ref[...] = total.astype(BF16)
    else:
        near_ref, far_ref = out_refs
    acts = functools.reduce(jnp.add, [ref[:ranks, :forks] for ref in first_refs])
    acts = acts.astype(BF16).astype(F32)
    adapters = lax.broadcasted_iota(jnp.int32, (ADAPTER_COUNT, forks), 0)
    onehot = (adapters == adapter_ref[...]).astype(F32)
    spread = jnp.concatenate(
        [acts[r : r + 1, :] * onehot for r in range(ranks)], axis=0
    ).astype(BF16)
    for i in range(part_ref.shape[1] // width):
        delta = lax.dot_general(
            spread,
            up_ref[:, start + i * width : start + (i + 1) * width],
            (((0,), (0,)), ((), ())),
            preferred_element_type=F32,
        )
        at = slice(i * width, (i + 1) * width)
        put_blocks(
            index_ref[0],
            part_ref[:, at] + delta,
            blocks_ref,
            near_ref.at[:, :, at],
            far_ref.at[:, :, at],
        )


def add_delta(index, adapter, first_parts, part, up, mem_count, start, new_width=0, width=256):
    forks, columns = part.shape
    line, fork_own = mem_count // 2, forks // mem_count
    ranks = ADAPTER_RANK // mem_count
    if new_width:
        out = (
            pltpu.VMEM((line, 2, fork_own, columns), F32),
            pltpu.VMEM((fork_own, new_width), BF16),
        )
    else:
        out = (pltpu.VMEM((line, fork_own, columns), F32),) * 2
    return pl.pallas_call(
        functools.partial(delta_kernel, line, ranks, start, new_width > 0),
        out_shape=out,
        in_specs=[SMEM_SPEC] + [VMEM_SPEC] * (line + 3),
        out_specs=(VMEM_SPEC,) * 2,
        scratch_shapes=[pltpu.VMEM((mem_count, fork_own, width), F32)],
        compiler_params=params(4 * MIB),
        cost_estimate=cost(
            2 * forks * up.shape[0] * columns, 2 * up.shape[0] * columns + 8 * forks * columns
        ),
        name="add_delta",
    )(index, in_vmem(adapter), *first_parts, in_vmem(part), in_vmem(up))


def put_terms(lse):
    heads, forks = lse.shape
    high = lse.astype(BF16).astype(F32)
    rest = lse - high
    middle = rest.astype(BF16).astype(F32)
    low = rest - middle
    spare = jnp.zeros((HEAD_WIDTH - 3 * heads, forks), F32)
    return jnp.concatenate([high, middle, low, spare], axis=0).T.astype(BF16)


def get_terms(terms, heads):
    terms = terms.astype(F32)
    return terms[:, :heads] + terms[:, heads : 2 * heads] + terms[:, 2 * heads : 3 * heads]


def attend_kernel(pieces, q_ref, mask_ref, *refs):
    k_refs, v_refs, (out_ref, score_ref, lse_ref) = (
        refs[:pieces],
        refs[pieces : 2 * pieces],
        refs[2 * pieces :],
    )
    forks = q_ref.shape[0]
    kv_local, group = lse_ref.shape[:2]
    pages = score_ref.shape[0] // 2
    held = pages // pieces
    scale = SCORE_SCALE * LOG2E
    chosen_by = mask_ref[...].reshape(forks, pages)
    spare = jnp.zeros((forks, HEAD_WIDTH - pages % HEAD_WIDTH), F32)
    chosen_by = jnp.concatenate([chosen_by, spare], axis=1).T[:pages]
    mask = jnp.concatenate([chosen_by] * group, axis=1) > 0
    ones = jnp.ones((8, score_ref.shape[1]), BF16)

    def score(kv_head, queries, p):
        lanes = slice(kv_head * HEAD_WIDTH, (kv_head + 1) * HEAD_WIDTH)
        scores = lax.dot_general(
            k_refs[p // held][p % held, :, lanes],
            queries,
            (((1,), (1,)), ((), ())),
            preferred_element_type=F32,
        )
        score_ref[kv_head % 2 * pages + p] = scores
        return jnp.max(scores, axis=0, keepdims=True)

    def term(kv_head, peaks, top, p):
        lanes = slice(kv_head * HEAD_WIDTH, (kv_head + 1) * HEAD_WIDTH)
        scores = score_ref[kv_head % 2 * pages + p]
        weights = jnp.exp2((scores - peaks[p]) * scale).astype(BF16)
        chosen = jnp.where(mask[p : p + 1], peaks[p], neg_floor)
        factor = jnp.where(mask[p : p + 1], jnp.exp2((chosen - top) * scale), 0.0)
        values = jnp.concatenate([v_refs[p // held][p % held, :, lanes].T, ones], axis=0)
        return jnp.dot(values, weights, preferred_element_type=F32) * factor

    def head_queries(kv_head):
        first = kv_head * group
        return jnp.concatenate(
            [
                q_ref[:, (first + g) * HEAD_WIDTH : (first + g + 1) * HEAD_WIDTH]
                for g in range(group)
            ],
            axis=0,
        )

    queries = head_queries(0)
    peaks = [score(0, queries, p) for p in range(pages)]
    for kv_head in range(kv_local):
        chosen = [jnp.where(mask[p : p + 1], peaks[p], neg_floor) for p in range(pages)]
        top = functools.reduce(jnp.maximum, chosen)
        if kv_head + 1 < kv_local:
            queries = head_queries(kv_head + 1)
        acc = None
        next_peaks = []
        for p in range(pages):
            if kv_head + 1 < kv_local:
                next_peaks.append(score(kv_head + 1, queries, p))
            part = term(kv_head, peaks, top, p)
            acc = part if acc is None else acc + part
        peaks = next_peaks
        mass = acc[HEAD_WIDTH : HEAD_WIDTH + 1]
        some = mass > 0
        safe = jnp.where(some, mass, 1.0)
        rows = (acc[:HEAD_WIDTH] * jnp.where(some, 1.0 / safe, 0.0)).T
        lse = jnp.where(some, top * scale + jnp.log2(safe), neg_floor)
        for g in range(group):
            at = (kv_head * group + g) * HEAD_WIDTH
            out_ref[:, at : at + HEAD_WIDTH] = rows[g * forks : (g + 1) * forks].astype(BF16)
        lse_ref[kv_head] = jnp.concatenate(
            [lse[:, g * forks : (g + 1) * forks] for g in range(group)], axis=0
        )

    heads = kv_local * group
    out_ref[:, heads * HEAD_WIDTH :] = put_terms(lse_ref[...].reshape(heads, forks))


def attend(queries, keys, values, mask):
    forks, width = queries.shape
    held, page_len, kv_width = keys[0].shape
    pieces = len(keys)
    pages = held * pieces
    kv_local = kv_width // HEAD_WIDTH
    group = width // kv_width
    rows = group * forks
    return pl.pallas_call(
        functools.partial(attend_kernel, pieces),
        out_shape=pltpu.VMEM((forks, width + HEAD_WIDTH), BF16),
        in_specs=[VMEM_SPEC] * (2 + 2 * pieces),
        out_specs=VMEM_SPEC,
        scratch_shapes=[
            pltpu.VMEM((2 * pages, page_len, rows), F32),
            pltpu.VMEM((kv_local, group, forks), F32),
        ],
        compiler_params=params(10 * pages * page_len * rows + 4 * MIB),
        cost_estimate=cost(
            4 * pages * page_len * kv_local * rows * HEAD_WIDTH,
            4 * pages * page_len * kv_width + 4 * forks * width,
            pages * page_len * kv_local * rows,
        ),
        name="attend",
    )(queries, *[in_vmem(x) for x in [mask, *keys, *values]])


def merge_kernel(heads, kv_heads, sources, *refs):
    parts, (q_ref, new_ref, _, out_ref) = refs[:sources], refs[sources:]
    group = heads // kv_heads
    width = heads * HEAD_WIDTH
    lses = [get_terms(ref[:, width : width + HEAD_WIDTH], heads) for ref in parts]

    def new_head(i):
        return new_ref[:, i * HEAD_WIDTH : (i + 1) * HEAD_WIDTH].astype(F32)

    scores = []
    for h in range(heads):
        query = q_ref[:, h * HEAD_WIDTH : (h + 1) * HEAD_WIDTH].astype(F32)
        scores.append(jnp.sum(query * new_head(h // group), axis=1, keepdims=True))
    own = jnp.concatenate(scores, axis=1) * (SCORE_SCALE * LOG2E)
    top = functools.reduce(jnp.maximum, lses, own)
    own_weight = jnp.exp2(own - top)
    weights = [jnp.exp2(lse - top) for lse in lses]
    inverse = 1.0 / functools.reduce(jnp.add, weights, own_weight)
    own_weight = own_weight * inverse
    weights = [weight * inverse for weight in weights]
    for h in range(heads):
        lanes = slice(h * HEAD_WIDTH, (h + 1) * HEAD_WIDTH)
        total = own_weight[:, h : h + 1] * new_head(kv_heads + h // group)
        for weight, ref in zip(weights, parts):
            total += weight[:, h : h + 1] * ref[:, lanes].astype(F32)
        out_ref[:, lanes] = total.astype(BF16)


def merge(parts, queries, new, after, heads, kv_heads):
    fork_own, width = parts[0].shape
    size = len(parts) * fork_own * width
    return pl.pallas_call(
        functools.partial(merge_kernel, heads, kv_heads, len(parts)),
        out_shape=pltpu.VMEM((fork_own, heads * HEAD_WIDTH), BF16),
        in_specs=[VMEM_SPEC] * (len(parts) + 2) + [ANY_SPEC],
        out_specs=VMEM_SPEC,
        compiler_params=params(4 * size + 4 * MIB),
        cost_estimate=pl.CostEstimate(flops=4 * size, bytes_accessed=2 * size, transcendentals=0),
        name="merge",
    )(*parts, queries, new, after)


def output_kernel(context_ref, *refs):
    weight_refs, out_ref = refs[:-1], refs[-1]
    total = None
    for i, ref in enumerate(weight_refs):
        depth = ref.shape[0]
        part = jnp.dot(
            context_ref[:, i * depth : (i + 1) * depth], ref[...], preferred_element_type=F32
        )
        total = part if total is None else total + part
    out_ref[...] = total


def output_project(context, weights):
    forks, rows = context.shape
    columns = weights[0].shape[1]
    return pl.pallas_call(
        output_kernel,
        out_shape=pltpu.VMEM((forks, columns), F32),
        in_specs=[VMEM_SPEC] * (1 + len(weights)),
        out_specs=VMEM_SPEC,
        compiler_params=params(4 * MIB),
        cost_estimate=cost(2 * forks * rows * columns, 2 * rows * columns),
        name="output_project",
    )(context, *[in_vmem(x) for x in weights])


def finish_kernel(count, line, index_ref, *refs):
    near_refs, far_refs, out_ref = refs[:count], refs[count : 2 * count], refs[-1]
    place, parity = index_ref[0] // 2, index_ref[0] % 2
    rows = out_ref.shape[1]
    for group, side in ((near_refs, parity), (far_refs, 1 - parity)):
        for i in range(line):
            total = functools.reduce(jnp.add, [ref[i * rows : (i + 1) * rows] for ref in group])
            out_ref[2 * (place ^ i) + side] = total.astype(BF16)


def finish(index, near, far, mem_count):
    rows, columns = near[0].shape
    line = mem_count // 2
    return pl.pallas_call(
        functools.partial(finish_kernel, len(near), line),
        out_shape=jax.ShapeDtypeStruct((mem_count, rows // line, columns), BF16),
        in_specs=[SMEM_SPEC] + [VMEM_SPEC] * (2 * len(near)),
        out_specs=VMEM_SPEC,
        compiler_params=params(4 * MIB),
        cost_estimate=cost(0, 8 * rows * columns * len(near)),
        name="finish",
    )(index, *near, *far)


def shards(
    hidden,
    adapter,
    page_cache_slot,
    selection,
    query_projection_weight,
    key_projection_weight,
    value_projection_weight,
    adapter_down_weight,
    adapter_up_weight,
    output_projection_weight,
    prefix_key_cache,
    prefix_value_cache,
):
    mem_count = lax.axis_size("mem")
    mem_index = lax.axis_index("mem")
    forks = hidden.shape[0]
    fork_own = forks // mem_count
    q_width = query_projection_weight.shape[1]
    kv_width = key_projection_weight.shape[1]
    heads, kv_heads = q_width // HEAD_WIDTH, kv_width // HEAD_WIDTH
    pages = prefix_key_cache.shape[0]
    line = mem_count // 2
    index = mem_index.reshape(1)
    place, parity = mem_index // 2, mem_index % 2

    def swapped(x, step, cross=0):
        pairs = [(i, i ^ (2 * step + cross)) for i in range(mem_count)]
        return lax.ppermute(x, "mem", pairs)

    def along(blocks, cross=0):
        return [
            swapped(blocks[i], i, cross) if i or cross else blocks[0] for i in range(line)
        ]

    def gather(x):
        return jnp.concatenate([x] + [swapped(x, i) for i in range(1, line)], axis=0)

    def pair(x):
        return swapped(x, 0, 1)

    near_1, far_1, hidden, adapter = project_first(
        index, adapter, hidden, adapter_down_weight, key_projection_weight, value_projection_weight, mem_count
    )
    cut = q_width * 10 // 16 // 256 * 256
    part_a, up = project(
        hidden, query_projection_weight, 0, cut, adapter_up_weight.reshape(-1, q_width)
    )
    first_parts = fold(near_1, pair(far_1))
    first_parts, part_a, hidden = lax.optimization_barrier((first_parts, part_a, hidden))
    (part_b,) = project(hidden, query_projection_weight, cut, q_width - cut)
    first_parts = two_first(along(first_parts))[::-1]

    near_a, far_a = add_delta(index, adapter, first_parts, part_a, up, mem_count, 0)
    near_a, far_a, part_b = lax.optimization_barrier((near_a, far_a, part_b))
    both_b, own_new = add_delta(
        index, adapter, first_parts, part_b, up, mem_count, cut, 2 * kv_width
    )
    sums_a = fold(near_a, pair(far_a))
    own_b, other_b = line_sum(two_first(along(both_b)), sums_a[0])
    own_a = functools.reduce(jnp.add, along(sums_a)[::-1]).astype(BF16)
    own_queries = join(own_a, own_b, pair(other_b))

    *staged, near_mask, far_mask = stage_cache(
        index, page_cache_slot, selection, prefix_key_cache, prefix_value_cache, mem_count
    )
    keys, values = staged[: len(staged) // 2], staged[len(staged) // 2 :]
    near_queries = gather(own_queries)
    far_queries = pair(near_queries)
    near = attend(near_queries, keys, values, near_mask)
    far = attend(far_queries, keys, values, far_mask)
    blocks = (line, fork_own, q_width + HEAD_WIDTH)
    far, out_weight = lax.optimization_barrier((far, output_projection_weight))
    parts = along(near.reshape(blocks)) + along(far.reshape(blocks), 1)
    out_weights = stage(out_weight)
    context_own = merge(parts, own_queries, own_new, out_weights[0], heads, kv_heads)

    near_context = gather(context_own)
    far_context = jnp.concatenate([pair(context_own), pair(near_context[fork_own:])], axis=0)
    tp_count = lax.axis_size("tp")
    outs = []
    for context in (near_context, far_context):
        part = output_project(context, out_weights)
        terms = [part]
        for shift in range(1, tp_count):
            pairs = [(i, (i + shift) % tp_count) for i in range(tp_count)]
            terms.append(lax.ppermute(part, "tp", pairs))
        outs.append(terms)
    return finish(index, *outs, mem_count).reshape(forks, -1)


def solution(mesh):
    return jax.shard_map(
        shards,
        mesh=mesh,
        in_specs=(
            P("groups", "mem"),
            P("groups"),
            P("groups"),
            P("groups", None),
            P("mem", "tp"),
            P("mem", "tp"),
            P("mem", "tp"),
            P("mem", None),
            P("mem", None, "tp"),
            P("tp", "mem"),
            P(("groups", "mem"), None, "tp"),
            P(("groups", "mem"), None, "tp"),
        ),
        out_specs=P("groups", "mem"),
        check_vma=False,
    )
```
